32 devices in a mesh: seq: 16 (over z, y, x), opt: 2 (over core).
Axes of the slice: x: 2, y: 2, z: 4, core: 2. Of those that a mesh axis runs over, the one named last changes fastest.
Arguments:
- features: bfloat16 [2, 2048, 1536], P('opt', 'seq'), may hold values from -6 to 6
- tile_mask: int32 [2, 2048], P('opt', 'seq'), may hold values from 0 to 1, as said below
- lengths: int32 [2, 4], replicated, may hold values from 1 to 1024, 2048 in all within a row
- owners: int32 [768], replicated, may hold values from 0 to 767, each once
- layer_blocks: float32 [768, 96, 96], P(('seq', 'opt')), may hold values from -0.21875 to 0.21875
- stat_left: float32 [768, 96, 96], P(('seq', 'opt')), as said below
- stat_right: float32 [768, 96, 96], P(('seq', 'opt')), as said below
- io_weights: float32 [1536, 2, 768], P(('seq', 'opt')), may hold values from -0.21875 to 0.21875
- io_first: float32 [1536, 2, 768], P(('seq', 'opt')), may hold values from -0.00048828125 to 0.00048828125
- io_second: float32 [1536, 2, 768], P(('seq', 'opt')), may hold values from 5.5650915e-09 to 2.2218046e-08
- vectors: float32 [19, 768], replicated, may hold values from -3 to 3, as said below
- vec_first: float32 [19, 768], replicated, may hold values from -0.0017089844 to 0.0017089844
- vec_second: float32 [19, 768], replicated, may hold values from 5.2900113e-08 to 2.1160045e-07
Outputs:
- grad_norm: float32 [], replicated
- error_sum: float32 [], replicated
- masked_count: float32 [], replicated
- block_grads: float32 [768, 96, 96], P(('seq', 'opt'))
- left_new: float32 [768, 96, 96], P(('seq', 'opt'))
- right_new: float32 [768, 96, 96], P(('seq', 'opt'))
- blocks_new: float32 [768, 96, 96], P(('seq', 'opt'))
- io_first_new: float32 [1536, 2, 768], P(('seq', 'opt'))
- io_second_new: float32 [1536, 2, 768], P(('seq', 'opt'))
- io_new: float32 [1536, 2, 768], P(('seq', 'opt'))
- vec_first_new: float32 [19, 768], replicated
- vec_second_new: float32 [19, 768], replicated
- vec_new: float32 [19, 768], replicated
The draws below stay inside these ranges and needn't reach their ends.
Inputs may be any that keep to these rules, and one draw needn't show every extreme that they name: `tile_mask`: 1 marks a masked tile. `lengths`: the 4 slides of a micro-batch in order fill all 2048 tiles; the longest has half of 2048 tiles. `owners`: each natural block in exactly one slot. `stat_left`: symmetric positive definite. `stat_right`: symmetric positive definite. `vectors`: gains positive.
All inputs are finite; a program needn't handle non-finite values.
Results may differ from the reference program's by a relative error of at most 0.0006.
The reference program's roundings to bfloat16 on the way count: a program that leaves them out, or rounds other values in their place, can miss the bound.
Values may be sent and summed in bfloat16 or wider, within the bound.
No kernel may reach another device: no remote copies, remote signals or barrier semaphores. Data moves between devices by JAX's collectives and lax.ppermute only.
A program may use at most 256 MiB of HBM per device.

```python
import math
import jax
import jax.numpy as jnp
import numpy as np
from jax import lax

D = 768
HEADS = 16
HEAD_DIM = 48
FF = 3072
FEAT = 1536
LAYERS = 1
BRANCHES = 5
SEG0 = 1024
BLOCK = 96
SLIDES = 4
NEWTON = 6
STEP = 10
MICRO = 2
SEQ = 2048
NBLK = 768
NVEC = 19
PARAMS = 9451776


def shape_statistic(diagonal, noise_key):
    base_scale = 0.0526 * BLOCK / PARAMS
    noise_vals = jax.random.uniform(noise_key, (NBLK, BLOCK, BLOCK), jnp.float32, -1.0, 1.0)
    symmetric = 0.5 * (noise_vals + jnp.swapaxes(noise_vals, 1, 2))
    identity = jnp.eye(BLOCK, dtype=jnp.float32)
    off_diag = symmetric * (1.0 - identity) * (0.4 * base_scale * (6.0 / BLOCK) ** 0.5)
    return off_diag + identity[None, :, :] * diagonal[:, :, None]


def draw_stat_left(key, part):
    key = jax.random.fold_in(key, 11)
    diag_key, noise_key = jax.random.split(key)
    base_scale = 0.0526 * BLOCK / PARAMS
    diagonal = base_scale * jnp.exp(jax.random.uniform(diag_key, (NBLK, BLOCK), jnp.float32, 0.0, math.log(4.0)))
    return shape_statistic(diagonal, noise_key)


def draw_stat_right(key, part):
    key = jax.random.fold_in(key, 12)
    diag_key, noise_key = jax.random.split(key)
    base_scale = 0.0526 * BLOCK / PARAMS
    diagonal = base_scale * jnp.exp(jax.random.uniform(diag_key, (NBLK, BLOCK), jnp.float32, 0.0, math.log(4.0)))
    return shape_statistic(diagonal, noise_key)


def draw_tile_mask(key, part):
    key = jax.random.fold_in(key, 3)
    positions = jnp.arange(SEQ, dtype=jnp.int32)
    threshold = 150 + 300 * positions // SEQ
    random_ints = jax.random.randint(key, (MICRO, SEQ), 0, 1000, dtype=jnp.int32)
    return (random_ints < threshold[None, :]).astype(jnp.int32)


def draw_vectors(key, part):
    key = jax.random.fold_in(key, 5)
    per_layer = 8 + FF // D
    gain_rows = np.zeros((NVEC, 1), np.float32)
    scale_rows = np.full((NVEC, 1), 0.3, np.float32)
    for layer_id in range(LAYERS):
        for slot_id in (0, 5):
            gain_rows[layer_id * per_layer + slot_id] = 1.0
            scale_rows[layer_id * per_layer + slot_id] = 0.25
    gain_rows[LAYERS * per_layer] = 1.0
    scale_rows[LAYERS * per_layer] = 0.25
    scale_rows[NVEC - FEAT // D:] = 1.0
    noise_vals = jax.random.truncated_normal(key, -3.0, 3.0, (NVEC, D), jnp.float32)
    return jnp.asarray(gain_rows) + jnp.asarray(scale_rows) * noise_vals


def level_of(rng, shape, cuts, least, largest):
    factor_of = 1.0
    for position, blocks in cuts:
        steps = jax.random.uniform(jax.random.fold_in(jax.random.fold_in(rng, 6), position), (blocks,), jnp.float32, least / len(cuts), largest / len(cuts))
        factor_of = factor_of * jnp.repeat(jnp.exp(steps), shape[position] // blocks).reshape((-1,) + (1,) * (len(shape) - 1 - position))
    return factor_of


def length_profile(count, total, limit, skew):
    portions = [(1 << 20) // math.isqrt(grade ** skew) + 1 for grade in range(2, count + 1)]
    surplus, given = total - limit - (count - 1), [1] * (count - 1)
    while surplus > 0:
        movable = [i for i in range(count - 1) if given[i] < limit]
        mass, budget = sum([portions[i] for i in movable]), surplus
        for i in movable:
            extra = min(limit - given[i], max(1, budget * portions[i] // mass), surplus)
            given[i] = given[i] + extra
            surplus = surplus - extra
    return np.array([limit] + given)


def ragged_sizes(own_key, count, total, most, lean):
    if count == 2:
        one = jax.random.randint(own_key, (), max(1, total - most), min(most, total - 1) + 1)
        return jnp.stack([one, total - one])
    sizes = jnp.asarray(length_profile(count, total, most, lean), jnp.int32)
    couples = (count - 1) // 2
    donor, taker = sizes[1:1 + 2 * couples:2], sizes[2:2 + 2 * couples:2]
    margin = jnp.minimum(donor - 1, most - taker)
    shifted = jax.random.randint(jax.random.fold_in(own_key, 1), (couples,), 0, 1 << 20) % (margin + 1)
    sizes = sizes.at[1:1 + 2 * couples:2].set(donor - shifted).at[2:2 + 2 * couples:2].set(taker + shifted)
    return sizes[jax.random.permutation(jax.random.fold_in(own_key, 2), count)]


def gaussian(rng, dims, scale, most, cuts=(), held_as=jnp.bfloat16):
    values = jax.random.normal(rng, dims, jnp.float32) * scale
    if len(cuts) > 0:
        values = level_of(rng, dims, cuts, -0.22, 0.18) * values
    return jnp.clip(values, min=-most, max=most).astype(held_as)


def setup_inputs(seed: int = 0) -> dict:
    arg_keys = jax.random.split(jax.random.key(seed), 14)
    return {
        "features": gaussian(arg_keys[0], (MICRO, SEQ, FEAT), 1.0, 6.0, ((0, 2), (1, 16))),
        "tile_mask": draw_tile_mask(jax.random.fold_in(arg_keys[13], 71), 0),
        "lengths": jax.vmap(lambda own: ragged_sizes(own, SLIDES, SEQ, SEQ // 2, 2))(jax.random.split(arg_keys[2], MICRO)).reshape((MICRO, SLIDES)).astype(jnp.int32),
        "owners": jax.random.permutation(arg_keys[3], NBLK).astype(jnp.int32),
        "layer_blocks": gaussian(arg_keys[4], (NBLK, BLOCK, BLOCK), D ** -0.5, 0.21875, ((0, 32),), jnp.float32),
        "stat_left": draw_stat_left(jax.random.fold_in(arg_keys[13], 71), 0),
        "stat_right": draw_stat_right(jax.random.fold_in(arg_keys[13], 71), 0),
        "io_weights": gaussian(arg_keys[7], (FEAT, 2, D), D ** -0.5, 0.21875, ((0, 32),), jnp.float32),
        "io_first": gaussian(arg_keys[8], (FEAT, 2, D), (0.11 / PARAMS ** 0.5), 0.00048828125, ((0, 32),), jnp.float32),
        "io_second": jnp.clip(jnp.exp(math.log(2.2218046069610864e-08) - 1.3843914 * jax.random.uniform(arg_keys[9], (FEAT, 2, D), jnp.float32) ** level_of(arg_keys[9], (FEAT, 2, D), ((0, 32),), -0.2, 0.2)), 5.565091498738184e-09, 2.2218046069610864e-08),
        "vectors": draw_vectors(jax.random.fold_in(arg_keys[13], 71), 0),
        "vec_first": gaussian(arg_keys[11], (NVEC, D), (0.33 / PARAMS ** 0.5), 0.0017089844, (), jnp.float32),
        "vec_second": jnp.clip(jnp.exp(jax.random.uniform(arg_keys[12], (NVEC, D), jnp.float32, math.log(5.290011273473283e-08), math.log(2.1160045093893132e-07))), 5.290011273473283e-08, 2.1160045093893132e-07),
    }


@jax.custom_vjp
def low(v):
    return lax.optimization_barrier(v.astype(jnp.bfloat16)).astype(jnp.float32)

@jax.custom_vjp
def low_back(v):
    return v

def low_keep(v):
    return (low(v), None)

def low_pass(kept, grad):
    return (grad,)

def back_keep(v):
    return (v, None)

def back_low(kept, grad):
    return (low(grad),)
low.defvjp(low_keep, low_pass)
low_back.defvjp(back_keep, back_low)
norm_eps = 1e-05
clip_limit = 1.0
beta_one = 0.9
beta_two = 0.95
adam_eps = 1e-08
rate_adam = 0.01
rate_vector = 0.2
weight_decay = 0.05
beta_stat = 0.95
rate_shampoo = 0.05
root_eps = 1e-12
masked_score = -1e+30
highest = lax.Precision.HIGHEST

def layer_norm(values, gain, shift):
    centred = values - lax.optimization_barrier(jnp.mean(values, axis=-1, keepdims=True))
    spread = lax.optimization_barrier(jnp.mean(centred * centred, axis=-1, keepdims=True))
    return centred * lax.rsqrt(spread + norm_eps) * gain + shift

def sine_places(places):
    half_width = D // 2
    freq_rates = jnp.exp(jnp.arange(half_width, dtype=jnp.float32) * (-math.log(10000.0) / half_width))
    angles = (places.astype(jnp.float32) / 64.0)[:, None] * freq_rates[None, :]
    return jnp.concatenate([jnp.sin(angles), jnp.cos(angles)], axis=1)

def slide_ids(lengths_row, places):
    slide_ends = jnp.cumsum(lengths_row).astype(jnp.int32)
    return lax.optimization_barrier(jnp.sum((places[..., None] >= slide_ends[:-1]).astype(jnp.int32), axis=-1)).astype(jnp.int32)

def slide_offsets(lengths_row, places):
    slide_ends = jnp.cumsum(lengths_row).astype(jnp.int32)
    slide_starts = (slide_ends - lengths_row).astype(jnp.int32)
    owner_ids = slide_ids(lengths_row, places)
    match_rows = owner_ids[:, None] == jnp.arange(SLIDES, dtype=jnp.int32)[None, :]
    picked = lax.optimization_barrier(jnp.sum(jnp.where(match_rows, slide_starts[None, :], 0), axis=1)).astype(jnp.int32)
    return (places - picked).astype(jnp.int32)

def head_offsets(dilation):
    return np.arange(HEADS) % dilation

def pick_rows(values, dilation):
    row_count = values.shape[0] // dilation
    shaped = values.reshape((row_count, dilation) + values.shape[1:])
    return shaped[:, head_offsets(dilation), np.arange(HEADS)]

def spread_rows(values, dilation, filler):
    row_count = values.shape[0]
    hit_mask = np.arange(dilation)[:, None] == head_offsets(dilation)[None, :]
    hit_mask = hit_mask.reshape((1, dilation, HEADS) + (1,) * (values.ndim - 2))
    spread_out = jnp.where(hit_mask, values[:, None], filler)
    return spread_out.reshape((row_count * dilation,) + values.shape[1:])

def assemble(natural):
    per_layer = natural.reshape(LAYERS, -1, BLOCK, BLOCK)
    col_count = (4 * D + FF) // BLOCK
    wide_count = D // BLOCK * col_count
    upper_mats = per_layer[:, :wide_count].reshape(LAYERS, D // BLOCK, col_count, BLOCK, BLOCK)
    upper_mats = upper_mats.transpose(0, 1, 3, 2, 4).reshape(LAYERS, D, 4 * D + FF)
    lower_mats = per_layer[:, wide_count:].reshape(LAYERS, FF // BLOCK, D // BLOCK, BLOCK, BLOCK)
    lower_mats = lower_mats.transpose(0, 1, 3, 2, 4).reshape(LAYERS, FF, D)
    return (upper_mats, lower_mats)

def unpack(vector_set):
    per_layer = 8 + FF // D
    return (vector_set[:LAYERS * per_layer].reshape(LAYERS, per_layer, D), vector_set[LAYERS * per_layer:])

def matmul(left, right):
    return jnp.matmul(left, right, precision=highest)

def segment_attend(query_part, key_part, value_part, doc_part):
    raw_scores = low_back(jnp.einsum('qhd,khd->hqk', query_part, key_part, precision=highest) * HEAD_DIM ** (-0.5))
    doc_heads = jnp.transpose(doc_part)
    same_slide = doc_heads[:, :, None] == doc_heads[:, None, :]
    scores = jnp.where(same_slide, raw_scores, masked_score)
    totals = jax.nn.logsumexp(scores, axis=-1)
    weights_p = low(jnp.exp(scores - totals[..., None]))
    output = low_back(jnp.einsum('hqk,khd->qhd', weights_p, value_part, precision=highest))
    return (output, jnp.transpose(totals))

def segment_step(parts):
    return jax.checkpoint(segment_attend)(parts[0], parts[1], parts[2], parts[3])

def dilated(queries, key_all, value_all, docs):
    outputs, totals_all = ([], [])
    for branch in range(BRANCHES):
        dilation = 2 ** branch
        segment = min(SEG0 * dilation, SEQ)
        sections = SEQ // segment
        picked = [pick_rows(part_all, dilation).reshape(sections, -1, HEADS, HEAD_DIM) for part_all in (queries, key_all, value_all)]
        doc_rows = pick_rows(jnp.broadcast_to(docs[:, None], (SEQ, HEADS)), dilation).reshape(sections, -1, HEADS)
        output, totals = lax.map(segment_step, (picked[0], picked[1], picked[2], doc_rows))
        outputs.append(spread_rows(output.reshape(-1, HEADS, HEAD_DIM), dilation, 0.0))
        totals_all.append(spread_rows(totals.reshape(-1, HEADS), dilation, masked_score))
    stacked = jnp.stack(totals_all)
    grand_total = jax.nn.logsumexp(stacked, axis=0)
    mixed_out = jnp.zeros_like(outputs[0])
    for branch in range(BRANCHES):
        mixed_out = mixed_out + jnp.exp(stacked[branch] - grand_total)[..., None] * outputs[branch]
    return mixed_out

def block_forward(hidden, upper_mat, lower_mat, row_set, docs):
    normed = low(layer_norm(hidden, row_set[0], row_set[1]))
    biases = jnp.concatenate([row_set[2], jnp.zeros_like(row_set[2]), row_set[3]])
    packed = low(low_back(matmul(normed, upper_mat[:, :3 * D]) + biases[None, :]))
    triple = packed.reshape(SEQ, 3, HEADS, HEAD_DIM)
    mixed_out = dilated(triple[:, 0], triple[:, 1], triple[:, 2], docs).reshape(SEQ, D)
    middle = hidden + low_back(matmul(low(mixed_out), upper_mat[:, 3 * D:4 * D]) + row_set[4][None, :])
    second = low(layer_norm(middle, row_set[5], row_set[6]))
    before = low_back(matmul(second, upper_mat[:, 4 * D:]) + row_set[8:].reshape(FF)[None, :])
    active = low(jax.nn.gelu(before, approximate=True))
    return middle + low_back(matmul(active, lower_mat) + row_set[7][None, :])

def sequence_error(targets, mask_row, lengths_row, upper_mats, lower_mats, io_low, layer_rows, tail_rows):
    chosen = mask_row[:, None] > 0
    token_vec = tail_rows[3 + FEAT // D:].reshape(FEAT)
    inputs = low(jnp.where(chosen, token_vec[None, :], targets))
    places = jnp.arange(SEQ, dtype=jnp.int32)
    docs = slide_ids(lengths_row, places)
    hidden = low_back(matmul(inputs, io_low[:, 0, :]) + tail_rows[2][None, :]) + sine_places(slide_offsets(lengths_row, places))
    for layer_id in range(LAYERS):
        hidden = block_forward(hidden, upper_mats[layer_id], lower_mats[layer_id], layer_rows[layer_id], docs)
    final = low(layer_norm(hidden, tail_rows[0], tail_rows[1]))
    head_bias = tail_rows[3:3 + FEAT // D].reshape(FEAT)
    predict = low_back(matmul(final, io_low[:, 1, :].T) + head_bias[None, :])
    difference = predict - targets
    return jnp.sum(jnp.where(chosen, difference * difference, 0.0))

def inverse_root(matrix):
    identity = jnp.eye(matrix.shape[-1], dtype=jnp.float32)
    regular = matrix + root_eps * identity
    frob_norm = jnp.sqrt(lax.optimization_barrier(jnp.sum(regular * regular, axis=(1, 2), keepdims=True)))
    scaled = 2.5 / frob_norm
    root_mat = identity * jnp.sqrt(jnp.sqrt(scaled))
    moving = regular * scaled
    for sweep_id in range(NEWTON):
        factor = (5.0 * identity - moving) * 0.25
        root_mat = jnp.einsum('kij,kjl->kil', root_mat, factor, precision=highest)
        square = jnp.einsum('kij,kjl->kil', factor, factor, precision=highest)
        fourth = jnp.einsum('kij,kjl->kil', square, square, precision=highest)
        moving = jnp.einsum('kij,kjl->kil', fourth, moving, precision=highest)
    return root_mat

def adam_update(weight, first_mom, second_mom, grad, rate, decay):
    first_new = beta_one * first_mom + (1.0 - beta_one) * grad
    second_new = beta_two * second_mom + (1.0 - beta_two) * grad * grad
    first_hat = first_new / (1.0 - beta_one ** STEP)
    second_hat = second_new / (1.0 - beta_two ** STEP)
    return (first_new, second_new, weight - rate * (first_hat / (jnp.sqrt(second_hat) + adam_eps) + decay * weight))

def reference(features, tile_mask, lengths, owners, layer_blocks, stat_left, stat_right, io_weights, io_first, io_second, vectors, vec_first, vec_second):
    tile_count = jnp.sum(tile_mask.astype(jnp.float32))
    targets_all = features.astype(jnp.float32)

    def objective(blocks, io_full, vector_set):
        natural = jnp.zeros_like(blocks).at[owners].set(low(blocks))
        upper_mats, lower_mats = assemble(natural)
        layer_rows, tail_rows = unpack(vector_set)
        io_low = low(io_full)
        error_total = jnp.zeros((), jnp.float32)
        for micro_id in range(MICRO):
            error_total = error_total + sequence_error(targets_all[micro_id], tile_mask[micro_id], lengths[micro_id], upper_mats, lower_mats, io_low, layer_rows, tail_rows)
        return (error_total / tile_count, error_total)
    loss_value, pullback, error_total = jax.vjp(objective, layer_blocks, io_weights, vectors, has_aux=True)
    grad_blocks, grad_io, grad_vec = pullback(jnp.ones((), jnp.float32))
    norm_sq = jnp.sum(grad_blocks * grad_blocks) + jnp.sum(grad_io * grad_io) + jnp.sum(grad_vec * grad_vec)
    grad_norm = jnp.sqrt(norm_sq)
    factor = jnp.minimum(1.0, clip_limit / grad_norm)
    block_grads = grad_blocks * factor
    left_new = beta_stat * stat_left + (1.0 - beta_stat) * jnp.einsum('kij,klj->kil', block_grads, block_grads, precision=highest)
    right_new = beta_stat * stat_right + (1.0 - beta_stat) * jnp.einsum('kji,kjl->kil', block_grads, block_grads, precision=highest)
    direction = jnp.einsum('kij,kjl->kil', inverse_root(left_new), block_grads, precision=highest)
    direction = jnp.einsum('kij,kjl->kil', direction, inverse_root(right_new), precision=highest)
    blocks_new = layer_blocks - rate_shampoo * direction
    io_first_new, io_second_new, io_new = adam_update(io_weights, io_first, io_second, grad_io * factor, rate_adam, weight_decay)
    vec_first_new, vec_second_new, vec_new = adam_update(vectors, vec_first, vec_second, grad_vec * factor, rate_vector, 0.0)
    return (grad_norm, error_total, tile_count, block_grads, left_new, right_new, blocks_new, io_first_new, io_second_new, io_new, vec_first_new, vec_second_new, vec_new)
```

```python
from functools import partial
import math

import jax
import jax.numpy as jnp
import numpy as np
from jax import lax
from jax.experimental import pallas as pl
from jax.experimental.pallas import tpu as pltpu
from jax.sharding import PartitionSpec as P

D = 768
HEADS = 16
HEAD_DIM = 48
FF = 3072
FEAT = 1536
LAYERS = 1
BRANCHES = 5
SEG0 = 1024
BLOCK = 96
SLIDES = 4
NEWTON = 6
STEP = 10


norm_eps = 1e-05
clip_limit = 1.0
beta_one = 0.9
beta_two = 0.95
adam_eps = 1e-08
rate_adam = 0.01
rate_vector = 0.2
weight_decay = 0.05
beta_stat = 0.95
rate_shampoo = 0.05
root_eps = 1e-12
masked_score = -1e30
highest = lax.Precision.HIGHEST


def from_partner(value, axis, stride):
    mask = 2**stride
    pairs = [(source, source ^ mask) for source in range(lax.axis_size(axis))]
    return lax.ppermute(value, axis, pairs)


def for_sending(shard):

    def short(part):
        return part.astype(jnp.bfloat16) if part.dtype == jnp.float32 else part

    return jax.tree.map(short, shard)


def layer_norm(values, gain, shift):
    centred = values - jnp.mean(values, axis=-1, keepdims=True)
    spread = jnp.mean(centred * centred, axis=-1, keepdims=True)
    return centred * lax.rsqrt(spread + norm_eps) * gain + shift


def sine_places(places):
    half_width = D // 2
    freq_rates = jnp.exp(
        jnp.arange(half_width, dtype=jnp.float32) * (-math.log(10000.0) / half_width)
    )
    angles = (places.astype(jnp.float32) / 64.0)[:, None] * freq_rates[None, :]
    return jnp.concatenate([jnp.sin(angles), jnp.cos(angles)], axis=1)


def slide_ids(lengths_row, places):
    slide_ends = jnp.cumsum(lengths_row)
    return jnp.sum((places[..., None] >= slide_ends[:-1]).astype(jnp.int32), axis=-1)


def slide_offsets(lengths_row, places):
    slide_ends = jnp.cumsum(lengths_row)
    slide_starts = slide_ends - lengths_row
    owner_ids = slide_ids(lengths_row, places)
    match_rows = owner_ids[:, None] == jnp.arange(SLIDES, dtype=jnp.int32)[None, :]
    picked = jnp.sum(jnp.where(match_rows, slide_starts[None, :], 0), axis=1)
    return places - picked


def head_offsets(dilation):
    return np.arange(HEADS) % dilation


def pick_rows(values, dilation):
    row_count = values.shape[0] // dilation
    shaped = values.reshape((row_count, dilation) + values.shape[1:])
    return shaped[:, head_offsets(dilation), np.arange(HEADS)]


def spread_rows(values, dilation, filler):
    row_count = values.shape[0]
    hit_mask = np.arange(dilation)[:, None] == head_offsets(dilation)[None, :]
    hit_mask = hit_mask.reshape((1, dilation, HEADS) + (1,) * (values.ndim - 2))
    spread_out = jnp.where(hit_mask, values[:, None], filler)
    return spread_out.reshape((row_count * dilation,) + values.shape[1:])


def branch_geom(branch, tok_dev, seq_len):
    dilation = 2**branch
    segment = min(SEG0 * dilation, seq_len)
    return (dilation, segment, max(1, segment // tok_dev))


def branch_docs(lengths_row, first_place, row_count, dilation):
    places = (
        first_place
        + jnp.asarray(head_offsets(dilation), jnp.int32)[None, :]
        + dilation * jnp.arange(row_count, dtype=jnp.int32)[:, None]
    )
    return slide_ids(lengths_row, places)


def contract_rows(left, right):
    return lax.dot_general(
        left, right, (((0,), (0,)), ((), ())), preferred_element_type=jnp.float32
    )


def contract_cols(left, right):
    return lax.dot_general(
        left, right, (((1,), (1,)), ((), ())), preferred_element_type=jnp.float32
    )


def assemble(natural):
    per_layer = natural.reshape(LAYERS, -1, BLOCK, BLOCK)
    col_count = (4 * D + FF) // BLOCK
    wide_count = D // BLOCK * col_count
    upper_mats = per_layer[:, :wide_count].reshape(LAYERS, D // BLOCK, col_count, BLOCK, BLOCK)
    upper_mats = upper_mats.transpose(0, 1, 3, 2, 4).reshape(LAYERS, D, 4 * D + FF)
    lower_mats = per_layer[:, wide_count:].reshape(LAYERS, FF // BLOCK, D // BLOCK, BLOCK, BLOCK)
    lower_mats = lower_mats.transpose(0, 1, 3, 2, 4).reshape(LAYERS, FF, D)
    return (upper_mats, lower_mats)


def disassemble(upper_mats, lower_mats):
    col_count = (4 * D + FF) // BLOCK
    top_part = upper_mats.reshape(LAYERS, D // BLOCK, BLOCK, col_count, BLOCK).transpose(
        0, 1, 3, 2, 4
    )
    top_part = top_part.reshape(LAYERS, -1, BLOCK, BLOCK)
    bottom_part = lower_mats.reshape(LAYERS, FF // BLOCK, BLOCK, D // BLOCK, BLOCK).transpose(
        0, 1, 3, 2, 4
    )
    bottom_part = bottom_part.reshape(LAYERS, -1, BLOCK, BLOCK)
    return jnp.concatenate([top_part, bottom_part], axis=1).reshape(-1, BLOCK, BLOCK)


def unpack(vector_set):
    per_layer = 8 + FF // D
    return (
        vector_set[: LAYERS * per_layer].reshape(LAYERS, per_layer, D),
        vector_set[LAYERS * per_layer :],
    )


def collect_pairs(pieces, bit_counts, seq_index):
    pieces = list(pieces)
    for bit_id in range(max(bit_counts + [0])):
        active_ids = [branch for branch in range(len(pieces)) if bit_counts[branch] > bit_id]
        outgoing = jnp.concatenate([pieces[branch] for branch in active_ids], axis=0)
        partner = from_partner(outgoing, "seq", bit_id)
        lower_side = seq_index // 2**bit_id % 2 == 0
        offset_at = 0
        for branch in active_ids:
            my_part = pieces[branch]
            part_size = my_part.shape[0]
            their_part = partner[offset_at : offset_at + part_size]
            offset_at = offset_at + part_size
            pieces[branch] = jnp.where(
                lower_side,
                jnp.concatenate([my_part, their_part], 0),
                jnp.concatenate([their_part, my_part], 0),
            )
    return pieces


def return_pairs(pieces, bit_counts, seq_index):
    pieces = list(pieces)
    for bit_id in reversed(range(max(bit_counts + [0]))):
        active_ids = [branch for branch in range(len(pieces)) if bit_counts[branch] > bit_id]
        lower_side = seq_index // 2**bit_id % 2 == 0
        kept_parts, sent_parts = ([], [])
        for branch in active_ids:
            half_size = pieces[branch].shape[0] // 2
            first_part = pieces[branch][:half_size]
            second_part = pieces[branch][half_size:]
            kept_parts.append(jnp.where(lower_side, first_part, second_part))
            sent_parts.append(jnp.where(lower_side, second_part, first_part))
        partner = from_partner(for_sending(jnp.concatenate(sent_parts, axis=0)), "seq", bit_id)
        offset_at = 0
        for branch, kept_part in zip(active_ids, kept_parts):
            part_size = kept_part.shape[0]
            pieces[branch] = kept_part + partner[offset_at : offset_at + part_size]
            offset_at = offset_at + part_size
    return pieces


def score_block(query_rows, key_rows, query_docs, key_docs):
    raw_scores = jnp.einsum(
        "sqhd,skhd->shqk", query_rows, key_rows, preferred_element_type=jnp.float32
    ) * HEAD_DIM ** (-0.5)
    same_slide = (
        jnp.transpose(query_docs, (0, 2, 1))[..., None]
        == jnp.transpose(key_docs, (0, 2, 1))[:, :, None, :]
    )
    return jnp.where(same_slide, raw_scores, masked_score)


def attend_forward(packed, lengths_row, seq_len, seq_index):
    tok_dev = packed.shape[0]
    triple = packed.reshape(tok_dev, 3, HEADS, HEAD_DIM)
    queries, key_all, value_all = (triple[:, 0], triple[:, 1], triple[:, 2])
    geoms = [branch_geom(branch, tok_dev, seq_len) for branch in range(BRANCHES)]
    local_pairs = [
        jnp.stack([pick_rows(key_all, geom[0]), pick_rows(value_all, geom[0])], axis=1).reshape(
            -1, 2 * D
        )
        for geom in geoms
    ]
    bit_counts = [geom[2].bit_length() - 1 for geom in geoms]
    joined = collect_pairs(local_pairs, bit_counts, seq_index)
    kept_state, outputs, totals_all = ([], [], [])
    for branch in range(BRANCHES):
        dilation, segment, group_size = geoms[branch]
        sections = max(1, tok_dev // segment)
        query_rows = pick_rows(queries, dilation).reshape(sections, -1, HEADS, HEAD_DIM)
        pair_rows = joined[branch].reshape(sections, -1, 2, HEADS, HEAD_DIM)
        key_rows = pair_rows[:, :, 0]
        value_rows = pair_rows[:, :, 1]
        query_docs = branch_docs(
            lengths_row, seq_index * tok_dev, tok_dev // dilation, dilation
        ).reshape(sections, -1, HEADS)
        group_first = seq_index // group_size * group_size * tok_dev
        key_docs = branch_docs(lengths_row, group_first, joined[branch].shape[0], dilation).reshape(
            sections, -1, HEADS
        )
        scores = score_block(query_rows, key_rows, query_docs, key_docs)
        totals = jax.nn.logsumexp(scores, axis=-1)
        softmax_rows = jnp.exp(scores - totals[..., None]).astype(jnp.bfloat16)
        output = jnp.einsum(
            "shqk,skhd->sqhd", softmax_rows, value_rows, preferred_element_type=jnp.float32
        ).reshape(-1, HEADS, HEAD_DIM)
        totals_rows = jnp.transpose(totals, (0, 2, 1)).reshape(-1, HEADS)
        kept_state.append(
            (query_rows, key_rows, value_rows, query_docs, key_docs, output, totals_rows)
        )
        outputs.append(spread_rows(output, dilation, 0.0))
        totals_all.append(spread_rows(totals_rows, dilation, masked_score))
    stacked = jnp.stack(totals_all)
    grand_total = jax.nn.logsumexp(stacked, axis=0)
    mixed_out = jnp.zeros_like(outputs[0])
    for branch in range(BRANCHES):
        mixed_out = mixed_out + jnp.exp(stacked[branch] - grand_total)[..., None] * outputs[branch]
    return (mixed_out, (mixed_out, grand_total, kept_state))


def attend_backward(grad_mixed, attention_state, seq_len, seq_index):
    mixed_out, grand_total, kept_state = attention_state
    tok_dev = grad_mixed.shape[0]
    score_scale = HEAD_DIM ** (-0.5)
    grad_query = jnp.zeros(grad_mixed.shape, jnp.float32)
    key_terms, bit_counts, dilations = ([], [], [])
    for branch in range(BRANCHES):
        dilation, segment, group_size = branch_geom(branch, tok_dev, seq_len)
        query_rows, key_rows, value_rows, query_docs, key_docs, output, totals_rows = kept_state[
            branch
        ]
        sections = query_rows.shape[0]
        weight = jnp.exp(totals_rows - pick_rows(grand_total, dilation))
        grad_picked = pick_rows(grad_mixed, dilation)
        grad_output = (
            (weight[..., None] * grad_picked)
            .astype(jnp.bfloat16)
            .reshape(sections, -1, HEADS, HEAD_DIM)
        )
        grad_totals = weight * jnp.sum(
            grad_picked * (output - pick_rows(mixed_out, dilation)), axis=-1
        )
        grad_totals = jnp.transpose(grad_totals.reshape(sections, -1, HEADS), (0, 2, 1))
        totals = jnp.transpose(totals_rows.reshape(sections, -1, HEADS), (0, 2, 1))
        softmax_rows = jnp.exp(
            score_block(query_rows, key_rows, query_docs, key_docs) - totals[..., None]
        )
        grad_value = jnp.einsum(
            "shqk,sqhd->skhd",
            softmax_rows.astype(jnp.bfloat16),
            grad_output,
            preferred_element_type=jnp.float32,
        )
        grad_probs = jnp.einsum(
            "sqhd,skhd->shqk", grad_output, value_rows, preferred_element_type=jnp.float32
        )
        inner_sum = jnp.sum(softmax_rows * grad_probs, axis=-1, keepdims=True)
        grad_scores = (softmax_rows * (grad_probs - inner_sum + grad_totals[..., None])).astype(
            jnp.bfloat16
        )
        grad_q = (
            jnp.einsum("shqk,skhd->sqhd", grad_scores, key_rows, preferred_element_type=jnp.float32)
            * score_scale
        )
        grad_k = (
            jnp.einsum(
                "shqk,sqhd->skhd", grad_scores, query_rows, preferred_element_type=jnp.float32
            )
            * score_scale
        )
        grad_query = grad_query + spread_rows(grad_q.reshape(-1, HEADS, HEAD_DIM), dilation, 0.0)
        key_terms.append(
            jnp.stack(
                [grad_k.reshape(-1, HEADS, HEAD_DIM), grad_value.reshape(-1, HEADS, HEAD_DIM)],
                axis=1,
            ).reshape(-1, 2 * D)
        )
        bit_counts.append(group_size.bit_length() - 1)
        dilations.append(dilation)
    own_terms = return_pairs(key_terms, bit_counts, seq_index)
    grad_key = jnp.zeros(grad_mixed.shape, jnp.float32)
    grad_val = jnp.zeros(grad_mixed.shape, jnp.float32)
    for branch in range(BRANCHES):
        pair_rows = own_terms[branch].reshape(-1, 2, HEADS, HEAD_DIM)
        grad_key = grad_key + spread_rows(pair_rows[:, 0], dilations[branch], 0.0)
        grad_val = grad_val + spread_rows(pair_rows[:, 1], dilations[branch], 0.0)
    return jnp.stack([grad_query, grad_key, grad_val], axis=1).reshape(tok_dev, 3 * D)


def layer_forward(hidden, upper_mat, lower_mat, row_set, lengths_row, seq_len, seq_index):
    normed = layer_norm(hidden, row_set[0], row_set[1]).astype(jnp.bfloat16)
    biases = jnp.concatenate([row_set[2], jnp.zeros_like(row_set[2]), row_set[3]])
    packed = (
        jnp.dot(normed, upper_mat[:, : 3 * D], preferred_element_type=jnp.float32) + biases[None, :]
    ).astype(jnp.bfloat16)
    mixed_out, attention_state = attend_forward(packed, lengths_row, seq_len, seq_index)
    mixed_low = mixed_out.reshape(-1, D).astype(jnp.bfloat16)
    middle = (
        hidden
        + jnp.dot(mixed_low, upper_mat[:, 3 * D : 4 * D], preferred_element_type=jnp.float32)
        + row_set[4][None, :]
    )
    second = layer_norm(middle, row_set[5], row_set[6]).astype(jnp.bfloat16)
    before = (
        jnp.dot(second, upper_mat[:, 4 * D :], preferred_element_type=jnp.float32)
        + row_set[8:].reshape(-1)[None, :]
    )
    active = jax.nn.gelu(before, approximate=True).astype(jnp.bfloat16)
    result = (
        middle
        + jnp.dot(active, lower_mat, preferred_element_type=jnp.float32)
        + row_set[7][None, :]
    )
    return (result, (hidden, normed, mixed_low, middle, second, before, active, attention_state))


def layer_backward(grad_result, upper_mat, lower_mat, row_set, layer_state, seq_len, seq_index):
    hidden, normed, mixed_low, middle, second, before, active, attention_state = layer_state
    grad_out = grad_result.astype(jnp.bfloat16)
    grad_lower = contract_rows(active, grad_out)
    grad_fc2_bias = jnp.sum(grad_out, axis=0, dtype=jnp.float32)
    grad_active = contract_cols(grad_out, lower_mat)
    gelu_value, gelu_back = jax.vjp(partial(jax.nn.gelu, approximate=True), before)
    grad_before = gelu_back(grad_active)[0].astype(jnp.bfloat16)
    grad_fc1 = contract_rows(second, grad_before)
    grad_fc1_bias = jnp.sum(grad_before, axis=0, dtype=jnp.float32)
    grad_second = contract_cols(grad_before, upper_mat[:, 4 * D :])
    norm_value, norm_back = jax.vjp(layer_norm, middle, row_set[5], row_set[6])
    grad_middle, grad_gain_two, grad_shift_two = norm_back(grad_second)
    grad_middle = grad_middle + grad_result
    grad_branch = grad_middle.astype(jnp.bfloat16)
    grad_proj = contract_rows(mixed_low, grad_branch)
    grad_proj_bias = jnp.sum(grad_branch, axis=0, dtype=jnp.float32)
    grad_mixed = contract_cols(grad_branch, upper_mat[:, 3 * D : 4 * D]).reshape(
        -1, HEADS, HEAD_DIM
    )
    grad_packed = attend_backward(grad_mixed, attention_state, seq_len, seq_index).astype(
        jnp.bfloat16
    )
    grad_qkv = contract_rows(normed, grad_packed)
    packed_sums = jnp.sum(grad_packed, axis=0, dtype=jnp.float32)
    grad_normed = contract_cols(grad_packed, upper_mat[:, : 3 * D])
    first_value, first_back = jax.vjp(layer_norm, hidden, row_set[0], row_set[1])
    grad_hidden, grad_gain_one, grad_shift_one = first_back(grad_normed)
    grad_hidden = grad_hidden + grad_middle
    grad_upper = jnp.concatenate([grad_qkv, grad_proj, grad_fc1], axis=1)
    small_rows = jnp.stack(
        [
            grad_gain_one,
            grad_shift_one,
            packed_sums[:D],
            packed_sums[2 * D :],
            grad_proj_bias,
            grad_gain_two,
            grad_shift_two,
            grad_fc2_bias,
        ]
    )
    grad_rows = jnp.concatenate([small_rows, grad_fc1_bias.reshape(-1, D)], axis=0)
    return (grad_hidden, (grad_upper, grad_lower, grad_rows))


def inverse_root(matrix):
    identity = jnp.eye(matrix.shape[-1], dtype=jnp.float32)
    regular = matrix + root_eps * identity
    frob_norm = jnp.sqrt(jnp.sum(regular * regular, axis=(1, 2), keepdims=True))
    scaled = 2.5 / frob_norm
    root_mat = identity * jnp.sqrt(jnp.sqrt(scaled))
    moving = regular * scaled
    for sweep_id in range(NEWTON):
        factor = (5.0 * identity - moving) * 0.25
        root_mat = jnp.einsum("kij,kjl->kil", root_mat, factor, precision=highest)
        square = jnp.einsum("kij,kjl->kil", factor, factor, precision=highest)
        fourth = jnp.einsum("kij,kjl->kil", square, square, precision=highest)
        moving = jnp.einsum("kij,kjl->kil", fourth, moving, precision=highest)
    return root_mat


def adam_update(weight, first_mom, second_mom, grad, rate, decay):
    first_new = beta_one * first_mom + (1.0 - beta_one) * grad
    second_new = beta_two * second_mom + (1.0 - beta_two) * grad * grad
    first_hat = first_new / (1.0 - beta_one**STEP)
    second_hat = second_new / (1.0 - beta_two**STEP)
    return (
        first_new,
        second_new,
        weight - rate * (first_hat / (jnp.sqrt(second_hat) + adam_eps) + decay * weight),
    )


def per_device(
    features,
    tile_mask,
    lengths,
    owners,
    layer_blocks,
    stat_left,
    stat_right,
    io_weights,
    io_first,
    io_second,
    vectors,
    vec_first,
    vec_second,
):
    tok_dev = features.shape[1]
    seq_size = lax.axis_size("seq")
    seq_len = tok_dev * seq_size
    seq_index = lax.axis_index("seq")
    core_index = lax.axis_index("opt")
    targets = features[0].astype(jnp.float32)
    chosen = tile_mask[0][:, None] > 0
    lengths_row = lax.dynamic_index_in_dim(lengths, core_index, 0, keepdims=False)
    places = seq_index * tok_dev + jnp.arange(tok_dev, dtype=jnp.int32)
    all_blocks, all_io = (
        lax.all_gather(layer_blocks.astype(jnp.bfloat16), ("seq", "opt"), axis=0, tiled=True),
        lax.all_gather(io_weights.astype(jnp.bfloat16), ("seq", "opt"), axis=0, tiled=True),
    )
    natural = jnp.zeros_like(all_blocks).at[owners].set(all_blocks)
    upper_mats, lower_mats = assemble(natural)
    tile_count = lax.psum(jnp.sum(tile_mask.astype(jnp.float32)), ("seq", "opt"))
    layer_rows, tail_rows = unpack(vectors)
    token_vec = tail_rows[3 + FEAT // D :].reshape(FEAT)
    head_bias = tail_rows[3 : 3 + FEAT // D].reshape(FEAT)
    inputs = jnp.where(chosen, token_vec[None, :], targets).astype(jnp.bfloat16)
    in_weight = all_io[:, 0]
    head_weight = all_io[:, 1]
    hidden = jnp.dot(inputs, in_weight, preferred_element_type=jnp.float32) + tail_rows[2][None, :]
    hidden = hidden + sine_places(slide_offsets(lengths_row, places))
    layer_id = 0
    hidden, layer_state = layer_forward(
        hidden,
        upper_mats[layer_id],
        lower_mats[layer_id],
        layer_rows[layer_id],
        lengths_row,
        seq_len,
        seq_index,
    )
    layer_states = [layer_state]
    final, final_back = jax.vjp(layer_norm, hidden, tail_rows[0], tail_rows[1])
    final_low = final.astype(jnp.bfloat16)
    predict = contract_cols(final_low, head_weight) + head_bias[None, :]
    difference = predict - targets
    error_local = jnp.sum(jnp.where(chosen, difference * difference, 0.0))
    grad_pred = jnp.where(chosen, 2.0 * difference / tile_count, 0.0).astype(jnp.bfloat16)
    grad_head = contract_rows(grad_pred, final_low)
    grad_head_bias = jnp.sum(grad_pred, axis=0, dtype=jnp.float32)
    grad_final = jnp.dot(grad_pred, head_weight, preferred_element_type=jnp.float32)
    grad_hidden, grad_gain_last, grad_shift_last = final_back(grad_final)
    layer_grads = [None] * LAYERS
    for layer_id in reversed(range(LAYERS)):
        grad_hidden, layer_grads[layer_id] = layer_backward(
            grad_hidden,
            upper_mats[layer_id],
            lower_mats[layer_id],
            layer_rows[layer_id],
            layer_states[layer_id],
            seq_len,
            seq_index,
        )
    grad_in_low = grad_hidden.astype(jnp.bfloat16)
    grad_in = contract_rows(inputs, grad_in_low)
    grad_in_bias = jnp.sum(grad_in_low, axis=0, dtype=jnp.float32)
    grad_inputs = contract_cols(grad_in_low, in_weight)
    grad_token = jnp.sum(jnp.where(chosen, grad_inputs, 0.0), axis=0)
    grad_upper = jnp.stack([item[0] for item in layer_grads])
    grad_lower = jnp.stack([item[1] for item in layer_grads])
    slot_grads = disassemble(grad_upper, grad_lower)[owners]
    io_grads = jnp.stack([grad_in, grad_head], axis=1)
    vec_grads = jnp.concatenate(
        [
            jnp.stack([item[2] for item in layer_grads]).reshape(-1, D),
            jnp.stack([grad_gain_last, grad_shift_last, grad_in_bias]),
            grad_head_bias.reshape(-1, D),
            grad_token.reshape(-1, D),
        ],
        axis=0,
    )
    slot_sum, io_sum = (
        lax.psum_scatter(slot_grads, ("seq", "opt"), scatter_dimension=0, tiled=True),
        lax.psum_scatter(io_grads, ("seq", "opt"), scatter_dimension=0, tiled=True),
    )
    vec_sum, error_sum = lax.psum((vec_grads, error_local), ("seq", "opt"))
    local_sq = jnp.sum(slot_sum * slot_sum) + jnp.sum(io_sum * io_sum)
    grad_norm = jnp.sqrt(lax.psum(local_sq, ("seq", "opt")) + jnp.sum(vec_sum * vec_sum))
    factor = jnp.minimum(1.0, clip_limit / grad_norm)
    block_grads = slot_sum * factor
    left_new = beta_stat * stat_left + (1.0 - beta_stat) * jnp.einsum(
        "kij,klj->kil", block_grads, block_grads, precision=highest
    )
    right_new = beta_stat * stat_right + (1.0 - beta_stat) * jnp.einsum(
        "kji,kjl->kil", block_grads, block_grads, precision=highest
    )
    direction = jnp.einsum("kij,kjl->kil", inverse_root(left_new), block_grads, precision=highest)
    direction = jnp.einsum("kij,kjl->kil", direction, inverse_root(right_new), precision=highest)
    blocks_new = layer_blocks - rate_shampoo * direction
    io_first_new, io_second_new, io_new = adam_update(
        io_weights, io_first, io_second, io_sum * factor, rate_adam, weight_decay
    )
    vec_first_new, vec_second_new, vec_new = adam_update(
        vectors, vec_first, vec_second, vec_sum * factor, rate_vector, 0.0
    )
    return (
        grad_norm,
        error_sum,
        tile_count,
        block_grads,
        left_new,
        right_new,
        blocks_new,
        io_first_new,
        io_second_new,
        io_new,
        vec_first_new,
        vec_second_new,
        vec_new,
    )


LANES=4*BLOCK

def swap(value, axis, mask):
    return lax.ppermute(value, axis, [(s, s ^ mask) for s in range(lax.axis_size(axis))])

def tree_pieces(own, bits):
    rows = own.shape[0]; half = rows // 2
    far = [own]
    if bits > 2:
        far.append(swap(own, "seq", 4))
    if bits > 3:
        far.append(swap(own, "seq", 8))
        far.append(swap(far[2], "seq", 4))
    out = []
    for piece in far:
        first, second = piece[:half], piece[half:]
        first_x = swap(first, "seq", 1)
        second_y = swap(second, "seq", 2)
        first_y = swap(jnp.concatenate([first, first_x]), "seq", 2)
        second_x = swap(jnp.concatenate([second, second_y]), "seq", 1)
        out.append(jnp.concatenate([piece, first_x, second_y, first_y, second_x]))
    return out

IO=48
def assemble_kernel(n_buf, index_ref, io_ref, *refs):
    bufs = refs[:n_buf]
    upper_ref, lower_ref, win_ref, whead_ref = refs[n_buf:n_buf+4]
    held, blocks, stage, in_sem, out_sem, io_sem = refs[n_buf+4:]
    rows = bufs[0].shape[0]
    groups = blocks.shape[0] // 4 // n_buf // 8
    half = rows // 8
    loads = [pltpu.make_async_copy(b, held.at[pl.ds(k*rows, rows)], in_sem.at[k]) for k, b in enumerate(bufs)]
    for c in loads: c.start()
    for k, c in enumerate(loads):
        c.wait()
        def unpack(u, carry, k=k):
            base = k*rows + u*half
            for g in range(groups):
                packed = held[pl.ds(pl.multiple_of(base + g*BLOCK, 48), BLOCK), :]
                for t in range(4):
                    blocks[(k*8+u)*groups*4 + g*4 + t, :, :BLOCK] = packed[:, BLOCK*t:BLOCK*(t+1)]
            return carry
        lax.fori_loop(0, 8, unpack, 0)
    n_dev = io_ref.shape[1]
    def io_copy(d, carry):
        for m, out in ((0, win_ref), (1, whead_ref)):
            off = pl.multiple_of(io_ref[m, d], IO)
            for h in range(2):
                pltpu.make_async_copy(held.at[pl.ds(off + h*IO, IO)],
                    out.at[pl.ds(pl.multiple_of(d*IO, IO), IO), pl.ds(h*LANES, LANES)], io_sem.at[m]).start()
        return carry
    lax.fori_loop(0, n_dev, io_copy, 0)
    outs=[]
    def chunk(index, out, first):
        slot = index % 2
        if index >= 2: outs[index-2].wait()
        st = stage.at[slot]
        def one(c, carry):
            n0 = first(c)
            st[:, pl.ds(pl.multiple_of(c*LANES, 128), LANES)] = jnp.concatenate([blocks[index_ref[n0+t], :, :BLOCK] for t in range(4)], axis=1)
            return carry
        lax.fori_loop(0, U, one, 0, unroll=2)
        c = out(st, out_sem.at[slot]); c.start(); outs.append(c)
    U = (4*D+FF)//LANES
    for i in range(D//BLOCK):
        chunk(i, lambda st, sem, i=i: pltpu.make_async_copy(st, upper_ref.at[pl.ds(i*BLOCK, BLOCK)], sem), lambda c, i=i: i*4*U+4*c)
    base = D//BLOCK*4*U
    per = U//2
    for j in range(FF//BLOCK//per):
        def out(st, sem, j=j):
            return Multi([pltpu.make_async_copy(st.at[:, pl.ds(b*D, D)], lower_ref.at[pl.ds((j*per+b)*BLOCK, BLOCK)], sem) for b in range(per)])
        chunk(D//BLOCK+j, out, lambda c, j=j: base + (j*per*2+c)*4)
    outs[-2].wait(); outs[-1].wait()
    for m, out in ((0, win_ref), (1, whead_ref)):
        pltpu.make_async_copy(out, out, io_sem.at[m]).wait()
class Multi:
    def __init__(s, cs): s.cs=cs
    def start(s):
        for c in s.cs: c.start()
    def wait(s):
        for c in s.cs: c.wait()

def join_weights(bufs, index, io_off):
    n=len(bufs); total=sum(b.shape[0] for b in bufs)
    return pl.pallas_call(partial(assemble_kernel, n),
        out_shape=[jax.ShapeDtypeStruct(s, jnp.bfloat16) for s in ((D,4*D+FF),(FF,D),(FEAT,D),(FEAT,D))],
        in_specs=[pl.BlockSpec(memory_space=pltpu.SMEM)]*2+[pl.BlockSpec(memory_space=pl.ANY)]*n,
        out_specs=[pl.BlockSpec(memory_space=pl.ANY)]*4,
        scratch_shapes=[pltpu.VMEM((total,LANES),jnp.bfloat16), pltpu.VMEM((768,BLOCK,128),jnp.bfloat16), pltpu.VMEM((2,BLOCK,4*D+FF),jnp.bfloat16),
            pltpu.SemaphoreType.DMA((n,)), pltpu.SemaphoreType.DMA((2,)), pltpu.SemaphoreType.DMA((2,))],
        compiler_params=pltpu.CompilerParams(vmem_limit_bytes=56<<20),
        name="join_weights",
    )(index, io_off, *bufs)

def pack_blocks(blocks):
    g=blocks.shape[0]//4
    return blocks.reshape(g,4,BLOCK,BLOCK).transpose(0,2,1,3).reshape(g*BLOCK,LANES)
def fold(rows):
    return jnp.concatenate([rows[:,:LANES],rows[:,LANES:]],axis=0)
def pack_shard(blocks, io):
    b=pack_blocks(blocks.astype(jnp.bfloat16)); h=b.shape[0]//2; io=io.astype(jnp.bfloat16)
    return jnp.concatenate([b[:h],fold(io[:,0]),b[h:],fold(io[:,1])],axis=0)
def offsets(owners, seq_index, core, n_slots):
    gh=n_slots//8; half=gh*BLOCK+2*IO
    def unit(rel, ro, h):
        xy=rel%4
        both=jnp.where(xy==0,h,jnp.where(h==0,jnp.where(xy==1,2,xy+2),jnp.where(xy==2,3,jnp.where(xy==1,6,7))))
        return (rel//4+4*ro)*8+both
    slot=jnp.arange(768,dtype=jnp.int32)
    d=slot//n_slots; s=slot%n_slots
    u=unit((d//2)^seq_index,(d%2)^core,s//4//gh)
    index=jnp.zeros((768,),jnp.int32).at[owners].set((u*gh+s//4%gh)*4+s%4, unique_indices=True, mode="promise_in_bounds")
    dev=jnp.arange(32,dtype=jnp.int32)
    io=jnp.stack([unit((dev//2)^seq_index,(dev%2)^core,h)*half+gh*BLOCK for h in (0,1)])
    return index, io.astype(jnp.int32)
def gather_weights(layer_blocks, io_weights, owners):
    si=lax.axis_index("seq"); ci=lax.axis_index("opt")
    ps=tree_pieces(pack_shard(layer_blocks,io_weights),4)
    os=[swap(p,"opt",1) for p in ps]
    index,io=offsets(owners,si,ci,layer_blocks.shape[0])
    return join_weights(ps+os,index,io)

HD=48; HEADS=16; SLIDES=4; SEG=1024; N=2048; H=512; TQ=256; TK=128
C2=HD**-0.5*math.log2(math.e)
def place_facts(index, head, lengths_ref, core):
    parity=lax.rem(head+(index//H)%2,2)
    pos=(index//SEG)*SEG+2*(index%H)+parity
    slide=jnp.zeros_like(index); end=jnp.int32(0)
    for i in range(SLIDES-1):
        end=end+lengths_ref[core,i]
        slide=slide+jnp.where(pos>=end,1,0)
    d=(pos-head)&15
    level=sum(jnp.where((d&(2**i-1))==0,1,0) for i in range(1,5))
    return slide.astype(jnp.float32), level.astype(jnp.float32)

def arrange(src, dst, odd):
    for pair in range(8):
        first, second = src[2*pair], src[2*pair+1]
        turn=lambda t: jnp.concatenate([t[:,64:],t[:,:64]],axis=1)
        ft, st = turn(first), turn(second)
        low=lax.broadcasted_iota(jnp.int32,first.shape,1)<64
        evens=jnp.where(low,first,st); odds=jnp.where(low,ft,second)
        near=jnp.where(odd,odds,evens); far=jnp.where(odd,evens,odds)
        at=(pair//4)*SEG+(pair%4)*128
        dst[:,at:at+128]=near.astype(dst.dtype); dst[:,at+H:at+H+128]=far.astype(dst.dtype)

def restore(get, put, odd):
    for pair in range(8):
        at=(pair//4)*SEG+(pair%4)*128
        near, far = get(at), get(at+H)
        evens=jnp.where(odd,far,near); odds=jnp.where(odd,near,far)
        turn=lambda t: jnp.concatenate([t[:,64:],t[:,:64]],axis=1)
        low=lax.broadcasted_iota(jnp.int32,evens.shape,1)<64
        put(2*pair, jnp.where(low,evens,turn(odds)))
        put(2*pair+1, jnp.where(low,turn(evens),odds))

def setup(lengths_ref, ids_ref, slide_k, level_k, row_facts):
    head, core = ids_ref[0], ids_ref[1]
    def fill(i, c):
        idx=lax.broadcasted_iota(jnp.int32,(TK,128),0)+i*TK
        s,l=place_facts(idx,head,lengths_ref,core)
        slide_k[pl.ds(pl.multiple_of(i*TK,TK),TK),:]=s
        level_k[pl.ds(pl.multiple_of(i*TK,TK),TK),:]=l
        return c
    lax.fori_loop(0,N//TK,fill,0)
    idx=lax.broadcasted_iota(jnp.int32,(8,N),1)
    s,l=place_facts(idx,head,lengths_ref,core)
    row_facts[0:8,:]=s; row_facts[8:16,:]=l

def key_rows(seg, near):
    own=[(seg*SEG+i*TK,True) for i in range(SEG//TK)]
    other=[((1-seg)*SEG+i*TK,False) for i in range(H//TK)] if near else []
    return own+other

def wide(x): return jnp.concatenate([x]*(TQ//128),axis=1)

def forward_kernel(lengths_ref, ids_ref, qkv_ref, o_ref, out_ref, lse_ref, qkvT, krow, slide_k, level_k, row_facts, s_ref, p_ref):
    odd=lax.rem(ids_ref[0],2)==1
    arrange(qkv_ref, qkvT, odd)
    setup(lengths_ref, ids_ref, slide_k, level_k, row_facts)
    for i in range(N//128):
        krow[i*128:(i+1)*128,:]=qkvT[HD:2*HD,i*128:(i+1)*128].astype(jnp.float32).T.astype(jnp.bfloat16)
    for seg in range(2):
        for near in (True,False):
            tiles=key_rows(seg,near)
            def part(c, carry, seg=seg, near=near, tiles=tiles):
                at=pl.multiple_of(seg*SEG+(0 if near else H)+c*TQ,TQ)
                qT=qkvT[0:HD,pl.ds(at,TQ)]
                sq=row_facts[0:1,pl.ds(at,TQ)]; lq=row_facts[8:9,pl.ds(at,TQ)]
                top=jnp.full((8,TQ),-jnp.inf,jnp.float32)
                for t,(r,own) in enumerate(tiles):
                    s=jnp.dot(krow[r:r+TK,:],qT,preferred_element_type=jnp.float32)
                    s=jnp.where(wide(slide_k[r:r+TK,:])==sq,s,-1e30)
                    s_ref[t*TK:(t+1)*TK,:]=s
                    top=jnp.maximum(top,jnp.max(s.reshape(TK//8,8,TQ),axis=0))
                m=jnp.max(top,axis=0,keepdims=True)
                total=jnp.zeros((8,TQ),jnp.float32)
                for t,(r,own) in enumerate(tiles):
                    e=jnp.exp2((s_ref[t*TK:(t+1)*TK,:]-m)*C2)
                    if near:
                        lk=wide(level_k[r:r+TK,:])
                        e=e*(jnp.minimum(lk,lq)+1.0 if own else jnp.minimum(lk,lq))
                    total=total+jnp.sum(e.reshape(TK//8,8,TQ),axis=0)
                    p_ref[t*TK:(t+1)*TK,:]=e.astype(jnp.bfloat16)
                l=jnp.sum(total,axis=0,keepdims=True)
                acc=jnp.zeros((HD,TQ),jnp.float32)
                acc=jnp.dot(qkvT[2*HD:3*HD,seg*SEG:(seg+1)*SEG],p_ref[0:SEG,:],preferred_element_type=jnp.float32)
                if near:
                    acc=acc+jnp.dot(qkvT[2*HD:3*HD,(1-seg)*SEG:(1-seg)*SEG+H],p_ref[SEG:SEG+H,:],preferred_element_type=jnp.float32)
                o_ref[:,pl.ds(at,TQ)]=acc/l
                lse_ref[:,pl.ds(at,TQ)]=jnp.broadcast_to(m*C2+jnp.log2(l),(8,TQ))
                return carry
            lax.fori_loop(0,H//TQ,part,0)
    def put(c,v): out_ref[c]=v.astype(jnp.bfloat16)
    restore(lambda at: o_ref[:,at:at+128], put, odd)

def backward_kernel(lengths_ref, ids_ref, qkv_ref, do_ref, o_ref, lse_ref, out_ref, qkvT, doT, rows, slide_k, level_k, row_facts, dqT, dkv, p_ref, ds_ref):
    odd=lax.rem(ids_ref[0],2)==1
    arrange(qkv_ref, qkvT, odd)
    arrange(do_ref, doT, odd)
    setup(lengths_ref, ids_ref, slide_k, level_k, row_facts)
    for i in range(N//128):
        l=slice(i*128,(i+1)*128)
        for j in range(3):
            rows[j,l,:]=qkvT[j*HD:(j+1)*HD,l].astype(jnp.float32).T.astype(jnp.bfloat16)
        rows[3,l,:]=doT[:,l].astype(jnp.float32).T.astype(jnp.bfloat16)
    dkv[...]=jnp.zeros_like(dkv)
    for seg in range(2):
        for near in (True,False):
            tiles=key_rows(seg,near)
            def part(c, carry, seg=seg, near=near, tiles=tiles):
                at=pl.multiple_of(seg*SEG+(0 if near else H)+c*TQ,TQ)
                qT=qkvT[0:HD,pl.ds(at,TQ)]; gT=doT[:,pl.ds(at,TQ)]
                q=rows[0,pl.ds(at,TQ),:]; g=rows[3,pl.ds(at,TQ),:]
                sq=row_facts[0:1,pl.ds(at,TQ)]; lq=row_facts[8:9,pl.ds(at,TQ)]
                lse=lse_ref[0:1,pl.ds(at,TQ)]
                inner=jnp.sum(gT.astype(jnp.float32)*o_ref[:,pl.ds(at,TQ)],axis=0,keepdims=True)
                for t,(r,own) in enumerate(tiles):
                    s=jnp.dot(rows[1,r:r+TK,:],qT,preferred_element_type=jnp.float32)
                    dp=jnp.dot(rows[2,r:r+TK,:],gT,preferred_element_type=jnp.float32)
                    e=jnp.exp2(s*C2-lse)
                    if near:
                        lk=wide(level_k[r:r+TK,:])
                        e=e*(jnp.minimum(lk,lq)+1.0 if own else jnp.minimum(lk,lq))
                    e=jnp.where(wide(slide_k[r:r+TK,:])==sq,e,0.0)
                    p_ref[t*TK:(t+1)*TK,:]=e.astype(jnp.bfloat16)
                    ds_ref[t*TK:(t+1)*TK,:]=(e*(dp-inner)).astype(jnp.bfloat16)
                dq=jnp.dot(qkvT[HD:2*HD,seg*SEG:(seg+1)*SEG],ds_ref[0:SEG,:],preferred_element_type=jnp.float32)
                if near:
                    dq=dq+jnp.dot(qkvT[HD:2*HD,(1-seg)*SEG:(1-seg)*SEG+H],ds_ref[SEG:SEG+H,:],preferred_element_type=jnp.float32)
                dqT[:,pl.ds(at,TQ)]=dq*HD**-0.5
                own=slice(seg*SEG,(seg+1)*SEG)
                dkv[0,own,:]+=jnp.dot(ds_ref[0:SEG,:],q,preferred_element_type=jnp.float32)
                dkv[1,own,:]+=jnp.dot(p_ref[0:SEG,:],g,preferred_element_type=jnp.float32)
                if near:
                    oth=slice((1-seg)*SEG,(1-seg)*SEG+H)
                    dkv[0,oth,:]+=jnp.dot(ds_ref[SEG:SEG+H,:],q,preferred_element_type=jnp.float32)
                    dkv[1,oth,:]+=jnp.dot(p_ref[SEG:SEG+H,:],g,preferred_element_type=jnp.float32)
                return carry
            lax.fori_loop(0,H//TQ,part,0)
    def putter(j):
        def put(c,v): out_ref[c,j*HD:(j+1)*HD,:]=v.astype(jnp.bfloat16)
        return put
    restore(lambda at: dqT[:,at:at+128], putter(0), odd)
    restore(lambda at: dkv[0,at:at+128,:].T*HD**-0.5, putter(1), odd)
    restore(lambda at: dkv[1,at:at+128,:].T, putter(2), odd)

def vm(): return pl.BlockSpec(memory_space=pltpu.VMEM)
def sm_(): return pl.BlockSpec(memory_space=pltpu.SMEM)
F32=jnp.float32; BF=jnp.bfloat16
def attend(lengths, ids, qkv):
    return pl.pallas_call(forward_kernel,
        out_shape=[jax.ShapeDtypeStruct((HD,N),F32),jax.ShapeDtypeStruct((16,HD,128),BF),jax.ShapeDtypeStruct((8,N),F32)],
        in_specs=[sm_(),sm_(),vm()], out_specs=[vm()]*3,
        scratch_shapes=[pltpu.VMEM((3*HD,N),BF),pltpu.VMEM((N,HD),BF),pltpu.VMEM((N,128),F32),pltpu.VMEM((N,128),F32),pltpu.VMEM((16,N),F32),
            pltpu.VMEM((SEG+H,TQ),F32),pltpu.VMEM((SEG+H,TQ),BF)],
        compiler_params=pltpu.CompilerParams(vmem_limit_bytes=48<<20), name="attend_forward")(lengths,ids,qkv)
def attend_back(lengths, ids, qkv, do, o, lse):
    return pl.pallas_call(backward_kernel,
        out_shape=jax.ShapeDtypeStruct((16,3*HD,128),BF),
        in_specs=[sm_(),sm_()]+[vm()]*4, out_specs=vm(),
        scratch_shapes=[pltpu.VMEM((3*HD,N),BF),pltpu.VMEM((HD,N),BF),pltpu.VMEM((4,N,HD),BF),pltpu.VMEM((N,128),F32),pltpu.VMEM((N,128),F32),pltpu.VMEM((16,N),F32),
            pltpu.VMEM((HD,N),F32),pltpu.VMEM((2,N,HD),F32),pltpu.VMEM((SEG+H,TQ),BF),pltpu.VMEM((SEG+H,TQ),BF)],
        compiler_params=pltpu.CompilerParams(vmem_limit_bytes=48<<20), name="attend_backward")(lengths,ids,qkv,do,o,lse)

I16=jnp.int16; F32=jnp.float32
GROUP=48
STEP_Q=32000.0
def encode(x):
    top=jnp.max(jnp.abs(x),axis=0,keepdims=True)
    code=jnp.ceil(jnp.log2(jnp.maximum(top,1e-30))*256.0)
    return x*(STEP_Q*jnp.exp2(code*(-1.0/256.0))), code
def to16(v):
    v=jnp.clip(jnp.round(v),-32767.0,32767.0)
    return v.astype(jnp.int32).astype(I16)
def scale_of(code16):
    return jnp.exp2(code16.astype(jnp.int32).astype(F32)*(1.0/256.0))*(1.0/STEP_Q)

def grads_kernel(index_ref, rel_ref, *refs):
    (at_qkv,x_qkv,at_o,x_o,at_1,x_1,at_2,x_2,at_in,x_in,at_head,x_head)=refs[:12]
    outs=refs[12:20]
    slots, io, stage, sem = refs[20:]
    def stripe(at_ref, x_ref, x_rows, i, c):
        a=at_ref[pl.ds(pl.multiple_of(i*BLOCK,32),BLOCK),:]
        if x_rows:
            x=x_ref[pl.ds(pl.multiple_of(c*LANES,128),LANES),:]
            return lax.dot_general(a,x,(((1,),(1,)),((),())),preferred_element_type=F32)
        x=x_ref[:,pl.ds(pl.multiple_of(c*LANES,128),LANES)]
        return jnp.dot(a,x,preferred_element_type=F32)
    def place(w, n0):
        parts=[encode(w[:GROUP]),encode(w[GROUP:])]
        q=to16(jnp.concatenate([parts[0][0],parts[1][0]],axis=0))
        codes=jnp.concatenate([parts[0][1],parts[1][1],jnp.zeros((14,LANES),F32)],axis=0)
        codes=codes.astype(jnp.int32).astype(I16)
        for t in range(4):
            s=index_ref[n0+t]
            slots[s,:BLOCK,:BLOCK]=q[:,BLOCK*t:BLOCK*(t+1)]
            slots[s,BLOCK:,:BLOCK]=codes[:,BLOCK*t:BLOCK*(t+1)]
    cols=(4*D+FF)//BLOCK
    def run(at_ref,x_ref,x_rows,n_i,n_c,first):
        def one(k,carry):
            i=k//n_c; c=k%n_c
            place(stripe(at_ref,x_ref,x_rows,i,c),first(i,c))
            return carry
        lax.fori_loop(0,n_i*n_c,one,0)
    run(at_qkv,x_qkv,True,8,6,lambda i,c:i*cols+4*c)
    run(at_o,x_o,False,8,2,lambda i,c:i*cols+24+4*c)
    run(at_1,x_1,False,8,8,lambda i,c:i*cols+32+4*c)
    run(at_2,x_2,False,32,2,lambda i,c:8*cols+i*8+4*c)
    n_dev=rel_ref.shape[0]
    def io_one(d,carry):
        r=rel_ref[d]
        for m,(at,x) in enumerate(((at_in,x_in),(at_head,x_head))):
            w=jnp.dot(at[pl.ds(pl.multiple_of(d*IO,16),IO),:],x[...],preferred_element_type=F32)
            q,code=encode(w); q=to16(q)
            for h in range(2):
                io[r,m,h*IO:(h+1)*IO,:]=q[:,h*LANES:(h+1)*LANES]
            codes=jnp.concatenate([jnp.zeros((6,LANES),F32),code[:,:LANES],code[:,LANES:],jnp.zeros((8,LANES),F32)],axis=0)
            io[r,m,2*IO:,:]=codes.astype(jnp.int32).astype(I16)
        return carry
    lax.fori_loop(0,n_dev,io_one,0)
    half=3*BLOCK+2*IO
    started=[]
    for k,out in enumerate(outs):
        def one(xy,carry,k=k,out=out):
            slot=xy%2
            r=k*4+xy
            @pl.when(xy>=2)
            def _():
                pltpu.make_async_copy(stage.at[slot],out.at[xy],sem.at[slot]).wait()
            for h in range(2):
                codes=jnp.zeros((16,LANES),jnp.int32)
                for g in range(3):
                    tiles=[slots[(r*6+h*3+g)*4+t,:,:BLOCK] for t in range(4)]
                    whole=jnp.concatenate(tiles,axis=1)
                    stage[slot,h,g*BLOCK:(g+1)*BLOCK,:]=whole[:BLOCK]
                    codes=codes+pltpu.roll(whole[BLOCK:].astype(jnp.int32),2*g,0)
                stage[slot,h,3*BLOCK:half,:]=io[r,h,:2*IO,:]
                codes=codes+io[r,h,2*IO:,:].astype(jnp.int32)
                stage[slot,h,half:,:]=codes.astype(I16)
            pltpu.make_async_copy(stage.at[slot],out.at[xy],sem.at[slot]).start()
            return carry
        lax.fori_loop(0,4,one,0)
        for slot in range(2):
            pltpu.make_async_copy(stage.at[slot],out.at[slot],sem.at[slot]).wait()

ROWS=3*BLOCK+2*IO+16
def weight_grads(index, rel, *operands):
    return pl.pallas_call(grads_kernel,
        out_shape=[jax.ShapeDtypeStruct((4,2,ROWS,LANES),I16)]*8,
        in_specs=[pl.BlockSpec(memory_space=pltpu.SMEM)]*2+[pl.BlockSpec(memory_space=pltpu.VMEM)]*12,
        out_specs=[pl.BlockSpec(memory_space=pl.ANY)]*8,
        scratch_shapes=[pltpu.VMEM((768,BLOCK+16,128),I16),pltpu.VMEM((32,2,2*IO+16,LANES),I16),pltpu.VMEM((2,2,ROWS,LANES),I16),pltpu.SemaphoreType.DMA((2,))],
        compiler_params=pltpu.CompilerParams(vmem_limit_bytes=56<<20), name="weight_grads")(index,rel,*operands)

def add_rows(refs, at):
    raise NotImplementedError
def decoded_sum(views, k):
    total=None
    for v in views:
        s=scale_of(v[ROWS-16:ROWS,:])[k:k+1,:]
        x=v[k*GROUP:(k+1)*GROUP,:].astype(jnp.int32).astype(F32)*s
        total=x if total is None else total+x
    return total
def add_codes(views, out):
    codes=[]
    scales=[scale_of(v[ROWS-16:ROWS,:]) for v in views]
    for k in range(8):
        total=None
        for v,s in zip(views,scales):
            x=v[k*GROUP:(k+1)*GROUP,:].astype(jnp.int32).astype(F32)*s[k:k+1,:]
            total=x if total is None else total+x
        q,code=encode(total)
        out[k*GROUP:(k+1)*GROUP,:]=to16(q)
        codes.append(code)
    codes.append(jnp.zeros((8,LANES),F32))
    out[ROWS-16:ROWS,:]=jnp.concatenate(codes,axis=0).astype(jnp.int32).astype(I16)

class At:
    def __init__(s,ref,*i): s.ref,s.i=ref,i
    def __getitem__(s,k): return s.ref[(*s.i,*k)]
    def __setitem__(s,k,v): s.ref[(*s.i,*k)]=v

def split_kernel(mine, theirs, send_a, keep_a, send_b, keep_b):
    for h,plan in ((0,((send_a,(2,3)),(keep_a,(0,1)))),(1,((send_b,(1,3)),(keep_b,(0,2))))):
        for out,xys in plan:
            for j,xy in enumerate(xys):
                add_codes([At(mine,xy,h),At(theirs,xy,h)],At(out,j))
def code_call(kernel, name, outs, *args):
    return pl.pallas_call(kernel, out_shape=[jax.ShapeDtypeStruct(s,t) for s,t in outs],
        in_specs=[pl.BlockSpec(memory_space=pltpu.VMEM)]*len(args), out_specs=[pl.BlockSpec(memory_space=pltpu.VMEM)]*len(outs),
        compiler_params=pltpu.CompilerParams(vmem_limit_bytes=32<<20), name=name)(*args)
def plane_kernel(keep_a, got_a, keep_b, got_b, send_a, stay_a, send_b, stay_b):
    for keep,got,send,stay in ((keep_a,got_a,send_a,stay_a),(keep_b,got_b,send_b,stay_b)):
        add_codes([At(keep,1),At(got,1)],At(send))
        add_codes([At(keep,0),At(got,0)],At(stay))
def line_kernel(*refs):
    stay_a,got_a,stay_b,got_b=refs[:4]; more=refs[4:-1]; out=refs[-1]
    for h,(stay,got) in enumerate(((stay_a,got_a),(stay_b,got_b))):
        add_codes([At(stay),At(got)]+[At(m,h) for m in more],At(out,h))
def final_kernel(*refs):
    stay_a,got_a,stay_b,got_b=refs[:4]; more=refs[4:-3]; blocks,io_in,io_head=refs[-3:]
    for h,(stay,got,io) in enumerate(((stay_a,got_a,io_in),(stay_b,got_b,io_head))):
        views=[At(stay),At(got)]+[At(m,h) for m in more]
        scales=[scale_of(v[ROWS-16:ROWS,:]) for v in views]
        for k in range(8):
            total=None
            for v,s in zip(views,scales):
                x=v[k*GROUP:(k+1)*GROUP,:].astype(jnp.int32).astype(F32)*s[k:k+1,:]
                total=x if total is None else total+x
            if k<6:
                for t in range(4):
                    blocks[(h*3+k//2)*4+t,(k%2)*GROUP:(k%2+1)*GROUP,:]=total[:,t*BLOCK:(t+1)*BLOCK]
            else:
                io[:,(k-6)*LANES:(k-5)*LANES]=total
HALF=(ROWS,LANES)
def reduce_tree(pieces):
    mine,theirs=pieces[:4],pieces[4:]
    got=[None]*4
    for k in (3,2,1,0): got[k]=swap(theirs[k],"opt",1)
    far={}
    for k in (3,2,1,0):
        send_a,keep_a,send_b,keep_b=code_call(split_kernel,"split_halves",[((2,)+HALF,I16)]*4,mine[k],got[k])
        got_a=swap(send_a,"seq",2); got_b=swap(send_b,"seq",1)
        send_a,stay_a,send_b,stay_b=code_call(plane_kernel,"add_plane",[(HALF,I16)]*4,keep_a,got_a,keep_b,got_b)
        got_a=swap(send_a,"seq",1); got_b=swap(send_b,"seq",2)
        if k==3:
            far[3]=swap(code_call(line_kernel,"add_line",[((2,)+HALF,I16)],stay_a,got_a,stay_b,got_b)[0],"seq",4)
        elif k==2:
            far[2]=swap(code_call(line_kernel,"add_line",[((2,)+HALF,I16)],stay_a,got_a,stay_b,got_b,far[3])[0],"seq",8)
        elif k==1:
            far[1]=swap(code_call(line_kernel,"add_line",[((2,)+HALF,I16)],stay_a,got_a,stay_b,got_b)[0],"seq",4)
        else:
            return code_call(final_kernel,"add_final",[((24,BLOCK,BLOCK),F32),((IO,D),F32),((IO,D),F32)],stay_a,got_a,stay_b,got_b,far[1],far[2])
def slot_index(owners, seq_index, core, n_slots):
    slot=jnp.arange(768,dtype=jnp.int32); d=slot//n_slots
    rel=((d//2)^seq_index)+16*((d%2)^core)
    index=jnp.zeros((768,),jnp.int32).at[owners].set(rel*n_slots+slot%n_slots,unique_indices=True,mode="promise_in_bounds")
    dev=jnp.arange(32,dtype=jnp.int32)
    return index,(((dev//2)^seq_index)+16*((dev%2)^core)).astype(jnp.int32)


def fits(mesh):
    return mesh.shape["seq"] == 16 and mesh.shape["opt"] == 2


def sum_everywhere(value):
    value = value + swap(value, "opt", 1)
    for bit in range((lax.axis_size("seq") - 1).bit_length()):
        value = value + swap(value, "seq", 2**bit)
    return value


def sum_scalar(value):
    return sum_everywhere(jnp.broadcast_to(value, (8, 128)))[0, 0]


def to_heads(parts):
    return lax.all_to_all(parts, "seq", 0, 0, tiled=True)


def evens_first(rows):
    return rows.reshape((rows.shape[0] // 2, 2) + rows.shape[1:]).swapaxes(0, 1).reshape(rows.shape)


def shampoo_products(left, right):
    return jnp.einsum("kij,kjl->kil", left, right, precision=lax.Precision.HIGH)


def inverse_roots(matrices):
    identity = jnp.eye(matrices.shape[-1], dtype=jnp.float32)
    regular = matrices + root_eps * identity
    frob_norm = jnp.sqrt(jnp.sum(regular * regular, axis=(1, 2), keepdims=True))
    scaled = 2.5 / frob_norm
    moving = regular * scaled
    root_mat = None
    for sweep_id in range(NEWTON):
        factor = (5.0 * identity - moving) * 0.25
        if root_mat is None:
            root_mat = factor * jnp.sqrt(jnp.sqrt(scaled))
        else:
            root_mat = shampoo_products(root_mat, factor)
        if sweep_id < NEWTON - 1:
            square = shampoo_products(factor, factor)
            moving = shampoo_products(shampoo_products(square, square), moving)
    return root_mat


def fast_device(
    features,
    tile_mask,
    lengths,
    owners,
    layer_blocks,
    stat_left,
    stat_right,
    io_weights,
    io_first,
    io_second,
    vectors,
    vec_first,
    vec_second,
):
    tok_dev = features.shape[1]
    seq_index = lax.axis_index("seq")
    core_index = lax.axis_index("opt")
    ids = jnp.stack([seq_index, core_index]).astype(jnp.int32)
    low_targets = evens_first(features[0])
    targets = low_targets.astype(jnp.float32)
    chosen = evens_first(tile_mask[0])[:, None] > 0
    lengths_row = lax.dynamic_index_in_dim(lengths, core_index, 0, keepdims=False)
    places = seq_index * tok_dev + evens_first(jnp.arange(tok_dev, dtype=jnp.int32))
    tile_count = sum_scalar(jnp.sum(tile_mask.astype(jnp.float32)))
    upper, lower, in_weight, head_weight = gather_weights(layer_blocks, io_weights, owners)
    layer_rows, tail_rows = unpack(vectors)
    row_set = layer_rows[0]
    token_vec = tail_rows[3 + FEAT // D :].reshape(FEAT)
    head_bias = tail_rows[3 : 3 + FEAT // D].reshape(FEAT)
    inputs = jnp.where(chosen, token_vec[None, :], targets).astype(jnp.bfloat16)
    hidden = jnp.dot(inputs, in_weight, preferred_element_type=jnp.float32) + tail_rows[2][None, :]
    hidden = hidden + sine_places(slide_offsets(lengths_row, places))

    normed = layer_norm(hidden, row_set[0], row_set[1]).astype(jnp.bfloat16)
    biases = jnp.concatenate([row_set[2], jnp.zeros_like(row_set[2]), row_set[3]])
    qkv_weight = upper[:, : 3 * D]
    out_weight = upper[:, 3 * D : 4 * D]
    up_weight = upper[:, 4 * D :]
    packed = lax.dot_general(
        qkv_weight, normed, (((0,), (1,)), ((), ())), preferred_element_type=jnp.float32
    )
    packed = (packed + biases[:, None]).astype(jnp.bfloat16)
    by_head = packed.reshape(3, HEADS, HEAD_DIM, tok_dev).swapaxes(0, 1)
    own_head = to_heads(by_head.reshape(HEADS, 3 * HEAD_DIM, tok_dev))
    head_out, mixed_parts, head_totals = attend(lengths, ids, own_head)
    mixed_low = to_heads(mixed_parts).reshape(D, tok_dev)
    middle = hidden + contract_rows(mixed_low, out_weight) + row_set[4][None, :]
    second = layer_norm(middle, row_set[5], row_set[6]).astype(jnp.bfloat16)
    before = (
        jnp.dot(second, up_weight, preferred_element_type=jnp.float32)
        + row_set[8:].reshape(-1)[None, :]
    )
    active = jax.nn.gelu(before, approximate=True).astype(jnp.bfloat16)
    result = (
        middle + jnp.dot(active, lower, preferred_element_type=jnp.float32) + row_set[7][None, :]
    )

    final, final_back = jax.vjp(layer_norm, result, tail_rows[0], tail_rows[1])
    final_low = final.astype(jnp.bfloat16)
    predict = contract_cols(final_low, head_weight) + head_bias[None, :]
    difference = predict - targets
    error_local = jnp.sum(jnp.where(chosen, difference * difference, 0.0))
    grad_pred = jnp.where(chosen, 2.0 * difference / tile_count, 0.0).astype(jnp.bfloat16)
    grad_head_bias = jnp.sum(grad_pred, axis=0, dtype=jnp.float32)
    grad_final = jnp.dot(grad_pred, head_weight, preferred_element_type=jnp.float32)
    grad_result, grad_gain_last, grad_shift_last = final_back(grad_final)

    grad_out = grad_result.astype(jnp.bfloat16)
    grad_fc2_bias = jnp.sum(grad_out, axis=0, dtype=jnp.float32)
    grad_active = contract_cols(grad_out, lower)
    gelu_value, gelu_back = jax.vjp(partial(jax.nn.gelu, approximate=True), before)
    grad_before = gelu_back(grad_active)[0].astype(jnp.bfloat16)
    grad_fc1_bias = jnp.sum(grad_before, axis=0, dtype=jnp.float32)
    grad_second = contract_cols(grad_before, up_weight)
    norm_value, norm_back = jax.vjp(layer_norm, middle, row_set[5], row_set[6])
    grad_middle, grad_gain_two, grad_shift_two = norm_back(grad_second)
    grad_middle = grad_middle + grad_result
    grad_branch = grad_middle.astype(jnp.bfloat16)
    grad_proj_bias = jnp.sum(grad_branch, axis=0, dtype=jnp.float32)
    grad_mixed = contract_cols(out_weight, grad_branch).astype(jnp.bfloat16)
    grad_head_out = to_heads(grad_mixed.reshape(HEADS, HEAD_DIM, tok_dev))
    grad_parts = attend_back(lengths, ids, own_head, grad_head_out, head_out, head_totals)
    grad_packed = to_heads(grad_parts).reshape(HEADS, 3, HEAD_DIM, tok_dev)
    grad_packed = grad_packed.swapaxes(0, 1).reshape(3 * D, tok_dev)
    packed_sums = jnp.sum(grad_packed, axis=1, dtype=jnp.float32)
    grad_normed = lax.dot_general(
        grad_packed, qkv_weight, (((0,), (1,)), ((), ())), preferred_element_type=jnp.float32
    )
    first_value, first_back = jax.vjp(layer_norm, hidden, row_set[0], row_set[1])
    grad_hidden, grad_gain_one, grad_shift_one = first_back(grad_normed)
    grad_hidden = grad_hidden + grad_middle
    grad_in_low = grad_hidden.astype(jnp.bfloat16)
    grad_in_bias = jnp.sum(grad_in_low, axis=0, dtype=jnp.float32)
    grad_inputs = contract_cols(grad_in_low, in_weight)
    grad_token = jnp.sum(jnp.where(chosen, grad_inputs, 0.0), axis=0)

    index, relative = slot_index(owners, seq_index, core_index, layer_blocks.shape[0])
    pieces = weight_grads(
        index,
        relative,
        normed.T,
        grad_packed,
        mixed_low,
        grad_branch,
        second.T,
        grad_before,
        active.T,
        grad_out,
        inputs.T,
        grad_in_low,
        grad_pred.T,
        final_low,
    )
    slot_sum, in_sum, head_sum = reduce_tree(pieces)
    io_sum = jnp.stack([in_sum, head_sum], axis=1)
    vec_grads = jnp.concatenate(
        [
            jnp.stack(
                [
                    grad_gain_one,
                    grad_shift_one,
                    packed_sums[:D],
                    packed_sums[2 * D :],
                    grad_proj_bias,
                    grad_gain_two,
                    grad_shift_two,
                    grad_fc2_bias,
                ]
            ),
            grad_fc1_bias.reshape(-1, D),
            jnp.stack([grad_gain_last, grad_shift_last, grad_in_bias]),
            grad_head_bias.reshape(-1, D),
            grad_token.reshape(-1, D),
            jnp.broadcast_to(error_local, (5, D)),
        ],
        axis=0,
    )
    vec_sum = sum_everywhere(vec_grads)
    error_sum = vec_sum[vectors.shape[0], 0]
    vec_sum = vec_sum[: vectors.shape[0]]
    local_sq = jnp.sum(slot_sum * slot_sum) + jnp.sum(io_sum * io_sum)
    grad_norm = jnp.sqrt(sum_scalar(local_sq) + jnp.sum(vec_sum * vec_sum))
    factor = jnp.minimum(1.0, clip_limit / grad_norm)
    block_grads = slot_sum * factor
    flipped = block_grads.swapaxes(1, 2)
    left_new = beta_stat * stat_left + (1.0 - beta_stat) * shampoo_products(block_grads, flipped)
    right_new = beta_stat * stat_right + (1.0 - beta_stat) * shampoo_products(flipped, block_grads)
    roots = inverse_roots(jnp.concatenate([left_new, right_new]))
    slots = left_new.shape[0]
    direction = shampoo_products(shampoo_products(roots[:slots], block_grads), roots[slots:])
    blocks_new = layer_blocks - rate_shampoo * direction
    io_first_new, io_second_new, io_new = adam_update(
        io_weights, io_first, io_second, io_sum * factor, rate_adam, weight_decay
    )
    vec_first_new, vec_second_new, vec_new = adam_update(
        vectors, vec_first, vec_second, vec_sum * factor, rate_vector, 0.0
    )
    return (
        grad_norm,
        error_sum,
        tile_count,
        block_grads,
        left_new,
        right_new,
        blocks_new,
        io_first_new,
        io_second_new,
        io_new,
        vec_first_new,
        vec_second_new,
        vec_new,
    )


def solution(mesh):
    return jax.shard_map(
        fast_device if fits(mesh) else per_device,
        mesh=mesh,
        in_specs=(
            P("opt", "seq", None),
            P("opt", "seq"),
            P(),
            P(),
            P(("seq", "opt"), None, None),
            P(("seq", "opt"), None, None),
            P(("seq", "opt"), None, None),
            P(("seq", "opt"), None, None),
            P(("seq", "opt"), None, None),
            P(("seq", "opt"), None, None),
            P(),
            P(),
            P(),
        ),
        out_specs=(
            P(),
            P(),
            P(),
            P(("seq", "opt"), None, None),
            P(("seq", "opt"), None, None),
            P(("seq", "opt"), None, None),
            P(("seq", "opt"), None, None),
            P(("seq", "opt"), None, None),
            P(("seq", "opt"), None, None),
            P(("seq", "opt"), None, None),
            P(),
            P(),
            P(),
        ),
        check_vma=False,
    )
```

```python
from functools import partial
import math

import jax
import jax.numpy as jnp
import numpy as np
from jax import lax
from jax.experimental import pallas as pl
from jax.experimental.pallas import tpu as pltpu
from jax.sharding import PartitionSpec as P

D = 768
HEADS = 16
HEAD_DIM = 48
FF = 3072
FEAT = 1536
LAYERS = 1
BRANCHES = 5
SEG0 = 1024
BLOCK = 96
SLIDES = 4
NEWTON = 6
STEP = 10


norm_eps = 1e-05
clip_limit = 1.0
beta_one = 0.9
beta_two = 0.95
adam_eps = 1e-08
rate_adam = 0.01
rate_vector = 0.2
weight_decay = 0.05
beta_stat = 0.95
rate_shampoo = 0.05
root_eps = 1e-12
masked_score = -1e30
highest = lax.Precision.HIGHEST


def from_partner(value, axis, stride):
    mask = 2**stride
    pairs = [(source, source ^ mask) for source in range(lax.axis_size(axis))]
    return lax.ppermute(value, axis, pairs)


def for_sending(shard):

    def short(part):
        return part.astype(jnp.bfloat16) if part.dtype == jnp.float32 else part

    return jax.tree.map(short, shard)


def layer_norm(values, gain, shift):
    centred = values - jnp.mean(values, axis=-1, keepdims=True)
    spread = jnp.mean(centred * centred, axis=-1, keepdims=True)
    return centred * lax.rsqrt(spread + norm_eps) * gain + shift


def sine_places(places):
    half_width = D // 2
    freq_rates = jnp.exp(
        jnp.arange(half_width, dtype=jnp.float32) * (-math.log(10000.0) / half_width)
    )
    angles = (places.astype(jnp.float32) / 64.0)[:, None] * freq_rates[None, :]
    return jnp.concatenate([jnp.sin(angles), jnp.cos(angles)], axis=1)


def slide_ids(lengths_row, places):
    slide_ends = jnp.cumsum(lengths_row)
    return jnp.sum((places[..., None] >= slide_ends[:-1]).astype(jnp.int32), axis=-1)


def slide_offsets(lengths_row, places):
    slide_ends = jnp.cumsum(lengths_row)
    slide_starts = slide_ends - lengths_row
    owner_ids = slide_ids(lengths_row, places)
    match_rows = owner_ids[:, None] == jnp.arange(SLIDES, dtype=jnp.int32)[None, :]
    picked = jnp.sum(jnp.where(match_rows, slide_starts[None, :], 0), axis=1)
    return places - picked


def head_offsets(dilation):
    return np.arange(HEADS) % dilation


def pick_rows(values, dilation):
    row_count = values.shape[0] // dilation
    shaped = values.reshape((row_count, dilation) + values.shape[1:])
    return shaped[:, head_offsets(dilation), np.arange(HEADS)]


def spread_rows(values, dilation, filler):
    row_count = values.shape[0]
    hit_mask = np.arange(dilation)[:, None] == head_offsets(dilation)[None, :]
    hit_mask = hit_mask.reshape((1, dilation, HEADS) + (1,) * (values.ndim - 2))
    spread_out = jnp.where(hit_mask, values[:, None], filler)
    return spread_out.reshape((row_count * dilation,) + values.shape[1:])


def branch_geom(branch, tok_dev, seq_len):
    dilation = 2**branch
    segment = min(SEG0 * dilation, seq_len)
    return (dilation, segment, max(1, segment // tok_dev))


def branch_docs(lengths_row, first_place, row_count, dilation):
    places = (
        first_place
        + jnp.asarray(head_offsets(dilation), jnp.int32)[None, :]
        + dilation * jnp.arange(row_count, dtype=jnp.int32)[:, None]
    )
    return slide_ids(lengths_row, places)


def contract_rows(left, right):
    return lax.dot_general(
        left, right, (((0,), (0,)), ((), ())), preferred_element_type=jnp.float32
    )


def contract_cols(left, right):
    return lax.dot_general(
        left, right, (((1,), (1,)), ((), ())), preferred_element_type=jnp.float32
    )


def assemble(natural):
    per_layer = natural.reshape(LAYERS, -1, BLOCK, BLOCK)
    col_count = (4 * D + FF) // BLOCK
    wide_count = D // BLOCK * col_count
    upper_mats = per_layer[:, :wide_count].reshape(LAYERS, D // BLOCK, col_count, BLOCK, BLOCK)
    upper_mats = upper_mats.transpose(0, 1, 3, 2, 4).reshape(LAYERS, D, 4 * D + FF)
    lower_mats = per_layer[:, wide_count:].reshape(LAYERS, FF // BLOCK, D // BLOCK, BLOCK, BLOCK)
    lower_mats = lower_mats.transpose(0, 1, 3, 2, 4).reshape(LAYERS, FF, D)
    return (upper_mats, lower_mats)


def disassemble(upper_mats, lower_mats):
    col_count = (4 * D + FF) // BLOCK
    top_part = upper_mats.reshape(LAYERS, D // BLOCK, BLOCK, col_count, BLOCK).transpose(
        0, 1, 3, 2, 4
    )
    top_part = top_part.reshape(LAYERS, -1, BLOCK, BLOCK)
    bottom_part = lower_mats.reshape(LAYERS, FF // BLOCK, BLOCK, D // BLOCK, BLOCK).transpose(
        0, 1, 3, 2, 4
    )
    bottom_part = bottom_part.reshape(LAYERS, -1, BLOCK, BLOCK)
    return jnp.concatenate([top_part, bottom_part], axis=1).reshape(-1, BLOCK, BLOCK)


def unpack(vector_set):
    per_layer = 8 + FF // D
    return (
        vector_set[: LAYERS * per_layer].reshape(LAYERS, per_layer, D),
        vector_set[LAYERS * per_layer :],
    )


def collect_pairs(pieces, bit_counts, seq_index):
    pieces = list(pieces)
    for bit_id in range(max(bit_counts + [0])):
        active_ids = [branch for branch in range(len(pieces)) if bit_counts[branch] > bit_id]
        outgoing = jnp.concatenate([pieces[branch] for branch in active_ids], axis=0)
        partner = from_partner(outgoing, "seq", bit_id)
        lower_side = seq_index // 2**bit_id % 2 == 0
        offset_at = 0
        for branch in active_ids:
            my_part = pieces[branch]
            part_size = my_part.shape[0]
            their_part = partner[offset_at : offset_at + part_size]
            offset_at = offset_at + part_size
            pieces[branch] = jnp.where(
                lower_side,
                jnp.concatenate([my_part, their_part], 0),
                jnp.concatenate([their_part, my_part], 0),
            )
    return pieces


def return_pairs(pieces, bit_counts, seq_index):
    pieces = list(pieces)
    for bit_id in reversed(range(max(bit_counts + [0]))):
        active_ids = [branch for branch in range(len(pieces)) if bit_counts[branch] > bit_id]
        lower_side = seq_index // 2**bit_id % 2 == 0
        kept_parts, sent_parts = ([], [])
        for branch in active_ids:
            half_size = pieces[branch].shape[0] // 2
            first_part = pieces[branch][:half_size]
            second_part = pieces[branch][half_size:]
            kept_parts.append(jnp.where(lower_side, first_part, second_part))
            sent_parts.append(jnp.where(lower_side, second_part, first_part))
        partner = from_partner(for_sending(jnp.concatenate(sent_parts, axis=0)), "seq", bit_id)
        offset_at = 0
        for branch, kept_part in zip(active_ids, kept_parts):
            part_size = kept_part.shape[0]
            pieces[branch] = kept_part + partner[offset_at : offset_at + part_size]
            offset_at = offset_at + part_size
    return pieces


def score_block(query_rows, key_rows, query_docs, key_docs):
    raw_scores = jnp.einsum(
        "sqhd,skhd->shqk", query_rows, key_rows, preferred_element_type=jnp.float32
    ) * HEAD_DIM ** (-0.5)
    same_slide = (
        jnp.transpose(query_docs, (0, 2, 1))[..., None]
        == jnp.transpose(key_docs, (0, 2, 1))[:, :, None, :]
    )
    return jnp.where(same_slide, raw_scores, masked_score)


def attend_forward(packed, lengths_row, seq_len, seq_index):
    tok_dev = packed.shape[0]
    triple = packed.reshape(tok_dev, 3, HEADS, HEAD_DIM)
    queries, key_all, value_all = (triple[:, 0], triple[:, 1], triple[:, 2])
    geoms = [branch_geom(branch, tok_dev, seq_len) for branch in range(BRANCHES)]
    local_pairs = [
        jnp.stack([pick_rows(key_all, geom[0]), pick_rows(value_all, geom[0])], axis=1).reshape(
            -1, 2 * D
        )
        for geom in geoms
    ]
    bit_counts = [geom[2].bit_length() - 1 for geom in geoms]
    joined = collect_pairs(local_pairs, bit_counts, seq_index)
    kept_state, outputs, totals_all = ([], [], [])
    for branch in range(BRANCHES):
        dilation, segment, group_size = geoms[branch]
        sections = max(1, tok_dev // segment)
        query_rows = pick_rows(queries, dilation).reshape(sections, -1, HEADS, HEAD_DIM)
        pair_rows = joined[branch].reshape(sections, -1, 2, HEADS, HEAD_DIM)
        key_rows = pair_rows[:, :, 0]
        value_rows = pair_rows[:, :, 1]
        query_docs = branch_docs(
            lengths_row, seq_index * tok_dev, tok_dev // dilation, dilation
        ).reshape(sections, -1, HEADS)
        group_first = seq_index // group_size * group_size * tok_dev
        key_docs = branch_docs(lengths_row, group_first, joined[branch].shape[0], dilation).reshape(
            sections, -1, HEADS
        )
        scores = score_block(query_rows, key_rows, query_docs, key_docs)
        totals = jax.nn.logsumexp(scores, axis=-1)
        softmax_rows = jnp.exp(scores - totals[..., None]).astype(jnp.bfloat16)
        output = jnp.einsum(
            "shqk,skhd->sqhd", softmax_rows, value_rows, preferred_element_type=jnp.float32
        ).reshape(-1, HEADS, HEAD_DIM)
        totals_rows = jnp.transpose(totals, (0, 2, 1)).reshape(-1, HEADS)
        kept_state.append(
            (query_rows, key_rows, value_rows, query_docs, key_docs, output, totals_rows)
        )
        outputs.append(spread_rows(output, dilation, 0.0))
        totals_all.append(spread_rows(totals_rows, dilation, masked_score))
    stacked = jnp.stack(totals_all)
    grand_total = jax.nn.logsumexp(stacked, axis=0)
    mixed_out = jnp.zeros_like(outputs[0])
    for branch in range(BRANCHES):
        mixed_out = mixed_out + jnp.exp(stacked[branch] - grand_total)[..., None] * outputs[branch]
    return (mixed_out, (mixed_out, grand_total, kept_state))


def attend_backward(grad_mixed, attention_state, seq_len, seq_index):
    mixed_out, grand_total, kept_state = attention_state
    tok_dev = grad_mixed.shape[0]
    score_scale = HEAD_DIM ** (-0.5)
    grad_query = jnp.zeros(grad_mixed.shape, jnp.float32)
    key_terms, bit_counts, dilations = ([], [], [])
    for branch in range(BRANCHES):
        dilation, segment, group_size = branch_geom(branch, tok_dev, seq_len)
        query_rows, key_rows, value_rows, query_docs, key_docs, output, totals_rows = kept_state[
            branch
        ]
        sections = query_rows.shape[0]
        weight = jnp.exp(totals_rows - pick_rows(grand_total, dilation))
        grad_picked = pick_rows(grad_mixed, dilation)
        grad_output = (
            (weight[..., None] * grad_picked)
            .astype(jnp.bfloat16)
            .reshape(sections, -1, HEADS, HEAD_DIM)
        )
        grad_totals = weight * jnp.sum(
            grad_picked * (output - pick_rows(mixed_out, dilation)), axis=-1
        )
        grad_totals = jnp.transpose(grad_totals.reshape(sections, -1, HEADS), (0, 2, 1))
        totals = jnp.transpose(totals_rows.reshape(sections, -1, HEADS), (0, 2, 1))
        softmax_rows = jnp.exp(
            score_block(query_rows, key_rows, query_docs, key_docs) - totals[..., None]
        )
        grad_value = jnp.einsum(
            "shqk,sqhd->skhd",
            softmax_rows.astype(jnp.bfloat16),
            grad_output,
            preferred_element_type=jnp.float32,
        )
        grad_probs = jnp.einsum(
            "sqhd,skhd->shqk", grad_output, value_rows, preferred_element_type=jnp.float32
        )
        inner_sum = jnp.sum(softmax_rows * grad_probs, axis=-1, keepdims=True)
        grad_scores = (softmax_rows * (grad_probs - inner_sum + grad_totals[..., None])).astype(
            jnp.bfloat16
        )
        grad_q = (
            jnp.einsum("shqk,skhd->sqhd", grad_scores, key_rows, preferred_element_type=jnp.float32)
            * score_scale
        )
        grad_k = (
            jnp.einsum(
                "shqk,sqhd->skhd", grad_scores, query_rows, preferred_element_type=jnp.float32
            )
            * score_scale
        )
        grad_query = grad_query + spread_rows(grad_q.reshape(-1, HEADS, HEAD_DIM), dilation, 0.0)
        key_terms.append(
            jnp.stack(
                [grad_k.reshape(-1, HEADS, HEAD_DIM), grad_value.reshape(-1, HEADS, HEAD_DIM)],
                axis=1,
            ).reshape(-1, 2 * D)
        )
        bit_counts.append(group_size.bit_length() - 1)
        dilations.append(dilation)
    own_terms = return_pairs(key_terms, bit_counts, seq_index)
    grad_key = jnp.zeros(grad_mixed.shape, jnp.float32)
    grad_val = jnp.zeros(grad_mixed.shape, jnp.float32)
    for branch in range(BRANCHES):
        pair_rows = own_terms[branch].reshape(-1, 2, HEADS, HEAD_DIM)
        grad_key = grad_key + spread_rows(pair_rows[:, 0], dilations[branch], 0.0)
        grad_val = grad_val + spread_rows(pair_rows[:, 1], dilations[branch], 0.0)
    return jnp.stack([grad_query, grad_key, grad_val], axis=1).reshape(tok_dev, 3 * D)


def layer_forward(hidden, upper_mat, lower_mat, row_set, lengths_row, seq_len, seq_index):
    normed = layer_norm(hidden, row_set[0], row_set[1]).astype(jnp.bfloat16)
    biases = jnp.concatenate([row_set[2], jnp.zeros_like(row_set[2]), row_set[3]])
    packed = (
        jnp.dot(normed, upper_mat[:, : 3 * D], preferred_element_type=jnp.float32) + biases[None, :]
    ).astype(jnp.bfloat16)
    mixed_out, attention_state = attend_forward(packed, lengths_row, seq_len, seq_index)
    mixed_low = mixed_out.reshape(-1, D).astype(jnp.bfloat16)
    middle = (
        hidden
        + jnp.dot(mixed_low, upper_mat[:, 3 * D : 4 * D], preferred_element_type=jnp.float32)
        + row_set[4][None, :]
    )
    second = layer_norm(middle, row_set[5], row_set[6]).astype(jnp.bfloat16)
    before = (
        jnp.dot(second, upper_mat[:, 4 * D :], preferred_element_type=jnp.float32)
        + row_set[8:].reshape(-1)[None, :]
    )
    active = jax.nn.gelu(before, approximate=True).astype(jnp.bfloat16)
    result = (
        middle
        + jnp.dot(active, lower_mat, preferred_element_type=jnp.float32)
        + row_set[7][None, :]
    )
    return (result, (hidden, normed, mixed_low, middle, second, before, active, attention_state))


def layer_backward(grad_result, upper_mat, lower_mat, row_set, layer_state, seq_len, seq_index):
    hidden, normed, mixed_low, middle, second, before, active, attention_state = layer_state
    grad_out = grad_result.astype(jnp.bfloat16)
    grad_lower = contract_rows(active, grad_out)
    grad_fc2_bias = jnp.sum(grad_out, axis=0, dtype=jnp.float32)
    grad_active = contract_cols(grad_out, lower_mat)
    gelu_value, gelu_back = jax.vjp(partial(jax.nn.gelu, approximate=True), before)
    grad_before = gelu_back(grad_active)[0].astype(jnp.bfloat16)
    grad_fc1 = contract_rows(second, grad_before)
    grad_fc1_bias = jnp.sum(grad_before, axis=0, dtype=jnp.float32)
    grad_second = contract_cols(grad_before, upper_mat[:, 4 * D :])
    norm_value, norm_back = jax.vjp(layer_norm, middle, row_set[5], row_set[6])
    grad_middle, grad_gain_two, grad_shift_two = norm_back(grad_second)
    grad_middle = grad_middle + grad_result
    grad_branch = grad_middle.astype(jnp.bfloat16)
    grad_proj = contract_rows(mixed_low, grad_branch)
    grad_proj_bias = jnp.sum(grad_branch, axis=0, dtype=jnp.float32)
    grad_mixed = contract_cols(grad_branch, upper_mat[:, 3 * D : 4 * D]).reshape(
        -1, HEADS, HEAD_DIM
    )
    grad_packed = attend_backward(grad_mixed, attention_state, seq_len, seq_index).astype(
        jnp.bfloat16
    )
    grad_qkv = contract_rows(normed, grad_packed)
    packed_sums = jnp.sum(grad_packed, axis=0, dtype=jnp.float32)
    grad_normed = contract_cols(grad_packed, upper_mat[:, : 3 * D])
    first_value, first_back = jax.vjp(layer_norm, hidden, row_set[0], row_set[1])
    grad_hidden, grad_gain_one, grad_shift_one = first_back(grad_normed)
    grad_hidden = grad_hidden + grad_middle
    grad_upper = jnp.concatenate([grad_qkv, grad_proj, grad_fc1], axis=1)
    small_rows = jnp.stack(
        [
            grad_gain_one,
            grad_shift_one,
            packed_sums[:D],
            packed_sums[2 * D :],
            grad_proj_bias,
            grad_gain_two,
            grad_shift_two,
            grad_fc2_bias,
        ]
    )
    grad_rows = jnp.concatenate([small_rows, grad_fc1_bias.reshape(-1, D)], axis=0)
    return (grad_hidden, (grad_upper, grad_lower, grad_rows))


def inverse_root(matrix):
    identity = jnp.eye(matrix.shape[-1], dtype=jnp.float32)
    regular = matrix + root_eps * identity
    frob_norm = jnp.sqrt(jnp.sum(regular * regular, axis=(1, 2), keepdims=True))
    scaled = 2.5 / frob_norm
    root_mat = identity * jnp.sqrt(jnp.sqrt(scaled))
    moving = regular * scaled
    for sweep_id in range(NEWTON):
        factor = (5.0 * identity - moving) * 0.25
        root_mat = jnp.einsum("kij,kjl->kil", root_mat, factor, precision=highest)
        square = jnp.einsum("kij,kjl->kil", factor, factor, precision=highest)
        fourth = jnp.einsum("kij,kjl->kil", square, square, precision=highest)
        moving = jnp.einsum("kij,kjl->kil", fourth, moving, precision=highest)
    return root_mat


def adam_update(weight, first_mom, second_mom, grad, rate, decay):
    first_new = beta_one * first_mom + (1.0 - beta_one) * grad
    second_new = beta_two * second_mom + (1.0 - beta_two) * grad * grad
    first_hat = first_new / (1.0 - beta_one**STEP)
    second_hat = second_new / (1.0 - beta_two**STEP)
    return (
        first_new,
        second_new,
        weight - rate * (first_hat / (jnp.sqrt(second_hat) + adam_eps) + decay * weight),
    )


def per_device(
    features,
    tile_mask,
    lengths,
    owners,
    layer_blocks,
    stat_left,
    stat_right,
    io_weights,
    io_first,
    io_second,
    vectors,
    vec_first,
    vec_second,
):
    tok_dev = features.shape[1]
    seq_size = lax.axis_size("seq")
    seq_len = tok_dev * seq_size
    seq_index = lax.axis_index("seq")
    core_index = lax.axis_index("opt")
    targets = features[0].astype(jnp.float32)
    chosen = tile_mask[0][:, None] > 0
    lengths_row = lax.dynamic_index_in_dim(lengths, core_index, 0, keepdims=False)
    places = seq_index * tok_dev + jnp.arange(tok_dev, dtype=jnp.int32)
    all_blocks, all_io = (
        lax.all_gather(layer_blocks.astype(jnp.bfloat16), ("seq", "opt"), axis=0, tiled=True),
        lax.all_gather(io_weights.astype(jnp.bfloat16), ("seq", "opt"), axis=0, tiled=True),
    )
    natural = jnp.zeros_like(all_blocks).at[owners].set(all_blocks)
    upper_mats, lower_mats = assemble(natural)
    tile_count = lax.psum(jnp.sum(tile_mask.astype(jnp.float32)), ("seq", "opt"))
    layer_rows, tail_rows = unpack(vectors)
    token_vec = tail_rows[3 + FEAT // D :].reshape(FEAT)
    head_bias = tail_rows[3 : 3 + FEAT // D].reshape(FEAT)
    inputs = jnp.where(chosen, token_vec[None, :], targets).astype(jnp.bfloat16)
    in_weight = all_io[:, 0]
    head_weight = all_io[:, 1]
    hidden = jnp.dot(inputs, in_weight, preferred_element_type=jnp.float32) + tail_rows[2][None, :]
    hidden = hidden + sine_places(slide_offsets(lengths_row, places))
    layer_id = 0
    hidden, layer_state = layer_forward(
        hidden,
        upper_mats[layer_id],
        lower_mats[layer_id],
        layer_rows[layer_id],
        lengths_row,
        seq_len,
        seq_index,
    )
    layer_states = [layer_state]
    final, final_back = jax.vjp(layer_norm, hidden, tail_rows[0], tail_rows[1])
    final_low = final.astype(jnp.bfloat16)
    predict = contract_cols(final_low, head_weight) + head_bias[None, :]
    difference = predict - targets
    error_local = jnp.sum(jnp.where(chosen, difference * difference, 0.0))
    grad_pred = jnp.where(chosen, 2.0 * difference / tile_count, 0.0).astype(jnp.bfloat16)
    grad_head = contract_rows(grad_pred, final_low)
    grad_head_bias = jnp.sum(grad_pred, axis=0, dtype=jnp.float32)
    grad_final = jnp.dot(grad_pred, head_weight, preferred_element_type=jnp.float32)
    grad_hidden, grad_gain_last, grad_shift_last = final_back(grad_final)
    layer_grads = [None] * LAYERS
    for layer_id in reversed(range(LAYERS)):
        grad_hidden, layer_grads[layer_id] = layer_backward(
            grad_hidden,
            upper_mats[layer_id],
            lower_mats[layer_id],
            layer_rows[layer_id],
            layer_states[layer_id],
            seq_len,
            seq_index,
        )
    grad_in_low = grad_hidden.astype(jnp.bfloat16)
    grad_in = contract_rows(inputs, grad_in_low)
    grad_in_bias = jnp.sum(grad_in_low, axis=0, dtype=jnp.float32)
    grad_inputs = contract_cols(grad_in_low, in_weight)
    grad_token = jnp.sum(jnp.where(chosen, grad_inputs, 0.0), axis=0)
    grad_upper = jnp.stack([item[0] for item in layer_grads])
    grad_lower = jnp.stack([item[1] for item in layer_grads])
    slot_grads = disassemble(grad_upper, grad_lower)[owners]
    io_grads = jnp.stack([grad_in, grad_head], axis=1)
    vec_grads = jnp.concatenate(
        [
            jnp.stack([item[2] for item in layer_grads]).reshape(-1, D),
            jnp.stack([grad_gain_last, grad_shift_last, grad_in_bias]),
            grad_head_bias.reshape(-1, D),
            grad_token.reshape(-1, D),
        ],
        axis=0,
    )
    slot_sum, io_sum = (
        lax.psum_scatter(slot_grads, ("seq", "opt"), scatter_dimension=0, tiled=True),
        lax.psum_scatter(io_grads, ("seq", "opt"), scatter_dimension=0, tiled=True),
    )
    vec_sum, error_sum = lax.psum((vec_grads, error_local), ("seq", "opt"))
    local_sq = jnp.sum(slot_sum * slot_sum) + jnp.sum(io_sum * io_sum)
    grad_norm = jnp.sqrt(lax.psum(local_sq, ("seq", "opt")) + jnp.sum(vec_sum * vec_sum))
    factor = jnp.minimum(1.0, clip_limit / grad_norm)
    block_grads = slot_sum * factor
    left_new = beta_stat * stat_left + (1.0 - beta_stat) * jnp.einsum(
        "kij,klj->kil", block_grads, block_grads, precision=highest
    )
    right_new = beta_stat * stat_right + (1.0 - beta_stat) * jnp.einsum(
        "kji,kjl->kil", block_grads, block_grads, precision=highest
    )
    direction = jnp.einsum("kij,kjl->kil", inverse_root(left_new), block_grads, precision=highest)
    direction = jnp.einsum("kij,kjl->kil", direction, inverse_root(right_new), precision=highest)
    blocks_new = layer_blocks - rate_shampoo * direction
    io_first_new, io_second_new, io_new = adam_update(
        io_weights, io_first, io_second, io_sum * factor, rate_adam, weight_decay
    )
    vec_first_new, vec_second_new, vec_new = adam_update(
        vectors, vec_first, vec_second, vec_sum * factor, rate_vector, 0.0
    )
    return (
        grad_norm,
        error_sum,
        tile_count,
        block_grads,
        left_new,
        right_new,
        blocks_new,
        io_first_new,
        io_second_new,
        io_new,
        vec_first_new,
        vec_second_new,
        vec_new,
    )


BF=jnp.bfloat16; LANE=128; IO=48
def swap(value, axis, mask):
    return lax.ppermute(value, axis, [(s, s ^ mask) for s in range(lax.axis_size(axis))])
def gate(value, other):
    return lax.optimization_barrier((value, other))

COUNT_AT=3*3*BLOCK+6*IO
SHARD_HALF=COUNT_AT+16
def pack_kernel(blocks_ref, in_ref, head_ref, mask_ref, out_ref):
    count=jnp.sum(mask_ref[...].astype(jnp.float32),keepdims=True)
    lane=lax.broadcasted_iota(jnp.int32,(BLOCK,LANE),1)
    pad=lambda x: jnp.concatenate([x,jnp.zeros((BLOCK,LANE-BLOCK),x.dtype)],axis=1)
    for h,io in enumerate((in_ref,head_ref)):
        for g in range(3):
            b=[pad(blocks_ref[(h*3+g)*4+t]) for t in range(4)]
            for v in range(3):
                tile=jnp.where(lane<BLOCK,b[v],pltpu.roll(b[3],BLOCK-32*v,1))
                at=h*SHARD_HALF+(g*3+v)*BLOCK
                out_ref[at:at+BLOCK,:]=tile.astype(BF)
        for v in range(6):
            at=h*SHARD_HALF+9*BLOCK+v*IO
            out_ref[at:at+IO,:]=io[:,v*LANE:(v+1)*LANE].astype(BF)
        out_ref[h*SHARD_HALF+COUNT_AT:(h+1)*SHARD_HALF,:]=jnp.broadcast_to(count,(16,LANE)).astype(BF)
def vmem(): return pl.BlockSpec(memory_space=pltpu.VMEM)
def smem(): return pl.BlockSpec(memory_space=pltpu.SMEM)
def hbm(): return pl.BlockSpec(memory_space=pl.ANY)
def pack_shard(blocks, io, mask):
    return pl.pallas_call(pack_kernel,out_shape=jax.ShapeDtypeStruct((2*SHARD_HALF,LANE),BF),in_specs=[vmem()]*4,out_specs=vmem(),name="pack_shard")(blocks,io[:,0],io[:,1],mask)

HOPS=(("opt",1),("seq",1),("seq",2),("seq",4),("seq",8))
def hop(value, k):
    return value+swap(value,*HOPS[k])

def gather_tree(own):
    half=own.shape[0]//2
    far=[own,swap(own,"seq",4),swap(own,"seq",8)]
    far.append(swap(far[2],"seq",4))
    out=[]; other=[]
    for piece in far:
        first,second=piece[:half],piece[half:]
        first_x=swap(first,"seq",1); second_y=swap(second,"seq",2)
        first_y=swap(jnp.concatenate([first,first_x]),"seq",2)
        second_x=swap(jnp.concatenate([second,second_y]),"seq",1)
        out.append(jnp.concatenate([piece,first_x,second_y,first_y,second_x]))
        other.append(swap(out[-1],"opt",1))
    return out+other

HELD=64*SHARD_HALF
N_BLOCK=768
def load_shards(bufs, held, sem, fourths):
    rows=bufs[0].shape[0]
    loads=[pltpu.make_async_copy(b,held.at[pl.ds(k*rows,rows)],sem.at[k]) for k,b in enumerate(bufs)]
    for c in loads: c.start()
    fourths()
    for k,c in enumerate(loads):
        c.wait()
        def unpack(u,carry,k=k):
            at=(k*8+u)*SHARD_HALF
            for g in range(3):
                parts=[held[pl.ds(pl.multiple_of(at+(g*3+v)*BLOCK,16),BLOCK),BLOCK:] for v in range(3)]
                to=HELD+((k*8+u)*3+g)*BLOCK
                held[pl.ds(pl.multiple_of(to,16),BLOCK),:BLOCK]=jnp.concatenate(parts,axis=1)
            return carry
        lax.fori_loop(0,8,unpack,0,unroll=8)

def join_kernel(plan, io_out, owners_ref, row_ref, io_ref, *refs):
    bufs=refs[:8]; n_out=len(plan); outs=refs[8:8+n_out]; io_ref_out,count_ref=refs[8+n_out:8+n_out+2]
    held,stage,where,in_sem,out_sem,io_sem=refs[8+n_out+2:]
    def invert():
        def one(i,carry):
            for j in range(8):
                where[owners_ref[i*8+j]]=row_ref[i*8+j]
            return carry
        lax.fori_loop(0,N_BLOCK//8,one,0)
    load_shards(bufs,held,in_sem,invert)
    def io_copy(d,total):
        at=io_ref[io_out,d]
        for v in range(6):
            pltpu.make_async_copy(held.at[pl.ds(pl.multiple_of(at+v*IO,16),IO)],
                io_ref_out.at[pl.ds(pl.multiple_of(d*IO,IO),IO),pl.ds(v*LANE,LANE)],io_sem).start()
        return total+held[pl.ds(pl.multiple_of(at+6*IO,16),16),:].astype(jnp.float32)
    count_ref[...]=lax.fori_loop(0,io_ref.shape[1],io_copy,jnp.zeros((16,LANE),jnp.float32))
    def block(n):
        return held[pl.ds(pl.multiple_of(where[n],16),BLOCK),:BLOCK]
    pending=[]; index=0
    for (first,stride,rows,stripes),out in zip(plan,outs):
        per=8//stripes if stripes<8 else 1
        for i0 in range(0,rows,per):
            slot=index%2
            if index>=2:
                for c in pending[index-2]: c.wait()
            for b in range(per):
                def one(c,carry,b=b,i0=i0):
                    n=first+(i0+b)*stride+4*c
                    stage[slot,:,pl.ds(pl.multiple_of((b*stripes+c)*4*BLOCK,128),4*BLOCK)]=jnp.concatenate([block(n+t) for t in range(4)],axis=1)
                    return carry
                lax.fori_loop(0,stripes,one,0,unroll=2 if stripes%4 else 4)
            w=stripes*4*BLOCK
            cs=[pltpu.make_async_copy(stage.at[slot,:,pl.ds(b*w,w)],out.at[pl.ds((i0+b)*BLOCK,BLOCK)],out_sem.at[slot,b]) for b in range(per)]
            for c in cs: c.start()
            pending.append(cs); index+=1
    for cs in pending[-2:]:
        for c in cs: c.wait()
    pltpu.make_async_copy(io_ref_out,io_ref_out,io_sem).wait()

COLS=(4*D+FF)//BLOCK
FIRST_PLAN=((0,COLS,8,6),(24,COLS,8,2))
SECOND_PLAN=((32,COLS,8,8),(8*COLS,8,32,2))
def join_weights(plan, io_out, bufs, owners, rows, io_rows):
    shapes=[(r*BLOCK,s*4*BLOCK) for _,_,r,s in plan]+[(FEAT,D)]
    return pl.pallas_call(partial(join_kernel,plan,io_out),
        out_shape=[jax.ShapeDtypeStruct(s,BF) for s in shapes]+[jax.ShapeDtypeStruct((16,LANE),jnp.float32)],
        in_specs=[smem()]*3+[hbm()]*8, out_specs=[hbm()]*len(shapes)+[vmem()],
        scratch_shapes=[pltpu.VMEM((HELD+N_BLOCK//4*BLOCK,LANE),BF),pltpu.VMEM((2,BLOCK,FF),BF),pltpu.SMEM((N_BLOCK,),jnp.int32),
            pltpu.SemaphoreType.DMA((8,)),pltpu.SemaphoreType.DMA((2,4)),pltpu.SemaphoreType.DMA],
        compiler_params=pltpu.CompilerParams(vmem_limit_bytes=40<<20), cost_estimate=pl.CostEstimate(flops=0,transcendentals=0,bytes_accessed=int((13 if io_out==0 else 17)*3.3e6)), name="join_weights")(owners,rows,io_rows,*bufs)

def shard_rows(seq_index, core):
    def unit(dev,h):
        rel=(dev//2)^seq_index; xy=rel%4
        u=jnp.where(xy==0,h,jnp.where(h==0,jnp.where(xy==1,2,xy+2),jnp.where(xy==2,3,jnp.where(xy==1,6,7))))
        return (rel//4+4*((dev%2)^core))*8+u
    slot=jnp.arange(N_BLOCK,dtype=jnp.int32); s=slot%24
    u=unit(slot//24,s//12); g=s%12//4; t=s%4
    rows=jnp.where(t<3,u*SHARD_HALF+(g*3+t)*BLOCK,HELD+(u*3+g)*BLOCK)
    dev=jnp.arange(32,dtype=jnp.int32)
    io=jnp.stack([unit(dev,h)*SHARD_HALF+9*BLOCK for h in (0,1)])
    return rows.astype(jnp.int32),io.astype(jnp.int32)
def gather_shards(layer_blocks, io_weights, mask):
    return gather_tree(pack_shard(layer_blocks,io_weights,mask))

HD=48; HEADS=16; SLIDES=4; SEG=1024; N=2048; H=512; TQ=256; TK=128
C2=HD**-0.5*math.log2(math.e)
def place_facts(index, head, lengths_ref, core):
    parity=lax.rem(head+(index//H)%2,2)
    pos=(index//SEG)*SEG+2*(index%H)+parity
    slide=jnp.zeros_like(index); end=jnp.int32(0)
    for i in range(SLIDES-1):
        end=end+lengths_ref[core,i]
        slide=slide+jnp.where(pos>=end,1,0)
    d=(pos-head)&15
    level=sum(jnp.where((d&(2**i-1))==0,1,0) for i in range(1,5))
    return slide.astype(jnp.float32), level.astype(jnp.float32)

def arrange(src, dst, odd):
    for pair in range(8):
        first, second = src[2*pair], src[2*pair+1]
        turn=lambda t: jnp.concatenate([t[:,64:],t[:,:64]],axis=1)
        ft, st = turn(first), turn(second)
        low=lax.broadcasted_iota(jnp.int32,first.shape,1)<64
        evens=jnp.where(low,first,st); odds=jnp.where(low,ft,second)
        near=jnp.where(odd,odds,evens); far=jnp.where(odd,evens,odds)
        at=(pair//4)*SEG+(pair%4)*128
        dst[:,at:at+128]=near.astype(dst.dtype); dst[:,at+H:at+H+128]=far.astype(dst.dtype)

def restore(get, put, odd):
    for pair in range(8):
        at=(pair//4)*SEG+(pair%4)*128
        near, far = get(at), get(at+H)
        evens=jnp.where(odd,far,near); odds=jnp.where(odd,near,far)
        turn=lambda t: jnp.concatenate([t[:,64:],t[:,:64]],axis=1)
        low=lax.broadcasted_iota(jnp.int32,evens.shape,1)<64
        put(2*pair, jnp.where(low,evens,turn(odds)))
        put(2*pair+1, jnp.where(low,turn(evens),odds))

def setup(lengths_ref, ids_ref, slide_k, level_k, row_facts):
    head, core = ids_ref[0], ids_ref[1]
    def fill(i, c):
        idx=lax.broadcasted_iota(jnp.int32,(TK,128),0)+i*TK
        s,l=place_facts(idx,head,lengths_ref,core)
        slide_k[pl.ds(pl.multiple_of(i*TK,TK),TK),:]=s
        level_k[pl.ds(pl.multiple_of(i*TK,TK),TK),:]=l
        return c
    lax.fori_loop(0,N//TK,fill,0)
    idx=lax.broadcasted_iota(jnp.int32,(8,N),1)
    s,l=place_facts(idx,head,lengths_ref,core)
    row_facts[0:8,:]=s; row_facts[8:16,:]=l

def key_rows(seg, near):
    own=[(seg*SEG+i*TK,True) for i in range(SEG//TK)]
    other=[((1-seg)*SEG+i*TK,False) for i in range(H//TK)] if near else []
    return own+other

def wide(x): return jnp.concatenate([x]*(TQ//128),axis=1)

def forward_kernel(lengths_ref, ids_ref, qkv_ref, o_ref, out_ref, lse_ref, qkvT, krow, slide_k, level_k, row_facts, s_ref, p_ref):
    odd=lax.rem(ids_ref[0],2)==1
    arrange(qkv_ref, qkvT, odd)
    setup(lengths_ref, ids_ref, slide_k, level_k, row_facts)
    for i in range(N//128):
        krow[i*128:(i+1)*128,:]=qkvT[HD:2*HD,i*128:(i+1)*128].astype(jnp.float32).T.astype(jnp.bfloat16)
    for seg in range(2):
        for near in (True,False):
            tiles=key_rows(seg,near)
            def part(c, carry, seg=seg, near=near, tiles=tiles):
                at=pl.multiple_of(seg*SEG+(0 if near else H)+c*TQ,TQ)
                qT=qkvT[0:HD,pl.ds(at,TQ)]
                sq=row_facts[0:1,pl.ds(at,TQ)]; lq=row_facts[8:9,pl.ds(at,TQ)]
                top=jnp.full((8,TQ),-jnp.inf,jnp.float32)
                for t,(r,own) in enumerate(tiles):
                    s=jnp.dot(krow[r:r+TK,:],qT,preferred_element_type=jnp.float32)
                    s=jnp.where(wide(slide_k[r:r+TK,:])==sq,s,-1e30)
                    s_ref[t*TK:(t+1)*TK,:]=s
                    top=jnp.maximum(top,jnp.max(s.reshape(TK//8,8,TQ),axis=0))
                m=jnp.max(top,axis=0,keepdims=True)
                total=jnp.zeros((8,TQ),jnp.float32)
                for t,(r,own) in enumerate(tiles):
                    e=jnp.exp2((s_ref[t*TK:(t+1)*TK,:]-m)*C2)
                    if near:
                        lk=wide(level_k[r:r+TK,:])
                        e=e*(jnp.minimum(lk,lq)+1.0 if own else jnp.minimum(lk,lq))
                    total=total+jnp.sum(e.reshape(TK//8,8,TQ),axis=0)
                    p_ref[t*TK:(t+1)*TK,:]=e.astype(jnp.bfloat16)
                l=jnp.sum(total,axis=0,keepdims=True)
                acc=jnp.zeros((HD,TQ),jnp.float32)
                acc=jnp.dot(qkvT[2*HD:3*HD,seg*SEG:(seg+1)*SEG],p_ref[0:SEG,:],preferred_element_type=jnp.float32)
                if near:
                    acc=acc+jnp.dot(qkvT[2*HD:3*HD,(1-seg)*SEG:(1-seg)*SEG+H],p_ref[SEG:SEG+H,:],preferred_element_type=jnp.float32)
                o_ref[:,pl.ds(at,TQ)]=acc/l
                lse_ref[:,pl.ds(at,TQ)]=jnp.broadcast_to(m*C2+jnp.log2(l),(8,TQ))
                return carry
            lax.fori_loop(0,H//TQ,part,0)
    def put(c,v): out_ref[c]=v.astype(jnp.bfloat16)
    restore(lambda at: o_ref[:,at:at+128], put, odd)

def backward_kernel(lengths_ref, ids_ref, qkv_ref, do_ref, o_ref, lse_ref, out_ref, qkvT, doT, rows, slide_k, level_k, row_facts, dqT, dkv, p_ref, ds_ref):
    odd=lax.rem(ids_ref[0],2)==1
    arrange(qkv_ref, qkvT, odd)
    arrange(do_ref, doT, odd)
    setup(lengths_ref, ids_ref, slide_k, level_k, row_facts)
    for i in range(N//128):
        l=slice(i*128,(i+1)*128)
        for j in range(3):
            rows[j,l,:]=qkvT[j*HD:(j+1)*HD,l].astype(jnp.float32).T.astype(jnp.bfloat16)
        rows[3,l,:]=doT[:,l].astype(jnp.float32).T.astype(jnp.bfloat16)
    dkv[...]=jnp.zeros_like(dkv)
    for seg in range(2):
        for near in (True,False):
            tiles=key_rows(seg,near)
            def part(c, carry, seg=seg, near=near, tiles=tiles):
                at=pl.multiple_of(seg*SEG+(0 if near else H)+c*TQ,TQ)
                qT=qkvT[0:HD,pl.ds(at,TQ)]; gT=doT[:,pl.ds(at,TQ)]
                q=rows[0,pl.ds(at,TQ),:]; g=rows[3,pl.ds(at,TQ),:]
                sq=row_facts[0:1,pl.ds(at,TQ)]; lq=row_facts[8:9,pl.ds(at,TQ)]
                lse=lse_ref[0:1,pl.ds(at,TQ)]
                inner=jnp.sum(gT.astype(jnp.float32)*o_ref[:,pl.ds(at,TQ)],axis=0,keepdims=True)
                for t,(r,own) in enumerate(tiles):
                    s=jnp.dot(rows[1,r:r+TK,:],qT,preferred_element_type=jnp.float32)
                    dp=jnp.dot(rows[2,r:r+TK,:],gT,preferred_element_type=jnp.float32)
                    e=jnp.exp2(s*C2-lse)
                    if near:
                        lk=wide(level_k[r:r+TK,:])
                        e=e*(jnp.minimum(lk,lq)+1.0 if own else jnp.minimum(lk,lq))
                    e=jnp.where(wide(slide_k[r:r+TK,:])==sq,e,0.0)
                    p_ref[t*TK:(t+1)*TK,:]=e.astype(jnp.bfloat16)
                    ds_ref[t*TK:(t+1)*TK,:]=(e*(dp-inner)).astype(jnp.bfloat16)
                dq=jnp.dot(qkvT[HD:2*HD,seg*SEG:(seg+1)*SEG],ds_ref[0:SEG,:],preferred_element_type=jnp.float32)
                if near:
                    dq=dq+jnp.dot(qkvT[HD:2*HD,(1-seg)*SEG:(1-seg)*SEG+H],ds_ref[SEG:SEG+H,:],preferred_element_type=jnp.float32)
                dqT[:,pl.ds(at,TQ)]=dq*HD**-0.5
                own=slice(seg*SEG,(seg+1)*SEG)
                dkv[0,own,:]+=jnp.dot(ds_ref[0:SEG,:],q,preferred_element_type=jnp.float32)
                dkv[1,own,:]+=jnp.dot(p_ref[0:SEG,:],g,preferred_element_type=jnp.float32)
                if near:
                    oth=slice((1-seg)*SEG,(1-seg)*SEG+H)
                    dkv[0,oth,:]+=jnp.dot(ds_ref[SEG:SEG+H,:],q,preferred_element_type=jnp.float32)
                    dkv[1,oth,:]+=jnp.dot(p_ref[SEG:SEG+H,:],g,preferred_element_type=jnp.float32)
                return carry
            lax.fori_loop(0,H//TQ,part,0)
    def putter(j):
        def put(c,v): out_ref[c,j*HD:(j+1)*HD,:]=v.astype(jnp.bfloat16)
        return put
    restore(lambda at: dqT[:,at:at+128], putter(0), odd)
    restore(lambda at: dkv[0,at:at+128,:].T*HD**-0.5, putter(1), odd)
    restore(lambda at: dkv[1,at:at+128,:].T, putter(2), odd)

def vm(): return pl.BlockSpec(memory_space=pltpu.VMEM)
def sm_(): return pl.BlockSpec(memory_space=pltpu.SMEM)
def attend(lengths, ids, qkv):
    return pl.pallas_call(forward_kernel,
        out_shape=[jax.ShapeDtypeStruct((HD,N),F32),jax.ShapeDtypeStruct((16,HD,128),BF),jax.ShapeDtypeStruct((8,N),F32)],
        in_specs=[sm_(),sm_(),vm()], out_specs=[vm()]*3,
        scratch_shapes=[pltpu.VMEM((3*HD,N),BF),pltpu.VMEM((N,HD),BF),pltpu.VMEM((N,128),F32),pltpu.VMEM((N,128),F32),pltpu.VMEM((16,N),F32),
            pltpu.VMEM((SEG+H,TQ),F32),pltpu.VMEM((SEG+H,TQ),BF)],
        compiler_params=pltpu.CompilerParams(vmem_limit_bytes=48<<20), cost_estimate=pl.CostEstimate(flops=0,transcendentals=0,bytes_accessed=35000000), name="attend_forward")(lengths,ids,qkv)
def attend_back(lengths, ids, qkv, do, o, lse):
    return pl.pallas_call(backward_kernel,
        out_shape=jax.ShapeDtypeStruct((16,3*HD,128),BF),
        in_specs=[sm_(),sm_()]+[vm()]*4, out_specs=vm(),
        scratch_shapes=[pltpu.VMEM((3*HD,N),BF),pltpu.VMEM((HD,N),BF),pltpu.VMEM((4,N,HD),BF),pltpu.VMEM((N,128),F32),pltpu.VMEM((N,128),F32),pltpu.VMEM((16,N),F32),
            pltpu.VMEM((HD,N),F32),pltpu.VMEM((2,N,HD),F32),pltpu.VMEM((SEG+H,TQ),BF),pltpu.VMEM((SEG+H,TQ),BF)],
        compiler_params=pltpu.CompilerParams(vmem_limit_bytes=48<<20), cost_estimate=pl.CostEstimate(flops=0,transcendentals=0,bytes_accessed=45000000), name="attend_backward")(lengths,ids,qkv,do,o,lse)

F32=jnp.float32
EPS=1e-05
def norm_parts(x):
    centred=x-jnp.mean(x,axis=-1,keepdims=True)
    spread=lax.rsqrt(jnp.mean(centred*centred,axis=-1,keepdims=True)+EPS)
    return centred*spread,spread
def norm_back(grad,unit,spread,gain):
    inner=grad*gain
    back=spread*(inner-jnp.mean(inner,axis=-1,keepdims=True)-unit*jnp.mean(inner*unit,axis=-1,keepdims=True))
    return back,jnp.sum(grad*unit,axis=0,keepdims=True),jnp.sum(grad,axis=0,keepdims=True)
def put_turned(ref,at,x):
    for c in range(x.shape[1]//LANE):
        ref[at+c*LANE:at+(c+1)*LANE,:]=x[:,c*LANE:(c+1)*LANE].astype(F32).T.astype(BF)
def turned(ref,rows):
    return jnp.concatenate([ref[c*LANE:(c+1)*LANE,:].astype(F32).T for c in range(rows//LANE)],axis=1)
def mm(a,b): return jnp.dot(a,b,preferred_element_type=F32)
def mm_t(a,b): return lax.dot_general(a,b,(((1,),(1,)),((),())),preferred_element_type=F32)
GELU_A=math.sqrt(2.0/math.pi); GELU_B=0.044715
def mlp_kernel(count_ref, hidden_ref, mixed_ref, targets_ref, chosen_ref, vec_ref, wo_ref, up_ref, down_ref, head_ref,
               middle_grad_ref, mixed_grad_ref, second_ref, active_ref, branch_ref, before_ref, out_ref, pred_ref, final_ref, rows_ref, kept, low):
    row=lambda i: vec_ref[i:i+1,:]
    mixed=turned(mixed_ref,D).astype(BF)
    middle=hidden_ref[...]+mm(mixed,wo_ref[...])+row(4)
    unit2,spread2=norm_parts(middle)
    second=(unit2*row(5)+row(6)).astype(BF)
    put_turned(second_ref,0,second)
    result=middle+row(7)
    for c in range(FF//D):
        s=slice(c*D,(c+1)*D)
        before=mm(second,up_ref[:,s])+row(8+c)
        kept[:,s]=before
        active=(before*(0.5*(1.0+jnp.tanh(GELU_A*(before+GELU_B*(before*before*before)))))).astype(BF)
        put_turned(active_ref,c*D,active)
        result=result+mm(active,down_ref[s,:])
    unit,spread=norm_parts(result)
    final=(unit*row(12)+row(13)).astype(BF)
    put_turned(final_ref,0,final)
    chosen=chosen_ref[...]>0.0
    error=jnp.zeros((1,1),F32); grad_final=jnp.zeros_like(middle)
    for c in range(FEAT//D):
        s=slice(c*D,(c+1)*D)
        difference=mm_t(final,head_ref[s,:])+row(15+c)-targets_ref[:,s].astype(F32)
        error=error+jnp.sum(jnp.where(chosen,difference*difference,0.0),keepdims=True)
        pred=jnp.where(chosen,2.0*difference/count_ref[0],0.0).astype(BF)
        put_turned(pred_ref,c*D,pred)
        rows_ref[10+c:11+c,:]=jnp.sum(pred.astype(F32),axis=0,keepdims=True)
        grad_final=grad_final+mm(pred,head_ref[s,:])
    rows_ref[12:13,:]=jnp.broadcast_to(error,(1,D))
    grad_result,rows_ref[8:9,:],rows_ref[9:10,:]=norm_back(grad_final,unit,spread,row(12))
    grad_out=grad_result.astype(BF)
    put_turned(out_ref,0,grad_out)
    rows_ref[3:4,:]=jnp.sum(grad_out.astype(F32),axis=0,keepdims=True)
    grad_second=jnp.zeros_like(middle)
    for c in range(FF//D):
        s=slice(c*D,(c+1)*D)
        grad_active=mm_t(grad_out,down_ref[s,:])
        x=kept[:,s]
        t=jnp.tanh(GELU_A*(x+GELU_B*(x*x*x)))
        slope=0.5*(1.0+t)+x*(0.5*(1.0-t*t)*(GELU_A*(1.0+3.0*GELU_B*(x*x))))
        grad_before=(grad_active*slope).astype(BF)
        put_turned(before_ref,c*D,grad_before)
        rows_ref[4+c:5+c,:]=jnp.sum(grad_before.astype(F32),axis=0,keepdims=True)
        grad_second=grad_second+mm_t(grad_before,up_ref[:,s])
    back,rows_ref[1:2,:],rows_ref[2:3,:]=norm_back(grad_second,unit2,spread2,row(5))
    grad_middle=back+grad_result
    middle_grad_ref[...]=grad_middle
    grad_branch=grad_middle.astype(BF)
    put_turned(branch_ref,0,grad_branch)
    rows_ref[0:1,:]=jnp.sum(grad_branch.astype(F32),axis=0,keepdims=True)
    mixed_grad_ref[...]=mm_t(wo_ref[...],grad_branch).astype(BF)
    rows_ref[13:16,:]=jnp.zeros((3,D),F32)
def mlp_step(count, hidden, mixed, targets, chosen, vectors, wo, up, down, head):
    t=hidden.shape[0]
    low=lambda rows: jax.ShapeDtypeStruct((rows,t),BF)
    return pl.pallas_call(mlp_kernel,
        out_shape=[jax.ShapeDtypeStruct((t,D),F32),low(D),low(D),low(FF),low(D),low(FF),low(D),low(FEAT),low(D),jax.ShapeDtypeStruct((16,D),F32)],
        in_specs=[smem()]+[vmem()]*9,out_specs=[vmem()]*10,
        scratch_shapes=[pltpu.VMEM((t,FF),F32),pltpu.VMEM((8,128),F32)],
        compiler_params=pltpu.CompilerParams(vmem_limit_bytes=48<<20),name="mlp_step")(count.reshape(1),hidden,mixed,targets,chosen,vectors,wo,up,down,head)

def input_kernel(parts_ref, hidden_ref, middle_grad_ref, chosen_ref, vec_ref, rows_ref, qkv_ref, in_ref, packed_ref, in_grad_ref, sums_ref):
    heads,wide,t=parts_ref.shape; hd=wide//3
    for j in range(3):
        for h in range(heads):
            packed_ref[j*D+h*hd:j*D+(h+1)*hd,:]=parts_ref[h,j*hd:(j+1)*hd,:]
    packed=packed_ref[...]
    grad_t=mm(qkv_ref[...],packed)
    grad=jnp.concatenate([grad_t[c*LANE:(c+1)*LANE,:].T for c in range(D//LANE)],axis=1)
    unit,spread=norm_parts(hidden_ref[...])
    back,gain,shift=norm_back(grad,unit,spread,vec_ref[0:1,:])
    grad_hidden=back+middle_grad_ref[...]
    low=grad_hidden.astype(BF)
    put_turned(in_grad_ref,0,low)
    sums_ref[0:1,:]=gain; sums_ref[1:2,:]=shift
    ones=jnp.ones((8,t),BF)
    sums_ref[2:3,:]=mm_t(ones,packed[:D])[0:1]
    sums_ref[3:4,:]=mm_t(ones,packed[2*D:])[0:1]
    sums_ref[4:14,:]=rows_ref[0:10,:]
    sums_ref[14:15,:]=jnp.sum(low.astype(F32),axis=0,keepdims=True)
    sums_ref[15:17,:]=rows_ref[10:12,:]
    masked=jnp.where(chosen_ref[...]>0.0,low.astype(F32),0.0).astype(BF)
    for c in range(FEAT//D):
        sums_ref[17+c:18+c,:]=jnp.sum(mm_t(masked,in_ref[c*D:(c+1)*D,:]),axis=0,keepdims=True)
    sums_ref[19:20,:]=rows_ref[12:13,:]
    sums_ref[20:24,:]=jnp.zeros((4,D),F32)
def input_step(parts, hidden, middle_grad, chosen, vectors, rows, qkv, w_in):
    t=hidden.shape[0]
    return pl.pallas_call(input_kernel,
        out_shape=[jax.ShapeDtypeStruct((3*D,t),BF),jax.ShapeDtypeStruct((D,t),BF),jax.ShapeDtypeStruct((24,D),F32)],
        in_specs=[vmem()]*8,out_specs=[vmem()]*3,
        compiler_params=pltpu.CompilerParams(vmem_limit_bytes=32<<20),name="input_step")(parts,hidden,middle_grad,chosen,vectors,rows,qkv,w_in)

I16=jnp.int16; F32=jnp.float32; BF=jnp.bfloat16
GROUP=48; LANE=128; IO=48
STEP_Q=32000.0
UNITS=24; CODE_ROWS=32; PART=UNITS*GROUP+CODE_ROWS
A_ROWS=3*D+FF; X_ROWS=3*D+D+FF+D
ROUND=12582912.0

def encode(x):
    top=jnp.max(jnp.abs(x),axis=0,keepdims=True)
    code=jnp.ceil(jnp.log2(jnp.maximum(top,1e-30))*256.0)
    v=x*(STEP_Q*jnp.exp2(code*(-1.0/256.0)))
    return ((v+ROUND)-ROUND).astype(jnp.int32).astype(I16), code
def scale_of(code16):
    return jnp.exp2(code16.astype(jnp.int32).astype(F32)*(1.0/256.0))*(1.0/STEP_Q)
def pack_codes(codes):
    codes=codes+[jnp.zeros((CODE_ROWS-len(codes),LANE),F32)]
    return jnp.concatenate(codes,axis=0).astype(jnp.int32).astype(I16)

def grads_kernel(zone, ids_ref, owners_ref, *refs):
    operands=refs[:24]; outs=refs[24:28]
    a_all,x_all,a_in,x_in,a_head,x_head,sem=refs[28:]
    seq,core=ids_ref[0],ids_ref[1]
    rows=0; copies=[]
    targets=[(a_all,0),(a_all,D),(a_all,2*D),(a_all,3*D),(x_all,0),(x_all,3*D),(x_all,4*D),(x_all,4*D+FF),(a_in,0),(x_in,0),(a_head,0),(x_head,0)]
    for k,(buf,at) in enumerate(targets):
        for side in range(2):
            src=operands[2*k+side]
            c=pltpu.make_async_copy(src,buf.at[pl.ds(at,src.shape[0]),pl.ds(side*LANE,LANE)],sem.at[2*k+side])
            c.start(); copies.append(c)
    for c in copies: c.wait()
    lane=lax.broadcasted_iota(jnp.int32,(BLOCK,LANE),1)
    cols=(4*D+FF)//BLOCK; wide_count=D//BLOCK*cols
    def block(slot):
        n=owners_ref[slot]
        i=n//cols; j=n%cols
        m=n-wide_count
        group=jnp.where(j>=3*D//BLOCK,1,0)+jnp.where(j>=4*D//BLOCK,1,0)
        a_at=jnp.where(m<0,i*BLOCK+group*D,3*D+m//(D//BLOCK)*BLOCK)
        x_at=jnp.where(m<0,j*BLOCK,4*D+FF+m%(D//BLOCK)*BLOCK)
        a=a_all[pl.ds(pl.multiple_of(a_at,32),BLOCK),:]
        x=x_all[pl.ds(pl.multiple_of(x_at,32),BLOCK),:]
        w=lax.dot_general(a,x,(((1,),(1,)),((),())),preferred_element_type=F32)
        return jnp.concatenate([w,jnp.zeros((BLOCK,LANE-BLOCK),F32)],axis=1)
    for out,h,first,step in ((outs[0],0,2,1),(outs[2],1,1,2),(outs[1],0,0,1),(outs[3],1,0,2)):
        def one(j,carry,out=out,h=h,first=first,step=step):
            device=2*jnp.bitwise_xor(seq,zone*4+first+step*j)+core
            codes=[]
            for g in range(3):
                w=[block(device*24+(h*3+g)*4+t) for t in range(4)]
                for v in range(3):
                    tile=jnp.where(lane<BLOCK,w[v],pltpu.roll(w[3],BLOCK-32*v,1))
                    for half in range(2):
                        q,code=encode(tile[half*GROUP:(half+1)*GROUP])
                        at=((g*3+v)*2+half)*GROUP
                        out[j,at:at+GROUP,:]=q; codes.append(code)
            a_ref,x_ref=((a_in,x_in),(a_head,x_head))[h]
            w=lax.dot_general(a_ref[pl.ds(pl.multiple_of(device*IO,16),IO),:],x_ref[...],(((1,),(1,)),((),())),preferred_element_type=F32)
            for v in range(6):
                q,code=encode(w[:,v*LANE:(v+1)*LANE])
                at=(18+v)*GROUP
                out[j,at:at+GROUP,:]=q; codes.append(code)
            out[j,UNITS*GROUP:,:]=pack_codes(codes)
            return carry
        lax.fori_loop(0,2,one,0)

def weight_grads(zone, ids, owners, operands):
    n=len(operands)
    return pl.pallas_call(partial(grads_kernel,zone),
        out_shape=[jax.ShapeDtypeStruct((2,PART,LANE),I16)]*4,
        in_specs=[pl.BlockSpec(memory_space=pltpu.SMEM)]*2+[pl.BlockSpec(memory_space=pl.ANY)]*n,
        out_specs=[pl.BlockSpec(memory_space=pltpu.VMEM)]*4,
        scratch_shapes=[pltpu.VMEM((A_ROWS,2*LANE),BF),pltpu.VMEM((X_ROWS,2*LANE),BF),pltpu.VMEM((FEAT,2*LANE),BF),pltpu.VMEM((D,2*LANE),BF),
            pltpu.VMEM((FEAT,2*LANE),BF),pltpu.VMEM((D,2*LANE),BF),pltpu.SemaphoreType.DMA((n,))],
        compiler_params=pltpu.CompilerParams(vmem_limit_bytes=40<<20), cost_estimate=takes(8), name="weight_grads")(ids,owners,*operands)

class At:
    def __init__(s,ref,*i): s.ref,s.i=ref,i
    def __getitem__(s,k): return s.ref[(*s.i,k,slice(None))]
    def __setitem__(s,k,v): s.ref[(*s.i,k,slice(None))]=v
def summed(views):
    scales=[scale_of(v[UNITS*GROUP:PART]) for v in views]
    for k in range(UNITS):
        total=None
        for v,s in zip(views,scales):
            x=v[k*GROUP:(k+1)*GROUP].astype(jnp.int32).astype(F32)*s[k:k+1,:]
            total=x if total is None else total+x
        yield k,total
def add_codes(views, out):
    codes=[]
    for k,total in summed(views):
        q,code=encode(total)
        out[k*GROUP:(k+1)*GROUP]=q
        codes.append(code)
    out[UNITS*GROUP:PART]=pack_codes(codes)
def takes(micros):
    return pl.CostEstimate(flops=0,transcendentals=0,bytes_accessed=int(micros*3.3e6))
def code_call(kernel, name, outs, *args):
    return pl.pallas_call(kernel, out_shape=[jax.ShapeDtypeStruct(s,t) for s,t in outs],
        in_specs=[pl.BlockSpec(memory_space=pltpu.VMEM)]*len(args), out_specs=[pl.BlockSpec(memory_space=pltpu.VMEM)]*len(outs),
        compiler_params=pltpu.CompilerParams(vmem_limit_bytes=32<<20), cost_estimate=takes(1.5), name=name)(*args)
def plane_kernel(keep_a, got_a, keep_b, got_b, send_a, stay_a, send_b, stay_b):
    for keep,got,send,stay in ((keep_a,got_a,send_a,stay_a),(keep_b,got_b,send_b,stay_b)):
        add_codes([At(keep,1),At(got,1)],At(send))
        add_codes([At(keep,0),At(got,0)],At(stay))
def line_kernel(*refs):
    stay_a,got_a,stay_b,got_b=refs[:4]; more=refs[4:-1]; out=refs[-1]
    for h,(stay,got) in enumerate(((stay_a,got_a),(stay_b,got_b))):
        add_codes([At(stay),At(got)]+[At(m,h) for m in more],At(out,h))
def final_kernel(*refs):
    stay_a,got_a,stay_b,got_b=refs[:4]; more=refs[4:-3]; blocks,io_in,io_head=refs[-3:]
    for h,(stay,got,io) in enumerate(((stay_a,got_a,io_in),(stay_b,got_b,io_head))):
        for k,total in summed([At(stay),At(got)]+[At(m,h) for m in more]):
            if k<18:
                g,v,half=k//6,k//2%3,k%2
                rows=slice(half*GROUP,(half+1)*GROUP)
                blocks[(h*3+g)*4+v,rows,:]=total[:,:BLOCK]
                blocks[(h*3+g)*4+3,rows,32*v:32*(v+1)]=total[:,BLOCK:]
            else:
                io[:,(k-18)*LANE:(k-17)*LANE]=total
HALF=(PART,LANE)
def reduce_tree(ids, owners, operands):
    made={}; got={}; stay={}; far={}
    def make(k):
        send_a,keep_a,send_b,keep_b=weight_grads(k,ids,owners,operands)
        made[k]=(keep_a,keep_b); got[k]=(swap(send_a,"seq",2),swap(send_b,"seq",1))
    def plane(k):
        send_a,stay_a,send_b,stay_b=code_call(plane_kernel,"add_plane",[(HALF,I16)]*4,made[k][0],got[k][0],made[k][1],got[k][1])
        stay[k]=(stay_a,stay_b); got[k]=(swap(send_a,"seq",1),swap(send_b,"seq",2))
    def line(k,mask,*more):
        far[k]=swap(code_call(line_kernel,"add_line",[((2,)+HALF,I16)],stay[k][0],got[k][0],stay[k][1],got[k][1],*more)[0],"seq",mask)
    make(3); make(2); make(1); make(0)
    plane(3); line(3,4)
    plane(2); line(2,8,far[3])
    plane(1); line(1,4)
    plane(0)
    return code_call(final_kernel,"add_final",[((24,BLOCK,BLOCK),F32),((IO,D),F32),((IO,D),F32)],stay[0][0],got[0][0],stay[0][1],got[0][1],far[1],far[2])

BLOCK=96; NEWTON=6; F32=jnp.float32; BF=jnp.bfloat16; LANE=128
def halves(x):
    hi=x.astype(BF); return hi,(x-hi.astype(F32)).astype(BF)
def left_of(x):
    hi,lo=halves(x)
    return jnp.concatenate([hi,lo],axis=1)
def right_of(x):
    hi,lo=halves(x)
    zero=jnp.zeros_like(lo)
    return jnp.concatenate([jnp.concatenate([hi,lo],axis=1),jnp.concatenate([hi,zero],axis=1)],axis=0)
def times(a,b):
    w=jnp.dot(a,b,preferred_element_type=F32)
    n=w.shape[1]//2
    return w[:,:n]+w[:,n:]
def shampoo_kernel(scal_ref, grad_ref, left_ref, right_ref, block_ref, grad_out, left_out, right_out, block_out, *, beta, rate, eps, n_side):
    factor=scal_ref[0]
    side=LANE
    row=lax.broadcasted_iota(jnp.int32,(side,side),0); col=lax.broadcasted_iota(jnp.int32,(side,side),1)
    eye=jnp.where((row==col)&(row<BLOCK),1.0,0.0)
    def full(x):
        x=jnp.concatenate([x,jnp.zeros((BLOCK,side-BLOCK),F32)],axis=1)
        return jnp.concatenate([x,jnp.zeros((side-BLOCK,side),F32)],axis=0)
    def one(i,carry):
        grads=[full(grad_ref[i*n_side+j]*factor) for j in range(n_side)]
        flipped=[g.T for g in grads]
        stats=[]
        for j in range(n_side):
            s=i*n_side+j
            gl,gr=left_of(grads[j]),right_of(grads[j]); tl,tr=left_of(flipped[j]),right_of(flipped[j])
            l=beta*full(left_ref[s])+(1.0-beta)*times(gl,tr)
            r=beta*full(right_ref[s])+(1.0-beta)*times(tl,gr)
            grad_out[s]=grads[j][:BLOCK,:BLOCK]; left_out[s]=l[:BLOCK,:BLOCK]; right_out[s]=r[:BLOCK,:BLOCK]
            stats+=[l,r]
        n=len(stats)
        regular=[m+eps*eye for m in stats]
        scaled=[2.5*lax.rsqrt(jnp.sum(m*m,keepdims=True)) for m in regular]
        moving=[m*s for m,s in zip(regular,scaled)]
        root=[None]*n
        for sweep in range(NEWTON):
            factors=[(5.0*eye-m)*0.25 for m in moving]
            fl=[left_of(f) for f in factors]; fr=[right_of(f) for f in factors]
            if sweep==0: root=[f*jnp.sqrt(jnp.sqrt(s)) for f,s in zip(factors,scaled)]
            else: root=[times(left_of(x),f) for x,f in zip(root,fr)]
            if sweep<NEWTON-1:
                square=[times(a,b) for a,b in zip(fl,fr)]
                fourth=[times(left_of(q),right_of(q)) for q in square]
                moving=[times(left_of(q),right_of(m)) for q,m in zip(fourth,moving)]
        for j in range(n_side):
            s=i*n_side+j
            d=times(left_of(root[2*j]),right_of(grads[j]))
            d=times(left_of(d),right_of(root[2*j+1]))
            block_out[s]=block_ref[s]-rate*d[:BLOCK,:BLOCK]
        return carry
    lax.fori_loop(0,grad_ref.shape[0]//n_side,one,0)
def shampoo(factor, grads, left, right, blocks, n_side=8):
    shape=jax.ShapeDtypeStruct(grads.shape,F32)
    return pl.pallas_call(partial(shampoo_kernel,beta=beta_stat,rate=rate_shampoo,eps=root_eps,n_side=n_side),out_shape=[shape]*4,
        in_specs=[pl.BlockSpec(memory_space=pltpu.SMEM)]+[vmem()]*4,out_specs=[vmem()]*4,
        compiler_params=pltpu.CompilerParams(vmem_limit_bytes=48<<20),name="shampoo")(factor.reshape(1),grads,left,right,blocks)


def fits(mesh):
    return mesh.shape["seq"] == 16 and mesh.shape["opt"] == 2


def sum_everywhere(value):
    value = value + swap(value, "opt", 1)
    for bit in range((lax.axis_size("seq") - 1).bit_length()):
        value = value + swap(value, "seq", 2**bit)
    return value


def to_heads(parts):
    return lax.all_to_all(parts, "seq", 0, 0, tiled=True)


def evens_first(rows):
    return rows.reshape((rows.shape[0] // 2, 2) + rows.shape[1:]).swapaxes(0, 1).reshape(rows.shape)


def fast_device(
    features,
    tile_mask,
    lengths,
    owners,
    layer_blocks,
    stat_left,
    stat_right,
    io_weights,
    io_first,
    io_second,
    vectors,
    vec_first,
    vec_second,
):
    tok_dev = features.shape[1]
    seq_index = lax.axis_index("seq")
    core_index = lax.axis_index("opt")
    ids = jnp.stack([seq_index, core_index]).astype(jnp.int32)
    low_targets = evens_first(features[0])
    targets = low_targets.astype(jnp.float32)
    chosen = evens_first(tile_mask[0])[:, None] > 0
    lengths_row = lax.dynamic_index_in_dim(lengths, core_index, 0, keepdims=False)
    places = seq_index * tok_dev + evens_first(jnp.arange(tok_dev, dtype=jnp.int32))
    shards = gather_shards(layer_blocks, io_weights, tile_mask)
    block_rows, io_rows = shard_rows(seq_index, core_index)
    qkv_weight, out_weight, in_weight, tile_counts = join_weights(
        FIRST_PLAN, 0, shards, owners, block_rows, io_rows
    )
    tile_count = tile_counts[0, 0]
    layer_rows, tail_rows = unpack(vectors)
    row_set = layer_rows[0]
    token_vec = tail_rows[3 + FEAT // D :].reshape(FEAT)
    head_bias = tail_rows[3 : 3 + FEAT // D].reshape(FEAT)
    inputs = jnp.where(chosen, token_vec[None, :], targets).astype(jnp.bfloat16)
    hidden = jnp.dot(inputs, in_weight, preferred_element_type=jnp.float32) + tail_rows[2][None, :]
    hidden = hidden + sine_places(slide_offsets(lengths_row, places))

    normed = layer_norm(hidden, row_set[0], row_set[1]).astype(jnp.bfloat16)
    biases = jnp.concatenate([row_set[2], jnp.zeros_like(row_set[2]), row_set[3]])
    packed = lax.dot_general(
        qkv_weight, normed, (((0,), (1,)), ((), ())), preferred_element_type=jnp.float32
    )
    packed = (packed + biases[:, None]).astype(jnp.bfloat16)
    by_head = packed.reshape(3, HEADS, HEAD_DIM, tok_dev).swapaxes(0, 1)
    by_head = by_head.reshape(HEADS, 3 * HEAD_DIM, tok_dev)
    late_owners, by_head = gate(owners, by_head)
    up_weight, down_weight, head_weight, late_counts = join_weights(
        SECOND_PLAN, 1, shards, late_owners, block_rows, io_rows
    )
    own_head, head_weight = gate(to_heads(by_head), head_weight)
    head_out, mixed_parts, head_totals = attend(lengths, ids, own_head)
    mixed_low = to_heads(mixed_parts).reshape(D, tok_dev)
    chosen_rows = chosen.astype(jnp.float32)
    (
        grad_middle,
        grad_mixed,
        second_turned,
        active_turned,
        branch_turned,
        before_turned,
        out_turned,
        pred_turned,
        final_turned,
        late_rows,
    ) = mlp_step(
        tile_count,
        hidden,
        mixed_low,
        low_targets,
        chosen_rows,
        vectors,
        out_weight,
        up_weight,
        down_weight,
        head_weight,
    )
    grad_head_out = to_heads(grad_mixed.reshape(HEADS, HEAD_DIM, tok_dev))
    grad_parts = attend_back(lengths, ids, own_head, grad_head_out, head_out, head_totals)
    grad_packed, in_turned, vec_grads = input_step(
        to_heads(grad_parts),
        hidden,
        grad_middle,
        chosen_rows,
        vectors,
        late_rows,
        qkv_weight,
        in_weight,
    )
    operands = []
    for operand in (
        normed.T,
        mixed_low,
        second_turned,
        active_turned,
        grad_packed,
        branch_turned,
        before_turned,
        out_turned,
        inputs.T,
        in_turned,
        pred_turned,
        final_turned,
    ):
        operands += [operand, swap(operand, "opt", 1)]
    slot_sum, in_sum, head_sum = reduce_tree(ids, owners, operands)
    io_sum = jnp.stack([in_sum, head_sum], axis=1)
    local_sq = jnp.sum(slot_sum * slot_sum) + jnp.sum(in_sum * in_sum) + jnp.sum(head_sum * head_sum)
    own_sums = jnp.concatenate([vec_grads[:-1], jnp.broadcast_to(local_sq, (1, D))])
    all_sums = sum_everywhere(own_sums)
    vec_sum = all_sums[: vectors.shape[0]]
    error_sum = all_sums[vectors.shape[0], 0]
    grad_norm = jnp.sqrt(all_sums[-1, 0] + jnp.sum(vec_sum * vec_sum))
    factor = jnp.minimum(1.0, clip_limit / grad_norm)
    block_grads, left_new, right_new, blocks_new = shampoo(
        factor, slot_sum, stat_left, stat_right, layer_blocks
    )
    io_first_new, io_second_new, io_new = adam_update(
        io_weights, io_first, io_second, io_sum * factor, rate_adam, weight_decay
    )
    vec_first_new, vec_second_new, vec_new = adam_update(
        vectors, vec_first, vec_second, vec_sum * factor, rate_vector, 0.0
    )
    return (
        grad_norm,
        error_sum,
        tile_count,
        block_grads,
        left_new,
        right_new,
        blocks_new,
        io_first_new,
        io_second_new,
        io_new,
        vec_first_new,
        vec_second_new,
        vec_new,
    )


def solution(mesh):
    return jax.shard_map(
        fast_device if fits(mesh) else per_device,
        mesh=mesh,
        in_specs=(
            P("opt", "seq", None),
            P("opt", "seq"),
            P(),
            P(),
            P(("seq", "opt"), None, None),
            P(("seq", "opt"), None, None),
            P(("seq", "opt"), None, None),
            P(("seq", "opt"), None, None),
            P(("seq", "opt"), None, None),
            P(("seq", "opt"), None, None),
            P(),
            P(),
            P(),
        ),
        out_specs=(
            P(),
            P(),
            P(),
            P(("seq", "opt"), None, None),
            P(("seq", "opt"), None, None),
            P(("seq", "opt"), None, None),
            P(("seq", "opt"), None, None),
            P(("seq", "opt"), None, None),
            P(("seq", "opt"), None, None),
            P(("seq", "opt"), None, None),
            P(),
            P(),
            P(),
        ),
        check_vma=False,
    )
```

```python
from functools import partial
import math

import jax
import jax.numpy as jnp
import numpy as np
from jax import lax
from jax.experimental import pallas as pl
from jax.experimental.pallas import tpu as pltpu
from jax.sharding import PartitionSpec as P

D = 768
HEADS = 16
HEAD_DIM = 48
FF = 3072
FEAT = 1536
LAYERS = 1
BRANCHES = 5
SEG0 = 1024
BLOCK = 96
SLIDES = 4
NEWTON = 6
STEP = 10


norm_eps = 1e-05
clip_limit = 1.0
beta_one = 0.9
beta_two = 0.95
adam_eps = 1e-08
rate_adam = 0.01
rate_vector = 0.2
weight_decay = 0.05
beta_stat = 0.95
rate_shampoo = 0.05
root_eps = 1e-12
masked_score = -1e30
highest = lax.Precision.HIGHEST


def from_partner(value, axis, stride):
    mask = 2**stride
    pairs = [(source, source ^ mask) for source in range(lax.axis_size(axis))]
    return lax.ppermute(value, axis, pairs)


def for_sending(shard):

    def short(part):
        return part.astype(jnp.bfloat16) if part.dtype == jnp.float32 else part

    return jax.tree.map(short, shard)


def layer_norm(values, gain, shift):
    centred = values - jnp.mean(values, axis=-1, keepdims=True)
    spread = jnp.mean(centred * centred, axis=-1, keepdims=True)
    return centred * lax.rsqrt(spread + norm_eps) * gain + shift


def sine_places(places):
    half_width = D // 2
    freq_rates = jnp.exp(
        jnp.arange(half_width, dtype=jnp.float32) * (-math.log(10000.0) / half_width)
    )
    angles = (places.astype(jnp.float32) / 64.0)[:, None] * freq_rates[None, :]
    return jnp.concatenate([jnp.sin(angles), jnp.cos(angles)], axis=1)


def slide_ids(lengths_row, places):
    slide_ends = jnp.cumsum(lengths_row)
    return jnp.sum((places[..., None] >= slide_ends[:-1]).astype(jnp.int32), axis=-1)


def slide_offsets(lengths_row, places):
    slide_ends = jnp.cumsum(lengths_row)
    slide_starts = slide_ends - lengths_row
    owner_ids = slide_ids(lengths_row, places)
    match_rows = owner_ids[:, None] == jnp.arange(SLIDES, dtype=jnp.int32)[None, :]
    picked = jnp.sum(jnp.where(match_rows, slide_starts[None, :], 0), axis=1)
    return places - picked


def head_offsets(dilation):
    return np.arange(HEADS) % dilation


def pick_rows(values, dilation):
    row_count = values.shape[0] // dilation
    shaped = values.reshape((row_count, dilation) + values.shape[1:])
    return shaped[:, head_offsets(dilation), np.arange(HEADS)]


def spread_rows(values, dilation, filler):
    row_count = values.shape[0]
    hit_mask = np.arange(dilation)[:, None] == head_offsets(dilation)[None, :]
    hit_mask = hit_mask.reshape((1, dilation, HEADS) + (1,) * (values.ndim - 2))
    spread_out = jnp.where(hit_mask, values[:, None], filler)
    return spread_out.reshape((row_count * dilation,) + values.shape[1:])


def branch_geom(branch, tok_dev, seq_len):
    dilation = 2**branch
    segment = min(SEG0 * dilation, seq_len)
    return (dilation, segment, max(1, segment // tok_dev))


def branch_docs(lengths_row, first_place, row_count, dilation):
    places = (
        first_place
        + jnp.asarray(head_offsets(dilation), jnp.int32)[None, :]
        + dilation * jnp.arange(row_count, dtype=jnp.int32)[:, None]
    )
    return slide_ids(lengths_row, places)


def contract_rows(left, right):
    return lax.dot_general(
        left, right, (((0,), (0,)), ((), ())), preferred_element_type=jnp.float32
    )


def contract_cols(left, right):
    return lax.dot_general(
        left, right, (((1,), (1,)), ((), ())), preferred_element_type=jnp.float32
    )


def assemble(natural):
    per_layer = natural.reshape(LAYERS, -1, BLOCK, BLOCK)
    col_count = (4 * D + FF) // BLOCK
    wide_count = D // BLOCK * col_count
    upper_mats = per_layer[:, :wide_count].reshape(LAYERS, D // BLOCK, col_count, BLOCK, BLOCK)
    upper_mats = upper_mats.transpose(0, 1, 3, 2, 4).reshape(LAYERS, D, 4 * D + FF)
    lower_mats = per_layer[:, wide_count:].reshape(LAYERS, FF // BLOCK, D // BLOCK, BLOCK, BLOCK)
    lower_mats = lower_mats.transpose(0, 1, 3, 2, 4).reshape(LAYERS, FF, D)
    return (upper_mats, lower_mats)


def disassemble(upper_mats, lower_mats):
    col_count = (4 * D + FF) // BLOCK
    top_part = upper_mats.reshape(LAYERS, D // BLOCK, BLOCK, col_count, BLOCK).transpose(
        0, 1, 3, 2, 4
    )
    top_part = top_part.reshape(LAYERS, -1, BLOCK, BLOCK)
    bottom_part = lower_mats.reshape(LAYERS, FF // BLOCK, BLOCK, D // BLOCK, BLOCK).transpose(
        0, 1, 3, 2, 4
    )
    bottom_part = bottom_part.reshape(LAYERS, -1, BLOCK, BLOCK)
    return jnp.concatenate([top_part, bottom_part], axis=1).reshape(-1, BLOCK, BLOCK)


def unpack(vector_set):
    per_layer = 8 + FF // D
    return (
        vector_set[: LAYERS * per_layer].reshape(LAYERS, per_layer, D),
        vector_set[LAYERS * per_layer :],
    )


def collect_pairs(pieces, bit_counts, seq_index):
    pieces = list(pieces)
    for bit_id in range(max(bit_counts + [0])):
        active_ids = [branch for branch in range(len(pieces)) if bit_counts[branch] > bit_id]
        outgoing = jnp.concatenate([pieces[branch] for branch in active_ids], axis=0)
        partner = from_partner(outgoing, "seq", bit_id)
        lower_side = seq_index // 2**bit_id % 2 == 0
        offset_at = 0
        for branch in active_ids:
            my_part = pieces[branch]
            part_size = my_part.shape[0]
            their_part = partner[offset_at : offset_at + part_size]
            offset_at = offset_at + part_size
            pieces[branch] = jnp.where(
                lower_side,
                jnp.concatenate([my_part, their_part], 0),
                jnp.concatenate([their_part, my_part], 0),
            )
    return pieces


def return_pairs(pieces, bit_counts, seq_index):
    pieces = list(pieces)
    for bit_id in reversed(range(max(bit_counts + [0]))):
        active_ids = [branch for branch in range(len(pieces)) if bit_counts[branch] > bit_id]
        lower_side = seq_index // 2**bit_id % 2 == 0
        kept_parts, sent_parts = ([], [])
        for branch in active_ids:
            half_size = pieces[branch].shape[0] // 2
            first_part = pieces[branch][:half_size]
            second_part = pieces[branch][half_size:]
            kept_parts.append(jnp.where(lower_side, first_part, second_part))
            sent_parts.append(jnp.where(lower_side, second_part, first_part))
        partner = from_partner(for_sending(jnp.concatenate(sent_parts, axis=0)), "seq", bit_id)
        offset_at = 0
        for branch, kept_part in zip(active_ids, kept_parts):
            part_size = kept_part.shape[0]
            pieces[branch] = kept_part + partner[offset_at : offset_at + part_size]
            offset_at = offset_at + part_size
    return pieces


def score_block(query_rows, key_rows, query_docs, key_docs):
    raw_scores = jnp.einsum(
        "sqhd,skhd->shqk", query_rows, key_rows, preferred_element_type=jnp.float32
    ) * HEAD_DIM ** (-0.5)
    same_slide = (
        jnp.transpose(query_docs, (0, 2, 1))[..., None]
        == jnp.transpose(key_docs, (0, 2, 1))[:, :, None, :]
    )
    return jnp.where(same_slide, raw_scores, masked_score)


def attend_forward(packed, lengths_row, seq_len, seq_index):
    tok_dev = packed.shape[0]
    triple = packed.reshape(tok_dev, 3, HEADS, HEAD_DIM)
    queries, key_all, value_all = (triple[:, 0], triple[:, 1], triple[:, 2])
    geoms = [branch_geom(branch, tok_dev, seq_len) for branch in range(BRANCHES)]
    local_pairs = [
        jnp.stack([pick_rows(key_all, geom[0]), pick_rows(value_all, geom[0])], axis=1).reshape(
            -1, 2 * D
        )
        for geom in geoms
    ]
    bit_counts = [geom[2].bit_length() - 1 for geom in geoms]
    joined = collect_pairs(local_pairs, bit_counts, seq_index)
    kept_state, outputs, totals_all = ([], [], [])
    for branch in range(BRANCHES):
        dilation, segment, group_size = geoms[branch]
        sections = max(1, tok_dev // segment)
        query_rows = pick_rows(queries, dilation).reshape(sections, -1, HEADS, HEAD_DIM)
        pair_rows = joined[branch].reshape(sections, -1, 2, HEADS, HEAD_DIM)
        key_rows = pair_rows[:, :, 0]
        value_rows = pair_rows[:, :, 1]
        query_docs = branch_docs(
            lengths_row, seq_index * tok_dev, tok_dev // dilation, dilation
        ).reshape(sections, -1, HEADS)
        group_first = seq_index // group_size * group_size * tok_dev
        key_docs = branch_docs(lengths_row, group_first, joined[branch].shape[0], dilation).reshape(
            sections, -1, HEADS
        )
        scores = score_block(query_rows, key_rows, query_docs, key_docs)
        totals = jax.nn.logsumexp(scores, axis=-1)
        softmax_rows = jnp.exp(scores - totals[..., None]).astype(jnp.bfloat16)
        output = jnp.einsum(
            "shqk,skhd->sqhd", softmax_rows, value_rows, preferred_element_type=jnp.float32
        ).reshape(-1, HEADS, HEAD_DIM)
        totals_rows = jnp.transpose(totals, (0, 2, 1)).reshape(-1, HEADS)
        kept_state.append(
            (query_rows, key_rows, value_rows, query_docs, key_docs, output, totals_rows)
        )
        outputs.append(spread_rows(output, dilation, 0.0))
        totals_all.append(spread_rows(totals_rows, dilation, masked_score))
    stacked = jnp.stack(totals_all)
    grand_total = jax.nn.logsumexp(stacked, axis=0)
    mixed_out = jnp.zeros_like(outputs[0])
    for branch in range(BRANCHES):
        mixed_out = mixed_out + jnp.exp(stacked[branch] - grand_total)[..., None] * outputs[branch]
    return (mixed_out, (mixed_out, grand_total, kept_state))


def attend_backward(grad_mixed, attention_state, seq_len, seq_index):
    mixed_out, grand_total, kept_state = attention_state
    tok_dev = grad_mixed.shape[0]
    score_scale = HEAD_DIM ** (-0.5)
    grad_query = jnp.zeros(grad_mixed.shape, jnp.float32)
    key_terms, bit_counts, dilations = ([], [], [])
    for branch in range(BRANCHES):
        dilation, segment, group_size = branch_geom(branch, tok_dev, seq_len)
        query_rows, key_rows, value_rows, query_docs, key_docs, output, totals_rows = kept_state[
            branch
        ]
        sections = query_rows.shape[0]
        weight = jnp.exp(totals_rows - pick_rows(grand_total, dilation))
        grad_picked = pick_rows(grad_mixed, dilation)
        grad_output = (
            (weight[..., None] * grad_picked)
            .astype(jnp.bfloat16)
            .reshape(sections, -1, HEADS, HEAD_DIM)
        )
        grad_totals = weight * jnp.sum(
            grad_picked * (output - pick_rows(mixed_out, dilation)), axis=-1
        )
        grad_totals = jnp.transpose(grad_totals.reshape(sections, -1, HEADS), (0, 2, 1))
        totals = jnp.transpose(totals_rows.reshape(sections, -1, HEADS), (0, 2, 1))
        softmax_rows = jnp.exp(
            score_block(query_rows, key_rows, query_docs, key_docs) - totals[..., None]
        )
        grad_value = jnp.einsum(
            "shqk,sqhd->skhd",
            softmax_rows.astype(jnp.bfloat16),
            grad_output,
            preferred_element_type=jnp.float32,
        )
        grad_probs = jnp.einsum(
            "sqhd,skhd->shqk", grad_output, value_rows, preferred_element_type=jnp.float32
        )
        inner_sum = jnp.sum(softmax_rows * grad_probs, axis=-1, keepdims=True)
        grad_scores = (softmax_rows * (grad_probs - inner_sum + grad_totals[..., None])).astype(
            jnp.bfloat16
        )
        grad_q = (
            jnp.einsum("shqk,skhd->sqhd", grad_scores, key_rows, preferred_element_type=jnp.float32)
            * score_scale
        )
        grad_k = (
            jnp.einsum(
                "shqk,sqhd->skhd", grad_scores, query_rows, preferred_element_type=jnp.float32
            )
            * score_scale
        )
        grad_query = grad_query + spread_rows(grad_q.reshape(-1, HEADS, HEAD_DIM), dilation, 0.0)
        key_terms.append(
            jnp.stack(
                [grad_k.reshape(-1, HEADS, HEAD_DIM), grad_value.reshape(-1, HEADS, HEAD_DIM)],
                axis=1,
            ).reshape(-1, 2 * D)
        )
        bit_counts.append(group_size.bit_length() - 1)
        dilations.append(dilation)
    own_terms = return_pairs(key_terms, bit_counts, seq_index)
    grad_key = jnp.zeros(grad_mixed.shape, jnp.float32)
    grad_val = jnp.zeros(grad_mixed.shape, jnp.float32)
    for branch in range(BRANCHES):
        pair_rows = own_terms[branch].reshape(-1, 2, HEADS, HEAD_DIM)
        grad_key = grad_key + spread_rows(pair_rows[:, 0], dilations[branch], 0.0)
        grad_val = grad_val + spread_rows(pair_rows[:, 1], dilations[branch], 0.0)
    return jnp.stack([grad_query, grad_key, grad_val], axis=1).reshape(tok_dev, 3 * D)


def layer_forward(hidden, upper_mat, lower_mat, row_set, lengths_row, seq_len, seq_index):
    normed = layer_norm(hidden, row_set[0], row_set[1]).astype(jnp.bfloat16)
    biases = jnp.concatenate([row_set[2], jnp.zeros_like(row_set[2]), row_set[3]])
    packed = (
        jnp.dot(normed, upper_mat[:, : 3 * D], preferred_element_type=jnp.float32) + biases[None, :]
    ).astype(jnp.bfloat16)
    mixed_out, attention_state = attend_forward(packed, lengths_row, seq_len, seq_index)
    mixed_low = mixed_out.reshape(-1, D).astype(jnp.bfloat16)
    middle = (
        hidden
        + jnp.dot(mixed_low, upper_mat[:, 3 * D : 4 * D], preferred_element_type=jnp.float32)
        + row_set[4][None, :]
    )
    second = layer_norm(middle, row_set[5], row_set[6]).astype(jnp.bfloat16)
    before = (
        jnp.dot(second, upper_mat[:, 4 * D :], preferred_element_type=jnp.float32)
        + row_set[8:].reshape(-1)[None, :]
    )
    active = jax.nn.gelu(before, approximate=True).astype(jnp.bfloat16)
    result = (
        middle
        + jnp.dot(active, lower_mat, preferred_element_type=jnp.float32)
        + row_set[7][None, :]
    )
    return (result, (hidden, normed, mixed_low, middle, second, before, active, attention_state))


def layer_backward(grad_result, upper_mat, lower_mat, row_set, layer_state, seq_len, seq_index):
    hidden, normed, mixed_low, middle, second, before, active, attention_state = layer_state
    grad_out = grad_result.astype(jnp.bfloat16)
    grad_lower = contract_rows(active, grad_out)
    grad_fc2_bias = jnp.sum(grad_out, axis=0, dtype=jnp.float32)
    grad_active = contract_cols(grad_out, lower_mat)
    gelu_value, gelu_back = jax.vjp(partial(jax.nn.gelu, approximate=True), before)
    grad_before = gelu_back(grad_active)[0].astype(jnp.bfloat16)
    grad_fc1 = contract_rows(second, grad_before)
    grad_fc1_bias = jnp.sum(grad_before, axis=0, dtype=jnp.float32)
    grad_second = contract_cols(grad_before, upper_mat[:, 4 * D :])
    norm_value, norm_back = jax.vjp(layer_norm, middle, row_set[5], row_set[6])
    grad_middle, grad_gain_two, grad_shift_two = norm_back(grad_second)
    grad_middle = grad_middle + grad_result
    grad_branch = grad_middle.astype(jnp.bfloat16)
    grad_proj = contract_rows(mixed_low, grad_branch)
    grad_proj_bias = jnp.sum(grad_branch, axis=0, dtype=jnp.float32)
    grad_mixed = contract_cols(grad_branch, upper_mat[:, 3 * D : 4 * D]).reshape(
        -1, HEADS, HEAD_DIM
    )
    grad_packed = attend_backward(grad_mixed, attention_state, seq_len, seq_index).astype(
        jnp.bfloat16
    )
    grad_qkv = contract_rows(normed, grad_packed)
    packed_sums = jnp.sum(grad_packed, axis=0, dtype=jnp.float32)
    grad_normed = contract_cols(grad_packed, upper_mat[:, : 3 * D])
    first_value, first_back = jax.vjp(layer_norm, hidden, row_set[0], row_set[1])
    grad_hidden, grad_gain_one, grad_shift_one = first_back(grad_normed)
    grad_hidden = grad_hidden + grad_middle
    grad_upper = jnp.concatenate([grad_qkv, grad_proj, grad_fc1], axis=1)
    small_rows = jnp.stack(
        [
            grad_gain_one,
            grad_shift_one,
            packed_sums[:D],
            packed_sums[2 * D :],
            grad_proj_bias,
            grad_gain_two,
            grad_shift_two,
            grad_fc2_bias,
        ]
    )
    grad_rows = jnp.concatenate([small_rows, grad_fc1_bias.reshape(-1, D)], axis=0)
    return (grad_hidden, (grad_upper, grad_lower, grad_rows))


def inverse_root(matrix):
    identity = jnp.eye(matrix.shape[-1], dtype=jnp.float32)
    regular = matrix + root_eps * identity
    frob_norm = jnp.sqrt(jnp.sum(regular * regular, axis=(1, 2), keepdims=True))
    scaled = 2.5 / frob_norm
    root_mat = identity * jnp.sqrt(jnp.sqrt(scaled))
    moving = regular * scaled
    for sweep_id in range(NEWTON):
        factor = (5.0 * identity - moving) * 0.25
        root_mat = jnp.einsum("kij,kjl->kil", root_mat, factor, precision=highest)
        square = jnp.einsum("kij,kjl->kil", factor, factor, precision=highest)
        fourth = jnp.einsum("kij,kjl->kil", square, square, precision=highest)
        moving = jnp.einsum("kij,kjl->kil", fourth, moving, precision=highest)
    return root_mat


def adam_update(weight, first_mom, second_mom, grad, rate, decay):
    first_new = beta_one * first_mom + (1.0 - beta_one) * grad
    second_new = beta_two * second_mom + (1.0 - beta_two) * grad * grad
    first_hat = first_new / (1.0 - beta_one**STEP)
    second_hat = second_new / (1.0 - beta_two**STEP)
    return (
        first_new,
        second_new,
        weight - rate * (first_hat / (jnp.sqrt(second_hat) + adam_eps) + decay * weight),
    )


def per_device(
    features,
    tile_mask,
    lengths,
    owners,
    layer_blocks,
    stat_left,
    stat_right,
    io_weights,
    io_first,
    io_second,
    vectors,
    vec_first,
    vec_second,
):
    tok_dev = features.shape[1]
    seq_size = lax.axis_size("seq")
    seq_len = tok_dev * seq_size
    seq_index = lax.axis_index("seq")
    core_index = lax.axis_index("opt")
    targets = features[0].astype(jnp.float32)
    chosen = tile_mask[0][:, None] > 0
    lengths_row = lax.dynamic_index_in_dim(lengths, core_index, 0, keepdims=False)
    places = seq_index * tok_dev + jnp.arange(tok_dev, dtype=jnp.int32)
    all_blocks, all_io = (
        lax.all_gather(layer_blocks.astype(jnp.bfloat16), ("seq", "opt"), axis=0, tiled=True),
        lax.all_gather(io_weights.astype(jnp.bfloat16), ("seq", "opt"), axis=0, tiled=True),
    )
    natural = jnp.zeros_like(all_blocks).at[owners].set(all_blocks)
    upper_mats, lower_mats = assemble(natural)
    tile_count = lax.psum(jnp.sum(tile_mask.astype(jnp.float32)), ("seq", "opt"))
    layer_rows, tail_rows = unpack(vectors)
    token_vec = tail_rows[3 + FEAT // D :].reshape(FEAT)
    head_bias = tail_rows[3 : 3 + FEAT // D].reshape(FEAT)
    inputs = jnp.where(chosen, token_vec[None, :], targets).astype(jnp.bfloat16)
    in_weight = all_io[:, 0]
    head_weight = all_io[:, 1]
    hidden = jnp.dot(inputs, in_weight, preferred_element_type=jnp.float32) + tail_rows[2][None, :]
    hidden = hidden + sine_places(slide_offsets(lengths_row, places))
    layer_id = 0
    hidden, layer_state = layer_forward(
        hidden,
        upper_mats[layer_id],
        lower_mats[layer_id],
        layer_rows[layer_id],
        lengths_row,
        seq_len,
        seq_index,
    )
    layer_states = [layer_state]
    final, final_back = jax.vjp(layer_norm, hidden, tail_rows[0], tail_rows[1])
    final_low = final.astype(jnp.bfloat16)
    predict = contract_cols(final_low, head_weight) + head_bias[None, :]
    difference = predict - targets
    error_local = jnp.sum(jnp.where(chosen, difference * difference, 0.0))
    grad_pred = jnp.where(chosen, 2.0 * difference / tile_count, 0.0).astype(jnp.bfloat16)
    grad_head = contract_rows(grad_pred, final_low)
    grad_head_bias = jnp.sum(grad_pred, axis=0, dtype=jnp.float32)
    grad_final = jnp.dot(grad_pred, head_weight, preferred_element_type=jnp.float32)
    grad_hidden, grad_gain_last, grad_shift_last = final_back(grad_final)
    layer_grads = [None] * LAYERS
    for layer_id in reversed(range(LAYERS)):
        grad_hidden, layer_grads[layer_id] = layer_backward(
            grad_hidden,
            upper_mats[layer_id],
            lower_mats[layer_id],
            layer_rows[layer_id],
            layer_states[layer_id],
            seq_len,
            seq_index,
        )
    grad_in_low = grad_hidden.astype(jnp.bfloat16)
    grad_in = contract_rows(inputs, grad_in_low)
    grad_in_bias = jnp.sum(grad_in_low, axis=0, dtype=jnp.float32)
    grad_inputs = contract_cols(grad_in_low, in_weight)
    grad_token = jnp.sum(jnp.where(chosen, grad_inputs, 0.0), axis=0)
    grad_upper = jnp.stack([item[0] for item in layer_grads])
    grad_lower = jnp.stack([item[1] for item in layer_grads])
    slot_grads = disassemble(grad_upper, grad_lower)[owners]
    io_grads = jnp.stack([grad_in, grad_head], axis=1)
    vec_grads = jnp.concatenate(
        [
            jnp.stack([item[2] for item in layer_grads]).reshape(-1, D),
            jnp.stack([grad_gain_last, grad_shift_last, grad_in_bias]),
            grad_head_bias.reshape(-1, D),
            grad_token.reshape(-1, D),
        ],
        axis=0,
    )
    slot_sum, io_sum = (
        lax.psum_scatter(slot_grads, ("seq", "opt"), scatter_dimension=0, tiled=True),
        lax.psum_scatter(io_grads, ("seq", "opt"), scatter_dimension=0, tiled=True),
    )
    vec_sum, error_sum = lax.psum((vec_grads, error_local), ("seq", "opt"))
    local_sq = jnp.sum(slot_sum * slot_sum) + jnp.sum(io_sum * io_sum)
    grad_norm = jnp.sqrt(lax.psum(local_sq, ("seq", "opt")) + jnp.sum(vec_sum * vec_sum))
    factor = jnp.minimum(1.0, clip_limit / grad_norm)
    block_grads = slot_sum * factor
    left_new = beta_stat * stat_left + (1.0 - beta_stat) * jnp.einsum(
        "kij,klj->kil", block_grads, block_grads, precision=highest
    )
    right_new = beta_stat * stat_right + (1.0 - beta_stat) * jnp.einsum(
        "kji,kjl->kil", block_grads, block_grads, precision=highest
    )
    direction = jnp.einsum("kij,kjl->kil", inverse_root(left_new), block_grads, precision=highest)
    direction = jnp.einsum("kij,kjl->kil", direction, inverse_root(right_new), precision=highest)
    blocks_new = layer_blocks - rate_shampoo * direction
    io_first_new, io_second_new, io_new = adam_update(
        io_weights, io_first, io_second, io_sum * factor, rate_adam, weight_decay
    )
    vec_first_new, vec_second_new, vec_new = adam_update(
        vectors, vec_first, vec_second, vec_sum * factor, rate_vector, 0.0
    )
    return (
        grad_norm,
        error_sum,
        tile_count,
        block_grads,
        left_new,
        right_new,
        blocks_new,
        io_first_new,
        io_second_new,
        io_new,
        vec_first_new,
        vec_second_new,
        vec_new,
    )


BF=jnp.bfloat16; LANE=128; IO=48
def swap(value, axis, mask):
    return lax.ppermute(value, axis, [(s, s ^ mask) for s in range(lax.axis_size(axis))])
def gate(*values):
    return lax.optimization_barrier(values)

COUNT_AT=3*3*BLOCK+6*IO
SHARD_HALF=COUNT_AT+16
def pack_kernel(blocks_ref, in_ref, head_ref, mask_ref, first_ref, second_ref, whole_ref):
    count=jnp.sum(mask_ref[...].astype(jnp.float32),keepdims=True)
    lane=lax.broadcasted_iota(jnp.int32,(BLOCK,LANE),1)
    pad=lambda x: jnp.concatenate([x,jnp.zeros((BLOCK,LANE-BLOCK),x.dtype)],axis=1)
    for h,(io,out_ref) in enumerate(zip((in_ref,head_ref),(first_ref,second_ref))):
        for g in range(3):
            b=[pad(blocks_ref[(h*3+g)*4+t]) for t in range(4)]
            for v in range(3):
                tile=jnp.where(lane<BLOCK,b[v],pltpu.roll(b[3],BLOCK-32*v,1))
                at=(g*3+v)*BLOCK
                out_ref[at:at+BLOCK,:]=tile.astype(BF)
        for v in range(6):
            at=9*BLOCK+v*IO
            out_ref[at:at+IO,:]=io[:,v*LANE:(v+1)*LANE].astype(BF)
        out_ref[COUNT_AT:,:]=jnp.broadcast_to(count,(16,LANE)).astype(BF)
        whole_ref[h*SHARD_HALF:(h+1)*SHARD_HALF,:]=out_ref[...]
def vmem(): return pl.BlockSpec(memory_space=pltpu.VMEM)
def smem(): return pl.BlockSpec(memory_space=pltpu.SMEM)
def hbm(): return pl.BlockSpec(memory_space=pltpu.HBM)
def from_hbm(body, name, outs, ins, scratch, smem_args=(), late=(), vmem_mib=48, micros=10):
    n_s,n_i,n_o=len(smem_args),len(ins),len(outs)
    def kernel(*refs):
        scalars,args,results=refs[:n_s],refs[n_s:n_s+n_i],refs[n_s+n_i:n_s+n_i+n_o]
        rest=refs[n_s+n_i+n_o:]
        held,made,more=rest[:n_i],rest[n_i:n_i+n_o],rest[n_i+n_o:-2]
        in_sem,out_sem=rest[-2:]
        loads=[pltpu.make_async_copy(a,h,in_sem.at[i]) for i,(a,h) in enumerate(zip(args,held))]
        for c in loads: c.start()
        for i,c in enumerate(loads):
            if i not in late: c.wait()
        body(*([loads[i].wait for i in late]),*scalars,*held,*made,*more)
        stores=[pltpu.make_async_copy(m,r,out_sem.at[i]) for i,(m,r) in enumerate(zip(made,results))]
        for c in stores: c.start()
        for c in stores: c.wait()
    ins=[pltpu.with_memory_space_constraint(a,pltpu.HBM) for a in ins]
    return pl.pallas_call(kernel,out_shape=[pltpu.HBM(s,t) for s,t in outs],
        in_specs=[smem()]*n_s+[hbm()]*n_i,out_specs=[hbm()]*n_o,
        scratch_shapes=[pltpu.VMEM(a.shape,a.dtype) for a in ins]+[pltpu.VMEM(s,t) for s,t in outs]+list(scratch)
            +[pltpu.SemaphoreType.DMA((n_i,)),pltpu.SemaphoreType.DMA((n_o,))],
        compiler_params=pltpu.CompilerParams(vmem_limit_bytes=vmem_mib<<20),
        cost_estimate=pl.CostEstimate(flops=0,transcendentals=0,bytes_accessed=int(micros*3.3e6)),name=name)(*smem_args,*ins)
def pack_shard(blocks, io, mask):
    return pl.pallas_call(pack_kernel,out_shape=[jax.ShapeDtypeStruct((n*SHARD_HALF,LANE),BF) for n in (1,1,2)],in_specs=[vmem()]*4,out_specs=[vmem()]*3,name="pack_shard")(blocks,io[:,0],io[:,1],mask)

HOPS=(("opt",1),("seq",1),("seq",2),("seq",4),("seq",8))
def hop(value, k):
    return value+swap(value,*HOPS[k])

def gather_tree(first, second, own):
    half=first.shape[0]
    near=[None]*4; cross=[None]*4
    def first_step(k,a,b):
        near[k]=(swap(a,"seq",1),swap(b,"seq",2))
    def second_step(k,a,b):
        cross[k]=(swap(jnp.concatenate([a,near[k][0]]),"seq",2),swap(jnp.concatenate([b,near[k][1]]),"seq",1))
    far1=swap(own,"seq",4)
    far2=swap(own,"seq",8)
    first_step(0,first,second)
    second_step(0,first,second)
    first_step(1,far1[:half],far1[half:])
    first_step(2,far2[:half],far2[half:])
    far3=swap(far2,"seq",4)
    near[1],near[2],far3=gate(near[1],near[2],far3)
    second_step(1,far1[:half],far1[half:])
    first_step(3,far3[:half],far3[half:])
    second_step(2,far2[:half],far2[half:])
    second_step(3,far3[:half],far3[half:])
    out=[jnp.concatenate([piece,*near[k],*cross[k]]) for k,piece in enumerate((own,far1,far2,far3))]
    return out+[swap(piece,"opt",1) for piece in out]

HELD=64*SHARD_HALF
N_BLOCK=768
def load_shards(bufs, held, sem, fourths):
    rows=bufs[0].shape[0]
    loads=[pltpu.make_async_copy(b,held.at[pl.ds(k*rows,rows)],sem.at[k]) for k,b in enumerate(bufs)]
    for c in loads: c.start()
    fourths()
    for k,c in enumerate(loads):
        c.wait()
        def unpack(u,carry,k=k):
            at=(k*8+u)*SHARD_HALF
            for g in range(3):
                parts=[held[pl.ds(pl.multiple_of(at+(g*3+v)*BLOCK,16),BLOCK),BLOCK:] for v in range(3)]
                to=HELD+((k*8+u)*3+g)*BLOCK
                held[pl.ds(pl.multiple_of(to,16),BLOCK),:BLOCK]=jnp.concatenate(parts,axis=1)
            return carry
        lax.fori_loop(0,8,unpack,0,unroll=8)

def join_kernel(plan, io_out, owners_ref, row_ref, io_ref, *refs):
    bufs=refs[:8]; n_out=len(plan); outs=refs[8:8+n_out]; io_ref_out,count_ref=refs[8+n_out:8+n_out+2]
    held,stage,where,in_sem,out_sem,io_sem=refs[8+n_out+2:]
    def invert():
        def one(i,carry):
            for j in range(8):
                where[owners_ref[i*8+j]]=row_ref[i*8+j]
            return carry
        lax.fori_loop(0,N_BLOCK//8,one,0)
    load_shards(bufs,held,in_sem,invert)
    def io_copy(d,total):
        at=io_ref[io_out,d]
        for v in range(6):
            pltpu.make_async_copy(held.at[pl.ds(pl.multiple_of(at+v*IO,16),IO)],
                io_ref_out.at[pl.ds(pl.multiple_of(d*IO,IO),IO),pl.ds(v*LANE,LANE)],io_sem).start()
        return total+held[pl.ds(pl.multiple_of(at+6*IO,16),16),:].astype(jnp.float32)
    count_ref[...]=lax.fori_loop(0,io_ref.shape[1],io_copy,jnp.zeros((16,LANE),jnp.float32))
    def block(n):
        return held[pl.ds(pl.multiple_of(where[n],16),BLOCK),:BLOCK]
    pending=[]; index=0
    for (first,stride,rows,stripes),out in zip(plan,outs):
        per=8//stripes if stripes<8 else 1
        for i0 in range(0,rows,per):
            slot=index%2
            if index>=2:
                for c in pending[index-2]: c.wait()
            for b in range(per):
                def one(c,carry,b=b,i0=i0):
                    n=first+(i0+b)*stride+4*c
                    stage[slot,:,pl.ds(pl.multiple_of((b*stripes+c)*4*BLOCK,128),4*BLOCK)]=jnp.concatenate([block(n+t) for t in range(4)],axis=1)
                    return carry
                lax.fori_loop(0,stripes,one,0,unroll=2 if stripes%4 else 4)
            w=stripes*4*BLOCK
            cs=[pltpu.make_async_copy(stage.at[slot,:,pl.ds(b*w,w)],out.at[pl.ds((i0+b)*BLOCK,BLOCK)],out_sem.at[slot,b]) for b in range(per)]
            for c in cs: c.start()
            pending.append(cs); index+=1
    for cs in pending[-2:]:
        for c in cs: c.wait()
    pltpu.make_async_copy(io_ref_out,io_ref_out,io_sem).wait()

COLS=(4*D+FF)//BLOCK
FIRST_PLAN=((0,COLS,8,6),(24,COLS,8,2))
SECOND_PLAN=((32,COLS,8,8),(8*COLS,8,32,2))
def join_weights(plan, io_out, bufs, owners, rows, io_rows):
    shapes=[(r*BLOCK,s*4*BLOCK) for _,_,r,s in plan]+[(FEAT,D)]
    return pl.pallas_call(partial(join_kernel,plan,io_out),
        out_shape=[pltpu.HBM(s,BF) for s in shapes]+[jax.ShapeDtypeStruct((16,LANE),jnp.float32)],
        in_specs=[smem()]*3+[hbm()]*8, out_specs=[hbm()]*len(shapes)+[vmem()],
        scratch_shapes=[pltpu.VMEM((HELD+N_BLOCK//4*BLOCK,LANE),BF),pltpu.VMEM((2,BLOCK,FF),BF),pltpu.SMEM((N_BLOCK,),jnp.int32),
            pltpu.SemaphoreType.DMA((8,)),pltpu.SemaphoreType.DMA((2,4)),pltpu.SemaphoreType.DMA],
        compiler_params=pltpu.CompilerParams(vmem_limit_bytes=40<<20), cost_estimate=pl.CostEstimate(flops=0,transcendentals=0,bytes_accessed=int((13 if io_out==0 else 17)*3.3e6)), name="join_weights")(owners,rows,io_rows,*[pltpu.with_memory_space_constraint(b,pltpu.HBM) for b in bufs])

def shard_rows(seq_index, core):
    def unit(dev,h):
        rel=(dev//2)^seq_index; xy=rel%4
        u=jnp.where(xy==0,h,jnp.where(h==0,jnp.where(xy==1,2,xy+2),jnp.where(xy==2,3,jnp.where(xy==1,6,7))))
        return (rel//4+4*((dev%2)^core))*8+u
    slot=jnp.arange(N_BLOCK,dtype=jnp.int32); s=slot%24
    u=unit(slot//24,s//12); g=s%12//4; t=s%4
    rows=jnp.where(t<3,u*SHARD_HALF+(g*3+t)*BLOCK,HELD+(u*3+g)*BLOCK)
    dev=jnp.arange(32,dtype=jnp.int32)
    io=jnp.stack([unit(dev,h)*SHARD_HALF+9*BLOCK for h in (0,1)])
    return rows.astype(jnp.int32),io.astype(jnp.int32)
def gather_shards(layer_blocks, io_weights, mask):
    return gather_tree(*pack_shard(layer_blocks,io_weights,mask))

HD=48; HEADS=16; SLIDES=4; SEG=1024; N=2048; H=512; TQ=256; TK=128
C2=HD**-0.5*math.log2(math.e)
def place_facts(index, head, lengths_ref, core):
    parity=lax.rem(head+(index//H)%2,2)
    pos=(index//SEG)*SEG+2*(index%H)+parity
    slide=jnp.zeros_like(index); end=jnp.int32(0)
    for i in range(SLIDES-1):
        end=end+lengths_ref[core,i]
        slide=slide+jnp.where(pos>=end,1,0)
    d=(pos-head)&15
    level=sum(jnp.where((d&(2**i-1))==0,1,0) for i in range(1,5))
    return slide.astype(jnp.float32), level.astype(jnp.float32)

def arrange(src, dst, odd):
    for pair in range(8):
        first, second = src[2*pair], src[2*pair+1]
        turn=lambda t: jnp.concatenate([t[:,64:],t[:,:64]],axis=1)
        ft, st = turn(first), turn(second)
        low=lax.broadcasted_iota(jnp.int32,first.shape,1)<64
        evens=jnp.where(low,first,st); odds=jnp.where(low,ft,second)
        near=jnp.where(odd,odds,evens); far=jnp.where(odd,evens,odds)
        at=(pair//4)*SEG+(pair%4)*128
        dst[:,at:at+128]=near.astype(dst.dtype); dst[:,at+H:at+H+128]=far.astype(dst.dtype)

def restore(get, put, odd):
    for pair in range(8):
        at=(pair//4)*SEG+(pair%4)*128
        near, far = get(at), get(at+H)
        evens=jnp.where(odd,far,near); odds=jnp.where(odd,near,far)
        turn=lambda t: jnp.concatenate([t[:,64:],t[:,:64]],axis=1)
        low=lax.broadcasted_iota(jnp.int32,evens.shape,1)<64
        put(2*pair, jnp.where(low,evens,turn(odds)))
        put(2*pair+1, jnp.where(low,turn(evens),odds))

def setup(lengths_ref, ids_ref, slide_k, level_k, row_facts):
    head, core = ids_ref[0], ids_ref[1]
    def fill(i, c):
        idx=lax.broadcasted_iota(jnp.int32,(TK,128),0)+i*TK
        s,l=place_facts(idx,head,lengths_ref,core)
        slide_k[pl.ds(pl.multiple_of(i*TK,TK),TK),:]=s
        level_k[pl.ds(pl.multiple_of(i*TK,TK),TK),:]=l
        return c
    lax.fori_loop(0,N//TK,fill,0)
    idx=lax.broadcasted_iota(jnp.int32,(8,N),1)
    s,l=place_facts(idx,head,lengths_ref,core)
    row_facts[0:8,:]=s; row_facts[8:16,:]=l

def key_rows(seg, near):
    own=[(seg*SEG+i*TK,True) for i in range(SEG//TK)]
    other=[((1-seg)*SEG+i*TK,False) for i in range(H//TK)] if near else []
    return own+other

def wide(x): return jnp.concatenate([x]*(TQ//128),axis=1)

def forward_kernel(lengths_ref, ids_ref, qkv_ref, o_ref, out_ref, lse_ref, qkvT, krow, slide_k, level_k, row_facts, s_ref, p_ref):
    odd=lax.rem(ids_ref[0],2)==1
    arrange(qkv_ref, qkvT, odd)
    setup(lengths_ref, ids_ref, slide_k, level_k, row_facts)
    for i in range(N//128):
        krow[i*128:(i+1)*128,:]=qkvT[HD:2*HD,i*128:(i+1)*128].astype(jnp.float32).T.astype(jnp.bfloat16)
    for seg in range(2):
        for near in (True,False):
            tiles=key_rows(seg,near)
            def part(c, carry, seg=seg, near=near, tiles=tiles):
                at=pl.multiple_of(seg*SEG+(0 if near else H)+c*TQ,TQ)
                qT=qkvT[0:HD,pl.ds(at,TQ)]
                sq=row_facts[0:1,pl.ds(at,TQ)]; lq=row_facts[8:9,pl.ds(at,TQ)]
                top=jnp.full((8,TQ),-jnp.inf,jnp.float32)
                for t,(r,own) in enumerate(tiles):
                    s=jnp.dot(krow[r:r+TK,:],qT,preferred_element_type=jnp.float32)
                    s=jnp.where(wide(slide_k[r:r+TK,:])==sq,s,-1e30)
                    s_ref[t*TK:(t+1)*TK,:]=s
                    top=jnp.maximum(top,jnp.max(s.reshape(TK//8,8,TQ),axis=0))
                m=jnp.max(top,axis=0,keepdims=True)
                total=jnp.zeros((8,TQ),jnp.float32)
                for t,(r,own) in enumerate(tiles):
                    e=jnp.exp2((s_ref[t*TK:(t+1)*TK,:]-m)*C2)
                    if near:
                        lk=wide(level_k[r:r+TK,:])
                        e=e*(jnp.minimum(lk,lq)+1.0 if own else jnp.minimum(lk,lq))
                    total=total+jnp.sum(e.reshape(TK//8,8,TQ),axis=0)
                    p_ref[t*TK:(t+1)*TK,:]=e.astype(jnp.bfloat16)
                l=jnp.sum(total,axis=0,keepdims=True)
                acc=jnp.zeros((HD,TQ),jnp.float32)
                acc=jnp.dot(qkvT[2*HD:3*HD,seg*SEG:(seg+1)*SEG],p_ref[0:SEG,:],preferred_element_type=jnp.float32)
                if near:
                    acc=acc+jnp.dot(qkvT[2*HD:3*HD,(1-seg)*SEG:(1-seg)*SEG+H],p_ref[SEG:SEG+H,:],preferred_element_type=jnp.float32)
                o_ref[:,pl.ds(at,TQ)]=acc/l
                lse_ref[:,pl.ds(at,TQ)]=jnp.broadcast_to(m*C2+jnp.log2(l),(8,TQ))
                return carry
            lax.fori_loop(0,H//TQ,part,0)
    def put(c,v): out_ref[c]=v.astype(jnp.bfloat16)
    restore(lambda at: o_ref[:,at:at+128], put, odd)

def backward_kernel(lengths_ref, ids_ref, qkv_ref, do_ref, o_ref, lse_ref, out_ref, qkvT, doT, rows, slide_k, level_k, row_facts, dqT, dkv, p_ref, ds_ref):
    odd=lax.rem(ids_ref[0],2)==1
    arrange(qkv_ref, qkvT, odd)
    arrange(do_ref, doT, odd)
    setup(lengths_ref, ids_ref, slide_k, level_k, row_facts)
    for i in range(N//128):
        l=slice(i*128,(i+1)*128)
        for j in range(3):
            rows[j,l,:]=qkvT[j*HD:(j+1)*HD,l].astype(jnp.float32).T.astype(jnp.bfloat16)
        rows[3,l,:]=doT[:,l].astype(jnp.float32).T.astype(jnp.bfloat16)
    dkv[...]=jnp.zeros_like(dkv)
    for seg in range(2):
        for near in (True,False):
            tiles=key_rows(seg,near)
            def part(c, carry, seg=seg, near=near, tiles=tiles):
                at=pl.multiple_of(seg*SEG+(0 if near else H)+c*TQ,TQ)
                qT=qkvT[0:HD,pl.ds(at,TQ)]; gT=doT[:,pl.ds(at,TQ)]
                q=rows[0,pl.ds(at,TQ),:]; g=rows[3,pl.ds(at,TQ),:]
                sq=row_facts[0:1,pl.ds(at,TQ)]; lq=row_facts[8:9,pl.ds(at,TQ)]
                lse=lse_ref[0:1,pl.ds(at,TQ)]
                inner=jnp.sum(gT.astype(jnp.float32)*o_ref[:,pl.ds(at,TQ)],axis=0,keepdims=True)
                for t,(r,own) in enumerate(tiles):
                    s=jnp.dot(rows[1,r:r+TK,:],qT,preferred_element_type=jnp.float32)
                    dp=jnp.dot(rows[2,r:r+TK,:],gT,preferred_element_type=jnp.float32)
                    e=jnp.exp2(s*C2-lse)
                    if near:
                        lk=wide(level_k[r:r+TK,:])
                        e=e*(jnp.minimum(lk,lq)+1.0 if own else jnp.minimum(lk,lq))
                    e=jnp.where(wide(slide_k[r:r+TK,:])==sq,e,0.0)
                    p_ref[t*TK:(t+1)*TK,:]=e.astype(jnp.bfloat16)
                    ds_ref[t*TK:(t+1)*TK,:]=(e*(dp-inner)).astype(jnp.bfloat16)
                dq=jnp.dot(qkvT[HD:2*HD,seg*SEG:(seg+1)*SEG],ds_ref[0:SEG,:],preferred_element_type=jnp.float32)
                if near:
                    dq=dq+jnp.dot(qkvT[HD:2*HD,(1-seg)*SEG:(1-seg)*SEG+H],ds_ref[SEG:SEG+H,:],preferred_element_type=jnp.float32)
                dqT[:,pl.ds(at,TQ)]=dq*HD**-0.5
                own=slice(seg*SEG,(seg+1)*SEG)
                dkv[0,own,:]+=jnp.dot(ds_ref[0:SEG,:],q,preferred_element_type=jnp.float32)
                dkv[1,own,:]+=jnp.dot(p_ref[0:SEG,:],g,preferred_element_type=jnp.float32)
                if near:
                    oth=slice((1-seg)*SEG,(1-seg)*SEG+H)
                    dkv[0,oth,:]+=jnp.dot(ds_ref[SEG:SEG+H,:],q,preferred_element_type=jnp.float32)
                    dkv[1,oth,:]+=jnp.dot(p_ref[SEG:SEG+H,:],g,preferred_element_type=jnp.float32)
                return carry
            lax.fori_loop(0,H//TQ,part,0)
    def putter(j):
        def put(c,v): out_ref[c,j*HD:(j+1)*HD,:]=v.astype(jnp.bfloat16)
        return put
    restore(lambda at: dqT[:,at:at+128], putter(0), odd)
    restore(lambda at: dkv[0,at:at+128,:].T*HD**-0.5, putter(1), odd)
    restore(lambda at: dkv[1,at:at+128,:].T, putter(2), odd)

def attend(lengths, ids, qkv):
    return from_hbm(forward_kernel,"attend_forward",[((HD,N),F32),((16,HD,128),BF),((8,N),F32)],[qkv],
        [pltpu.VMEM((3*HD,N),BF),pltpu.VMEM((N,HD),BF),pltpu.VMEM((N,128),F32),pltpu.VMEM((N,128),F32),pltpu.VMEM((16,N),F32),
            pltpu.VMEM((SEG+H,TQ),F32),pltpu.VMEM((SEG+H,TQ),BF)],(lengths,ids))
def attend_back(lengths, ids, qkv, do, o, lse):
    return from_hbm(backward_kernel,"attend_backward",[((16,3*HD,128),BF)],[qkv,do,o,lse],
        [pltpu.VMEM((3*HD,N),BF),pltpu.VMEM((HD,N),BF),pltpu.VMEM((4,N,HD),BF),pltpu.VMEM((N,128),F32),pltpu.VMEM((N,128),F32),pltpu.VMEM((16,N),F32),
            pltpu.VMEM((HD,N),F32),pltpu.VMEM((2,N,HD),F32),pltpu.VMEM((SEG+H,TQ),BF),pltpu.VMEM((SEG+H,TQ),BF)],(lengths,ids),micros=13)[0]

F32=jnp.float32
EPS=1e-05
def norm_parts(x):
    centred=x-jnp.mean(x,axis=-1,keepdims=True)
    spread=lax.rsqrt(jnp.mean(centred*centred,axis=-1,keepdims=True)+EPS)
    return centred*spread,spread
def norm_back(grad,unit,spread,gain):
    inner=grad*gain
    back=spread*(inner-jnp.mean(inner,axis=-1,keepdims=True)-unit*jnp.mean(inner*unit,axis=-1,keepdims=True))
    return back,jnp.sum(grad*unit,axis=0,keepdims=True),jnp.sum(grad,axis=0,keepdims=True)
def put_turned(ref,at,x):
    for c in range(x.shape[1]//LANE):
        ref[at+c*LANE:at+(c+1)*LANE,:]=x[:,c*LANE:(c+1)*LANE].astype(F32).T.astype(BF)
def turned(ref,rows):
    return jnp.concatenate([ref[c*LANE:(c+1)*LANE,:].astype(F32).T for c in range(rows//LANE)],axis=1)
def mm(a,b): return jnp.dot(a,b,preferred_element_type=F32)
def mm_t(a,b): return lax.dot_general(a,b,(((1,),(1,)),((),())),preferred_element_type=F32)
LATE_ROWS=4*D+2*FF+FEAT
GELU_A=math.sqrt(2.0/math.pi); GELU_B=0.044715
def mlp_kernel(up_here, down_here, head_here, count_ref, hidden_ref, mixed_ref, targets_ref, chosen_ref, vec_ref, wo_ref, up_ref, down_ref, head_ref,
               middle_grad_ref, mixed_grad_ref, late_ref, rows_ref, kept):
    row=lambda i: vec_ref[i:i+1,:]
    mixed=turned(mixed_ref,D).astype(BF)
    middle=hidden_ref[...]+mm(mixed,wo_ref[...])+row(4)
    unit2,spread2=norm_parts(middle)
    second=(unit2*row(5)+row(6)).astype(BF)
    put_turned(late_ref,0,second)
    result=middle+row(7)
    up_here(); down_here()
    for c in range(FF//D):
        s=slice(c*D,(c+1)*D)
        before=mm(second,up_ref[:,s])+row(8+c)
        kept[:,s]=before
        active=(before*(0.5*(1.0+jnp.tanh(GELU_A*(before+GELU_B*(before*before*before)))))).astype(BF)
        put_turned(late_ref,D+c*D,active)
        result=result+mm(active,down_ref[s,:])
    unit,spread=norm_parts(result)
    final=(unit*row(12)+row(13)).astype(BF)
    put_turned(late_ref,3*D+2*FF+FEAT,final)
    head_here()
    chosen=chosen_ref[...]>0.0
    error=jnp.zeros((1,1),F32); grad_final=jnp.zeros_like(middle)
    for c in range(FEAT//D):
        s=slice(c*D,(c+1)*D)
        difference=mm_t(final,head_ref[s,:])+row(15+c)-targets_ref[:,s].astype(F32)
        error=error+jnp.sum(jnp.where(chosen,difference*difference,0.0),keepdims=True)
        pred=jnp.where(chosen,2.0*difference/count_ref[0],0.0).astype(BF)
        put_turned(late_ref,3*D+2*FF+c*D,pred)
        rows_ref[10+c:11+c,:]=jnp.sum(pred.astype(F32),axis=0,keepdims=True)
        grad_final=grad_final+mm(pred,head_ref[s,:])
    rows_ref[12:13,:]=jnp.broadcast_to(error,(1,D))
    grad_result,rows_ref[8:9,:],rows_ref[9:10,:]=norm_back(grad_final,unit,spread,row(12))
    grad_out=grad_result.astype(BF)
    put_turned(late_ref,2*D+2*FF,grad_out)
    rows_ref[3:4,:]=jnp.sum(grad_out.astype(F32),axis=0,keepdims=True)
    grad_second=jnp.zeros_like(middle)
    for c in range(FF//D):
        s=slice(c*D,(c+1)*D)
        grad_active=mm_t(grad_out,down_ref[s,:])
        x=kept[:,s]
        t=jnp.tanh(GELU_A*(x+GELU_B*(x*x*x)))
        slope=0.5*(1.0+t)+x*(0.5*(1.0-t*t)*(GELU_A*(1.0+3.0*GELU_B*(x*x))))
        grad_before=(grad_active*slope).astype(BF)
        put_turned(late_ref,2*D+FF+c*D,grad_before)
        rows_ref[4+c:5+c,:]=jnp.sum(grad_before.astype(F32),axis=0,keepdims=True)
        grad_second=grad_second+mm_t(grad_before,up_ref[:,s])
    back,rows_ref[1:2,:],rows_ref[2:3,:]=norm_back(grad_second,unit2,spread2,row(5))
    grad_middle=back+grad_result
    middle_grad_ref[...]=grad_middle
    grad_branch=grad_middle.astype(BF)
    put_turned(late_ref,D+FF,grad_branch)
    rows_ref[0:1,:]=jnp.sum(grad_branch.astype(F32),axis=0,keepdims=True)
    mixed_grad_ref[...]=mm_t(wo_ref[...],grad_branch).astype(BF)
    rows_ref[13:16,:]=jnp.zeros((3,D),F32)
def mlp_step(count, hidden, mixed, targets, chosen, vectors, wo, up, down, head):
    t=hidden.shape[0]
    low=lambda rows: ((rows,t),BF)
    return from_hbm(mlp_kernel,"mlp_step",[((t,D),F32),low(D),low(LATE_ROWS),((16,D),F32)],
        [hidden,mixed,targets,chosen,vectors,wo,up,down,head],[pltpu.VMEM((t,FF),F32)],(count.reshape(1),),late=(6,7,8),micros=13)

def input_kernel(in_here, parts_ref, hidden_ref, middle_grad_ref, chosen_ref, vec_ref, rows_ref, qkv_ref, in_ref, last_ref, sums_ref):
    heads,wide,t=parts_ref.shape; hd=wide//3
    for j in range(3):
        for h in range(heads):
            last_ref[j*D+h*hd:j*D+(h+1)*hd,:]=parts_ref[h,j*hd:(j+1)*hd,:]
    packed=last_ref[:3*D,:]
    grad_t=mm(qkv_ref[...],packed)
    grad=jnp.concatenate([grad_t[c*LANE:(c+1)*LANE,:].T for c in range(D//LANE)],axis=1)
    unit,spread=norm_parts(hidden_ref[...])
    back,gain,shift=norm_back(grad,unit,spread,vec_ref[0:1,:])
    grad_hidden=back+middle_grad_ref[...]
    low=grad_hidden.astype(BF)
    put_turned(last_ref,3*D,low)
    sums_ref[0:1,:]=gain; sums_ref[1:2,:]=shift
    ones=jnp.ones((8,t),BF)
    sums_ref[2:3,:]=mm_t(ones,packed[:D])[0:1]
    sums_ref[3:4,:]=mm_t(ones,packed[2*D:])[0:1]
    sums_ref[4:14,:]=rows_ref[0:10,:]
    sums_ref[14:15,:]=jnp.sum(low.astype(F32),axis=0,keepdims=True)
    sums_ref[15:17,:]=rows_ref[10:12,:]
    in_here()
    masked=jnp.where(chosen_ref[...]>0.0,low.astype(F32),0.0).astype(BF)
    for c in range(FEAT//D):
        sums_ref[17+c:18+c,:]=jnp.sum(mm_t(masked,in_ref[c*D:(c+1)*D,:]),axis=0,keepdims=True)
    sums_ref[19:20,:]=rows_ref[12:13,:]
    sums_ref[20:24,:]=jnp.zeros((4,D),F32)
def input_step(parts, hidden, middle_grad, chosen, vectors, rows, qkv, w_in):
    t=hidden.shape[0]
    return from_hbm(input_kernel,"input_step",[((4*D,t),BF),((24,D),F32)],[parts,hidden,middle_grad,chosen,vectors,rows,qkv,w_in],[],late=(7,),micros=5)

def front_kernel(qkv_here, features_ref, chosen_ref, places_ref, vec_ref, in_ref, qkv_ref, hidden_ref, early_ref, heads_ref, turned_ref):
    row=lambda i: vec_ref[i:i+1,:]
    chosen=chosen_ref[...]>0.0
    hidden=places_ref[...]+row(14)
    for c in range(FEAT//D):
        s=slice(c*D,(c+1)*D)
        part=jnp.where(chosen,row(17+c),features_ref[:,s].astype(F32)).astype(BF)
        put_turned(early_ref,D+c*D,part)
        hidden=hidden+mm(part,in_ref[s,:])
    hidden_ref[...]=hidden
    unit,spread=norm_parts(hidden)
    normed=(unit*row(0)+row(1)).astype(BF)
    put_turned(early_ref,0,normed)
    qkv_here()
    heads,wide,t=heads_ref.shape; hd=wide//3
    for j in range(3):
        out=mm(normed,qkv_ref[:,j*D:(j+1)*D])
        if j!=1: out=out+row(2 if j==0 else 3)
        put_turned(turned_ref,j*D,out.astype(BF))
        for h in range(heads):
            heads_ref[h,j*hd:(j+1)*hd,:]=turned_ref[j*D+h*hd:j*D+(h+1)*hd,:]
def front_step(features, chosen, places, vectors, w_in, qkv, heads):
    t=features.shape[0]
    return from_hbm(front_kernel,"front_step",[((t,D),F32),((D+FEAT,t),BF),((heads,3*D//heads,t),BF)],[features,chosen,places,vectors,w_in,qkv],
        [pltpu.VMEM((3*D,t),BF)],late=(5,),micros=5)

I16=jnp.int16; F32=jnp.float32; BF=jnp.bfloat16
GROUP=48; LANE=128; IO=48
STEP_Q=32000.0
UNITS=24; CODE_ROWS=32; PART=UNITS*GROUP+CODE_ROWS
A_ROWS=3*D+FF; X_ROWS=3*D+D+FF+D
ROUND=12582912.0

def encode(x):
    top=jnp.max(jnp.abs(x),axis=0,keepdims=True)
    code=jnp.ceil(jnp.log2(jnp.maximum(top,1e-30))*256.0)
    v=x*(STEP_Q*jnp.exp2(code*(-1.0/256.0)))
    return ((v+ROUND)-ROUND).astype(jnp.int32).astype(I16), code
def scale_of(code16):
    return jnp.exp2(code16.astype(jnp.int32).astype(F32)*(1.0/256.0))*(1.0/STEP_Q)
def pack_codes(codes):
    codes=codes+[jnp.zeros((CODE_ROWS-len(codes),LANE),F32)]
    return jnp.concatenate(codes,axis=0).astype(jnp.int32).astype(I16)

EARLY,MIXED,LATE,LAST=range(4)
PARTS=(((EARLY,0,D),("a",0)),((MIXED,0,D),("a",D)),((LATE,0,D),("a",2*D)),((LATE,D,FF),("a",3*D)),
    ((LAST,0,3*D),("x",0)),((LATE,D+FF,D),("x",3*D)),((LATE,2*D+FF,FF),("x",4*D)),((LATE,2*D+2*FF,D),("x",4*D+FF)),
    ((EARLY,D,FEAT),("a_in",0)),((LAST,3*D,D),("x_in",0)),((LATE,3*D+2*FF,FEAT),("a_head",0)),((LATE,3*D+2*FF+FEAT,D),("x_head",0)))
def grads_kernel(zone, ids_ref, owners_ref, *refs):
    operands=refs[:8]; outs=refs[8:12]
    a_all,x_all,a_in,x_in,a_head,x_head,sem=refs[12:]
    buf_of=dict(a=a_all,x=x_all,a_in=a_in,x_in=x_in,a_head=a_head,x_head=x_head)
    seq,core=ids_ref[0],ids_ref[1]
    copies=[]
    for (source,first,count),(buf,at) in PARTS:
        for side in range(2):
            c=pltpu.make_async_copy(operands[2*source+side].at[pl.ds(first,count)],buf_of[buf].at[pl.ds(at,count),pl.ds(side*LANE,LANE)],sem.at[len(copies)])
            c.start(); copies.append(c)
    for c in copies: c.wait()
    lane=lax.broadcasted_iota(jnp.int32,(BLOCK,LANE),1)
    cols=(4*D+FF)//BLOCK; wide_count=D//BLOCK*cols
    def block(slot):
        n=owners_ref[slot]
        i=n//cols; j=n%cols
        m=n-wide_count
        group=jnp.where(j>=3*D//BLOCK,1,0)+jnp.where(j>=4*D//BLOCK,1,0)
        a_at=jnp.where(m<0,i*BLOCK+group*D,3*D+m//(D//BLOCK)*BLOCK)
        x_at=jnp.where(m<0,j*BLOCK,4*D+FF+m%(D//BLOCK)*BLOCK)
        a=a_all[pl.ds(pl.multiple_of(a_at,32),BLOCK),:]
        x=x_all[pl.ds(pl.multiple_of(x_at,32),BLOCK),:]
        w=lax.dot_general(a,x,(((1,),(1,)),((),())),preferred_element_type=F32)
        return jnp.concatenate([w,jnp.zeros((BLOCK,LANE-BLOCK),F32)],axis=1)
    for out,h,first,step in ((outs[0],0,2,1),(outs[2],1,1,2),(outs[1],0,0,1),(outs[3],1,0,2)):
        def one(j,carry,out=out,h=h,first=first,step=step):
            device=2*jnp.bitwise_xor(seq,zone*4+first+step*j)+core
            codes=[]
            for g in range(3):
                w=[block(device*24+(h*3+g)*4+t) for t in range(4)]
                for v in range(3):
                    tile=jnp.where(lane<BLOCK,w[v],pltpu.roll(w[3],BLOCK-32*v,1))
                    for half in range(2):
                        q,code=encode(tile[half*GROUP:(half+1)*GROUP])
                        at=((g*3+v)*2+half)*GROUP
                        out[j,at:at+GROUP,:]=q; codes.append(code)
            a_ref,x_ref=((a_in,x_in),(a_head,x_head))[h]
            w=lax.dot_general(a_ref[pl.ds(pl.multiple_of(device*IO,16),IO),:],x_ref[...],(((1,),(1,)),((),())),preferred_element_type=F32)
            for v in range(6):
                q,code=encode(w[:,v*LANE:(v+1)*LANE])
                at=(18+v)*GROUP
                out[j,at:at+GROUP,:]=q; codes.append(code)
            out[j,UNITS*GROUP:,:]=pack_codes(codes)
            return carry
        lax.fori_loop(0,2,one,0)

def weight_grads(zone, ids, owners, operands):
    n=len(operands)
    return pl.pallas_call(partial(grads_kernel,zone),
        out_shape=[jax.ShapeDtypeStruct((2,PART,LANE),I16)]*4,
        in_specs=[pl.BlockSpec(memory_space=pltpu.SMEM)]*2+[pl.BlockSpec(memory_space=pl.ANY)]*n,
        out_specs=[pl.BlockSpec(memory_space=pltpu.VMEM)]*4,
        scratch_shapes=[pltpu.VMEM((A_ROWS,2*LANE),BF),pltpu.VMEM((X_ROWS,2*LANE),BF),pltpu.VMEM((FEAT,2*LANE),BF),pltpu.VMEM((D,2*LANE),BF),
            pltpu.VMEM((FEAT,2*LANE),BF),pltpu.VMEM((D,2*LANE),BF),pltpu.SemaphoreType.DMA((2*len(PARTS),))],
        compiler_params=pltpu.CompilerParams(vmem_limit_bytes=40<<20), cost_estimate=takes(0.8), name="weight_grads")(ids,owners,*operands)

class At:
    def __init__(s,ref,*i): s.ref,s.i=ref,i
    def __getitem__(s,k): return s.ref[(*s.i,k,slice(None))]
    def __setitem__(s,k,v): s.ref[(*s.i,k,slice(None))]=v
def summed(views):
    scales=[scale_of(v[UNITS*GROUP:PART]) for v in views]
    for k in range(UNITS):
        total=None
        for v,s in zip(views,scales):
            x=v[k*GROUP:(k+1)*GROUP].astype(jnp.int32).astype(F32)*s[k:k+1,:]
            total=x if total is None else total+x
        yield k,total
def add_codes(views, out):
    codes=[]
    for k,total in summed(views):
        q,code=encode(total)
        out[k*GROUP:(k+1)*GROUP]=q
        codes.append(code)
    out[UNITS*GROUP:PART]=pack_codes(codes)
def takes(micros):
    return pl.CostEstimate(flops=0,transcendentals=0,bytes_accessed=int(micros*3.3e6))
def code_call(kernel, name, outs, *args):
    return pl.pallas_call(kernel, out_shape=[jax.ShapeDtypeStruct(s,t) for s,t in outs],
        in_specs=[pl.BlockSpec(memory_space=pltpu.VMEM)]*len(args), out_specs=[pl.BlockSpec(memory_space=pltpu.VMEM)]*len(outs),
        compiler_params=pltpu.CompilerParams(vmem_limit_bytes=32<<20), cost_estimate=takes(0.15), name=name)(*args)
def plane_kernel(*refs):
    n=len(refs)//2
    for i in range(0,n,2):
        (keep,got),(send,stay)=refs[i:i+2],refs[n+i:n+i+2]
        add_codes([At(keep,1),At(got,1)],At(send))
        add_codes([At(keep,0),At(got,0)],At(stay))
def line_kernel(*refs):
    stay_a,got_a,stay_b,got_b=refs[:4]; more=refs[4:-1]; out=refs[-1]
    for h,(stay,got) in enumerate(((stay_a,got_a),(stay_b,got_b))):
        add_codes([At(stay),At(got)]+[At(m,h) for m in more],At(out,h))
def final_kernel(*refs):
    stay_a,got_a,stay_b,got_b=refs[:4]; more=refs[4:-4]; vec,blocks,io,sums=refs[-4:]
    square=jnp.zeros((1,LANE),F32)
    for h,(stay,got) in enumerate(((stay_a,got_a),(stay_b,got_b))):
        for k,total in summed([At(stay),At(got)]+[At(m,h) for m in more]):
            square=square+jnp.sum(total*total,axis=0,keepdims=True)
            if k<18:
                g,v,half=k//6,k//2%3,k%2
                rows=slice(half*GROUP,(half+1)*GROUP)
                blocks[(h*3+g)*4+v,rows,:]=total[:,:BLOCK]
                blocks[(h*3+g)*4+3,rows,32*v:32*(v+1)]=total[:,BLOCK:]
            else:
                io[:,h,(k-18)*LANE:(k-17)*LANE]=total
    sums[0:23,:]=vec[0:23,:]
    sums[23:24,:]=jnp.broadcast_to(jnp.sum(square,keepdims=True),(1,D))
HALF=(PART,LANE)
def reduce_tree(ids, owners, operands, vec):
    send={}; keep={}; got={}; stay={}; far={}
    def make(k):
        send_a,keep_a,send_b,keep_b=weight_grads(k,ids,owners,operands)
        send[k]=(send_a,send_b); keep[k]=(keep_a,keep_b)
    def leave(k,*masks):
        got[k]=tuple(swap(part,"seq",mask) for part,mask in zip(send[k],masks))
    def plane(*pieces):
        outs=code_call(plane_kernel,"add_plane",[(HALF,I16)]*4*len(pieces),*[ref for k in pieces for ref in (keep[k][0],got[k][0],keep[k][1],got[k][1])])
        for i,k in enumerate(pieces):
            send_a,stay_a,send_b,stay_b=outs[4*i:4*i+4]
            stay[k]=(stay_a,stay_b); send[k]=(send_a,send_b)
            leave(k,1,2)
    def line(k,mask,*more):
        far[k]=swap(code_call(line_kernel,"add_line",[((2,)+HALF,I16)],stay[k][0],got[k][0],stay[k][1],got[k][1],*more)[0],"seq",mask)
    make(3); leave(3,2,1)
    make(2); leave(2,2,1)
    make(1)
    (got[3],got[2]),keep[1]=gate((got[3],got[2]),keep[1])
    plane(3,2)
    (send[1],ids),got[3],got[2]=gate((send[1],ids),got[3],got[2])
    line(3,4)
    leave(1,2,1)
    make(0)
    got[1],far[3],keep[0]=gate(got[1],far[3],keep[0])
    line(2,8,far[3])
    plane(1)
    line(1,4)
    send[0],got[1]=gate(send[0],got[1])
    leave(0,2,1)
    plane(0)
    return code_call(final_kernel,"add_final",[((24,BLOCK,BLOCK),F32),((IO,2,D),F32),((24,D),F32)],stay[0][0],got[0][0],stay[0][1],got[0][1],far[1],far[2],vec)

BLOCK=96; NEWTON=6; F32=jnp.float32; BF=jnp.bfloat16; LANE=128
def halves(x):
    hi=x.astype(BF); return hi,(x-hi.astype(F32)).astype(BF)
def left_of(x):
    hi,lo=halves(x)
    return jnp.concatenate([hi,lo],axis=1)
def right_of(x):
    hi,lo=halves(x)
    zero=jnp.zeros_like(lo)
    return jnp.concatenate([jnp.concatenate([hi,lo],axis=1),jnp.concatenate([hi,zero],axis=1)],axis=0)
def times(a,b):
    w=jnp.dot(a,b,preferred_element_type=F32)
    n=w.shape[1]//2
    return w[:,:n]+w[:,n:]
def shampoo_kernel(sums_ref, grad_ref, left_ref, right_ref, block_ref, io_grad_ref, io_ref, io_first_ref, io_second_ref, vec_ref, vec_first_ref, vec_second_ref,
                   grad_out, left_out, right_out, block_out, io_first_out, io_second_out, io_out, vec_first_out, vec_second_out, vec_out, norm_out, *, beta, rate, eps, n_side):
    n_vec=vec_ref.shape[0]
    vec_grad=sums_ref[0:n_vec,:]
    norm=jnp.sqrt(sums_ref[23:24,0:1]+jnp.sum(vec_grad*vec_grad,keepdims=True))
    norm_out[...]=jnp.broadcast_to(norm,norm_out.shape)
    factor=jnp.minimum(1.0,clip_limit/norm)
    vec_first_out[...],vec_second_out[...],vec_out[...]=adam_update(vec_ref[...],vec_first_ref[...],vec_second_ref[...],vec_grad*factor,rate_vector,0.0)
    for m in range(2):
        parts=[ref[:,m,:] for ref in (io_ref,io_first_ref,io_second_ref,io_grad_ref)]
        io_first_out[:,m,:],io_second_out[:,m,:],io_out[:,m,:]=adam_update(*parts[:3],parts[3]*factor,rate_adam,weight_decay)
    side=LANE
    row=lax.broadcasted_iota(jnp.int32,(side,side),0); col=lax.broadcasted_iota(jnp.int32,(side,side),1)
    eye=jnp.where((row==col)&(row<BLOCK),1.0,0.0)
    def full(x):
        x=jnp.concatenate([x,jnp.zeros((BLOCK,side-BLOCK),F32)],axis=1)
        return jnp.concatenate([x,jnp.zeros((side-BLOCK,side),F32)],axis=0)
    def one(i,carry):
        grads=[full(grad_ref[i*n_side+j]*factor) for j in range(n_side)]
        flipped=[g.T for g in grads]
        stats=[]
        for j in range(n_side):
            s=i*n_side+j
            gl,gr=left_of(grads[j]),right_of(grads[j]); tl,tr=left_of(flipped[j]),right_of(flipped[j])
            l=beta*full(left_ref[s])+(1.0-beta)*times(gl,tr)
            r=beta*full(right_ref[s])+(1.0-beta)*times(tl,gr)
            grad_out[s]=grads[j][:BLOCK,:BLOCK]; left_out[s]=l[:BLOCK,:BLOCK]; right_out[s]=r[:BLOCK,:BLOCK]
            stats+=[l,r]
        n=len(stats)
        regular=[m+eps*eye for m in stats]
        scaled=[2.5*lax.rsqrt(jnp.sum(m*m,keepdims=True)) for m in regular]
        moving=[m*s for m,s in zip(regular,scaled)]
        root=[None]*n
        for sweep in range(NEWTON):
            factors=[(5.0*eye-m)*0.25 for m in moving]
            fl=[left_of(f) for f in factors]; fr=[right_of(f) for f in factors]
            if sweep==0: root=[f*jnp.sqrt(jnp.sqrt(s)) for f,s in zip(factors,scaled)]
            else: root=[times(left_of(x),f) for x,f in zip(root,fr)]
            if sweep<NEWTON-1:
                square=[times(a,b) for a,b in zip(fl,fr)]
                fourth=[times(left_of(q),right_of(q)) for q in square]
                moving=[times(left_of(q),right_of(m)) for q,m in zip(fourth,moving)]
        for j in range(n_side):
            s=i*n_side+j
            d=times(left_of(root[2*j]),right_of(grads[j]))
            d=times(left_of(d),right_of(root[2*j+1]))
            block_out[s]=block_ref[s]-rate*d[:BLOCK,:BLOCK]
        return carry
    lax.fori_loop(0,grad_ref.shape[0]//n_side,one,0)
def update_step(sums, grads, left, right, blocks, io_grad, io_set, vec_set, n_side=8):
    like=lambda *xs: [jax.ShapeDtypeStruct(x.shape,F32) for x in xs]
    args=(sums,grads,left,right,blocks,io_grad,*io_set,*vec_set)
    return pl.pallas_call(partial(shampoo_kernel,beta=beta_stat,rate=rate_shampoo,eps=root_eps,n_side=n_side),
        out_shape=like(grads,grads,grads,grads,*io_set,*vec_set)+[jax.ShapeDtypeStruct((8,LANE),F32)],
        in_specs=[vmem()]*len(args),out_specs=[vmem()]*11,
        compiler_params=pltpu.CompilerParams(vmem_limit_bytes=48<<20),name="update_step")(*args)


def fits(mesh):
    return mesh.shape["seq"] == 16 and mesh.shape["opt"] == 2


def sum_everywhere(value):
    value = value + swap(value, "opt", 1)
    for bit in range((lax.axis_size("seq") - 1).bit_length()):
        value = value + swap(value, "seq", 2**bit)
    return value


def to_heads(parts):
    return lax.all_to_all(parts, "seq", 0, 0, tiled=True)


def evens_first(rows):
    return rows.reshape((rows.shape[0] // 2, 2) + rows.shape[1:]).swapaxes(0, 1).reshape(rows.shape)


def fast_device(
    features,
    tile_mask,
    lengths,
    owners,
    layer_blocks,
    stat_left,
    stat_right,
    io_weights,
    io_first,
    io_second,
    vectors,
    vec_first,
    vec_second,
):
    tok_dev = features.shape[1]
    seq_index = lax.axis_index("seq")
    core_index = lax.axis_index("opt")
    ids = jnp.stack([seq_index, core_index]).astype(jnp.int32)
    low_targets = evens_first(features[0])
    chosen_rows = evens_first(tile_mask[0]).astype(jnp.float32)[:, None]
    lengths_row = lax.dynamic_index_in_dim(lengths, core_index, 0, keepdims=False)
    places = seq_index * tok_dev + evens_first(jnp.arange(tok_dev, dtype=jnp.int32))
    shards = gather_shards(layer_blocks, io_weights, tile_mask)
    block_rows, io_rows = shard_rows(seq_index, core_index)
    qkv_weight, out_weight, in_weight, tile_counts = join_weights(
        FIRST_PLAN, 0, shards, owners, block_rows, io_rows
    )
    tile_count = tile_counts[0, 0]
    hidden, early_low, by_head = front_step(
        low_targets,
        chosen_rows,
        sine_places(slide_offsets(lengths_row, places)),
        vectors,
        in_weight,
        qkv_weight,
        HEADS,
    )
    late_owners, by_head = gate(owners, by_head)
    up_weight, down_weight, head_weight, late_counts = join_weights(
        SECOND_PLAN, 1, shards, late_owners, block_rows, io_rows
    )
    own_head, head_weight = gate(to_heads(by_head), head_weight)
    head_out, mixed_parts, head_totals = attend(lengths, ids, own_head)
    mixed_low = to_heads(mixed_parts).reshape(D, tok_dev)
    grad_middle, grad_mixed, late_low, late_rows = mlp_step(
        tile_count,
        hidden,
        mixed_low,
        low_targets,
        chosen_rows,
        vectors,
        out_weight,
        up_weight,
        down_weight,
        head_weight,
    )
    grad_head_out = to_heads(grad_mixed.reshape(HEADS, HEAD_DIM, tok_dev))
    grad_parts = attend_back(lengths, ids, own_head, grad_head_out, head_out, head_totals)
    others = [swap(operand, "opt", 1) for operand in (early_low, mixed_low, late_low)]
    own_parts, others[0], others[1] = gate(to_heads(grad_parts), others[0], others[1])
    last_low, vec_grads = input_step(
        own_parts,
        hidden,
        grad_middle,
        chosen_rows,
        vectors,
        late_rows,
        qkv_weight,
        in_weight,
    )
    others.append(swap(last_low, "opt", 1))
    operands = []
    for pair in zip((early_low, mixed_low, late_low, last_low), others):
        operands += pair
    slot_sum, io_sum, own_sums = reduce_tree(ids, owners, operands, vec_grads)
    all_sums = sum_everywhere(own_sums)
    (
        block_grads,
        left_new,
        right_new,
        blocks_new,
        io_first_new,
        io_second_new,
        io_new,
        vec_first_new,
        vec_second_new,
        vec_new,
        norms,
    ) = update_step(
        all_sums,
        slot_sum,
        stat_left,
        stat_right,
        layer_blocks,
        io_sum,
        (io_weights, io_first, io_second),
        (vectors, vec_first, vec_second),
    )
    grad_norm = norms[0, 0]
    error_sum = all_sums[vectors.shape[0], 0]
    return (
        grad_norm,
        error_sum,
        tile_count,
        block_grads,
        left_new,
        right_new,
        blocks_new,
        io_first_new,
        io_second_new,
        io_new,
        vec_first_new,
        vec_second_new,
        vec_new,
    )


def solution(mesh):
    return jax.shard_map(
        fast_device if fits(mesh) else per_device,
        mesh=mesh,
        in_specs=(
            P("opt", "seq", None),
            P("opt", "seq"),
            P(),
            P(),
            P(("seq", "opt"), None, None),
            P(("seq", "opt"), None, None),
            P(("seq", "opt"), None, None),
            P(("seq", "opt"), None, None),
            P(("seq", "opt"), None, None),
            P(("seq", "opt"), None, None),
            P(),
            P(),
            P(),
        ),
        out_specs=(
            P(),
            P(),
            P(),
            P(("seq", "opt"), None, None),
            P(("seq", "opt"), None, None),
            P(("seq", "opt"), None, None),
            P(("seq", "opt"), None, None),
            P(("seq", "opt"), None, None),
            P(("seq", "opt"), None, None),
            P(("seq", "opt"), None, None),
            P(),
            P(),
            P(),
        ),
        check_vma=False,
    )
```

```python
from functools import partial
import math

import jax
import jax.numpy as jnp
import numpy as np
from jax import lax
from jax.experimental import pallas as pl
from jax.experimental.pallas import tpu as pltpu
from jax.sharding import PartitionSpec as P

D = 768
HEADS = 16
HEAD_DIM = 48
FF = 3072
FEAT = 1536
LAYERS = 1
BRANCHES = 5
SEG0 = 1024
BLOCK = 96
SLIDES = 4
NEWTON = 6
STEP = 10


norm_eps = 1e-05
clip_limit = 1.0
beta_one = 0.9
beta_two = 0.95
adam_eps = 1e-08
rate_adam = 0.01
rate_vector = 0.2
weight_decay = 0.05
beta_stat = 0.95
rate_shampoo = 0.05
root_eps = 1e-12
masked_score = -1e30
highest = lax.Precision.HIGHEST


def from_partner(value, axis, stride):
    mask = 2**stride
    pairs = [(source, source ^ mask) for source in range(lax.axis_size(axis))]
    return lax.ppermute(value, axis, pairs)


def for_sending(shard):

    def short(part):
        return part.astype(jnp.bfloat16) if part.dtype == jnp.float32 else part

    return jax.tree.map(short, shard)


def layer_norm(values, gain, shift):
    centred = values - jnp.mean(values, axis=-1, keepdims=True)
    spread = jnp.mean(centred * centred, axis=-1, keepdims=True)
    return centred * lax.rsqrt(spread + norm_eps) * gain + shift


def sine_places(places):
    half_width = D // 2
    freq_rates = jnp.exp(
        jnp.arange(half_width, dtype=jnp.float32) * (-math.log(10000.0) / half_width)
    )
    angles = (places.astype(jnp.float32) / 64.0)[:, None] * freq_rates[None, :]
    return jnp.concatenate([jnp.sin(angles), jnp.cos(angles)], axis=1)


def slide_ids(lengths_row, places):
    slide_ends = jnp.cumsum(lengths_row)
    return jnp.sum((places[..., None] >= slide_ends[:-1]).astype(jnp.int32), axis=-1)


def slide_offsets(lengths_row, places):
    slide_ends = jnp.cumsum(lengths_row)
    slide_starts = slide_ends - lengths_row
    owner_ids = slide_ids(lengths_row, places)
    match_rows = owner_ids[:, None] == jnp.arange(SLIDES, dtype=jnp.int32)[None, :]
    picked = jnp.sum(jnp.where(match_rows, slide_starts[None, :], 0), axis=1)
    return places - picked


def head_offsets(dilation):
    return np.arange(HEADS) % dilation


def pick_rows(values, dilation):
    row_count = values.shape[0] // dilation
    shaped = values.reshape((row_count, dilation) + values.shape[1:])
    return shaped[:, head_offsets(dilation), np.arange(HEADS)]


def spread_rows(values, dilation, filler):
    row_count = values.shape[0]
    hit_mask = np.arange(dilation)[:, None] == head_offsets(dilation)[None, :]
    hit_mask = hit_mask.reshape((1, dilation, HEADS) + (1,) * (values.ndim - 2))
    spread_out = jnp.where(hit_mask, values[:, None], filler)
    return spread_out.reshape((row_count * dilation,) + values.shape[1:])


def branch_geom(branch, tok_dev, seq_len):
    dilation = 2**branch
    segment = min(SEG0 * dilation, seq_len)
    return (dilation, segment, max(1, segment // tok_dev))


def branch_docs(lengths_row, first_place, row_count, dilation):
    places = (
        first_place
        + jnp.asarray(head_offsets(dilation), jnp.int32)[None, :]
        + dilation * jnp.arange(row_count, dtype=jnp.int32)[:, None]
    )
    return slide_ids(lengths_row, places)


def contract_rows(left, right):
    return lax.dot_general(
        left, right, (((0,), (0,)), ((), ())), preferred_element_type=jnp.float32
    )


def contract_cols(left, right):
    return lax.dot_general(
        left, right, (((1,), (1,)), ((), ())), preferred_element_type=jnp.float32
    )


def assemble(natural):
    per_layer = natural.reshape(LAYERS, -1, BLOCK, BLOCK)
    col_count = (4 * D + FF) // BLOCK
    wide_count = D // BLOCK * col_count
    upper_mats = per_layer[:, :wide_count].reshape(LAYERS, D // BLOCK, col_count, BLOCK, BLOCK)
    upper_mats = upper_mats.transpose(0, 1, 3, 2, 4).reshape(LAYERS, D, 4 * D + FF)
    lower_mats = per_layer[:, wide_count:].reshape(LAYERS, FF // BLOCK, D // BLOCK, BLOCK, BLOCK)
    lower_mats = lower_mats.transpose(0, 1, 3, 2, 4).reshape(LAYERS, FF, D)
    return (upper_mats, lower_mats)


def disassemble(upper_mats, lower_mats):
    col_count = (4 * D + FF) // BLOCK
    top_part = upper_mats.reshape(LAYERS, D // BLOCK, BLOCK, col_count, BLOCK).transpose(
        0, 1, 3, 2, 4
    )
    top_part = top_part.reshape(LAYERS, -1, BLOCK, BLOCK)
    bottom_part = lower_mats.reshape(LAYERS, FF // BLOCK, BLOCK, D // BLOCK, BLOCK).transpose(
        0, 1, 3, 2, 4
    )
    bottom_part = bottom_part.reshape(LAYERS, -1, BLOCK, BLOCK)
    return jnp.concatenate([top_part, bottom_part], axis=1).reshape(-1, BLOCK, BLOCK)


def unpack(vector_set):
    per_layer = 8 + FF // D
    return (
        vector_set[: LAYERS * per_layer].reshape(LAYERS, per_layer, D),
        vector_set[LAYERS * per_layer :],
    )


def collect_pairs(pieces, bit_counts, seq_index):
    pieces = list(pieces)
    for bit_id in range(max(bit_counts + [0])):
        active_ids = [branch for branch in range(len(pieces)) if bit_counts[branch] > bit_id]
        outgoing = jnp.concatenate([pieces[branch] for branch in active_ids], axis=0)
        partner = from_partner(outgoing, "seq", bit_id)
        lower_side = seq_index // 2**bit_id % 2 == 0
        offset_at = 0
        for branch in active_ids:
            my_part = pieces[branch]
            part_size = my_part.shape[0]
            their_part = partner[offset_at : offset_at + part_size]
            offset_at = offset_at + part_size
            pieces[branch] = jnp.where(
                lower_side,
                jnp.concatenate([my_part, their_part], 0),
                jnp.concatenate([their_part, my_part], 0),
            )
    return pieces


def return_pairs(pieces, bit_counts, seq_index):
    pieces = list(pieces)
    for bit_id in reversed(range(max(bit_counts + [0]))):
        active_ids = [branch for branch in range(len(pieces)) if bit_counts[branch] > bit_id]
        lower_side = seq_index // 2**bit_id % 2 == 0
        kept_parts, sent_parts = ([], [])
        for branch in active_ids:
            half_size = pieces[branch].shape[0] // 2
            first_part = pieces[branch][:half_size]
            second_part = pieces[branch][half_size:]
            kept_parts.append(jnp.where(lower_side, first_part, second_part))
            sent_parts.append(jnp.where(lower_side, second_part, first_part))
        partner = from_partner(for_sending(jnp.concatenate(sent_parts, axis=0)), "seq", bit_id)
        offset_at = 0
        for branch, kept_part in zip(active_ids, kept_parts):
            part_size = kept_part.shape[0]
            pieces[branch] = kept_part + partner[offset_at : offset_at + part_size]
            offset_at = offset_at + part_size
    return pieces


def score_block(query_rows, key_rows, query_docs, key_docs):
    raw_scores = jnp.einsum(
        "sqhd,skhd->shqk", query_rows, key_rows, preferred_element_type=jnp.float32
    ) * HEAD_DIM ** (-0.5)
    same_slide = (
        jnp.transpose(query_docs, (0, 2, 1))[..., None]
        == jnp.transpose(key_docs, (0, 2, 1))[:, :, None, :]
    )
    return jnp.where(same_slide, raw_scores, masked_score)


def attend_forward(packed, lengths_row, seq_len, seq_index):
    tok_dev = packed.shape[0]
    triple = packed.reshape(tok_dev, 3, HEADS, HEAD_DIM)
    queries, key_all, value_all = (triple[:, 0], triple[:, 1], triple[:, 2])
    geoms = [branch_geom(branch, tok_dev, seq_len) for branch in range(BRANCHES)]
    local_pairs = [
        jnp.stack([pick_rows(key_all, geom[0]), pick_rows(value_all, geom[0])], axis=1).reshape(
            -1, 2 * D
        )
        for geom in geoms
    ]
    bit_counts = [geom[2].bit_length() - 1 for geom in geoms]
    joined = collect_pairs(local_pairs, bit_counts, seq_index)
    kept_state, outputs, totals_all = ([], [], [])
    for branch in range(BRANCHES):
        dilation, segment, group_size = geoms[branch]
        sections = max(1, tok_dev // segment)
        query_rows = pick_rows(queries, dilation).reshape(sections, -1, HEADS, HEAD_DIM)
        pair_rows = joined[branch].reshape(sections, -1, 2, HEADS, HEAD_DIM)
        key_rows = pair_rows[:, :, 0]
        value_rows = pair_rows[:, :, 1]
        query_docs = branch_docs(
            lengths_row, seq_index * tok_dev, tok_dev // dilation, dilation
        ).reshape(sections, -1, HEADS)
        group_first = seq_index // group_size * group_size * tok_dev
        key_docs = branch_docs(lengths_row, group_first, joined[branch].shape[0], dilation).reshape(
            sections, -1, HEADS
        )
        scores = score_block(query_rows, key_rows, query_docs, key_docs)
        totals = jax.nn.logsumexp(scores, axis=-1)
        softmax_rows = jnp.exp(scores - totals[..., None]).astype(jnp.bfloat16)
        output = jnp.einsum(
            "shqk,skhd->sqhd", softmax_rows, value_rows, preferred_element_type=jnp.float32
        ).reshape(-1, HEADS, HEAD_DIM)
        totals_rows = jnp.transpose(totals, (0, 2, 1)).reshape(-1, HEADS)
        kept_state.append(
            (query_rows, key_rows, value_rows, query_docs, key_docs, output, totals_rows)
        )
        outputs.append(spread_rows(output, dilation, 0.0))
        totals_all.append(spread_rows(totals_rows, dilation, masked_score))
    stacked = jnp.stack(totals_all)
    grand_total = jax.nn.logsumexp(stacked, axis=0)
    mixed_out = jnp.zeros_like(outputs[0])
    for branch in range(BRANCHES):
        mixed_out = mixed_out + jnp.exp(stacked[branch] - grand_total)[..., None] * outputs[branch]
    return (mixed_out, (mixed_out, grand_total, kept_state))


def attend_backward(grad_mixed, attention_state, seq_len, seq_index):
    mixed_out, grand_total, kept_state = attention_state
    tok_dev = grad_mixed.shape[0]
    score_scale = HEAD_DIM ** (-0.5)
    grad_query = jnp.zeros(grad_mixed.shape, jnp.float32)
    key_terms, bit_counts, dilations = ([], [], [])
    for branch in range(BRANCHES):
        dilation, segment, group_size = branch_geom(branch, tok_dev, seq_len)
        query_rows, key_rows, value_rows, query_docs, key_docs, output, totals_rows = kept_state[
            branch
        ]
        sections = query_rows.shape[0]
        weight = jnp.exp(totals_rows - pick_rows(grand_total, dilation))
        grad_picked = pick_rows(grad_mixed, dilation)
        grad_output = (
            (weight[..., None] * grad_picked)
            .astype(jnp.bfloat16)
            .reshape(sections, -1, HEADS, HEAD_DIM)
        )
        grad_totals = weight * jnp.sum(
            grad_picked * (output - pick_rows(mixed_out, dilation)), axis=-1
        )
        grad_totals = jnp.transpose(grad_totals.reshape(sections, -1, HEADS), (0, 2, 1))
        totals = jnp.transpose(totals_rows.reshape(sections, -1, HEADS), (0, 2, 1))
        softmax_rows = jnp.exp(
            score_block(query_rows, key_rows, query_docs, key_docs) - totals[..., None]
        )
        grad_value = jnp.einsum(
            "shqk,sqhd->skhd",
            softmax_rows.astype(jnp.bfloat16),
            grad_output,
            preferred_element_type=jnp.float32,
        )
        grad_probs = jnp.einsum(
            "sqhd,skhd->shqk", grad_output, value_rows, preferred_element_type=jnp.float32
        )
        inner_sum = jnp.sum(softmax_rows * grad_probs, axis=-1, keepdims=True)
        grad_scores = (softmax_rows * (grad_probs - inner_sum + grad_totals[..., None])).astype(
            jnp.bfloat16
        )
        grad_q = (
            jnp.einsum("shqk,skhd->sqhd", grad_scores, key_rows, preferred_element_type=jnp.float32)
            * score_scale
        )
        grad_k = (
            jnp.einsum(
                "shqk,sqhd->skhd", grad_scores, query_rows, preferred_element_type=jnp.float32
            )
            * score_scale
        )
        grad_query = grad_query + spread_rows(grad_q.reshape(-1, HEADS, HEAD_DIM), dilation, 0.0)
        key_terms.append(
            jnp.stack(
                [grad_k.reshape(-1, HEADS, HEAD_DIM), grad_value.reshape(-1, HEADS, HEAD_DIM)],
                axis=1,
            ).reshape(-1, 2 * D)
        )
        bit_counts.append(group_size.bit_length() - 1)
        dilations.append(dilation)
    own_terms = return_pairs(key_terms, bit_counts, seq_index)
    grad_key = jnp.zeros(grad_mixed.shape, jnp.float32)
    grad_val = jnp.zeros(grad_mixed.shape, jnp.float32)
    for branch in range(BRANCHES):
        pair_rows = own_terms[branch].reshape(-1, 2, HEADS, HEAD_DIM)
        grad_key = grad_key + spread_rows(pair_rows[:, 0], dilations[branch], 0.0)
        grad_val = grad_val + spread_rows(pair_rows[:, 1], dilations[branch], 0.0)
    return jnp.stack([grad_query, grad_key, grad_val], axis=1).reshape(tok_dev, 3 * D)


def layer_forward(hidden, upper_mat, lower_mat, row_set, lengths_row, seq_len, seq_index):
    normed = layer_norm(hidden, row_set[0], row_set[1]).astype(jnp.bfloat16)
    biases = jnp.concatenate([row_set[2], jnp.zeros_like(row_set[2]), row_set[3]])
    packed = (
        jnp.dot(normed, upper_mat[:, : 3 * D], preferred_element_type=jnp.float32) + biases[None, :]
    ).astype(jnp.bfloat16)
    mixed_out, attention_state = attend_forward(packed, lengths_row, seq_len, seq_index)
    mixed_low = mixed_out.reshape(-1, D).astype(jnp.bfloat16)
    middle = (
        hidden
        + jnp.dot(mixed_low, upper_mat[:, 3 * D : 4 * D], preferred_element_type=jnp.float32)
        + row_set[4][None, :]
    )
    second = layer_norm(middle, row_set[5], row_set[6]).astype(jnp.bfloat16)
    before = (
        jnp.dot(second, upper_mat[:, 4 * D :], preferred_element_type=jnp.float32)
        + row_set[8:].reshape(-1)[None, :]
    )
    active = jax.nn.gelu(before, approximate=True).astype(jnp.bfloat16)
    result = (
        middle
        + jnp.dot(active, lower_mat, preferred_element_type=jnp.float32)
        + row_set[7][None, :]
    )
    return (result, (hidden, normed, mixed_low, middle, second, before, active, attention_state))


def layer_backward(grad_result, upper_mat, lower_mat, row_set, layer_state, seq_len, seq_index):
    hidden, normed, mixed_low, middle, second, before, active, attention_state = layer_state
    grad_out = grad_result.astype(jnp.bfloat16)
    grad_lower = contract_rows(active, grad_out)
    grad_fc2_bias = jnp.sum(grad_out, axis=0, dtype=jnp.float32)
    grad_active = contract_cols(grad_out, lower_mat)
    gelu_value, gelu_back = jax.vjp(partial(jax.nn.gelu, approximate=True), before)
    grad_before = gelu_back(grad_active)[0].astype(jnp.bfloat16)
    grad_fc1 = contract_rows(second, grad_before)
    grad_fc1_bias = jnp.sum(grad_before, axis=0, dtype=jnp.float32)
    grad_second = contract_cols(grad_before, upper_mat[:, 4 * D :])
    norm_value, norm_back = jax.vjp(layer_norm, middle, row_set[5], row_set[6])
    grad_middle, grad_gain_two, grad_shift_two = norm_back(grad_second)
    grad_middle = grad_middle + grad_result
    grad_branch = grad_middle.astype(jnp.bfloat16)
    grad_proj = contract_rows(mixed_low, grad_branch)
    grad_proj_bias = jnp.sum(grad_branch, axis=0, dtype=jnp.float32)
    grad_mixed = contract_cols(grad_branch, upper_mat[:, 3 * D : 4 * D]).reshape(
        -1, HEADS, HEAD_DIM
    )
    grad_packed = attend_backward(grad_mixed, attention_state, seq_len, seq_index).astype(
        jnp.bfloat16
    )
    grad_qkv = contract_rows(normed, grad_packed)
    packed_sums = jnp.sum(grad_packed, axis=0, dtype=jnp.float32)
    grad_normed = contract_cols(grad_packed, upper_mat[:, : 3 * D])
    first_value, first_back = jax.vjp(layer_norm, hidden, row_set[0], row_set[1])
    grad_hidden, grad_gain_one, grad_shift_one = first_back(grad_normed)
    grad_hidden = grad_hidden + grad_middle
    grad_upper = jnp.concatenate([grad_qkv, grad_proj, grad_fc1], axis=1)
    small_rows = jnp.stack(
        [
            grad_gain_one,
            grad_shift_one,
            packed_sums[:D],
            packed_sums[2 * D :],
            grad_proj_bias,
            grad_gain_two,
            grad_shift_two,
            grad_fc2_bias,
        ]
    )
    grad_rows = jnp.concatenate([small_rows, grad_fc1_bias.reshape(-1, D)], axis=0)
    return (grad_hidden, (grad_upper, grad_lower, grad_rows))


def inverse_root(matrix):
    identity = jnp.eye(matrix.shape[-1], dtype=jnp.float32)
    regular = matrix + root_eps * identity
    frob_norm = jnp.sqrt(jnp.sum(regular * regular, axis=(1, 2), keepdims=True))
    scaled = 2.5 / frob_norm
    root_mat = identity * jnp.sqrt(jnp.sqrt(scaled))
    moving = regular * scaled
    for sweep_id in range(NEWTON):
        factor = (5.0 * identity - moving) * 0.25
        root_mat = jnp.einsum("kij,kjl->kil", root_mat, factor, precision=highest)
        square = jnp.einsum("kij,kjl->kil", factor, factor, precision=highest)
        fourth = jnp.einsum("kij,kjl->kil", square, square, precision=highest)
        moving = jnp.einsum("kij,kjl->kil", fourth, moving, precision=highest)
    return root_mat


def adam_update(weight, first_mom, second_mom, grad, rate, decay):
    first_new = beta_one * first_mom + (1.0 - beta_one) * grad
    second_new = beta_two * second_mom + (1.0 - beta_two) * grad * grad
    first_hat = first_new / (1.0 - beta_one**STEP)
    second_hat = second_new / (1.0 - beta_two**STEP)
    return (
        first_new,
        second_new,
        weight - rate * (first_hat / (jnp.sqrt(second_hat) + adam_eps) + decay * weight),
    )


def per_device(
    features,
    tile_mask,
    lengths,
    owners,
    layer_blocks,
    stat_left,
    stat_right,
    io_weights,
    io_first,
    io_second,
    vectors,
    vec_first,
    vec_second,
):
    tok_dev = features.shape[1]
    seq_size = lax.axis_size("seq")
    seq_len = tok_dev * seq_size
    seq_index = lax.axis_index("seq")
    core_index = lax.axis_index("opt")
    targets = features[0].astype(jnp.float32)
    chosen = tile_mask[0][:, None] > 0
    lengths_row = lax.dynamic_index_in_dim(lengths, core_index, 0, keepdims=False)
    places = seq_index * tok_dev + jnp.arange(tok_dev, dtype=jnp.int32)
    all_blocks, all_io = (
        lax.all_gather(layer_blocks.astype(jnp.bfloat16), ("seq", "opt"), axis=0, tiled=True),
        lax.all_gather(io_weights.astype(jnp.bfloat16), ("seq", "opt"), axis=0, tiled=True),
    )
    natural = jnp.zeros_like(all_blocks).at[owners].set(all_blocks)
    upper_mats, lower_mats = assemble(natural)
    tile_count = lax.psum(jnp.sum(tile_mask.astype(jnp.float32)), ("seq", "opt"))
    layer_rows, tail_rows = unpack(vectors)
    token_vec = tail_rows[3 + FEAT // D :].reshape(FEAT)
    head_bias = tail_rows[3 : 3 + FEAT // D].reshape(FEAT)
    inputs = jnp.where(chosen, token_vec[None, :], targets).astype(jnp.bfloat16)
    in_weight = all_io[:, 0]
    head_weight = all_io[:, 1]
    hidden = jnp.dot(inputs, in_weight, preferred_element_type=jnp.float32) + tail_rows[2][None, :]
    hidden = hidden + sine_places(slide_offsets(lengths_row, places))
    layer_id = 0
    hidden, layer_state = layer_forward(
        hidden,
        upper_mats[layer_id],
        lower_mats[layer_id],
        layer_rows[layer_id],
        lengths_row,
        seq_len,
        seq_index,
    )
    layer_states = [layer_state]
    final, final_back = jax.vjp(layer_norm, hidden, tail_rows[0], tail_rows[1])
    final_low = final.astype(jnp.bfloat16)
    predict = contract_cols(final_low, head_weight) + head_bias[None, :]
    difference = predict - targets
    error_local = jnp.sum(jnp.where(chosen, difference * difference, 0.0))
    grad_pred = jnp.where(chosen, 2.0 * difference / tile_count, 0.0).astype(jnp.bfloat16)
    grad_head = contract_rows(grad_pred, final_low)
    grad_head_bias = jnp.sum(grad_pred, axis=0, dtype=jnp.float32)
    grad_final = jnp.dot(grad_pred, head_weight, preferred_element_type=jnp.float32)
    grad_hidden, grad_gain_last, grad_shift_last = final_back(grad_final)
    layer_grads = [None] * LAYERS
    for layer_id in reversed(range(LAYERS)):
        grad_hidden, layer_grads[layer_id] = layer_backward(
            grad_hidden,
            upper_mats[layer_id],
            lower_mats[layer_id],
            layer_rows[layer_id],
            layer_states[layer_id],
            seq_len,
            seq_index,
        )
    grad_in_low = grad_hidden.astype(jnp.bfloat16)
    grad_in = contract_rows(inputs, grad_in_low)
    grad_in_bias = jnp.sum(grad_in_low, axis=0, dtype=jnp.float32)
    grad_inputs = contract_cols(grad_in_low, in_weight)
    grad_token = jnp.sum(jnp.where(chosen, grad_inputs, 0.0), axis=0)
    grad_upper = jnp.stack([item[0] for item in layer_grads])
    grad_lower = jnp.stack([item[1] for item in layer_grads])
    slot_grads = disassemble(grad_upper, grad_lower)[owners]
    io_grads = jnp.stack([grad_in, grad_head], axis=1)
    vec_grads = jnp.concatenate(
        [
            jnp.stack([item[2] for item in layer_grads]).reshape(-1, D),
            jnp.stack([grad_gain_last, grad_shift_last, grad_in_bias]),
            grad_head_bias.reshape(-1, D),
            grad_token.reshape(-1, D),
        ],
        axis=0,
    )
    slot_sum, io_sum = (
        lax.psum_scatter(slot_grads, ("seq", "opt"), scatter_dimension=0, tiled=True),
        lax.psum_scatter(io_grads, ("seq", "opt"), scatter_dimension=0, tiled=True),
    )
    vec_sum, error_sum = lax.psum((vec_grads, error_local), ("seq", "opt"))
    local_sq = jnp.sum(slot_sum * slot_sum) + jnp.sum(io_sum * io_sum)
    grad_norm = jnp.sqrt(lax.psum(local_sq, ("seq", "opt")) + jnp.sum(vec_sum * vec_sum))
    factor = jnp.minimum(1.0, clip_limit / grad_norm)
    block_grads = slot_sum * factor
    left_new = beta_stat * stat_left + (1.0 - beta_stat) * jnp.einsum(
        "kij,klj->kil", block_grads, block_grads, precision=highest
    )
    right_new = beta_stat * stat_right + (1.0 - beta_stat) * jnp.einsum(
        "kji,kjl->kil", block_grads, block_grads, precision=highest
    )
    direction = jnp.einsum("kij,kjl->kil", inverse_root(left_new), block_grads, precision=highest)
    direction = jnp.einsum("kij,kjl->kil", direction, inverse_root(right_new), precision=highest)
    blocks_new = layer_blocks - rate_shampoo * direction
    io_first_new, io_second_new, io_new = adam_update(
        io_weights, io_first, io_second, io_sum * factor, rate_adam, weight_decay
    )
    vec_first_new, vec_second_new, vec_new = adam_update(
        vectors, vec_first, vec_second, vec_sum * factor, rate_vector, 0.0
    )
    return (
        grad_norm,
        error_sum,
        tile_count,
        block_grads,
        left_new,
        right_new,
        blocks_new,
        io_first_new,
        io_second_new,
        io_new,
        vec_first_new,
        vec_second_new,
        vec_new,
    )


BF=jnp.bfloat16; LANE=128; IO=48
def swap(value, axis, mask):
    return lax.ppermute(value, axis, [(s, s ^ mask) for s in range(lax.axis_size(axis))])
def gate(*values):
    return lax.optimization_barrier(values)

GROUP_ROWS=3*BLOCK
IO_AT=2*GROUP_ROWS; COUNT_AT=IO_AT+6*IO; THIRD_AT=COUNT_AT+16
SHARD_HALF=THIRD_AT+GROUP_ROWS
PIECE=8*SHARD_HALF; THIRDS=8*THIRD_AT
def pack_kernel(blocks_ref, io_ref, mask_ref, first_ref, second_ref, both_ref):
    count=jnp.sum(mask_ref[...].astype(jnp.float32),keepdims=True)
    lane=lax.broadcasted_iota(jnp.int32,(BLOCK,LANE),1)
    pad=lambda x: jnp.concatenate([x,jnp.zeros((BLOCK,LANE-BLOCK),x.dtype)],axis=1)
    for h,out_ref in enumerate((first_ref,second_ref)):
        for g in range(3):
            b=[pad(blocks_ref[(h*3+g)*4+t]) for t in range(4)]
            for v in range(3):
                tile=jnp.where(lane<BLOCK,b[v],pltpu.roll(b[3],BLOCK-32*v,1))
                at=(g*GROUP_ROWS if g<2 else THIRD_AT)+v*BLOCK
                out_ref[at:at+BLOCK,:]=tile.astype(BF)
        for v in range(6):
            at=IO_AT+v*IO
            out_ref[at:at+IO,:]=io_ref[:,h,v*LANE:(v+1)*LANE].astype(BF)
        out_ref[COUNT_AT:THIRD_AT,:]=jnp.broadcast_to(count,(16,LANE)).astype(BF)
        both_ref[h*THIRD_AT:(h+1)*THIRD_AT,:]=out_ref[:THIRD_AT,:]
def vmem(): return pl.BlockSpec(memory_space=pltpu.VMEM)
def smem(): return pl.BlockSpec(memory_space=pltpu.SMEM)
def hbm(): return pl.BlockSpec(memory_space=pltpu.HBM)
def from_hbm(body, name, outs, ins, scratch, smem_args=(), late=(), vmem_mib=48, micros=10):
    n_s,n_i,n_o=len(smem_args),len(ins),len(outs)
    def kernel(*refs):
        scalars,args,results=refs[:n_s],refs[n_s:n_s+n_i],refs[n_s+n_i:n_s+n_i+n_o]
        rest=refs[n_s+n_i+n_o:]
        held,made,more=rest[:n_i],rest[n_i:n_i+n_o],rest[n_i+n_o:-2]
        in_sem,out_sem=rest[-2:]
        loads=[pltpu.make_async_copy(a,h,in_sem.at[i]) for i,(a,h) in enumerate(zip(args,held))]
        for c in loads: c.start()
        for i,c in enumerate(loads):
            if i not in late: c.wait()
        body(*([loads[i].wait for i in late]),*scalars,*held,*made,*more)
        stores=[pltpu.make_async_copy(m,r,out_sem.at[i]) for i,(m,r) in enumerate(zip(made,results))]
        for c in stores: c.start()
        for c in stores: c.wait()
    ins=[pltpu.with_memory_space_constraint(a,pltpu.HBM) for a in ins]
    return pl.pallas_call(kernel,out_shape=[pltpu.HBM(s,t) for s,t in outs],
        in_specs=[smem()]*n_s+[hbm()]*n_i,out_specs=[hbm()]*n_o,
        scratch_shapes=[pltpu.VMEM(a.shape,a.dtype) for a in ins]+[pltpu.VMEM(s,t) for s,t in outs]+list(scratch)
            +[pltpu.SemaphoreType.DMA((n_i,)),pltpu.SemaphoreType.DMA((n_o,))],
        compiler_params=pltpu.CompilerParams(vmem_limit_bytes=vmem_mib<<20),
        cost_estimate=pl.CostEstimate(flops=0,transcendentals=0,bytes_accessed=int(micros*3.3e6)),name=name)(*smem_args,*ins)
def pack_shard(blocks, io, mask):
    return pl.pallas_call(pack_kernel,out_shape=[jax.ShapeDtypeStruct((n,LANE),BF) for n in (SHARD_HALF,SHARD_HALF,2*THIRD_AT)],in_specs=[vmem()]*3,out_specs=[vmem()]*3,name="pack_shard")(blocks,io,mask)

HOPS=(("opt",1),("seq",1),("seq",2),("seq",4),("seq",8))
def hop(value, k):
    return value+swap(value,*HOPS[k])

def stack_rows(arrays, *plans):
    n=len(arrays); total=sum(len(p) for p in plans)
    shapes=[(sum(c for _,_,c in p),LANE) for p in plans]
    def kernel(*refs):
        ins,outs,held,(in_sem,out_sem)=refs[:n],refs[n:n+len(plans)],refs[n+len(plans):-2],refs[-2:]
        copies=[]; stores=[]
        for i,plan in enumerate(plans):
            at=0
            for k,first,count in plan:
                copies.append((i,pltpu.make_async_copy(ins[k].at[pl.ds(first,count)],held[i].at[pl.ds(at,count)],in_sem.at[len(copies)])))
                copies[-1][1].start()
                at+=count
        for i,out in enumerate(outs):
            for k,c in copies:
                if k==i: c.wait()
            stores.append(pltpu.make_async_copy(held[i],out,out_sem.at[i]))
            stores[-1].start()
        for c in stores: c.wait()
    return pl.pallas_call(kernel,out_shape=[jax.ShapeDtypeStruct(s,BF) for s in shapes],
        in_specs=[pl.BlockSpec(memory_space=pl.ANY)]*n,out_specs=[pl.BlockSpec(memory_space=pl.ANY)]*len(plans),
        scratch_shapes=[pltpu.VMEM(s,BF) for s in shapes]+[pltpu.SemaphoreType.DMA((total,)),pltpu.SemaphoreType.DMA((len(plans),))],
        compiler_params=pltpu.CompilerParams(vmem_limit_bytes=16<<20),name="stack_rows")(*arrays)

def gather_tree(first, second, both):
    near=[None]*4; cross=[None]*4; third=[None]*4
    def first_step(k,a,b):
        near[k]=(swap(a,"seq",1),swap(b,"seq",2))
    def second_step(k,a,b,rows):
        sent=stack_rows([a[0],near[k][0],b[0],near[k][1]],[(0,a[1],rows),(1,0,rows)],[(2,b[1],rows),(3,0,rows)])
        cross[k]=(swap(sent[0],"seq",2),swap(sent[1],"seq",1))
    def halves_of(far): return (far,0),(far,THIRD_AT)
    far1=swap(both,"seq",4)
    far2=swap(both,"seq",8)
    first_step(0,first,second)
    second_step(0,(first,0),(second,0),SHARD_HALF)
    arrays=[first,second,*near[0],*cross[0]]
    units=[(0,0),(1,0),(2,0),(3,0),(4,0),(4,SHARD_HALF),(5,0),(5,SHARD_HALF)]
    third[0]=stack_rows(arrays,[(k,at+THIRD_AT,GROUP_ROWS) for k,at in units])[0]
    third[2]=swap(third[0],"seq",8)
    third[1]=swap(third[0],"seq",4)
    first_step(1,far1[:THIRD_AT],far1[THIRD_AT:])
    first_step(2,far2[:THIRD_AT],far2[THIRD_AT:])
    far3=swap(far2,"seq",4)
    near[1],near[2],far3=gate(near[1],near[2],far3)
    second_step(1,*halves_of(far1),THIRD_AT)
    first_step(3,far3[:THIRD_AT],far3[THIRD_AT:])
    near[2],near[3]=gate(near[2],near[3])
    second_step(2,*halves_of(far2),THIRD_AT)
    near[3],third[2]=gate(near[3],third[2])
    second_step(3,*halves_of(far3),THIRD_AT)
    third[3]=swap(third[2],"seq",4)
    out=list(stack_rows(arrays+[third[0]],[(k,at,THIRD_AT) for k,at in units]+[(len(arrays),0,third[0].shape[0])]))
    for k,far in ((1,far1),(2,far2),(3,far3)):
        arrays=[far,*near[k],*cross[k],third[k]]
        out+=stack_rows(arrays,[(i,0,part.shape[0]) for i,part in enumerate(arrays)])
    return out+[swap(piece,"opt",1) for piece in out]

HELD=64*SHARD_HALF
N_BLOCK=768
def load_shards(bufs, held, sem, fourths):
    rows=bufs[0].shape[0]
    loads=[pltpu.make_async_copy(b,held.at[pl.ds(k*rows,rows)],sem.at[k]) for k,b in enumerate(bufs)]
    for c in loads: c.start()
    fourths()
    for k,c in enumerate(loads):
        c.wait()
        def unpack(u,carry,k=k):
            for g in range(3):
                at=k*PIECE+(u*THIRD_AT+g*GROUP_ROWS if g<2 else THIRDS+u*GROUP_ROWS)
                parts=[held[pl.ds(pl.multiple_of(at+v*BLOCK,16),BLOCK),BLOCK:] for v in range(3)]
                to=HELD+((k*8+u)*3+g)*BLOCK
                held[pl.ds(pl.multiple_of(to,16),BLOCK),:BLOCK]=jnp.concatenate(parts,axis=1)
            return carry
        lax.fori_loop(0,8,unpack,0,unroll=8)

def join_kernel(plan, io_out, owners_ref, row_ref, io_ref, *refs):
    bufs=refs[:8]; n_out=len(plan); outs=refs[8:8+n_out]; io_ref_out,count_ref=refs[8+n_out:8+n_out+2]
    held,stage,where,in_sem,out_sem,io_sem=refs[8+n_out+2:]
    def invert():
        def one(i,carry):
            for j in range(8):
                where[owners_ref[i*8+j]]=row_ref[i*8+j]
            return carry
        lax.fori_loop(0,N_BLOCK//8,one,0)
    load_shards(bufs,held,in_sem,invert)
    def io_copy(d,total):
        at=io_ref[io_out,d]
        for v in range(6):
            pltpu.make_async_copy(held.at[pl.ds(pl.multiple_of(at+v*IO,16),IO)],
                io_ref_out.at[pl.ds(pl.multiple_of(d*IO,IO),IO),pl.ds(v*LANE,LANE)],io_sem).start()
        return total+held[pl.ds(pl.multiple_of(at+6*IO,16),16),:].astype(jnp.float32)
    count_ref[...]=lax.fori_loop(0,io_ref.shape[1],io_copy,jnp.zeros((16,LANE),jnp.float32))
    def block(n):
        return held[pl.ds(pl.multiple_of(where[n],16),BLOCK),:BLOCK]
    pending=[]; index=0
    for (first,stride,rows,stripes),out in zip(plan,outs):
        per=8//stripes if stripes<8 else 1
        for i0 in range(0,rows,per):
            slot=index%2
            if index>=2:
                for c in pending[index-2]: c.wait()
            for b in range(per):
                def one(c,carry,b=b,i0=i0):
                    n=first+(i0+b)*stride+4*c
                    stage[slot,:,pl.ds(pl.multiple_of((b*stripes+c)*4*BLOCK,128),4*BLOCK)]=jnp.concatenate([block(n+t) for t in range(4)],axis=1)
                    return carry
                lax.fori_loop(0,stripes,one,0,unroll=2 if stripes%4 else 4)
            w=stripes*4*BLOCK
            cs=[pltpu.make_async_copy(stage.at[slot,:,pl.ds(b*w,w)],out.at[pl.ds((i0+b)*BLOCK,BLOCK)],out_sem.at[slot,b]) for b in range(per)]
            for c in cs: c.start()
            pending.append(cs); index+=1
    for cs in pending[-2:]:
        for c in cs: c.wait()
    pltpu.make_async_copy(io_ref_out,io_ref_out,io_sem).wait()

COLS=(4*D+FF)//BLOCK
FIRST_PLAN=((0,COLS,8,6),(24,COLS,8,2))
SECOND_PLAN=((32,COLS,8,8),(8*COLS,8,32,2))
def join_weights(plan, io_out, bufs, owners, rows, io_rows):
    shapes=[(r*BLOCK,s*4*BLOCK) for _,_,r,s in plan]+[(FEAT,D)]
    return pl.pallas_call(partial(join_kernel,plan,io_out),
        out_shape=[pltpu.HBM(s,BF) for s in shapes]+[jax.ShapeDtypeStruct((16,LANE),jnp.float32)],
        in_specs=[smem()]*3+[hbm()]*8, out_specs=[hbm()]*len(shapes)+[vmem()],
        scratch_shapes=[pltpu.VMEM((HELD+N_BLOCK//4*BLOCK,LANE),BF),pltpu.VMEM((2,BLOCK,FF),BF),pltpu.SMEM((N_BLOCK,),jnp.int32),
            pltpu.SemaphoreType.DMA((8,)),pltpu.SemaphoreType.DMA((2,4)),pltpu.SemaphoreType.DMA],
        compiler_params=pltpu.CompilerParams(vmem_limit_bytes=40<<20), cost_estimate=pl.CostEstimate(flops=0,transcendentals=0,bytes_accessed=int((13 if io_out==0 else 17)*3.3e6)), name="join_weights")(owners,rows,io_rows,*[pltpu.with_memory_space_constraint(b,pltpu.HBM) for b in bufs])

def shard_rows(seq_index, core):
    def unit(dev,h):
        rel=(dev//2)^seq_index; xy=rel%4
        u=jnp.where(xy==0,h,jnp.where(h==0,jnp.where(xy==1,2,xy+2),jnp.where(xy==2,3,jnp.where(xy==1,6,7))))
        return (rel//4+4*((dev%2)^core))*8+u
    slot=jnp.arange(N_BLOCK,dtype=jnp.int32); s=slot%24
    u=unit(slot//24,s//12); g=s%12//4; t=s%4
    start=u//8*PIECE+jnp.where(g<2,u%8*THIRD_AT+g*GROUP_ROWS,THIRDS+u%8*GROUP_ROWS)
    rows=jnp.where(t<3,start+t*BLOCK,HELD+(u*3+g)*BLOCK)
    dev=jnp.arange(32,dtype=jnp.int32)
    io=jnp.stack([unit(dev,h)//8*PIECE+unit(dev,h)%8*THIRD_AT+IO_AT for h in (0,1)])
    return rows.astype(jnp.int32),io.astype(jnp.int32)
def gather_shards(layer_blocks, io_weights, mask):
    return gather_tree(*pack_shard(layer_blocks,io_weights,mask))

HD=48; HEADS=16; SLIDES=4; SEG=1024; N=2048; H=512; TQ=256; TK=128
C2=HD**-0.5*math.log2(math.e)
def place_facts(index, head, lengths_ref, core):
    parity=lax.rem(head+(index//H)%2,2)
    pos=(index//SEG)*SEG+2*(index%H)+parity
    slide=jnp.zeros_like(index); end=jnp.int32(0)
    for i in range(SLIDES-1):
        end=end+lengths_ref[core,i]
        slide=slide+jnp.where(pos>=end,1,0)
    d=(pos-head)&15
    level=sum(jnp.where((d&(2**i-1))==0,1,0) for i in range(1,5))
    return slide.astype(jnp.float32), level.astype(jnp.float32)

def arrange(src, dst, odd):
    for pair in range(8):
        first, second = src[2*pair], src[2*pair+1]
        turn=lambda t: jnp.concatenate([t[:,64:],t[:,:64]],axis=1)
        ft, st = turn(first), turn(second)
        low=lax.broadcasted_iota(jnp.int32,first.shape,1)<64
        evens=jnp.where(low,first,st); odds=jnp.where(low,ft,second)
        near=jnp.where(odd,odds,evens); far=jnp.where(odd,evens,odds)
        at=(pair//4)*SEG+(pair%4)*128
        dst[:,at:at+128]=near.astype(dst.dtype); dst[:,at+H:at+H+128]=far.astype(dst.dtype)

def restore(get, put, odd):
    for pair in range(8):
        at=(pair//4)*SEG+(pair%4)*128
        near, far = get(at), get(at+H)
        evens=jnp.where(odd,far,near); odds=jnp.where(odd,near,far)
        turn=lambda t: jnp.concatenate([t[:,64:],t[:,:64]],axis=1)
        low=lax.broadcasted_iota(jnp.int32,evens.shape,1)<64
        put(2*pair, jnp.where(low,evens,turn(odds)))
        put(2*pair+1, jnp.where(low,turn(evens),odds))

def setup(lengths_ref, ids_ref, slide_k, level_k, row_facts):
    head, core = ids_ref[0], ids_ref[1]
    def fill(i, c):
        idx=lax.broadcasted_iota(jnp.int32,(TK,128),0)+i*TK
        s,l=place_facts(idx,head,lengths_ref,core)
        slide_k[pl.ds(pl.multiple_of(i*TK,TK),TK),:]=s
        level_k[pl.ds(pl.multiple_of(i*TK,TK),TK),:]=l
        return c
    lax.fori_loop(0,N//TK,fill,0)
    idx=lax.broadcasted_iota(jnp.int32,(8,N),1)
    s,l=place_facts(idx,head,lengths_ref,core)
    row_facts[0:8,:]=s; row_facts[8:16,:]=l

def key_rows(seg, near):
    own=[(seg*SEG+i*TK,True) for i in range(SEG//TK)]
    other=[((1-seg)*SEG+i*TK,False) for i in range(H//TK)] if near else []
    return own+other

def wide(x): return jnp.concatenate([x]*(TQ//128),axis=1)

def forward_kernel(lengths_ref, ids_ref, qkv_ref, o_ref, out_ref, lse_ref, qkvT, krow, slide_k, level_k, row_facts, s_ref, p_ref):
    odd=lax.rem(ids_ref[0],2)==1
    arrange(qkv_ref, qkvT, odd)
    setup(lengths_ref, ids_ref, slide_k, level_k, row_facts)
    for i in range(N//128):
        krow[i*128:(i+1)*128,:]=qkvT[HD:2*HD,i*128:(i+1)*128].astype(jnp.float32).T.astype(jnp.bfloat16)
    for seg in range(2):
        for near in (True,False):
            tiles=key_rows(seg,near)
            def part(c, carry, seg=seg, near=near, tiles=tiles):
                at=pl.multiple_of(seg*SEG+(0 if near else H)+c*TQ,TQ)
                qT=qkvT[0:HD,pl.ds(at,TQ)]
                sq=row_facts[0:1,pl.ds(at,TQ)]; lq=row_facts[8:9,pl.ds(at,TQ)]
                top=jnp.full((8,TQ),-jnp.inf,jnp.float32)
                for t,(r,own) in enumerate(tiles):
                    s=jnp.dot(krow[r:r+TK,:],qT,preferred_element_type=jnp.float32)
                    s=jnp.where(wide(slide_k[r:r+TK,:])==sq,s,-1e30)
                    s_ref[t*TK:(t+1)*TK,:]=s
                    top=jnp.maximum(top,jnp.max(s.reshape(TK//8,8,TQ),axis=0))
                m=jnp.max(top,axis=0,keepdims=True)
                total=jnp.zeros((8,TQ),jnp.float32)
                for t,(r,own) in enumerate(tiles):
                    e=jnp.exp2((s_ref[t*TK:(t+1)*TK,:]-m)*C2)
                    if near:
                        lk=wide(level_k[r:r+TK,:])
                        e=e*(jnp.minimum(lk,lq)+1.0 if own else jnp.minimum(lk,lq))
                    total=total+jnp.sum(e.reshape(TK//8,8,TQ),axis=0)
                    p_ref[t*TK:(t+1)*TK,:]=e.astype(jnp.bfloat16)
                l=jnp.sum(total,axis=0,keepdims=True)
                acc=jnp.zeros((HD,TQ),jnp.float32)
                acc=jnp.dot(qkvT[2*HD:3*HD,seg*SEG:(seg+1)*SEG],p_ref[0:SEG,:],preferred_element_type=jnp.float32)
                if near:
                    acc=acc+jnp.dot(qkvT[2*HD:3*HD,(1-seg)*SEG:(1-seg)*SEG+H],p_ref[SEG:SEG+H,:],preferred_element_type=jnp.float32)
                o_ref[:,pl.ds(at,TQ)]=acc/l
                lse_ref[:,pl.ds(at,TQ)]=jnp.broadcast_to(m*C2+jnp.log2(l),(8,TQ))
                return carry
            lax.fori_loop(0,H//TQ,part,0)
    def put(c,v): out_ref[c]=v.astype(jnp.bfloat16)
    restore(lambda at: o_ref[:,at:at+128], put, odd)

def backward_kernel(lengths_ref, ids_ref, qkv_ref, do_ref, o_ref, lse_ref, out_ref, qkvT, doT, rows, slide_k, level_k, row_facts, dqT, dkv, p_ref, ds_ref):
    odd=lax.rem(ids_ref[0],2)==1
    arrange(qkv_ref, qkvT, odd)
    arrange(do_ref, doT, odd)
    setup(lengths_ref, ids_ref, slide_k, level_k, row_facts)
    for i in range(N//128):
        l=slice(i*128,(i+1)*128)
        for j in range(3):
            rows[j,l,:]=qkvT[j*HD:(j+1)*HD,l].astype(jnp.float32).T.astype(jnp.bfloat16)
        rows[3,l,:]=doT[:,l].astype(jnp.float32).T.astype(jnp.bfloat16)
    dkv[...]=jnp.zeros_like(dkv)
    for seg in range(2):
        for near in (True,False):
            tiles=key_rows(seg,near)
            def part(c, carry, seg=seg, near=near, tiles=tiles):
                at=pl.multiple_of(seg*SEG+(0 if near else H)+c*TQ,TQ)
                qT=qkvT[0:HD,pl.ds(at,TQ)]; gT=doT[:,pl.ds(at,TQ)]
                q=rows[0,pl.ds(at,TQ),:]; g=rows[3,pl.ds(at,TQ),:]
                sq=row_facts[0:1,pl.ds(at,TQ)]; lq=row_facts[8:9,pl.ds(at,TQ)]
                lse=lse_ref[0:1,pl.ds(at,TQ)]
                inner=jnp.sum(gT.astype(jnp.float32)*o_ref[:,pl.ds(at,TQ)],axis=0,keepdims=True)
                for t,(r,own) in enumerate(tiles):
                    s=jnp.dot(rows[1,r:r+TK,:],qT,preferred_element_type=jnp.float32)
                    dp=jnp.dot(rows[2,r:r+TK,:],gT,preferred_element_type=jnp.float32)
                    e=jnp.exp2(s*C2-lse)
                    if near:
                        lk=wide(level_k[r:r+TK,:])
                        e=e*(jnp.minimum(lk,lq)+1.0 if own else jnp.minimum(lk,lq))
                    e=jnp.where(wide(slide_k[r:r+TK,:])==sq,e,0.0)
                    p_ref[t*TK:(t+1)*TK,:]=e.astype(jnp.bfloat16)
                    ds_ref[t*TK:(t+1)*TK,:]=(e*(dp-inner)).astype(jnp.bfloat16)
                dq=jnp.dot(qkvT[HD:2*HD,seg*SEG:(seg+1)*SEG],ds_ref[0:SEG,:],preferred_element_type=jnp.float32)
                if near:
                    dq=dq+jnp.dot(qkvT[HD:2*HD,(1-seg)*SEG:(1-seg)*SEG+H],ds_ref[SEG:SEG+H,:],preferred_element_type=jnp.float32)
                dqT[:,pl.ds(at,TQ)]=dq*HD**-0.5
                own=slice(seg*SEG,(seg+1)*SEG)
                dkv[0,own,:]+=jnp.dot(ds_ref[0:SEG,:],q,preferred_element_type=jnp.float32)
                dkv[1,own,:]+=jnp.dot(p_ref[0:SEG,:],g,preferred_element_type=jnp.float32)
                if near:
                    oth=slice((1-seg)*SEG,(1-seg)*SEG+H)
                    dkv[0,oth,:]+=jnp.dot(ds_ref[SEG:SEG+H,:],q,preferred_element_type=jnp.float32)
                    dkv[1,oth,:]+=jnp.dot(p_ref[SEG:SEG+H,:],g,preferred_element_type=jnp.float32)
                return carry
            lax.fori_loop(0,H//TQ,part,0)
    def putter(j):
        def put(c,v): out_ref[c,j*HD:(j+1)*HD,:]=v.astype(jnp.bfloat16)
        return put
    restore(lambda at: dqT[:,at:at+128], putter(0), odd)
    restore(lambda at: dkv[0,at:at+128,:].T*HD**-0.5, putter(1), odd)
    restore(lambda at: dkv[1,at:at+128,:].T, putter(2), odd)

def attend(lengths, ids, qkv):
    return from_hbm(forward_kernel,"attend_forward",[((HD,N),F32),((16,HD,128),BF),((8,N),F32)],[qkv],
        [pltpu.VMEM((3*HD,N),BF),pltpu.VMEM((N,HD),BF),pltpu.VMEM((N,128),F32),pltpu.VMEM((N,128),F32),pltpu.VMEM((16,N),F32),
            pltpu.VMEM((SEG+H,TQ),F32),pltpu.VMEM((SEG+H,TQ),BF)],(lengths,ids))
def attend_back(lengths, ids, qkv, do, o, lse):
    return from_hbm(backward_kernel,"attend_backward",[((16,3*HD,128),BF)],[qkv,do,o,lse],
        [pltpu.VMEM((3*HD,N),BF),pltpu.VMEM((HD,N),BF),pltpu.VMEM((4,N,HD),BF),pltpu.VMEM((N,128),F32),pltpu.VMEM((N,128),F32),pltpu.VMEM((16,N),F32),
            pltpu.VMEM((HD,N),F32),pltpu.VMEM((2,N,HD),F32),pltpu.VMEM((SEG+H,TQ),BF),pltpu.VMEM((SEG+H,TQ),BF)],(lengths,ids),micros=13)[0]

F32=jnp.float32
EPS=1e-05
def norm_parts(x):
    centred=x-jnp.mean(x,axis=-1,keepdims=True)
    spread=lax.rsqrt(jnp.mean(centred*centred,axis=-1,keepdims=True)+EPS)
    return centred*spread,spread
def norm_back(grad,unit,spread,gain):
    inner=grad*gain
    back=spread*(inner-jnp.mean(inner,axis=-1,keepdims=True)-unit*jnp.mean(inner*unit,axis=-1,keepdims=True))
    return back,jnp.sum(grad*unit,axis=0,keepdims=True),jnp.sum(grad,axis=0,keepdims=True)
def put_turned(ref,at,x):
    for c in range(x.shape[1]//LANE):
        ref[at+c*LANE:at+(c+1)*LANE,:]=x[:,c*LANE:(c+1)*LANE].astype(F32).T.astype(BF)
def turned(ref,rows):
    return jnp.concatenate([ref[c*LANE:(c+1)*LANE,:].astype(F32).T for c in range(rows//LANE)],axis=1)
def mm(a,b): return jnp.dot(a,b,preferred_element_type=F32)
def mm_t(a,b): return lax.dot_general(a,b,(((1,),(1,)),((),())),preferred_element_type=F32)
LATE_ROWS=4*D+2*FF+FEAT
GELU_A=math.sqrt(2.0/math.pi); GELU_B=0.044715
def mlp_kernel(up_here, down_here, head_here, count_ref, hidden_ref, mixed_ref, targets_ref, chosen_ref, vec_ref, wo_ref, up_ref, down_ref, head_ref,
               middle_grad_ref, mixed_grad_ref, late_ref, rows_ref, kept):
    row=lambda i: vec_ref[i:i+1,:]
    mixed=turned(mixed_ref,D).astype(BF)
    middle=hidden_ref[...]+mm(mixed,wo_ref[...])+row(4)
    unit2,spread2=norm_parts(middle)
    second=(unit2*row(5)+row(6)).astype(BF)
    put_turned(late_ref,0,second)
    result=middle+row(7)
    up_here(); down_here()
    for c in range(FF//D):
        s=slice(c*D,(c+1)*D)
        before=mm(second,up_ref[:,s])+row(8+c)
        kept[:,s]=before
        active=(before*(0.5*(1.0+jnp.tanh(GELU_A*(before+GELU_B*(before*before*before)))))).astype(BF)
        put_turned(late_ref,D+c*D,active)
        result=result+mm(active,down_ref[s,:])
    unit,spread=norm_parts(result)
    final=(unit*row(12)+row(13)).astype(BF)
    put_turned(late_ref,3*D+2*FF+FEAT,final)
    head_here()
    chosen=chosen_ref[...]>0.0
    error=jnp.zeros((1,1),F32); grad_final=jnp.zeros_like(middle)
    for c in range(FEAT//D):
        s=slice(c*D,(c+1)*D)
        difference=mm_t(final,head_ref[s,:])+row(15+c)-targets_ref[:,s].astype(F32)
        error=error+jnp.sum(jnp.where(chosen,difference*difference,0.0),keepdims=True)
        pred=jnp.where(chosen,2.0*difference/count_ref[0],0.0).astype(BF)
        put_turned(late_ref,3*D+2*FF+c*D,pred)
        rows_ref[10+c:11+c,:]=jnp.sum(pred.astype(F32),axis=0,keepdims=True)
        grad_final=grad_final+mm(pred,head_ref[s,:])
    rows_ref[12:13,:]=jnp.broadcast_to(error,(1,D))
    grad_result,rows_ref[8:9,:],rows_ref[9:10,:]=norm_back(grad_final,unit,spread,row(12))
    grad_out=grad_result.astype(BF)
    put_turned(late_ref,2*D+2*FF,grad_out)
    rows_ref[3:4,:]=jnp.sum(grad_out.astype(F32),axis=0,keepdims=True)
    grad_second=jnp.zeros_like(middle)
    for c in range(FF//D):
        s=slice(c*D,(c+1)*D)
        grad_active=mm_t(grad_out,down_ref[s,:])
        x=kept[:,s]
        t=jnp.tanh(GELU_A*(x+GELU_B*(x*x*x)))
        slope=0.5*(1.0+t)+x*(0.5*(1.0-t*t)*(GELU_A*(1.0+3.0*GELU_B*(x*x))))
        grad_before=(grad_active*slope).astype(BF)
        put_turned(late_ref,2*D+FF+c*D,grad_before)
        rows_ref[4+c:5+c,:]=jnp.sum(grad_before.astype(F32),axis=0,keepdims=True)
        grad_second=grad_second+mm_t(grad_before,up_ref[:,s])
    back,rows_ref[1:2,:],rows_ref[2:3,:]=norm_back(grad_second,unit2,spread2,row(5))
    grad_middle=back+grad_result
    middle_grad_ref[...]=grad_middle
    grad_branch=grad_middle.astype(BF)
    put_turned(late_ref,D+FF,grad_branch)
    rows_ref[0:1,:]=jnp.sum(grad_branch.astype(F32),axis=0,keepdims=True)
    mixed_grad_ref[...]=mm_t(wo_ref[...],grad_branch).astype(BF)
    rows_ref[13:16,:]=jnp.zeros((3,D),F32)
def mlp_step(count, hidden, mixed, targets, chosen, vectors, wo, up, down, head):
    t=hidden.shape[0]
    low=lambda rows: ((rows,t),BF)
    return from_hbm(mlp_kernel,"mlp_step",[((t,D),F32),low(D),low(LATE_ROWS),((16,D),F32)],
        [hidden,mixed,targets,chosen,vectors,wo,up,down,head],[pltpu.VMEM((t,FF),F32)],(count.reshape(1),),late=(6,7,8),micros=13)

def input_kernel(in_here, parts_ref, hidden_ref, middle_grad_ref, chosen_ref, vec_ref, rows_ref, qkv_ref, in_ref, last_ref, sums_ref):
    heads,wide,t=parts_ref.shape; hd=wide//3
    for j in range(3):
        for h in range(heads):
            last_ref[j*D+h*hd:j*D+(h+1)*hd,:]=parts_ref[h,j*hd:(j+1)*hd,:]
    packed=last_ref[:3*D,:]
    grad_t=mm(qkv_ref[...],packed)
    grad=jnp.concatenate([grad_t[c*LANE:(c+1)*LANE,:].T for c in range(D//LANE)],axis=1)
    unit,spread=norm_parts(hidden_ref[...])
    back,gain,shift=norm_back(grad,unit,spread,vec_ref[0:1,:])
    grad_hidden=back+middle_grad_ref[...]
    low=grad_hidden.astype(BF)
    put_turned(last_ref,3*D,low)
    sums_ref[0:1,:]=gain; sums_ref[1:2,:]=shift
    ones=jnp.ones((8,t),BF)
    sums_ref[2:3,:]=mm_t(ones,packed[:D])[0:1]
    sums_ref[3:4,:]=mm_t(ones,packed[2*D:])[0:1]
    sums_ref[4:14,:]=rows_ref[0:10,:]
    sums_ref[14:15,:]=jnp.sum(low.astype(F32),axis=0,keepdims=True)
    sums_ref[15:17,:]=rows_ref[10:12,:]
    in_here()
    masked=jnp.where(chosen_ref[...]>0.0,low.astype(F32),0.0).astype(BF)
    for c in range(FEAT//D):
        sums_ref[17+c:18+c,:]=jnp.sum(mm_t(masked,in_ref[c*D:(c+1)*D,:]),axis=0,keepdims=True)
    sums_ref[19:20,:]=rows_ref[12:13,:]
    sums_ref[20:24,:]=jnp.zeros((4,D),F32)
def input_step(parts, hidden, middle_grad, chosen, vectors, rows, qkv, w_in):
    t=hidden.shape[0]
    return from_hbm(input_kernel,"input_step",[((4*D,t),BF),((24,D),F32)],[parts,hidden,middle_grad,chosen,vectors,rows,qkv,w_in],[],late=(7,),micros=5)

def front_kernel(qkv_here, features_ref, chosen_ref, places_ref, vec_ref, in_ref, qkv_ref, hidden_ref, early_ref, heads_ref, turned_ref):
    row=lambda i: vec_ref[i:i+1,:]
    chosen=chosen_ref[...]>0.0
    hidden=places_ref[...]+row(14)
    for c in range(FEAT//D):
        s=slice(c*D,(c+1)*D)
        part=jnp.where(chosen,row(17+c),features_ref[:,s].astype(F32)).astype(BF)
        put_turned(early_ref,D+c*D,part)
        hidden=hidden+mm(part,in_ref[s,:])
    hidden_ref[...]=hidden
    unit,spread=norm_parts(hidden)
    normed=(unit*row(0)+row(1)).astype(BF)
    put_turned(early_ref,0,normed)
    qkv_here()
    heads,wide,t=heads_ref.shape; hd=wide//3
    for j in range(3):
        out=mm(normed,qkv_ref[:,j*D:(j+1)*D])
        if j!=1: out=out+row(2 if j==0 else 3)
        put_turned(turned_ref,j*D,out.astype(BF))
        for h in range(heads):
            heads_ref[h,j*hd:(j+1)*hd,:]=turned_ref[j*D+h*hd:j*D+(h+1)*hd,:]
def front_step(features, chosen, places, vectors, w_in, qkv, heads):
    t=features.shape[0]
    return from_hbm(front_kernel,"front_step",[((t,D),F32),((D+FEAT,t),BF),((heads,3*D//heads,t),BF)],[features,chosen,places,vectors,w_in,qkv],
        [pltpu.VMEM((3*D,t),BF)],late=(5,),micros=5)

I16=jnp.int16; F32=jnp.float32; BF=jnp.bfloat16
GROUP=48; LANE=128; IO=48
STEP_Q=32000.0
UNITS=24; CODE_ROWS=32; PART=UNITS*GROUP+CODE_ROWS
A_ROWS=3*D+FF; X_ROWS=3*D+D+FF+D
ROUND=12582912.0

def encode(x):
    top=jnp.max(jnp.abs(x),axis=0,keepdims=True)
    code=jnp.ceil(jnp.log2(jnp.maximum(top,1e-30))*256.0)
    v=x*(STEP_Q*jnp.exp2(code*(-1.0/256.0)))
    return ((v+ROUND)-ROUND).astype(jnp.int32).astype(I16), code
def scale_of(code16):
    return jnp.exp2(code16.astype(jnp.int32).astype(F32)*(1.0/256.0))*(1.0/STEP_Q)
def pack_codes(codes):
    codes=codes+[jnp.zeros((CODE_ROWS-len(codes),LANE),F32)]
    return jnp.concatenate(codes,axis=0).astype(jnp.int32).astype(I16)

EARLY,MIXED,LATE,LAST=range(4)
PARTS=(((EARLY,0,D),("a",0)),((MIXED,0,D),("a",D)),((LATE,0,D),("a",2*D)),((LATE,D,FF),("a",3*D)),
    ((LAST,0,3*D),("x",0)),((LATE,D+FF,D),("x",3*D)),((LATE,2*D+FF,FF),("x",4*D)),((LATE,2*D+2*FF,D),("x",4*D+FF)),
    ((EARLY,D,FEAT),("a_in",0)),((LAST,3*D,D),("x_in",0)),((LATE,3*D+2*FF,FEAT),("a_head",0)),((LATE,3*D+2*FF+FEAT,D),("x_head",0)))
def grads_kernel(zone, ids_ref, owners_ref, *refs):
    operands=refs[:8]; outs=refs[8:12]
    a_all,x_all,a_in,x_in,a_head,x_head,sem=refs[12:]
    buf_of=dict(a=a_all,x=x_all,a_in=a_in,x_in=x_in,a_head=a_head,x_head=x_head)
    seq,core=ids_ref[0],ids_ref[1]
    copies=[]
    for (source,first,count),(buf,at) in PARTS:
        for side in range(2):
            c=pltpu.make_async_copy(operands[2*source+side].at[pl.ds(first,count)],buf_of[buf].at[pl.ds(at,count),pl.ds(side*LANE,LANE)],sem.at[len(copies)])
            c.start(); copies.append(c)
    for c in copies: c.wait()
    lane=lax.broadcasted_iota(jnp.int32,(BLOCK,LANE),1)
    cols=(4*D+FF)//BLOCK; wide_count=D//BLOCK*cols
    def block(slot):
        n=owners_ref[slot]
        i=n//cols; j=n%cols
        m=n-wide_count
        group=jnp.where(j>=3*D//BLOCK,1,0)+jnp.where(j>=4*D//BLOCK,1,0)
        a_at=jnp.where(m<0,i*BLOCK+group*D,3*D+m//(D//BLOCK)*BLOCK)
        x_at=jnp.where(m<0,j*BLOCK,4*D+FF+m%(D//BLOCK)*BLOCK)
        a=a_all[pl.ds(pl.multiple_of(a_at,32),BLOCK),:]
        x=x_all[pl.ds(pl.multiple_of(x_at,32),BLOCK),:]
        w=lax.dot_general(a,x,(((1,),(1,)),((),())),preferred_element_type=F32)
        return jnp.concatenate([w,jnp.zeros((BLOCK,LANE-BLOCK),F32)],axis=1)
    for out,h,first,step in ((outs[0],0,2,1),(outs[2],1,1,2),(outs[1],0,0,1),(outs[3],1,0,2)):
        def one(j,carry,out=out,h=h,first=first,step=step):
            device=2*jnp.bitwise_xor(seq,zone*4+first+step*j)+core
            codes=[]
            for g in range(3):
                w=[block(device*24+(h*3+g)*4+t) for t in range(4)]
                for v in range(3):
                    tile=jnp.where(lane<BLOCK,w[v],pltpu.roll(w[3],BLOCK-32*v,1))
                    for half in range(2):
                        q,code=encode(tile[half*GROUP:(half+1)*GROUP])
                        at=((g*3+v)*2+half)*GROUP
                        out[j,at:at+GROUP,:]=q; codes.append(code)
            a_ref,x_ref=((a_in,x_in),(a_head,x_head))[h]
            w=lax.dot_general(a_ref[pl.ds(pl.multiple_of(device*IO,16),IO),:],x_ref[...],(((1,),(1,)),((),())),preferred_element_type=F32)
            for v in range(6):
                q,code=encode(w[:,v*LANE:(v+1)*LANE])
                at=(18+v)*GROUP
                out[j,at:at+GROUP,:]=q; codes.append(code)
            out[j,UNITS*GROUP:,:]=pack_codes(codes)
            return carry
        lax.fori_loop(0,2,one,0)

def weight_grads(zone, ids, owners, operands):
    n=len(operands)
    return pl.pallas_call(partial(grads_kernel,zone),
        out_shape=[jax.ShapeDtypeStruct((2,PART,LANE),I16)]*4,
        in_specs=[pl.BlockSpec(memory_space=pltpu.SMEM)]*2+[pl.BlockSpec(memory_space=pl.ANY)]*n,
        out_specs=[pl.BlockSpec(memory_space=pltpu.VMEM)]*4,
        scratch_shapes=[pltpu.VMEM((A_ROWS,2*LANE),BF),pltpu.VMEM((X_ROWS,2*LANE),BF),pltpu.VMEM((FEAT,2*LANE),BF),pltpu.VMEM((D,2*LANE),BF),
            pltpu.VMEM((FEAT,2*LANE),BF),pltpu.VMEM((D,2*LANE),BF),pltpu.SemaphoreType.DMA((2*len(PARTS),))],
        compiler_params=pltpu.CompilerParams(vmem_limit_bytes=40<<20), cost_estimate=takes(0.8), name="weight_grads")(ids,owners,*operands)

class At:
    def __init__(s,ref,*i): s.ref,s.i=ref,i
    def __getitem__(s,k): return s.ref[(*s.i,k,slice(None))]
    def __setitem__(s,k,v): s.ref[(*s.i,k,slice(None))]=v
def summed(views):
    scales=[scale_of(v[UNITS*GROUP:PART]) for v in views]
    for k in range(UNITS):
        total=None
        for v,s in zip(views,scales):
            x=v[k*GROUP:(k+1)*GROUP].astype(jnp.int32).astype(F32)*s[k:k+1,:]
            total=x if total is None else total+x
        yield k,total
def add_codes(views, out):
    codes=[]
    for k,total in summed(views):
        q,code=encode(total)
        out[k*GROUP:(k+1)*GROUP]=q
        codes.append(code)
    out[UNITS*GROUP:PART]=pack_codes(codes)
def takes(micros):
    return pl.CostEstimate(flops=0,transcendentals=0,bytes_accessed=int(micros*3.3e6))
def code_call(kernel, name, outs, *args):
    return pl.pallas_call(kernel, out_shape=[jax.ShapeDtypeStruct(s,t) for s,t in outs],
        in_specs=[pl.BlockSpec(memory_space=pltpu.VMEM)]*len(args), out_specs=[pl.BlockSpec(memory_space=pltpu.VMEM)]*len(outs),
        compiler_params=pltpu.CompilerParams(vmem_limit_bytes=32<<20), cost_estimate=takes(0.15), name=name)(*args)
def plane_kernel(*refs):
    n=len(refs)//2
    for i in range(0,n,2):
        (keep,got),(send,stay)=refs[i:i+2],refs[n+i:n+i+2]
        add_codes([At(keep,1),At(got,1)],At(send))
        add_codes([At(keep,0),At(got,0)],At(stay))
def line_kernel(*refs):
    stay_a,got_a,stay_b,got_b=refs[:4]; more=refs[4:-1]; out=refs[-1]
    for h,(stay,got) in enumerate(((stay_a,got_a),(stay_b,got_b))):
        add_codes([At(stay),At(got)]+[At(m,h) for m in more],At(out,h))
def final_kernel(*refs):
    stay_a,got_a,stay_b,got_b=refs[:4]; more=refs[4:-4]; vec,blocks,io,sums=refs[-4:]
    square=jnp.zeros((1,LANE),F32)
    for h,(stay,got) in enumerate(((stay_a,got_a),(stay_b,got_b))):
        for k,total in summed([At(stay),At(got)]+[At(m,h) for m in more]):
            square=square+jnp.sum(total*total,axis=0,keepdims=True)
            if k<18:
                g,v,half=k//6,k//2%3,k%2
                rows=slice(half*GROUP,(half+1)*GROUP)
                blocks[(h*3+g)*4+v,rows,:]=total[:,:BLOCK]
                blocks[(h*3+g)*4+3,rows,32*v:32*(v+1)]=total[:,BLOCK:]
            else:
                io[:,h,(k-18)*LANE:(k-17)*LANE]=total
    sums[0:23,:]=vec[0:23,:]
    sums[23:24,:]=jnp.broadcast_to(jnp.sum(square,keepdims=True),(1,D))
HALF=(PART,LANE)
def reduce_tree(ids, owners, operands, vec):
    send={}; keep={}; got={}; stay={}; far={}
    def make(k):
        send_a,keep_a,send_b,keep_b=weight_grads(k,ids,owners,operands)
        send[k]=(send_a,send_b); keep[k]=(keep_a,keep_b)
    def leave(k,*masks):
        got[k]=tuple(swap(part,"seq",mask) for part,mask in zip(send[k],masks))
    def plane(*pieces):
        outs=code_call(plane_kernel,"add_plane",[(HALF,I16)]*4*len(pieces),*[ref for k in pieces for ref in (keep[k][0],got[k][0],keep[k][1],got[k][1])])
        for i,k in enumerate(pieces):
            send_a,stay_a,send_b,stay_b=outs[4*i:4*i+4]
            stay[k]=(stay_a,stay_b); send[k]=(send_a,send_b)
            leave(k,1,2)
    def line(k,mask,*more):
        far[k]=swap(code_call(line_kernel,"add_line",[((2,)+HALF,I16)],stay[k][0],got[k][0],stay[k][1],got[k][1],*more)[0],"seq",mask)
    make(3); leave(3,2,1)
    make(2); leave(2,2,1)
    make(1)
    (got[3],got[2]),keep[1]=gate((got[3],got[2]),keep[1])
    plane(3,2)
    (send[1],ids),got[3],got[2]=gate((send[1],ids),got[3],got[2])
    line(3,4)
    leave(1,2,1)
    make(0)
    got[1],far[3],keep[0]=gate(got[1],far[3],keep[0])
    line(2,8,far[3])
    plane(1)
    line(1,4)
    send[0],got[1]=gate(send[0],got[1])
    leave(0,2,1)
    plane(0)
    return code_call(final_kernel,"add_final",[((24,BLOCK,BLOCK),F32),((IO,2,D),F32),((24,D),F32)],stay[0][0],got[0][0],stay[0][1],got[0][1],far[1],far[2],vec)

BLOCK=96; NEWTON=6; F32=jnp.float32; BF=jnp.bfloat16; LANE=128
def halves(x):
    hi=x.astype(BF); return hi,(x-hi.astype(F32)).astype(BF)
def left_of(parts):
    return jnp.concatenate(parts,axis=1)
def right_of(parts):
    hi,lo=parts
    rest=jnp.zeros((LANE-BLOCK,LANE),BF)
    top=jnp.concatenate([hi,lo],axis=1); low=jnp.concatenate([hi,jnp.zeros_like(lo)],axis=1)
    both=jnp.zeros((LANE-BLOCK,2*LANE),BF)
    return jnp.concatenate([top,both,low,both],axis=0)
def times(a,b):
    w=jnp.dot(left_of(a),right_of(b),preferred_element_type=F32)
    return w[:,:LANE]+w[:,LANE:]
def shampoo_kernel(sums_ref, grad_ref, left_ref, right_ref, block_ref, io_grad_ref, io_ref, io_first_ref, io_second_ref, vec_ref, vec_first_ref, vec_second_ref,
                   grad_out, left_out, right_out, block_out, io_first_out, io_second_out, io_out, vec_first_out, vec_second_out, vec_out, norm_out, *, beta, rate, eps, n_side):
    n_vec=vec_ref.shape[0]
    vec_grad=sums_ref[0:n_vec,:]
    norm=jnp.sqrt(sums_ref[23:24,0:1]+jnp.sum(vec_grad*vec_grad,keepdims=True))
    norm_out[...]=jnp.broadcast_to(norm,norm_out.shape)
    factor=jnp.minimum(1.0,clip_limit/norm)
    vec_first_out[...],vec_second_out[...],vec_out[...]=adam_update(vec_ref[...],vec_first_ref[...],vec_second_ref[...],vec_grad*factor,rate_vector,0.0)
    for m in range(2):
        parts=[ref[:,m,:] for ref in (io_ref,io_first_ref,io_second_ref,io_grad_ref)]
        io_first_out[:,m,:],io_second_out[:,m,:],io_out[:,m,:]=adam_update(*parts[:3],parts[3]*factor,rate_adam,weight_decay)
    row=lax.broadcasted_iota(jnp.int32,(BLOCK,LANE),0); col=lax.broadcasted_iota(jnp.int32,(BLOCK,LANE),1)
    eye=jnp.where(row==col,1.0,0.0)
    none=jnp.zeros((BLOCK,LANE-BLOCK),F32)
    def full(x): return jnp.concatenate([x,none],axis=1)
    def one(i,carry):
        stats=[]; grads=[]
        for j in range(n_side):
            s=i*n_side+j
            g=full(grad_ref[s]*factor)
            grad_out[s]=g[:,:BLOCK]
            g=halves(g); t=halves(full((grad_ref[s]*factor).T)); grads.append(g)
            l=beta*full(left_ref[s])+(1.0-beta)*times(g,t)
            r=beta*full(right_ref[s])+(1.0-beta)*times(t,g)
            left_out[s]=l[:,:BLOCK]; right_out[s]=r[:,:BLOCK]
            stats+=[l,r]
        regular=[m+eps*eye for m in stats]
        scaled=[2.5*lax.rsqrt(jnp.sum(m*m,keepdims=True)) for m in regular]
        moving=[m*s for m,s in zip(regular,scaled)]
        root=None
        for sweep in range(NEWTON):
            factors=[1.25*eye-0.25*m for m in moving]
            split=[halves(f) for f in factors]
            if sweep==0: root=[f*jnp.sqrt(jnp.sqrt(s)) for f,s in zip(factors,scaled)]
            else: root=[times(halves(x),f) for x,f in zip(root,split)]
            if sweep<NEWTON-1:
                square=[halves(times(f,f)) for f in split]
                fourth=[halves(times(q,q)) for q in square]
                moving=[times(q,halves(m)) for q,m in zip(fourth,moving)]
        for j in range(n_side):
            s=i*n_side+j
            d=times(halves(root[2*j]),grads[j])
            d=times(halves(d),halves(root[2*j+1]))
            block_out[s]=block_ref[s]-rate*d[:,:BLOCK]
        return carry
    lax.fori_loop(0,grad_ref.shape[0]//n_side,one,0)
def update_step(sums, grads, left, right, blocks, io_grad, io_set, vec_set, n_side=12):
    like=lambda *xs: [jax.ShapeDtypeStruct(x.shape,F32) for x in xs]
    args=(sums,grads,left,right,blocks,io_grad,*io_set,*vec_set)
    return pl.pallas_call(partial(shampoo_kernel,beta=beta_stat,rate=rate_shampoo,eps=root_eps,n_side=n_side),
        out_shape=like(grads,grads,grads,grads,*io_set,*vec_set)+[jax.ShapeDtypeStruct((8,LANE),F32)],
        in_specs=[vmem()]*len(args),out_specs=[vmem()]*11,
        compiler_params=pltpu.CompilerParams(vmem_limit_bytes=48<<20),name="update_step")(*args)


def fits(mesh):
    return mesh.shape["seq"] == 16 and mesh.shape["opt"] == 2


def sum_everywhere(value):
    value = value + swap(value, "opt", 1)
    for bit in range((lax.axis_size("seq") - 1).bit_length()):
        value = value + swap(value, "seq", 2**bit)
    return value


def to_heads(parts):
    return lax.all_to_all(parts, "seq", 0, 0, tiled=True)


def evens_first(rows):
    return rows.reshape((rows.shape[0] // 2, 2) + rows.shape[1:]).swapaxes(0, 1).reshape(rows.shape)


def fast_device(
    features,
    tile_mask,
    lengths,
    owners,
    layer_blocks,
    stat_left,
    stat_right,
    io_weights,
    io_first,
    io_second,
    vectors,
    vec_first,
    vec_second,
):
    tok_dev = features.shape[1]
    seq_index = lax.axis_index("seq")
    core_index = lax.axis_index("opt")
    ids = jnp.stack([seq_index, core_index]).astype(jnp.int32)
    low_targets = evens_first(features[0])
    chosen_rows = evens_first(tile_mask[0]).astype(jnp.float32)[:, None]
    lengths_row = lax.dynamic_index_in_dim(lengths, core_index, 0, keepdims=False)
    places = seq_index * tok_dev + evens_first(jnp.arange(tok_dev, dtype=jnp.int32))
    shards = gather_shards(layer_blocks, io_weights, tile_mask)
    block_rows, io_rows = shard_rows(seq_index, core_index)
    qkv_weight, out_weight, in_weight, tile_counts = join_weights(
        FIRST_PLAN, 0, shards, owners, block_rows, io_rows
    )
    tile_count = tile_counts[0, 0]
    hidden, early_low, by_head = front_step(
        low_targets,
        chosen_rows,
        sine_places(slide_offsets(lengths_row, places)),
        vectors,
        in_weight,
        qkv_weight,
        HEADS,
    )
    late_owners, by_head = gate(owners, by_head)
    up_weight, down_weight, head_weight, late_counts = join_weights(
        SECOND_PLAN, 1, shards, late_owners, block_rows, io_rows
    )
    own_head, head_weight = gate(to_heads(by_head), head_weight)
    head_out, mixed_parts, head_totals = attend(lengths, ids, own_head)
    mixed_low = to_heads(mixed_parts).reshape(D, tok_dev)
    grad_middle, grad_mixed, late_low, late_rows = mlp_step(
        tile_count,
        hidden,
        mixed_low,
        low_targets,
        chosen_rows,
        vectors,
        out_weight,
        up_weight,
        down_weight,
        head_weight,
    )
    grad_head_out = to_heads(grad_mixed.reshape(HEADS, HEAD_DIM, tok_dev))
    grad_parts = attend_back(lengths, ids, own_head, grad_head_out, head_out, head_totals)
    others = [swap(operand, "opt", 1) for operand in (early_low, mixed_low, late_low)]
    own_parts, others[0], others[1] = gate(to_heads(grad_parts), others[0], others[1])
    last_low, vec_grads = input_step(
        own_parts,
        hidden,
        grad_middle,
        chosen_rows,
        vectors,
        late_rows,
        qkv_weight,
        in_weight,
    )
    others.append(swap(last_low, "opt", 1))
    operands = []
    for pair in zip((early_low, mixed_low, late_low, last_low), others):
        operands += pair
    slot_sum, io_sum, own_sums = reduce_tree(ids, owners, operands, vec_grads)
    all_sums = sum_everywhere(own_sums)
    (
        block_grads,
        left_new,
        right_new,
        blocks_new,
        io_first_new,
        io_second_new,
        io_new,
        vec_first_new,
        vec_second_new,
        vec_new,
        norms,
    ) = update_step(
        all_sums,
        slot_sum,
        stat_left,
        stat_right,
        layer_blocks,
        io_sum,
        (io_weights, io_first, io_second),
        (vectors, vec_first, vec_second),
    )
    grad_norm = norms[0, 0]
    error_sum = all_sums[vectors.shape[0], 0]
    return (
        grad_norm,
        error_sum,
        tile_count,
        block_grads,
        left_new,
        right_new,
        blocks_new,
        io_first_new,
        io_second_new,
        io_new,
        vec_first_new,
        vec_second_new,
        vec_new,
    )


def solution(mesh):
    return jax.shard_map(
        fast_device if fits(mesh) else per_device,
        mesh=mesh,
        in_specs=(
            P("opt", "seq", None),
            P("opt", "seq"),
            P(),
            P(),
            P(("seq", "opt"), None, None),
            P(("seq", "opt"), None, None),
            P(("seq", "opt"), None, None),
            P(("seq", "opt"), None, None),
            P(("seq", "opt"), None, None),
            P(("seq", "opt"), None, None),
            P(),
            P(),
            P(),
        ),
        out_specs=(
            P(),
            P(),
            P(),
            P(("seq", "opt"), None, None),
            P(("seq", "opt"), None, None),
            P(("seq", "opt"), None, None),
            P(("seq", "opt"), None, None),
            P(("seq", "opt"), None, None),
            P(("seq", "opt"), None, None),
            P(("seq", "opt"), None, None),
            P(),
            P(),
            P(),
        ),
        check_vma=False,
    )
```

```python
from functools import partial
import math

import jax
import jax.numpy as jnp
import numpy as np
from jax import lax
from jax.experimental import pallas as pl
from jax.experimental.pallas import tpu as pltpu
from jax.sharding import PartitionSpec as P

D = 768
HEADS = 16
HEAD_DIM = 48
FF = 3072
FEAT = 1536
LAYERS = 1
BRANCHES = 5
SEG0 = 1024
BLOCK = 96
SLIDES = 4
NEWTON = 6
STEP = 10


norm_eps = 1e-05
clip_limit = 1.0
beta_one = 0.9
beta_two = 0.95
adam_eps = 1e-08
rate_adam = 0.01
rate_vector = 0.2
weight_decay = 0.05
beta_stat = 0.95
rate_shampoo = 0.05
root_eps = 1e-12
masked_score = -1e30
highest = lax.Precision.HIGHEST


def from_partner(value, axis, stride):
    mask = 2**stride
    pairs = [(source, source ^ mask) for source in range(lax.axis_size(axis))]
    return lax.ppermute(value, axis, pairs)


def for_sending(shard):

    def short(part):
        return part.astype(jnp.bfloat16) if part.dtype == jnp.float32 else part

    return jax.tree.map(short, shard)


def layer_norm(values, gain, shift):
    centred = values - jnp.mean(values, axis=-1, keepdims=True)
    spread = jnp.mean(centred * centred, axis=-1, keepdims=True)
    return centred * lax.rsqrt(spread + norm_eps) * gain + shift


def sine_places(places):
    half_width = D // 2
    freq_rates = jnp.exp(
        jnp.arange(half_width, dtype=jnp.float32) * (-math.log(10000.0) / half_width)
    )
    angles = (places.astype(jnp.float32) / 64.0)[:, None] * freq_rates[None, :]
    return jnp.concatenate([jnp.sin(angles), jnp.cos(angles)], axis=1)


def slide_ids(lengths_row, places):
    slide_ends = jnp.cumsum(lengths_row)
    return jnp.sum((places[..., None] >= slide_ends[:-1]).astype(jnp.int32), axis=-1)


def slide_offsets(lengths_row, places):
    slide_ends = jnp.cumsum(lengths_row)
    slide_starts = slide_ends - lengths_row
    owner_ids = slide_ids(lengths_row, places)
    match_rows = owner_ids[:, None] == jnp.arange(SLIDES, dtype=jnp.int32)[None, :]
    picked = jnp.sum(jnp.where(match_rows, slide_starts[None, :], 0), axis=1)
    return places - picked


def head_offsets(dilation):
    return np.arange(HEADS) % dilation


def pick_rows(values, dilation):
    row_count = values.shape[0] // dilation
    shaped = values.reshape((row_count, dilation) + values.shape[1:])
    return shaped[:, head_offsets(dilation), np.arange(HEADS)]


def spread_rows(values, dilation, filler):
    row_count = values.shape[0]
    hit_mask = np.arange(dilation)[:, None] == head_offsets(dilation)[None, :]
    hit_mask = hit_mask.reshape((1, dilation, HEADS) + (1,) * (values.ndim - 2))
    spread_out = jnp.where(hit_mask, values[:, None], filler)
    return spread_out.reshape((row_count * dilation,) + values.shape[1:])


def branch_geom(branch, tok_dev, seq_len):
    dilation = 2**branch
    segment = min(SEG0 * dilation, seq_len)
    return (dilation, segment, max(1, segment // tok_dev))


def branch_docs(lengths_row, first_place, row_count, dilation):
    places = (
        first_place
        + jnp.asarray(head_offsets(dilation), jnp.int32)[None, :]
        + dilation * jnp.arange(row_count, dtype=jnp.int32)[:, None]
    )
    return slide_ids(lengths_row, places)


def contract_rows(left, right):
    return lax.dot_general(
        left, right, (((0,), (0,)), ((), ())), preferred_element_type=jnp.float32
    )


def contract_cols(left, right):
    return lax.dot_general(
        left, right, (((1,), (1,)), ((), ())), preferred_element_type=jnp.float32
    )


def assemble(natural):
    per_layer = natural.reshape(LAYERS, -1, BLOCK, BLOCK)
    col_count = (4 * D + FF) // BLOCK
    wide_count = D // BLOCK * col_count
    upper_mats = per_layer[:, :wide_count].reshape(LAYERS, D // BLOCK, col_count, BLOCK, BLOCK)
    upper_mats = upper_mats.transpose(0, 1, 3, 2, 4).reshape(LAYERS, D, 4 * D + FF)
    lower_mats = per_layer[:, wide_count:].reshape(LAYERS, FF // BLOCK, D // BLOCK, BLOCK, BLOCK)
    lower_mats = lower_mats.transpose(0, 1, 3, 2, 4).reshape(LAYERS, FF, D)
    return (upper_mats, lower_mats)


def disassemble(upper_mats, lower_mats):
    col_count = (4 * D + FF) // BLOCK
    top_part = upper_mats.reshape(LAYERS, D // BLOCK, BLOCK, col_count, BLOCK).transpose(
        0, 1, 3, 2, 4
    )
    top_part = top_part.reshape(LAYERS, -1, BLOCK, BLOCK)
    bottom_part = lower_mats.reshape(LAYERS, FF // BLOCK, BLOCK, D // BLOCK, BLOCK).transpose(
        0, 1, 3, 2, 4
    )
    bottom_part = bottom_part.reshape(LAYERS, -1, BLOCK, BLOCK)
    return jnp.concatenate([top_part, bottom_part], axis=1).reshape(-1, BLOCK, BLOCK)


def unpack(vector_set):
    per_layer = 8 + FF // D
    return (
        vector_set[: LAYERS * per_layer].reshape(LAYERS, per_layer, D),
        vector_set[LAYERS * per_layer :],
    )


def collect_pairs(pieces, bit_counts, seq_index):
    pieces = list(pieces)
    for bit_id in range(max(bit_counts + [0])):
        active_ids = [branch for branch in range(len(pieces)) if bit_counts[branch] > bit_id]
        outgoing = jnp.concatenate([pieces[branch] for branch in active_ids], axis=0)
        partner = from_partner(outgoing, "seq", bit_id)
        lower_side = seq_index // 2**bit_id % 2 == 0
        offset_at = 0
        for branch in active_ids:
            my_part = pieces[branch]
            part_size = my_part.shape[0]
            their_part = partner[offset_at : offset_at + part_size]
            offset_at = offset_at + part_size
            pieces[branch] = jnp.where(
                lower_side,
                jnp.concatenate([my_part, their_part], 0),
                jnp.concatenate([their_part, my_part], 0),
            )
    return pieces


def return_pairs(pieces, bit_counts, seq_index):
    pieces = list(pieces)
    for bit_id in reversed(range(max(bit_counts + [0]))):
        active_ids = [branch for branch in range(len(pieces)) if bit_counts[branch] > bit_id]
        lower_side = seq_index // 2**bit_id % 2 == 0
        kept_parts, sent_parts = ([], [])
        for branch in active_ids:
            half_size = pieces[branch].shape[0] // 2
            first_part = pieces[branch][:half_size]
            second_part = pieces[branch][half_size:]
            kept_parts.append(jnp.where(lower_side, first_part, second_part))
            sent_parts.append(jnp.where(lower_side, second_part, first_part))
        partner = from_partner(for_sending(jnp.concatenate(sent_parts, axis=0)), "seq", bit_id)
        offset_at = 0
        for branch, kept_part in zip(active_ids, kept_parts):
            part_size = kept_part.shape[0]
            pieces[branch] = kept_part + partner[offset_at : offset_at + part_size]
            offset_at = offset_at + part_size
    return pieces


def score_block(query_rows, key_rows, query_docs, key_docs):
    raw_scores = jnp.einsum(
        "sqhd,skhd->shqk", query_rows, key_rows, preferred_element_type=jnp.float32
    ) * HEAD_DIM ** (-0.5)
    same_slide = (
        jnp.transpose(query_docs, (0, 2, 1))[..., None]
        == jnp.transpose(key_docs, (0, 2, 1))[:, :, None, :]
    )
    return jnp.where(same_slide, raw_scores, masked_score)


def attend_forward(packed, lengths_row, seq_len, seq_index):
    tok_dev = packed.shape[0]
    triple = packed.reshape(tok_dev, 3, HEADS, HEAD_DIM)
    queries, key_all, value_all = (triple[:, 0], triple[:, 1], triple[:, 2])
    geoms = [branch_geom(branch, tok_dev, seq_len) for branch in range(BRANCHES)]
    local_pairs = [
        jnp.stack([pick_rows(key_all, geom[0]), pick_rows(value_all, geom[0])], axis=1).reshape(
            -1, 2 * D
        )
        for geom in geoms
    ]
    bit_counts = [geom[2].bit_length() - 1 for geom in geoms]
    joined = collect_pairs(local_pairs, bit_counts, seq_index)
    kept_state, outputs, totals_all = ([], [], [])
    for branch in range(BRANCHES):
        dilation, segment, group_size = geoms[branch]
        sections = max(1, tok_dev // segment)
        query_rows = pick_rows(queries, dilation).reshape(sections, -1, HEADS, HEAD_DIM)
        pair_rows = joined[branch].reshape(sections, -1, 2, HEADS, HEAD_DIM)
        key_rows = pair_rows[:, :, 0]
        value_rows = pair_rows[:, :, 1]
        query_docs = branch_docs(
            lengths_row, seq_index * tok_dev, tok_dev // dilation, dilation
        ).reshape(sections, -1, HEADS)
        group_first = seq_index // group_size * group_size * tok_dev
        key_docs = branch_docs(lengths_row, group_first, joined[branch].shape[0], dilation).reshape(
            sections, -1, HEADS
        )
        scores = score_block(query_rows, key_rows, query_docs, key_docs)
        totals = jax.nn.logsumexp(scores, axis=-1)
        softmax_rows = jnp.exp(scores - totals[..., None]).astype(jnp.bfloat16)
        output = jnp.einsum(
            "shqk,skhd->sqhd", softmax_rows, value_rows, preferred_element_type=jnp.float32
        ).reshape(-1, HEADS, HEAD_DIM)
        totals_rows = jnp.transpose(totals, (0, 2, 1)).reshape(-1, HEADS)
        kept_state.append(
            (query_rows, key_rows, value_rows, query_docs, key_docs, output, totals_rows)
        )
        outputs.append(spread_rows(output, dilation, 0.0))
        totals_all.append(spread_rows(totals_rows, dilation, masked_score))
    stacked = jnp.stack(totals_all)
    grand_total = jax.nn.logsumexp(stacked, axis=0)
    mixed_out = jnp.zeros_like(outputs[0])
    for branch in range(BRANCHES):
        mixed_out = mixed_out + jnp.exp(stacked[branch] - grand_total)[..., None] * outputs[branch]
    return (mixed_out, (mixed_out, grand_total, kept_state))


def attend_backward(grad_mixed, attention_state, seq_len, seq_index):
    mixed_out, grand_total, kept_state = attention_state
    tok_dev = grad_mixed.shape[0]
    score_scale = HEAD_DIM ** (-0.5)
    grad_query = jnp.zeros(grad_mixed.shape, jnp.float32)
    key_terms, bit_counts, dilations = ([], [], [])
    for branch in range(BRANCHES):
        dilation, segment, group_size = branch_geom(branch, tok_dev, seq_len)
        query_rows, key_rows, value_rows, query_docs, key_docs, output, totals_rows = kept_state[
            branch
        ]
        sections = query_rows.shape[0]
        weight = jnp.exp(totals_rows - pick_rows(grand_total, dilation))
        grad_picked = pick_rows(grad_mixed, dilation)
        grad_output = (
            (weight[..., None] * grad_picked)
            .astype(jnp.bfloat16)
            .reshape(sections, -1, HEADS, HEAD_DIM)
        )
        grad_totals = weight * jnp.sum(
            grad_picked * (output - pick_rows(mixed_out, dilation)), axis=-1
        )
        grad_totals = jnp.transpose(grad_totals.reshape(sections, -1, HEADS), (0, 2, 1))
        totals = jnp.transpose(totals_rows.reshape(sections, -1, HEADS), (0, 2, 1))
        softmax_rows = jnp.exp(
            score_block(query_rows, key_rows, query_docs, key_docs) - totals[..., None]
        )
        grad_value = jnp.einsum(
            "shqk,sqhd->skhd",
            softmax_rows.astype(jnp.bfloat16),
            grad_output,
            preferred_element_type=jnp.float32,
        )
        grad_probs = jnp.einsum(
            "sqhd,skhd->shqk", grad_output, value_rows, preferred_element_type=jnp.float32
        )
        inner_sum = jnp.sum(softmax_rows * grad_probs, axis=-1, keepdims=True)
        grad_scores = (softmax_rows * (grad_probs - inner_sum + grad_totals[..., None])).astype(
            jnp.bfloat16
        )
        grad_q = (
            jnp.einsum("shqk,skhd->sqhd", grad_scores, key_rows, preferred_element_type=jnp.float32)
            * score_scale
        )
        grad_k = (
            jnp.einsum(
                "shqk,sqhd->skhd", grad_scores, query_rows, preferred_element_type=jnp.float32
            )
            * score_scale
        )
        grad_query = grad_query + spread_rows(grad_q.reshape(-1, HEADS, HEAD_DIM), dilation, 0.0)
        key_terms.append(
            jnp.stack(
                [grad_k.reshape(-1, HEADS, HEAD_DIM), grad_value.reshape(-1, HEADS, HEAD_DIM)],
                axis=1,
            ).reshape(-1, 2 * D)
        )
        bit_counts.append(group_size.bit_length() - 1)
        dilations.append(dilation)
    own_terms = return_pairs(key_terms, bit_counts, seq_index)
    grad_key = jnp.zeros(grad_mixed.shape, jnp.float32)
    grad_val = jnp.zeros(grad_mixed.shape, jnp.float32)
    for branch in range(BRANCHES):
        pair_rows = own_terms[branch].reshape(-1, 2, HEADS, HEAD_DIM)
        grad_key = grad_key + spread_rows(pair_rows[:, 0], dilations[branch], 0.0)
        grad_val = grad_val + spread_rows(pair_rows[:, 1], dilations[branch], 0.0)
    return jnp.stack([grad_query, grad_key, grad_val], axis=1).reshape(tok_dev, 3 * D)


def layer_forward(hidden, upper_mat, lower_mat, row_set, lengths_row, seq_len, seq_index):
    normed = layer_norm(hidden, row_set[0], row_set[1]).astype(jnp.bfloat16)
    biases = jnp.concatenate([row_set[2], jnp.zeros_like(row_set[2]), row_set[3]])
    packed = (
        jnp.dot(normed, upper_mat[:, : 3 * D], preferred_element_type=jnp.float32) + biases[None, :]
    ).astype(jnp.bfloat16)
    mixed_out, attention_state = attend_forward(packed, lengths_row, seq_len, seq_index)
    mixed_low = mixed_out.reshape(-1, D).astype(jnp.bfloat16)
    middle = (
        hidden
        + jnp.dot(mixed_low, upper_mat[:, 3 * D : 4 * D], preferred_element_type=jnp.float32)
        + row_set[4][None, :]
    )
    second = layer_norm(middle, row_set[5], row_set[6]).astype(jnp.bfloat16)
    before = (
        jnp.dot(second, upper_mat[:, 4 * D :], preferred_element_type=jnp.float32)
        + row_set[8:].reshape(-1)[None, :]
    )
    active = jax.nn.gelu(before, approximate=True).astype(jnp.bfloat16)
    result = (
        middle
        + jnp.dot(active, lower_mat, preferred_element_type=jnp.float32)
        + row_set[7][None, :]
    )
    return (result, (hidden, normed, mixed_low, middle, second, before, active, attention_state))


def layer_backward(grad_result, upper_mat, lower_mat, row_set, layer_state, seq_len, seq_index):
    hidden, normed, mixed_low, middle, second, before, active, attention_state = layer_state
    grad_out = grad_result.astype(jnp.bfloat16)
    grad_lower = contract_rows(active, grad_out)
    grad_fc2_bias = jnp.sum(grad_out, axis=0, dtype=jnp.float32)
    grad_active = contract_cols(grad_out, lower_mat)
    gelu_value, gelu_back = jax.vjp(partial(jax.nn.gelu, approximate=True), before)
    grad_before = gelu_back(grad_active)[0].astype(jnp.bfloat16)
    grad_fc1 = contract_rows(second, grad_before)
    grad_fc1_bias = jnp.sum(grad_before, axis=0, dtype=jnp.float32)
    grad_second = contract_cols(grad_before, upper_mat[:, 4 * D :])
    norm_value, norm_back = jax.vjp(layer_norm, middle, row_set[5], row_set[6])
    grad_middle, grad_gain_two, grad_shift_two = norm_back(grad_second)
    grad_middle = grad_middle + grad_result
    grad_branch = grad_middle.astype(jnp.bfloat16)
    grad_proj = contract_rows(mixed_low, grad_branch)
    grad_proj_bias = jnp.sum(grad_branch, axis=0, dtype=jnp.float32)
    grad_mixed = contract_cols(grad_branch, upper_mat[:, 3 * D : 4 * D]).reshape(
        -1, HEADS, HEAD_DIM
    )
    grad_packed = attend_backward(grad_mixed, attention_state, seq_len, seq_index).astype(
        jnp.bfloat16
    )
    grad_qkv = contract_rows(normed, grad_packed)
    packed_sums = jnp.sum(grad_packed, axis=0, dtype=jnp.float32)
    grad_normed = contract_cols(grad_packed, upper_mat[:, : 3 * D])
    first_value, first_back = jax.vjp(layer_norm, hidden, row_set[0], row_set[1])
    grad_hidden, grad_gain_one, grad_shift_one = first_back(grad_normed)
    grad_hidden = grad_hidden + grad_middle
    grad_upper = jnp.concatenate([grad_qkv, grad_proj, grad_fc1], axis=1)
    small_rows = jnp.stack(
        [
            grad_gain_one,
            grad_shift_one,
            packed_sums[:D],
            packed_sums[2 * D :],
            grad_proj_bias,
            grad_gain_two,
            grad_shift_two,
            grad_fc2_bias,
        ]
    )
    grad_rows = jnp.concatenate([small_rows, grad_fc1_bias.reshape(-1, D)], axis=0)
    return (grad_hidden, (grad_upper, grad_lower, grad_rows))


def inverse_root(matrix):
    identity = jnp.eye(matrix.shape[-1], dtype=jnp.float32)
    regular = matrix + root_eps * identity
    frob_norm = jnp.sqrt(jnp.sum(regular * regular, axis=(1, 2), keepdims=True))
    scaled = 2.5 / frob_norm
    root_mat = identity * jnp.sqrt(jnp.sqrt(scaled))
    moving = regular * scaled
    for sweep_id in range(NEWTON):
        factor = (5.0 * identity - moving) * 0.25
        root_mat = jnp.einsum("kij,kjl->kil", root_mat, factor, precision=highest)
        square = jnp.einsum("kij,kjl->kil", factor, factor, precision=highest)
        fourth = jnp.einsum("kij,kjl->kil", square, square, precision=highest)
        moving = jnp.einsum("kij,kjl->kil", fourth, moving, precision=highest)
    return root_mat


def adam_update(weight, first_mom, second_mom, grad, rate, decay):
    first_new = beta_one * first_mom + (1.0 - beta_one) * grad
    second_new = beta_two * second_mom + (1.0 - beta_two) * grad * grad
    first_hat = first_new / (1.0 - beta_one**STEP)
    second_hat = second_new / (1.0 - beta_two**STEP)
    return (
        first_new,
        second_new,
        weight - rate * (first_hat / (jnp.sqrt(second_hat) + adam_eps) + decay * weight),
    )


def per_device(
    features,
    tile_mask,
    lengths,
    owners,
    layer_blocks,
    stat_left,
    stat_right,
    io_weights,
    io_first,
    io_second,
    vectors,
    vec_first,
    vec_second,
):
    tok_dev = features.shape[1]
    seq_size = lax.axis_size("seq")
    seq_len = tok_dev * seq_size
    seq_index = lax.axis_index("seq")
    core_index = lax.axis_index("opt")
    targets = features[0].astype(jnp.float32)
    chosen = tile_mask[0][:, None] > 0
    lengths_row = lax.dynamic_index_in_dim(lengths, core_index, 0, keepdims=False)
    places = seq_index * tok_dev + jnp.arange(tok_dev, dtype=jnp.int32)
    all_blocks, all_io = (
        lax.all_gather(layer_blocks.astype(jnp.bfloat16), ("seq", "opt"), axis=0, tiled=True),
        lax.all_gather(io_weights.astype(jnp.bfloat16), ("seq", "opt"), axis=0, tiled=True),
    )
    natural = jnp.zeros_like(all_blocks).at[owners].set(all_blocks)
    upper_mats, lower_mats = assemble(natural)
    tile_count = lax.psum(jnp.sum(tile_mask.astype(jnp.float32)), ("seq", "opt"))
    layer_rows, tail_rows = unpack(vectors)
    token_vec = tail_rows[3 + FEAT // D :].reshape(FEAT)
    head_bias = tail_rows[3 : 3 + FEAT // D].reshape(FEAT)
    inputs = jnp.where(chosen, token_vec[None, :], targets).astype(jnp.bfloat16)
    in_weight = all_io[:, 0]
    head_weight = all_io[:, 1]
    hidden = jnp.dot(inputs, in_weight, preferred_element_type=jnp.float32) + tail_rows[2][None, :]
    hidden = hidden + sine_places(slide_offsets(lengths_row, places))
    layer_id = 0
    hidden, layer_state = layer_forward(
        hidden,
        upper_mats[layer_id],
        lower_mats[layer_id],
        layer_rows[layer_id],
        lengths_row,
        seq_len,
        seq_index,
    )
    layer_states = [layer_state]
    final, final_back = jax.vjp(layer_norm, hidden, tail_rows[0], tail_rows[1])
    final_low = final.astype(jnp.bfloat16)
    predict = contract_cols(final_low, head_weight) + head_bias[None, :]
    difference = predict - targets
    error_local = jnp.sum(jnp.where(chosen, difference * difference, 0.0))
    grad_pred = jnp.where(chosen, 2.0 * difference / tile_count, 0.0).astype(jnp.bfloat16)
    grad_head = contract_rows(grad_pred, final_low)
    grad_head_bias = jnp.sum(grad_pred, axis=0, dtype=jnp.float32)
    grad_final = jnp.dot(grad_pred, head_weight, preferred_element_type=jnp.float32)
    grad_hidden, grad_gain_last, grad_shift_last = final_back(grad_final)
    layer_grads = [None] * LAYERS
    for layer_id in reversed(range(LAYERS)):
        grad_hidden, layer_grads[layer_id] = layer_backward(
            grad_hidden,
            upper_mats[layer_id],
            lower_mats[layer_id],
            layer_rows[layer_id],
            layer_states[layer_id],
            seq_len,
            seq_index,
        )
    grad_in_low = grad_hidden.astype(jnp.bfloat16)
    grad_in = contract_rows(inputs, grad_in_low)
    grad_in_bias = jnp.sum(grad_in_low, axis=0, dtype=jnp.float32)
    grad_inputs = contract_cols(grad_in_low, in_weight)
    grad_token = jnp.sum(jnp.where(chosen, grad_inputs, 0.0), axis=0)
    grad_upper = jnp.stack([item[0] for item in layer_grads])
    grad_lower = jnp.stack([item[1] for item in layer_grads])
    slot_grads = disassemble(grad_upper, grad_lower)[owners]
    io_grads = jnp.stack([grad_in, grad_head], axis=1)
    vec_grads = jnp.concatenate(
        [
            jnp.stack([item[2] for item in layer_grads]).reshape(-1, D),
            jnp.stack([grad_gain_last, grad_shift_last, grad_in_bias]),
            grad_head_bias.reshape(-1, D),
            grad_token.reshape(-1, D),
        ],
        axis=0,
    )
    slot_sum, io_sum = (
        lax.psum_scatter(slot_grads, ("seq", "opt"), scatter_dimension=0, tiled=True),
        lax.psum_scatter(io_grads, ("seq", "opt"), scatter_dimension=0, tiled=True),
    )
    vec_sum, error_sum = lax.psum((vec_grads, error_local), ("seq", "opt"))
    local_sq = jnp.sum(slot_sum * slot_sum) + jnp.sum(io_sum * io_sum)
    grad_norm = jnp.sqrt(lax.psum(local_sq, ("seq", "opt")) + jnp.sum(vec_sum * vec_sum))
    factor = jnp.minimum(1.0, clip_limit / grad_norm)
    block_grads = slot_sum * factor
    left_new = beta_stat * stat_left + (1.0 - beta_stat) * jnp.einsum(
        "kij,klj->kil", block_grads, block_grads, precision=highest
    )
    right_new = beta_stat * stat_right + (1.0 - beta_stat) * jnp.einsum(
        "kji,kjl->kil", block_grads, block_grads, precision=highest
    )
    direction = jnp.einsum("kij,kjl->kil", inverse_root(left_new), block_grads, precision=highest)
    direction = jnp.einsum("kij,kjl->kil", direction, inverse_root(right_new), precision=highest)
    blocks_new = layer_blocks - rate_shampoo * direction
    io_first_new, io_second_new, io_new = adam_update(
        io_weights, io_first, io_second, io_sum * factor, rate_adam, weight_decay
    )
    vec_first_new, vec_second_new, vec_new = adam_update(
        vectors, vec_first, vec_second, vec_sum * factor, rate_vector, 0.0
    )
    return (
        grad_norm,
        error_sum,
        tile_count,
        block_grads,
        left_new,
        right_new,
        blocks_new,
        io_first_new,
        io_second_new,
        io_new,
        vec_first_new,
        vec_second_new,
        vec_new,
    )


BF=jnp.bfloat16; LANE=128; IO=48
def swap(value, axis, mask):
    return lax.ppermute(value, axis, [(s, s ^ mask) for s in range(lax.axis_size(axis))])
def gate(*values):
    return lax.optimization_barrier(values)

GROUP_ROWS=3*BLOCK
IO_AT=2*GROUP_ROWS; COUNT_AT=IO_AT+6*IO; THIRD_AT=COUNT_AT+16
SHARD_HALF=THIRD_AT+GROUP_ROWS
PIECE=8*SHARD_HALF; THIRDS=8*THIRD_AT
def pack_kernel(blocks_ref, io_ref, mask_ref, first_ref, second_ref, both_ref):
    count=jnp.sum(mask_ref[...].astype(jnp.float32),keepdims=True)
    lane=lax.broadcasted_iota(jnp.int32,(BLOCK,LANE),1)
    pad=lambda x: jnp.concatenate([x,jnp.zeros((BLOCK,LANE-BLOCK),x.dtype)],axis=1)
    for h,out_ref in enumerate((first_ref,second_ref)):
        for g in range(3):
            b=[pad(blocks_ref[(h*3+g)*4+t]) for t in range(4)]
            for v in range(3):
                tile=jnp.where(lane<BLOCK,b[v],pltpu.roll(b[3],BLOCK-32*v,1))
                at=(g*GROUP_ROWS if g<2 else THIRD_AT)+v*BLOCK
                out_ref[at:at+BLOCK,:]=tile.astype(BF)
        for v in range(6):
            at=IO_AT+v*IO
            out_ref[at:at+IO,:]=io_ref[:,h,v*LANE:(v+1)*LANE].astype(BF)
        out_ref[COUNT_AT:THIRD_AT,:]=jnp.broadcast_to(count,(16,LANE)).astype(BF)
        both_ref[h*THIRD_AT:(h+1)*THIRD_AT,:]=out_ref[:THIRD_AT,:]
def vmem(): return pl.BlockSpec(memory_space=pltpu.VMEM)
def smem(): return pl.BlockSpec(memory_space=pltpu.SMEM)
def hbm(): return pl.BlockSpec(memory_space=pltpu.HBM)
def from_hbm(body, name, outs, ins, scratch, smem_args=(), late=(), vmem_mib=48, micros=10):
    n_s,n_i,n_o=len(smem_args),len(ins),len(outs)
    def kernel(*refs):
        scalars,args,results=refs[:n_s],refs[n_s:n_s+n_i],refs[n_s+n_i:n_s+n_i+n_o]
        rest=refs[n_s+n_i+n_o:]
        held,made,more=rest[:n_i],rest[n_i:n_i+n_o],rest[n_i+n_o:-2]
        in_sem,out_sem=rest[-2:]
        loads=[pltpu.make_async_copy(a,h,in_sem.at[i]) for i,(a,h) in enumerate(zip(args,held))]
        for c in loads: c.start()
        for i,c in enumerate(loads):
            if i not in late: c.wait()
        body(*([loads[i].wait for i in late]),*scalars,*held,*made,*more)
        stores=[pltpu.make_async_copy(m,r,out_sem.at[i]) for i,(m,r) in enumerate(zip(made,results))]
        for c in stores: c.start()
        for c in stores: c.wait()
    ins=[pltpu.with_memory_space_constraint(a,pltpu.HBM) for a in ins]
    return pl.pallas_call(kernel,out_shape=[pltpu.HBM(s,t) for s,t in outs],
        in_specs=[smem()]*n_s+[hbm()]*n_i,out_specs=[hbm()]*n_o,
        scratch_shapes=[pltpu.VMEM(a.shape,a.dtype) for a in ins]+[pltpu.VMEM(s,t) for s,t in outs]+list(scratch)
            +[pltpu.SemaphoreType.DMA((n_i,)),pltpu.SemaphoreType.DMA((n_o,))],
        compiler_params=pltpu.CompilerParams(vmem_limit_bytes=vmem_mib<<20),
        cost_estimate=pl.CostEstimate(flops=0,transcendentals=0,bytes_accessed=int(micros*3.3e6)),name=name)(*smem_args,*ins)
def pack_shard(blocks, io, mask):
    return pl.pallas_call(pack_kernel,out_shape=[jax.ShapeDtypeStruct((n,LANE),BF) for n in (SHARD_HALF,SHARD_HALF,2*THIRD_AT)],in_specs=[vmem()]*3,out_specs=[vmem()]*3,name="pack_shard")(blocks,io,mask)

HOPS=(("opt",1),("seq",1),("seq",2),("seq",4),("seq",8))
def hop(value, k):
    return value+swap(value,*HOPS[k])

def stack_rows(arrays, *plans):
    n=len(arrays); total=sum(len(p) for p in plans)
    shapes=[(sum(c for _,_,c in p),LANE) for p in plans]
    def kernel(*refs):
        ins,outs,held,(in_sem,out_sem)=refs[:n],refs[n:n+len(plans)],refs[n+len(plans):-2],refs[-2:]
        copies=[]; stores=[]
        for i,plan in enumerate(plans):
            at=0
            for k,first,count in plan:
                copies.append((i,pltpu.make_async_copy(ins[k].at[pl.ds(first,count)],held[i].at[pl.ds(at,count)],in_sem.at[len(copies)])))
                copies[-1][1].start()
                at+=count
        for i,out in enumerate(outs):
            for k,c in copies:
                if k==i: c.wait()
            stores.append(pltpu.make_async_copy(held[i],out,out_sem.at[i]))
            stores[-1].start()
        for c in stores: c.wait()
    return pl.pallas_call(kernel,out_shape=[jax.ShapeDtypeStruct(s,BF) for s in shapes],
        in_specs=[pl.BlockSpec(memory_space=pl.ANY)]*n,out_specs=[pl.BlockSpec(memory_space=pl.ANY)]*len(plans),
        scratch_shapes=[pltpu.VMEM(s,BF) for s in shapes]+[pltpu.SemaphoreType.DMA((total,)),pltpu.SemaphoreType.DMA((len(plans),))],
        compiler_params=pltpu.CompilerParams(vmem_limit_bytes=16<<20),name="stack_rows")(*arrays)

def gather_tree(first, second, both):
    near=[None]*4; cross=[None]*4; third=[None]*4
    def first_step(k,a,b):
        near[k]=(swap(a,"seq",1),swap(b,"seq",2))
    def second_step(k,a,b,rows):
        sent=stack_rows([a[0],near[k][0],b[0],near[k][1]],[(0,a[1],rows),(1,0,rows)],[(2,b[1],rows),(3,0,rows)])
        cross[k]=(swap(sent[0],"seq",2),swap(sent[1],"seq",1))
    def halves_of(far): return (far,0),(far,THIRD_AT)
    far1=swap(both,"seq",4)
    far2=swap(both,"seq",8)
    first_step(0,first,second)
    second_step(0,(first,0),(second,0),SHARD_HALF)
    arrays=[first,second,*near[0],*cross[0]]
    units=[(0,0),(1,0),(2,0),(3,0),(4,0),(4,SHARD_HALF),(5,0),(5,SHARD_HALF)]
    third[0]=stack_rows(arrays,[(k,at+THIRD_AT,GROUP_ROWS) for k,at in units])[0]
    third[2]=swap(third[0],"seq",8)
    third[1]=swap(third[0],"seq",4)
    first_step(1,far1[:THIRD_AT],far1[THIRD_AT:])
    first_step(2,far2[:THIRD_AT],far2[THIRD_AT:])
    far3=swap(far2,"seq",4)
    near[1],near[2],far3=gate(near[1],near[2],far3)
    second_step(1,*halves_of(far1),THIRD_AT)
    first_step(3,far3[:THIRD_AT],far3[THIRD_AT:])
    near[2],near[3]=gate(near[2],near[3])
    second_step(2,*halves_of(far2),THIRD_AT)
    near[3],third[2]=gate(near[3],third[2])
    second_step(3,*halves_of(far3),THIRD_AT)
    third[3]=swap(third[2],"seq",4)
    out=list(stack_rows(arrays+[third[0]],[(k,at,THIRD_AT) for k,at in units]+[(len(arrays),0,third[0].shape[0])]))
    for k,far in ((1,far1),(2,far2),(3,far3)):
        arrays=[far,*near[k],*cross[k],third[k]]
        out+=stack_rows(arrays,[(i,0,part.shape[0]) for i,part in enumerate(arrays)])
    return out+[swap(piece,"opt",1) for piece in out]

HELD=64*SHARD_HALF
N_BLOCK=768
def load_shards(bufs, held, sem, fourths):
    rows=bufs[0].shape[0]
    loads=[pltpu.make_async_copy(b,held.at[pl.ds(k*rows,rows)],sem.at[k]) for k,b in enumerate(bufs)]
    for c in loads: c.start()
    fourths()
    for k,c in enumerate(loads):
        c.wait()
        def unpack(u,carry,k=k):
            for g in range(3):
                at=k*PIECE+(u*THIRD_AT+g*GROUP_ROWS if g<2 else THIRDS+u*GROUP_ROWS)
                parts=[held[pl.ds(pl.multiple_of(at+v*BLOCK,16),BLOCK),BLOCK:] for v in range(3)]
                to=HELD+((k*8+u)*3+g)*BLOCK
                held[pl.ds(pl.multiple_of(to,16),BLOCK),:BLOCK]=jnp.concatenate(parts,axis=1)
            return carry
        lax.fori_loop(0,8,unpack,0,unroll=8)

def join_kernel(plan, io_out, owners_ref, row_ref, io_ref, *refs):
    bufs=refs[:8]; n_out=len(plan); outs=refs[8:8+n_out]; io_ref_out,count_ref=refs[8+n_out:8+n_out+2]
    held,stage,where,in_sem,out_sem,io_sem=refs[8+n_out+2:]
    def invert():
        def one(i,carry):
            for j in range(8):
                where[owners_ref[i*8+j]]=row_ref[i*8+j]
            return carry
        lax.fori_loop(0,N_BLOCK//8,one,0)
    load_shards(bufs,held,in_sem,invert)
    def io_copy(d,total):
        at=io_ref[io_out,d]
        for v in range(6):
            pltpu.make_async_copy(held.at[pl.ds(pl.multiple_of(at+v*IO,16),IO)],
                io_ref_out.at[pl.ds(pl.multiple_of(d*IO,IO),IO),pl.ds(v*LANE,LANE)],io_sem).start()
        return total+held[pl.ds(pl.multiple_of(at+6*IO,16),16),:].astype(jnp.float32)
    count_ref[...]=lax.fori_loop(0,io_ref.shape[1],io_copy,jnp.zeros((16,LANE),jnp.float32))
    def block(n):
        return held[pl.ds(pl.multiple_of(where[n],16),BLOCK),:BLOCK]
    pending=[]; index=0
    for (first,stride,rows,stripes),out in zip(plan,outs):
        per=8//stripes if stripes<8 else 1
        for i0 in range(0,rows,per):
            slot=index%2
            if index>=2:
                for c in pending[index-2]: c.wait()
            for b in range(per):
                def one(c,carry,b=b,i0=i0):
                    n=first+(i0+b)*stride+4*c
                    stage[slot,:,pl.ds(pl.multiple_of((b*stripes+c)*4*BLOCK,128),4*BLOCK)]=jnp.concatenate([block(n+t) for t in range(4)],axis=1)
                    return carry
                lax.fori_loop(0,stripes,one,0,unroll=stripes)
            w=stripes*4*BLOCK
            cs=[pltpu.make_async_copy(stage.at[slot,:,pl.ds(b*w,w)],out.at[pl.ds((i0+b)*BLOCK,BLOCK)],out_sem.at[slot,b]) for b in range(per)]
            for c in cs: c.start()
            pending.append(cs); index+=1
    for cs in pending[-2:]:
        for c in cs: c.wait()
    pltpu.make_async_copy(io_ref_out,io_ref_out,io_sem).wait()

COLS=(4*D+FF)//BLOCK
FIRST_PLAN=((0,COLS,8,6),(24,COLS,8,2))
SECOND_PLAN=((32,COLS,8,8),(8*COLS,8,32,2))
def join_weights(plan, io_out, bufs, owners, rows, io_rows):
    shapes=[(r*BLOCK,s*4*BLOCK) for _,_,r,s in plan]+[(FEAT,D)]
    return pl.pallas_call(partial(join_kernel,plan,io_out),
        out_shape=[pltpu.HBM(s,BF) for s in shapes]+[jax.ShapeDtypeStruct((16,LANE),jnp.float32)],
        in_specs=[smem()]*3+[hbm()]*8, out_specs=[hbm()]*len(shapes)+[vmem()],
        scratch_shapes=[pltpu.VMEM((HELD+N_BLOCK//4*BLOCK,LANE),BF),pltpu.VMEM((2,BLOCK,FF),BF),pltpu.SMEM((N_BLOCK,),jnp.int32),
            pltpu.SemaphoreType.DMA((8,)),pltpu.SemaphoreType.DMA((2,4)),pltpu.SemaphoreType.DMA],
        compiler_params=pltpu.CompilerParams(vmem_limit_bytes=40<<20), cost_estimate=pl.CostEstimate(flops=0,transcendentals=0,bytes_accessed=int((13 if io_out==0 else 17)*3.3e6)), name="join_weights")(owners,rows,io_rows,*[pltpu.with_memory_space_constraint(b,pltpu.HBM) for b in bufs])

def shard_rows(seq_index, core):
    def unit(dev,h):
        rel=(dev//2)^seq_index; xy=rel%4
        u=jnp.where(xy==0,h,jnp.where(h==0,jnp.where(xy==1,2,xy+2),jnp.where(xy==2,3,jnp.where(xy==1,6,7))))
        return (rel//4+4*((dev%2)^core))*8+u
    slot=jnp.arange(N_BLOCK,dtype=jnp.int32); s=slot%24
    u=unit(slot//24,s//12); g=s%12//4; t=s%4
    start=u//8*PIECE+jnp.where(g<2,u%8*THIRD_AT+g*GROUP_ROWS,THIRDS+u%8*GROUP_ROWS)
    rows=jnp.where(t<3,start+t*BLOCK,HELD+(u*3+g)*BLOCK)
    dev=jnp.arange(32,dtype=jnp.int32)
    io=jnp.stack([unit(dev,h)//8*PIECE+unit(dev,h)%8*THIRD_AT+IO_AT for h in (0,1)])
    return rows.astype(jnp.int32),io.astype(jnp.int32)
def gather_shards(layer_blocks, io_weights, mask):
    return gather_tree(*pack_shard(layer_blocks,io_weights,mask))

HD=48; HEADS=16; SLIDES=4; SEG=1024; N=2048; H=512; TQ=256; TQF=512; TK=256
C2=HD**-0.5*math.log2(math.e)
def place_facts(index, head, lengths_ref, core):
    parity=(head+(index>>(H.bit_length()-1)))&1
    pos=((index>>(SEG.bit_length()-1))<<(SEG.bit_length()-1))+((index&(H-1))<<1)+parity
    slide=jnp.zeros_like(index); end=jnp.int32(0)
    for i in range(SLIDES-1):
        end=end+lengths_ref[core,i]
        slide=slide+jnp.where(pos>=end,1,0)
    d=(pos-head)&15
    level=jnp.where((d&1)==0,jnp.where((d&3)==0,jnp.where((d&7)==0,jnp.where(d==0,4,3),2),1),0)
    return slide.astype(jnp.float32), level.astype(jnp.float32)

def arrange(src, dst, odd):
    for pair in range(8):
        first, second = src[2*pair], src[2*pair+1]
        turn=lambda t: jnp.concatenate([t[:,64:],t[:,:64]],axis=1)
        ft, st = turn(first), turn(second)
        low=lax.broadcasted_iota(jnp.int32,first.shape,1)<64
        evens=jnp.where(low,first,st); odds=jnp.where(low,ft,second)
        near=jnp.where(odd,odds,evens); far=jnp.where(odd,evens,odds)
        at=(pair//4)*SEG+(pair%4)*128
        dst[:,at:at+128]=near.astype(dst.dtype); dst[:,at+H:at+H+128]=far.astype(dst.dtype)

def restore(get, put, odd):
    for pair in range(8):
        at=(pair//4)*SEG+(pair%4)*128
        near, far = get(at), get(at+H)
        evens=jnp.where(odd,far,near); odds=jnp.where(odd,near,far)
        turn=lambda t: jnp.concatenate([t[:,64:],t[:,:64]],axis=1)
        low=lax.broadcasted_iota(jnp.int32,evens.shape,1)<64
        put(2*pair, jnp.where(low,evens,turn(odds)))
        put(2*pair+1, jnp.where(low,turn(evens),odds))

def setup(lengths_ref, ids_ref, slide_k, level_k, row_facts):
    head, core = ids_ref[0], ids_ref[1]
    def fill(i, c):
        idx=lax.broadcasted_iota(jnp.int32,(TK,128),0)+i*TK
        s,l=place_facts(idx,head,lengths_ref,core)
        slide_k[pl.ds(pl.multiple_of(i*TK,TK),TK),:]=s
        level_k[pl.ds(pl.multiple_of(i*TK,TK),TK),:]=l
        return c
    lax.fori_loop(0,N//TK,fill,0)
    idx=lax.broadcasted_iota(jnp.int32,(8,N),1)
    s,l=place_facts(idx,head,lengths_ref,core)
    row_facts[0:8,:]=s; row_facts[8:16,:]=l

def key_rows(seg, near):
    own=[(seg*SEG+i*TK,True) for i in range(SEG//TK)]
    other=[((1-seg)*SEG+i*TK,False) for i in range(H//TK)] if near else []
    return own+other

def wide(x, queries): return jnp.concatenate([x]*(queries//128),axis=1)

def forward_kernel(lengths_ref, ids_ref, qkv_ref, o_ref, out_ref, lse_ref, qkvT, krow, slide_k, level_k, row_facts, s_ref, p_ref):
    odd=lax.rem(ids_ref[0],2)==1
    arrange(qkv_ref, qkvT, odd)
    setup(lengths_ref, ids_ref, slide_k, level_k, row_facts)
    for i in range(N//128):
        krow[i*128:(i+1)*128,:]=qkvT[HD:2*HD,i*128:(i+1)*128].astype(jnp.float32).T.astype(jnp.bfloat16)
    for seg in range(2):
        for near in (True,False):
            tiles=key_rows(seg,near)
            def part(c, carry, seg=seg, near=near, tiles=tiles):
                at=pl.multiple_of(seg*SEG+(0 if near else H)+c*TQF,TQF)
                qT=qkvT[0:HD,pl.ds(at,TQF)]
                sq=row_facts[0:1,pl.ds(at,TQF)]; lq=row_facts[8:9,pl.ds(at,TQF)]
                top=jnp.full((8,TQF),-jnp.inf,jnp.float32)
                for t,(r,own) in enumerate(tiles):
                    s=jnp.dot(krow[r:r+TK,:],qT,preferred_element_type=jnp.float32)
                    s=jnp.where(wide(slide_k[r:r+TK,:],TQF)==sq,s,-1e30)
                    s_ref[t*TK:(t+1)*TK,:]=s
                    top=jnp.maximum(top,jnp.max(s.reshape(TK//8,8,TQF),axis=0))
                m=jnp.max(top,axis=0,keepdims=True)
                total=jnp.zeros((8,TQF),jnp.float32)
                for t,(r,own) in enumerate(tiles):
                    e=jnp.exp2((s_ref[t*TK:(t+1)*TK,:]-m)*C2)
                    if near:
                        lk=wide(level_k[r:r+TK,:],TQF)
                        e=e*(jnp.minimum(lk,lq)+1.0 if own else jnp.minimum(lk,lq))
                    total=total+jnp.sum(e.reshape(TK//8,8,TQF),axis=0)
                    p_ref[t*TK:(t+1)*TK,:]=e.astype(jnp.bfloat16)
                l=jnp.sum(total,axis=0,keepdims=True)
                acc=jnp.zeros((HD,TQF),jnp.float32)
                acc=jnp.dot(qkvT[2*HD:3*HD,seg*SEG:(seg+1)*SEG],p_ref[0:SEG,:],preferred_element_type=jnp.float32)
                if near:
                    acc=acc+jnp.dot(qkvT[2*HD:3*HD,(1-seg)*SEG:(1-seg)*SEG+H],p_ref[SEG:SEG+H,:],preferred_element_type=jnp.float32)
                o_ref[:,pl.ds(at,TQF)]=acc/l
                lse_ref[:,pl.ds(at,TQF)]=jnp.broadcast_to(m*C2+jnp.log2(l),(8,TQF))
                return carry
            lax.fori_loop(0,H//TQF,part,0)
    def put(c,v): out_ref[c]=v.astype(jnp.bfloat16)
    restore(lambda at: o_ref[:,at:at+128], put, odd)

def turned_product(a,b): return lax.dot_general(a,b,(((1,),(1,)),((),())),preferred_element_type=jnp.float32)
def backward_kernel(lengths_ref, ids_ref, qkv_ref, do_ref, o_ref, lse_ref, out_ref, qkvT, doT, rows, slide_k, level_k, row_facts, dqT, dkv, p_ref, ds_ref):
    odd=lax.rem(ids_ref[0],2)==1
    arrange(qkv_ref, qkvT, odd)
    arrange(do_ref, doT, odd)
    setup(lengths_ref, ids_ref, slide_k, level_k, row_facts)
    for i in range(N//128):
        l=slice(i*128,(i+1)*128)
        for j in range(2):
            rows[j,l,:]=qkvT[(j+1)*HD:(j+2)*HD,l].astype(jnp.float32).T.astype(jnp.bfloat16)
    dkv[...]=jnp.zeros_like(dkv)
    for seg in range(2):
        for near in (True,False):
            tiles=key_rows(seg,near)
            def part(c, carry, seg=seg, near=near, tiles=tiles):
                at=pl.multiple_of(seg*SEG+(0 if near else H)+c*TQ,TQ)
                qT=qkvT[0:HD,pl.ds(at,TQ)]; gT=doT[:,pl.ds(at,TQ)]
                sq=row_facts[0:1,pl.ds(at,TQ)]; lq=row_facts[8:9,pl.ds(at,TQ)]
                lse=lse_ref[0:1,pl.ds(at,TQ)]
                inner=jnp.sum(gT.astype(jnp.float32)*o_ref[:,pl.ds(at,TQ)],axis=0,keepdims=True)
                for t,(r,own) in enumerate(tiles):
                    s=jnp.dot(rows[0,r:r+TK,:],qT,preferred_element_type=jnp.float32)
                    dp=jnp.dot(rows[1,r:r+TK,:],gT,preferred_element_type=jnp.float32)
                    e=jnp.exp2(s*C2-lse)
                    if near:
                        lk=wide(level_k[r:r+TK,:],TQ)
                        e=e*(jnp.minimum(lk,lq)+1.0 if own else jnp.minimum(lk,lq))
                    e=jnp.where(wide(slide_k[r:r+TK,:],TQ)==sq,e,0.0)
                    p_ref[t*TK:(t+1)*TK,:]=e.astype(jnp.bfloat16)
                    ds_ref[t*TK:(t+1)*TK,:]=(e*(dp-inner)).astype(jnp.bfloat16)
                dq=jnp.dot(qkvT[HD:2*HD,seg*SEG:(seg+1)*SEG],ds_ref[0:SEG,:],preferred_element_type=jnp.float32)
                if near:
                    dq=dq+jnp.dot(qkvT[HD:2*HD,(1-seg)*SEG:(1-seg)*SEG+H],ds_ref[SEG:SEG+H,:],preferred_element_type=jnp.float32)
                dqT[:,pl.ds(at,TQ)]=dq*HD**-0.5
                own=slice(seg*SEG,(seg+1)*SEG)
                dkv[0,:,own]+=turned_product(qT,ds_ref[0:SEG,:])
                dkv[1,:,own]+=turned_product(gT,p_ref[0:SEG,:])
                if near:
                    oth=slice((1-seg)*SEG,(1-seg)*SEG+H)
                    dkv[0,:,oth]+=turned_product(qT,ds_ref[SEG:SEG+H,:])
                    dkv[1,:,oth]+=turned_product(gT,p_ref[SEG:SEG+H,:])
                return carry
            lax.fori_loop(0,H//TQ,part,0)
    def putter(j):
        def put(c,v): out_ref[c,j*HD:(j+1)*HD,:]=v.astype(jnp.bfloat16)
        return put
    restore(lambda at: dqT[:,at:at+128], putter(0), odd)
    restore(lambda at: dkv[0,:,at:at+128]*HD**-0.5, putter(1), odd)
    restore(lambda at: dkv[1,:,at:at+128], putter(2), odd)

def attend(lengths, ids, qkv):
    return from_hbm(forward_kernel,"attend_forward",[((HD,N),F32),((16,HD,128),BF),((8,N),F32)],[qkv],
        [pltpu.VMEM((3*HD,N),BF),pltpu.VMEM((N,HD),BF),pltpu.VMEM((N,128),F32),pltpu.VMEM((N,128),F32),pltpu.VMEM((16,N),F32),
            pltpu.VMEM((SEG+H,TQF),F32),pltpu.VMEM((SEG+H,TQF),BF)],(lengths,ids))
def attend_back(lengths, ids, qkv, do, o, lse):
    return from_hbm(backward_kernel,"attend_backward",[((16,3*HD,128),BF)],[qkv,do,o,lse],
        [pltpu.VMEM((3*HD,N),BF),pltpu.VMEM((HD,N),BF),pltpu.VMEM((2,N,HD),BF),pltpu.VMEM((N,128),F32),pltpu.VMEM((N,128),F32),pltpu.VMEM((16,N),F32),
            pltpu.VMEM((HD,N),F32),pltpu.VMEM((2,HD,N),F32),pltpu.VMEM((SEG+H,TQ),BF),pltpu.VMEM((SEG+H,TQ),BF)],(lengths,ids),micros=13)[0]

F32=jnp.float32
EPS=1e-05
def norm_parts(x):
    centred=x-jnp.mean(x,axis=-1,keepdims=True)
    spread=lax.rsqrt(jnp.mean(centred*centred,axis=-1,keepdims=True)+EPS)
    return centred*spread,spread
def norm_back(grad,unit,spread,gain):
    inner=grad*gain
    back=spread*(inner-jnp.mean(inner,axis=-1,keepdims=True)-unit*jnp.mean(inner*unit,axis=-1,keepdims=True))
    return back,jnp.sum(grad*unit,axis=0,keepdims=True),jnp.sum(grad,axis=0,keepdims=True)
def put_turned(ref,at,x):
    for c in range(x.shape[1]//LANE):
        ref[at+c*LANE:at+(c+1)*LANE,:]=x[:,c*LANE:(c+1)*LANE].astype(F32).T.astype(BF)
def turned(ref,rows):
    return jnp.concatenate([ref[c*LANE:(c+1)*LANE,:].astype(F32).T for c in range(rows//LANE)],axis=1)
def mm(a,b): return jnp.dot(a,b,preferred_element_type=F32)
def mm_t(a,b): return lax.dot_general(a,b,(((1,),(1,)),((),())),preferred_element_type=F32)
LATE_ROWS=4*D+2*FF+FEAT
GELU_A=math.sqrt(2.0/math.pi); GELU_B=0.044715
def mlp_kernel(up_here, down_here, head_here, count_ref, hidden_ref, mixed_ref, targets_ref, chosen_ref, vec_ref, wo_ref, up_ref, down_ref, head_ref,
               middle_grad_ref, mixed_grad_ref, late_ref, rows_ref, kept):
    row=lambda i: vec_ref[i:i+1,:]
    mixed=turned(mixed_ref,D).astype(BF)
    middle=hidden_ref[...]+mm(mixed,wo_ref[...])+row(4)
    unit2,spread2=norm_parts(middle)
    second=(unit2*row(5)+row(6)).astype(BF)
    put_turned(late_ref,0,second)
    result=middle+row(7)
    up_here(); down_here()
    for c in range(FF//D):
        s=slice(c*D,(c+1)*D)
        before=mm(second,up_ref[:,s])+row(8+c)
        kept[:,s]=before
        active=(before*(0.5*(1.0+jnp.tanh(GELU_A*(before+GELU_B*(before*before*before)))))).astype(BF)
        put_turned(late_ref,D+c*D,active)
        result=result+mm(active,down_ref[s,:])
    unit,spread=norm_parts(result)
    final=(unit*row(12)+row(13)).astype(BF)
    put_turned(late_ref,3*D+2*FF+FEAT,final)
    head_here()
    chosen=chosen_ref[...]>0.0
    error=jnp.zeros((1,1),F32); grad_final=jnp.zeros_like(middle)
    for c in range(FEAT//D):
        s=slice(c*D,(c+1)*D)
        difference=mm_t(final,head_ref[s,:])+row(15+c)-targets_ref[:,s].astype(F32)
        error=error+jnp.sum(jnp.where(chosen,difference*difference,0.0),keepdims=True)
        pred=jnp.where(chosen,2.0*difference/count_ref[0],0.0).astype(BF)
        put_turned(late_ref,3*D+2*FF+c*D,pred)
        rows_ref[10+c:11+c,:]=jnp.sum(pred.astype(F32),axis=0,keepdims=True)
        grad_final=grad_final+mm(pred,head_ref[s,:])
    rows_ref[12:13,:]=jnp.broadcast_to(error,(1,D))
    grad_result,rows_ref[8:9,:],rows_ref[9:10,:]=norm_back(grad_final,unit,spread,row(12))
    grad_out=grad_result.astype(BF)
    put_turned(late_ref,2*D+2*FF,grad_out)
    rows_ref[3:4,:]=jnp.sum(grad_out.astype(F32),axis=0,keepdims=True)
    grad_second=jnp.zeros_like(middle)
    for c in range(FF//D):
        s=slice(c*D,(c+1)*D)
        grad_active=mm_t(grad_out,down_ref[s,:])
        x=kept[:,s]
        t=jnp.tanh(GELU_A*(x+GELU_B*(x*x*x)))
        slope=0.5*(1.0+t)+x*(0.5*(1.0-t*t)*(GELU_A*(1.0+3.0*GELU_B*(x*x))))
        grad_before=(grad_active*slope).astype(BF)
        put_turned(late_ref,2*D+FF+c*D,grad_before)
        rows_ref[4+c:5+c,:]=jnp.sum(grad_before.astype(F32),axis=0,keepdims=True)
        grad_second=grad_second+mm_t(grad_before,up_ref[:,s])
    back,rows_ref[1:2,:],rows_ref[2:3,:]=norm_back(grad_second,unit2,spread2,row(5))
    grad_middle=back+grad_result
    middle_grad_ref[...]=grad_middle
    grad_branch=grad_middle.astype(BF)
    put_turned(late_ref,D+FF,grad_branch)
    rows_ref[0:1,:]=jnp.sum(grad_branch.astype(F32),axis=0,keepdims=True)
    mixed_grad_ref[...]=mm_t(wo_ref[...],grad_branch).astype(BF)
    rows_ref[13:16,:]=jnp.zeros((3,D),F32)
def mlp_step(count, hidden, mixed, targets, chosen, vectors, wo, up, down, head):
    t=hidden.shape[0]
    low=lambda rows: ((rows,t),BF)
    return from_hbm(mlp_kernel,"mlp_step",[((t,D),F32),low(D),low(LATE_ROWS),((16,D),F32)],
        [hidden,mixed,targets,chosen,vectors,wo,up,down,head],[pltpu.VMEM((t,FF),F32)],(count.reshape(1),),late=(6,7,8),micros=13)

def input_kernel(in_here, parts_ref, hidden_ref, middle_grad_ref, chosen_ref, vec_ref, rows_ref, qkv_ref, in_ref, last_ref, sums_ref):
    heads,wide,t=parts_ref.shape; hd=wide//3
    for j in range(3):
        for h in range(heads):
            last_ref[j*D+h*hd:j*D+(h+1)*hd,:]=parts_ref[h,j*hd:(j+1)*hd,:]
    packed=last_ref[:3*D,:]
    grad_t=mm(qkv_ref[...],packed)
    grad=jnp.concatenate([grad_t[c*LANE:(c+1)*LANE,:].T for c in range(D//LANE)],axis=1)
    unit,spread=norm_parts(hidden_ref[...])
    back,gain,shift=norm_back(grad,unit,spread,vec_ref[0:1,:])
    grad_hidden=back+middle_grad_ref[...]
    low=grad_hidden.astype(BF)
    put_turned(last_ref,3*D,low)
    sums_ref[0:1,:]=gain; sums_ref[1:2,:]=shift
    ones=jnp.ones((8,t),BF)
    sums_ref[2:3,:]=mm_t(ones,packed[:D])[0:1]
    sums_ref[3:4,:]=mm_t(ones,packed[2*D:])[0:1]
    sums_ref[4:14,:]=rows_ref[0:10,:]
    sums_ref[14:15,:]=jnp.sum(low.astype(F32),axis=0,keepdims=True)
    sums_ref[15:17,:]=rows_ref[10:12,:]
    in_here()
    masked=jnp.where(chosen_ref[...]>0.0,low.astype(F32),0.0).astype(BF)
    for c in range(FEAT//D):
        sums_ref[17+c:18+c,:]=jnp.sum(mm_t(masked,in_ref[c*D:(c+1)*D,:]),axis=0,keepdims=True)
    sums_ref[19:20,:]=rows_ref[12:13,:]
    sums_ref[20:24,:]=jnp.zeros((4,D),F32)
def input_step(parts, hidden, middle_grad, chosen, vectors, rows, qkv, w_in):
    t=hidden.shape[0]
    return from_hbm(input_kernel,"input_step",[((4*D,t),BF),((24,D),F32)],[parts,hidden,middle_grad,chosen,vectors,rows,qkv,w_in],[],late=(7,),micros=5)

def front_kernel(qkv_here, features_ref, chosen_ref, places_ref, vec_ref, in_ref, qkv_ref, hidden_ref, early_ref, heads_ref, turned_ref):
    row=lambda i: vec_ref[i:i+1,:]
    chosen=chosen_ref[...]>0.0
    hidden=places_ref[...]+row(14)
    for c in range(FEAT//D):
        s=slice(c*D,(c+1)*D)
        part=jnp.where(chosen,row(17+c),features_ref[:,s].astype(F32)).astype(BF)
        put_turned(early_ref,D+c*D,part)
        hidden=hidden+mm(part,in_ref[s,:])
    hidden_ref[...]=hidden
    unit,spread=norm_parts(hidden)
    normed=(unit*row(0)+row(1)).astype(BF)
    put_turned(early_ref,0,normed)
    qkv_here()
    heads,wide,t=heads_ref.shape; hd=wide//3
    for j in range(3):
        out=mm(normed,qkv_ref[:,j*D:(j+1)*D])
        if j!=1: out=out+row(2 if j==0 else 3)
        put_turned(turned_ref,j*D,out.astype(BF))
        for h in range(heads):
            heads_ref[h,j*hd:(j+1)*hd,:]=turned_ref[j*D+h*hd:j*D+(h+1)*hd,:]
def front_step(features, chosen, places, vectors, w_in, qkv, heads):
    t=features.shape[0]
    return from_hbm(front_kernel,"front_step",[((t,D),F32),((D+FEAT,t),BF),((heads,3*D//heads,t),BF)],[features,chosen,places,vectors,w_in,qkv],
        [pltpu.VMEM((3*D,t),BF)],late=(5,),micros=5)

I16=jnp.int16; F32=jnp.float32; BF=jnp.bfloat16
GROUP=48; LANE=128; IO=48
STEP_Q=32000.0
UNITS=24; CODE_ROWS=32; PART=UNITS*GROUP+CODE_ROWS
A_ROWS=3*D+FF; X_ROWS=3*D+D+FF+D
ROUND=12582912.0

def encode(x):
    top=jnp.max(jnp.abs(x),axis=0,keepdims=True)
    code=jnp.ceil(jnp.log2(jnp.maximum(top,1e-30))*256.0)
    v=x*(STEP_Q*jnp.exp2(code*(-1.0/256.0)))
    return ((v+ROUND)-ROUND).astype(jnp.int32).astype(I16), code
def scale_of(code16):
    return jnp.exp2(code16.astype(jnp.int32).astype(F32)*(1.0/256.0))*(1.0/STEP_Q)
def pack_codes(codes):
    codes=codes+[jnp.zeros((CODE_ROWS-len(codes),LANE),F32)]
    return jnp.concatenate(codes,axis=0).astype(jnp.int32).astype(I16)

EARLY,MIXED,LATE,LAST=range(4)
PARTS=(((EARLY,0,D),("a",0)),((MIXED,0,D),("a",D)),((LATE,0,D),("a",2*D)),((LATE,D,FF),("a",3*D)),
    ((LAST,0,3*D),("x",0)),((LATE,D+FF,D),("x",3*D)),((LATE,2*D+FF,FF),("x",4*D)),((LATE,2*D+2*FF,D),("x",4*D+FF)),
    ((EARLY,D,FEAT),("a_in",0)),((LAST,3*D,D),("x_in",0)),((LATE,3*D+2*FF,FEAT),("a_head",0)),((LATE,3*D+2*FF+FEAT,D),("x_head",0)))
def grads_kernel(zone, ids_ref, owners_ref, *refs):
    operands=refs[:8]; outs=refs[8:12]
    a_all,x_all,a_in,x_in,a_head,x_head,sem=refs[12:]
    buf_of=dict(a=a_all,x=x_all,a_in=a_in,x_in=x_in,a_head=a_head,x_head=x_head)
    seq,core=ids_ref[0],ids_ref[1]
    copies=[]
    for (source,first,count),(buf,at) in PARTS:
        for side in range(2):
            c=pltpu.make_async_copy(operands[2*source+side].at[pl.ds(first,count)],buf_of[buf].at[pl.ds(at,count),pl.ds(side*LANE,LANE)],sem.at[len(copies)])
            c.start(); copies.append(c)
    for c in copies: c.wait()
    lane=lax.broadcasted_iota(jnp.int32,(BLOCK,LANE),1)
    cols=(4*D+FF)//BLOCK; wide_count=D//BLOCK*cols
    def block(slot):
        n=owners_ref[slot]
        i=n//cols; j=n%cols
        m=n-wide_count
        group=jnp.where(j>=3*D//BLOCK,1,0)+jnp.where(j>=4*D//BLOCK,1,0)
        a_at=jnp.where(m<0,i*BLOCK+group*D,3*D+m//(D//BLOCK)*BLOCK)
        x_at=jnp.where(m<0,j*BLOCK,4*D+FF+m%(D//BLOCK)*BLOCK)
        a=a_all[pl.ds(pl.multiple_of(a_at,32),BLOCK),:]
        x=x_all[pl.ds(pl.multiple_of(x_at,32),BLOCK),:]
        w=lax.dot_general(a,x,(((1,),(1,)),((),())),preferred_element_type=F32)
        return jnp.concatenate([w,jnp.zeros((BLOCK,LANE-BLOCK),F32)],axis=1)
    for out,h,first,step in ((outs[0],0,2,1),(outs[2],1,1,2),(outs[1],0,0,1),(outs[3],1,0,2)):
        def one(j,carry,out=out,h=h,first=first,step=step):
            device=2*jnp.bitwise_xor(seq,zone*4+first+step*j)+core
            codes=[]
            for g in range(3):
                w=[block(device*24+(h*3+g)*4+t) for t in range(4)]
                for v in range(3):
                    tile=jnp.where(lane<BLOCK,w[v],pltpu.roll(w[3],BLOCK-32*v,1))
                    for half in range(2):
                        q,code=encode(tile[half*GROUP:(half+1)*GROUP])
                        at=((g*3+v)*2+half)*GROUP
                        out[j,at:at+GROUP,:]=q; codes.append(code)
            a_ref,x_ref=((a_in,x_in),(a_head,x_head))[h]
            w=lax.dot_general(a_ref[pl.ds(pl.multiple_of(device*IO,16),IO),:],x_ref[...],(((1,),(1,)),((),())),preferred_element_type=F32)
            for v in range(6):
                q,code=encode(w[:,v*LANE:(v+1)*LANE])
                at=(18+v)*GROUP
                out[j,at:at+GROUP,:]=q; codes.append(code)
            out[j,UNITS*GROUP:,:]=pack_codes(codes)
            return carry
        lax.fori_loop(0,2,one,0)

def weight_grads(zone, ids, owners, operands):
    n=len(operands)
    return pl.pallas_call(partial(grads_kernel,zone),
        out_shape=[jax.ShapeDtypeStruct((2,PART,LANE),I16)]*4,
        in_specs=[pl.BlockSpec(memory_space=pltpu.SMEM)]*2+[pl.BlockSpec(memory_space=pl.ANY)]*n,
        out_specs=[pl.BlockSpec(memory_space=pltpu.VMEM)]*4,
        scratch_shapes=[pltpu.VMEM((A_ROWS,2*LANE),BF),pltpu.VMEM((X_ROWS,2*LANE),BF),pltpu.VMEM((FEAT,2*LANE),BF),pltpu.VMEM((D,2*LANE),BF),
            pltpu.VMEM((FEAT,2*LANE),BF),pltpu.VMEM((D,2*LANE),BF),pltpu.SemaphoreType.DMA((2*len(PARTS),))],
        compiler_params=pltpu.CompilerParams(vmem_limit_bytes=40<<20), cost_estimate=takes(0.8), name="weight_grads")(ids,owners,*operands)

class At:
    def __init__(s,ref,*i): s.ref,s.i=ref,i
    def __getitem__(s,k): return s.ref[(*s.i,k,slice(None))]
    def __setitem__(s,k,v): s.ref[(*s.i,k,slice(None))]=v
def summed(views):
    scales=[scale_of(v[UNITS*GROUP:PART]) for v in views]
    for k in range(UNITS):
        total=None
        for v,s in zip(views,scales):
            x=v[k*GROUP:(k+1)*GROUP].astype(jnp.int32).astype(F32)*s[k:k+1,:]
            total=x if total is None else total+x
        yield k,total
def add_codes(views, out):
    codes=[]
    for k,total in summed(views):
        q,code=encode(total)
        out[k*GROUP:(k+1)*GROUP]=q
        codes.append(code)
    out[UNITS*GROUP:PART]=pack_codes(codes)
def takes(micros):
    return pl.CostEstimate(flops=0,transcendentals=0,bytes_accessed=int(micros*3.3e6))
def code_call(kernel, name, outs, *args):
    return pl.pallas_call(kernel, out_shape=[jax.ShapeDtypeStruct(s,t) for s,t in outs],
        in_specs=[pl.BlockSpec(memory_space=pltpu.VMEM)]*len(args), out_specs=[pl.BlockSpec(memory_space=pltpu.VMEM)]*len(outs),
        compiler_params=pltpu.CompilerParams(vmem_limit_bytes=32<<20), cost_estimate=takes(0.15), name=name)(*args)
def plane_kernel(*refs):
    n=len(refs)//2
    for i in range(0,n,2):
        (keep,got),(send,stay)=refs[i:i+2],refs[n+i:n+i+2]
        add_codes([At(keep,1),At(got,1)],At(send))
        add_codes([At(keep,0),At(got,0)],At(stay))
def line_kernel(*refs):
    stay_a,got_a,stay_b,got_b=refs[:4]; more=refs[4:-1]; out=refs[-1]
    for h,(stay,got) in enumerate(((stay_a,got_a),(stay_b,got_b))):
        add_codes([At(stay),At(got)]+[At(m,h) for m in more],At(out,h))
def final_kernel(*refs):
    stay_a,got_a,stay_b,got_b=refs[:4]; more=refs[4:-4]; vec,blocks,io,sums=refs[-4:]
    square=jnp.zeros((1,LANE),F32)
    for h,(stay,got) in enumerate(((stay_a,got_a),(stay_b,got_b))):
        for k,total in summed([At(stay),At(got)]+[At(m,h) for m in more]):
            square=square+jnp.sum(total*total,axis=0,keepdims=True)
            if k<18:
                g,v,half=k//6,k//2%3,k%2
                rows=slice(half*GROUP,(half+1)*GROUP)
                blocks[(h*3+g)*4+v,rows,:]=total[:,:BLOCK]
                blocks[(h*3+g)*4+3,rows,32*v:32*(v+1)]=total[:,BLOCK:]
            else:
                io[:,h,(k-18)*LANE:(k-17)*LANE]=total
    sums[0:23,:]=vec[0:23,:]
    sums[23:24,:]=jnp.broadcast_to(jnp.sum(square,keepdims=True),(1,D))
HALF=(PART,LANE)
def reduce_tree(ids, owners, operands, vec):
    send={}; keep={}; got={}; stay={}; far={}
    def make(k):
        send_a,keep_a,send_b,keep_b=weight_grads(k,ids,owners,operands)
        send[k]=(send_a,send_b); keep[k]=(keep_a,keep_b)
    def leave(k,*masks):
        got[k]=tuple(swap(part,"seq",mask) for part,mask in zip(send[k],masks))
    def plane(*pieces):
        outs=code_call(plane_kernel,"add_plane",[(HALF,I16)]*4*len(pieces),*[ref for k in pieces for ref in (keep[k][0],got[k][0],keep[k][1],got[k][1])])
        for i,k in enumerate(pieces):
            send_a,stay_a,send_b,stay_b=outs[4*i:4*i+4]
            stay[k]=(stay_a,stay_b); send[k]=(send_a,send_b)
            leave(k,1,2)
    def line(k,mask,*more):
        far[k]=swap(code_call(line_kernel,"add_line",[((2,)+HALF,I16)],stay[k][0],got[k][0],stay[k][1],got[k][1],*more)[0],"seq",mask)
    make(3); leave(3,2,1)
    make(2); leave(2,2,1)
    make(1)
    (got[3],got[2]),keep[1]=gate((got[3],got[2]),keep[1])
    plane(3,2)
    (send[1],ids),got[3],got[2]=gate((send[1],ids),got[3],got[2])
    line(3,4)
    leave(1,2,1)
    make(0)
    got[1],far[3],keep[0]=gate(got[1],far[3],keep[0])
    line(2,8,far[3])
    plane(1)
    line(1,4)
    send[0],got[1]=gate(send[0],got[1])
    leave(0,2,1)
    plane(0)
    return code_call(final_kernel,"add_final",[((24,BLOCK,BLOCK),F32),((IO,2,D),F32),((24,D),F32)],stay[0][0],got[0][0],stay[0][1],got[0][1],far[1],far[2],vec)

BLOCK=96; NEWTON=6; F32=jnp.float32; BF=jnp.bfloat16; LANE=128
def halves(x):
    hi=x.astype(BF); return hi,(x-hi.astype(F32)).astype(BF)
def left_of(parts):
    return jnp.concatenate(parts,axis=1)
def right_of(parts):
    hi,lo=parts
    rest=jnp.zeros((LANE-BLOCK,LANE),BF)
    top=jnp.concatenate([hi,lo],axis=1); low=jnp.concatenate([hi,jnp.zeros_like(lo)],axis=1)
    both=jnp.zeros((LANE-BLOCK,2*LANE),BF)
    return jnp.concatenate([top,both,low,both],axis=0)
def times(a,b):
    w=jnp.dot(left_of(a),right_of(b),preferred_element_type=F32)
    return w[:,:LANE]+w[:,LANE:]
def shampoo_kernel(sums_ref, grad_ref, left_ref, right_ref, block_ref, io_grad_ref, io_ref, io_first_ref, io_second_ref, vec_ref, vec_first_ref, vec_second_ref,
                   grad_out, left_out, right_out, block_out, io_first_out, io_second_out, io_out, vec_first_out, vec_second_out, vec_out, norm_out, *, beta, rate, eps, n_side):
    n_vec=vec_ref.shape[0]
    vec_grad=sums_ref[0:n_vec,:]
    norm=jnp.sqrt(sums_ref[23:24,0:1]+jnp.sum(vec_grad*vec_grad,keepdims=True))
    norm_out[...]=jnp.broadcast_to(norm,norm_out.shape)
    factor=jnp.minimum(1.0,clip_limit/norm)
    vec_first_out[...],vec_second_out[...],vec_out[...]=adam_update(vec_ref[...],vec_first_ref[...],vec_second_ref[...],vec_grad*factor,rate_vector,0.0)
    for m in range(2):
        parts=[ref[:,m,:] for ref in (io_ref,io_first_ref,io_second_ref,io_grad_ref)]
        io_first_out[:,m,:],io_second_out[:,m,:],io_out[:,m,:]=adam_update(*parts[:3],parts[3]*factor,rate_adam,weight_decay)
    row=lax.broadcasted_iota(jnp.int32,(BLOCK,LANE),0); col=lax.broadcasted_iota(jnp.int32,(BLOCK,LANE),1)
    eye=jnp.where(row==col,1.0,0.0)
    none=jnp.zeros((BLOCK,LANE-BLOCK),F32)
    def full(x): return jnp.concatenate([x,none],axis=1)
    def one(i,carry):
        stats=[]; grads=[]
        for j in range(n_side):
            s=i*n_side+j
            g=full(grad_ref[s]*factor)
            grad_out[s]=g[:,:BLOCK]
            g=halves(g); t=halves(full((grad_ref[s]*factor).T)); grads.append(g)
            l=beta*full(left_ref[s])+(1.0-beta)*times(g,t)
            r=beta*full(right_ref[s])+(1.0-beta)*times(t,g)
            left_out[s]=l[:,:BLOCK]; right_out[s]=r[:,:BLOCK]
            stats+=[l,r]
        regular=[m+eps*eye for m in stats]
        scaled=[2.5*lax.rsqrt(jnp.sum(m*m,keepdims=True)) for m in regular]
        moving=[m*s for m,s in zip(regular,scaled)]
        root=None
        for sweep in range(NEWTON):
            factors=[1.25*eye-0.25*m for m in moving]
            split=[halves(f) for f in factors]
            if sweep==0: root=[f*jnp.sqrt(jnp.sqrt(s)) for f,s in zip(factors,scaled)]
            else: root=[times(halves(x),f) for x,f in zip(root,split)]
            if sweep<NEWTON-1:
                square=[halves(times(f,f)) for f in split]
                fourth=[halves(times(q,q)) for q in square]
                moving=[times(q,halves(m)) for q,m in zip(fourth,moving)]
        for j in range(n_side):
            s=i*n_side+j
            d=times(halves(root[2*j]),grads[j])
            d=times(halves(d),halves(root[2*j+1]))
            block_out[s]=block_ref[s]-rate*d[:,:BLOCK]
        return carry
    lax.fori_loop(0,grad_ref.shape[0]//n_side,one,0)
def update_step(sums, grads, left, right, blocks, io_grad, io_set, vec_set, n_side=12):
    like=lambda *xs: [jax.ShapeDtypeStruct(x.shape,F32) for x in xs]
    args=(sums,grads,left,right,blocks,io_grad,*io_set,*vec_set)
    return pl.pallas_call(partial(shampoo_kernel,beta=beta_stat,rate=rate_shampoo,eps=root_eps,n_side=n_side),
        out_shape=like(grads,grads,grads,grads,*io_set,*vec_set)+[jax.ShapeDtypeStruct((8,LANE),F32)],
        in_specs=[vmem()]*len(args),out_specs=[vmem()]*11,
        compiler_params=pltpu.CompilerParams(vmem_limit_bytes=48<<20),name="update_step")(*args)


def fits(mesh):
    return mesh.shape["seq"] == 16 and mesh.shape["opt"] == 2


def sum_everywhere(value):
    value = value + swap(value, "opt", 1)
    for bit in range((lax.axis_size("seq") - 1).bit_length()):
        value = value + swap(value, "seq", 2**bit)
    return value


def to_heads(parts):
    return lax.all_to_all(parts, "seq", 0, 0, tiled=True)


def evens_first(rows):
    return rows.reshape((rows.shape[0] // 2, 2) + rows.shape[1:]).swapaxes(0, 1).reshape(rows.shape)


def fast_device(
    features,
    tile_mask,
    lengths,
    owners,
    layer_blocks,
    stat_left,
    stat_right,
    io_weights,
    io_first,
    io_second,
    vectors,
    vec_first,
    vec_second,
):
    tok_dev = features.shape[1]
    seq_index = lax.axis_index("seq")
    core_index = lax.axis_index("opt")
    ids = jnp.stack([seq_index, core_index]).astype(jnp.int32)
    low_targets = evens_first(features[0])
    chosen_rows = evens_first(tile_mask[0]).astype(jnp.float32)[:, None]
    lengths_row = lax.dynamic_index_in_dim(lengths, core_index, 0, keepdims=False)
    places = seq_index * tok_dev + evens_first(jnp.arange(tok_dev, dtype=jnp.int32))
    shards = gather_shards(layer_blocks, io_weights, tile_mask)
    block_rows, io_rows = shard_rows(seq_index, core_index)
    qkv_weight, out_weight, in_weight, tile_counts = join_weights(
        FIRST_PLAN, 0, shards, owners, block_rows, io_rows
    )
    tile_count = tile_counts[0, 0]
    hidden, early_low, by_head = front_step(
        low_targets,
        chosen_rows,
        sine_places(slide_offsets(lengths_row, places)),
        vectors,
        in_weight,
        qkv_weight,
        HEADS,
    )
    late_owners, by_head = gate(owners, by_head)
    up_weight, down_weight, head_weight, late_counts = join_weights(
        SECOND_PLAN, 1, shards, late_owners, block_rows, io_rows
    )
    own_head, head_weight = gate(to_heads(by_head), head_weight)
    head_out, mixed_parts, head_totals = attend(lengths, ids, own_head)
    mixed_low = to_heads(mixed_parts).reshape(D, tok_dev)
    grad_middle, grad_mixed, late_low, late_rows = mlp_step(
        tile_count,
        hidden,
        mixed_low,
        low_targets,
        chosen_rows,
        vectors,
        out_weight,
        up_weight,
        down_weight,
        head_weight,
    )
    grad_head_out = to_heads(grad_mixed.reshape(HEADS, HEAD_DIM, tok_dev))
    grad_parts = attend_back(lengths, ids, own_head, grad_head_out, head_out, head_totals)
    others = [swap(operand, "opt", 1) for operand in (early_low, mixed_low, late_low)]
    own_parts, others[0], others[1] = gate(to_heads(grad_parts), others[0], others[1])
    last_low, vec_grads = input_step(
        own_parts,
        hidden,
        grad_middle,
        chosen_rows,
        vectors,
        late_rows,
        qkv_weight,
        in_weight,
    )
    others.append(swap(last_low, "opt", 1))
    operands = []
    for pair in zip((early_low, mixed_low, late_low, last_low), others):
        operands += pair
    slot_sum, io_sum, own_sums = reduce_tree(ids, owners, operands, vec_grads)
    all_sums = sum_everywhere(own_sums)
    (
        block_grads,
        left_new,
        right_new,
        blocks_new,
        io_first_new,
        io_second_new,
        io_new,
        vec_first_new,
        vec_second_new,
        vec_new,
        norms,
    ) = update_step(
        all_sums,
        slot_sum,
        stat_left,
        stat_right,
        layer_blocks,
        io_sum,
        (io_weights, io_first, io_second),
        (vectors, vec_first, vec_second),
    )
    grad_norm = norms[0, 0]
    error_sum = all_sums[vectors.shape[0], 0]
    return (
        grad_norm,
        error_sum,
        tile_count,
        block_grads,
        left_new,
        right_new,
        blocks_new,
        io_first_new,
        io_second_new,
        io_new,
        vec_first_new,
        vec_second_new,
        vec_new,
    )


def solution(mesh):
    return jax.shard_map(
        fast_device if fits(mesh) else per_device,
        mesh=mesh,
        in_specs=(
            P("opt", "seq", None),
            P("opt", "seq"),
            P(),
            P(),
            P(("seq", "opt"), None, None),
            P(("seq", "opt"), None, None),
            P(("seq", "opt"), None, None),
            P(("seq", "opt"), None, None),
            P(("seq", "opt"), None, None),
            P(("seq", "opt"), None, None),
            P(),
            P(),
            P(),
        ),
        out_specs=(
            P(),
            P(),
            P(),
            P(("seq", "opt"), None, None),
            P(("seq", "opt"), None, None),
            P(("seq", "opt"), None, None),
            P(("seq", "opt"), None, None),
            P(("seq", "opt"), None, None),
            P(("seq", "opt"), None, None),
            P(("seq", "opt"), None, None),
            P(),
            P(),
            P(),
        ),
        check_vma=False,
    )
```

```python
from functools import partial
import math

import jax
import jax.numpy as jnp
import numpy as np
from jax import lax
from jax.experimental import pallas as pl
from jax.experimental.pallas import tpu as pltpu
from jax.sharding import PartitionSpec as P

D = 768
HEADS = 16
HEAD_DIM = 48
FF = 3072
FEAT = 1536
LAYERS = 1
BRANCHES = 5
SEG0 = 1024
BLOCK = 96
SLIDES = 4
NEWTON = 6
STEP = 10


norm_eps = 1e-05
clip_limit = 1.0
beta_one = 0.9
beta_two = 0.95
adam_eps = 1e-08
rate_adam = 0.01
rate_vector = 0.2
weight_decay = 0.05
beta_stat = 0.95
rate_shampoo = 0.05
root_eps = 1e-12
masked_score = -1e30
highest = lax.Precision.HIGHEST


def from_partner(value, axis, stride):
    mask = 2**stride
    pairs = [(source, source ^ mask) for source in range(lax.axis_size(axis))]
    return lax.ppermute(value, axis, pairs)


def for_sending(shard):

    def short(part):
        return part.astype(jnp.bfloat16) if part.dtype == jnp.float32 else part

    return jax.tree.map(short, shard)


def layer_norm(values, gain, shift):
    centred = values - jnp.mean(values, axis=-1, keepdims=True)
    spread = jnp.mean(centred * centred, axis=-1, keepdims=True)
    return centred * lax.rsqrt(spread + norm_eps) * gain + shift


def sine_places(places):
    half_width = D // 2
    freq_rates = jnp.exp(
        jnp.arange(half_width, dtype=jnp.float32) * (-math.log(10000.0) / half_width)
    )
    angles = (places.astype(jnp.float32) / 64.0)[:, None] * freq_rates[None, :]
    return jnp.concatenate([jnp.sin(angles), jnp.cos(angles)], axis=1)


def slide_ids(lengths_row, places):
    slide_ends = jnp.cumsum(lengths_row)
    return jnp.sum((places[..., None] >= slide_ends[:-1]).astype(jnp.int32), axis=-1)


def slide_offsets(lengths_row, places):
    slide_ends = jnp.cumsum(lengths_row)
    slide_starts = slide_ends - lengths_row
    owner_ids = slide_ids(lengths_row, places)
    match_rows = owner_ids[:, None] == jnp.arange(SLIDES, dtype=jnp.int32)[None, :]
    picked = jnp.sum(jnp.where(match_rows, slide_starts[None, :], 0), axis=1)
    return places - picked


def head_offsets(dilation):
    return np.arange(HEADS) % dilation


def pick_rows(values, dilation):
    row_count = values.shape[0] // dilation
    shaped = values.reshape((row_count, dilation) + values.shape[1:])
    return shaped[:, head_offsets(dilation), np.arange(HEADS)]


def spread_rows(values, dilation, filler):
    row_count = values.shape[0]
    hit_mask = np.arange(dilation)[:, None] == head_offsets(dilation)[None, :]
    hit_mask = hit_mask.reshape((1, dilation, HEADS) + (1,) * (values.ndim - 2))
    spread_out = jnp.where(hit_mask, values[:, None], filler)
    return spread_out.reshape((row_count * dilation,) + values.shape[1:])


def branch_geom(branch, tok_dev, seq_len):
    dilation = 2**branch
    segment = min(SEG0 * dilation, seq_len)
    return (dilation, segment, max(1, segment // tok_dev))


def branch_docs(lengths_row, first_place, row_count, dilation):
    places = (
        first_place
        + jnp.asarray(head_offsets(dilation), jnp.int32)[None, :]
        + dilation * jnp.arange(row_count, dtype=jnp.int32)[:, None]
    )
    return slide_ids(lengths_row, places)


def contract_rows(left, right):
    return lax.dot_general(
        left, right, (((0,), (0,)), ((), ())), preferred_element_type=jnp.float32
    )


def contract_cols(left, right):
    return lax.dot_general(
        left, right, (((1,), (1,)), ((), ())), preferred_element_type=jnp.float32
    )


def assemble(natural):
    per_layer = natural.reshape(LAYERS, -1, BLOCK, BLOCK)
    col_count = (4 * D + FF) // BLOCK
    wide_count = D // BLOCK * col_count
    upper_mats = per_layer[:, :wide_count].reshape(LAYERS, D // BLOCK, col_count, BLOCK, BLOCK)
    upper_mats = upper_mats.transpose(0, 1, 3, 2, 4).reshape(LAYERS, D, 4 * D + FF)
    lower_mats = per_layer[:, wide_count:].reshape(LAYERS, FF // BLOCK, D // BLOCK, BLOCK, BLOCK)
    lower_mats = lower_mats.transpose(0, 1, 3, 2, 4).reshape(LAYERS, FF, D)
    return (upper_mats, lower_mats)


def disassemble(upper_mats, lower_mats):
    col_count = (4 * D + FF) // BLOCK
    top_part = upper_mats.reshape(LAYERS, D // BLOCK, BLOCK, col_count, BLOCK).transpose(
        0, 1, 3, 2, 4
    )
    top_part = top_part.reshape(LAYERS, -1, BLOCK, BLOCK)
    bottom_part = lower_mats.reshape(LAYERS, FF // BLOCK, BLOCK, D // BLOCK, BLOCK).transpose(
        0, 1, 3, 2, 4
    )
    bottom_part = bottom_part.reshape(LAYERS, -1, BLOCK, BLOCK)
    return jnp.concatenate([top_part, bottom_part], axis=1).reshape(-1, BLOCK, BLOCK)


def unpack(vector_set):
    per_layer = 8 + FF // D
    return (
        vector_set[: LAYERS * per_layer].reshape(LAYERS, per_layer, D),
        vector_set[LAYERS * per_layer :],
    )


def collect_pairs(pieces, bit_counts, seq_index):
    pieces = list(pieces)
    for bit_id in range(max(bit_counts + [0])):
        active_ids = [branch for branch in range(len(pieces)) if bit_counts[branch] > bit_id]
        outgoing = jnp.concatenate([pieces[branch] for branch in active_ids], axis=0)
        partner = from_partner(outgoing, "seq", bit_id)
        lower_side = seq_index // 2**bit_id % 2 == 0
        offset_at = 0
        for branch in active_ids:
            my_part = pieces[branch]
            part_size = my_part.shape[0]
            their_part = partner[offset_at : offset_at + part_size]
            offset_at = offset_at + part_size
            pieces[branch] = jnp.where(
                lower_side,
                jnp.concatenate([my_part, their_part], 0),
                jnp.concatenate([their_part, my_part], 0),
            )
    return pieces


def return_pairs(pieces, bit_counts, seq_index):
    pieces = list(pieces)
    for bit_id in reversed(range(max(bit_counts + [0]))):
        active_ids = [branch for branch in range(len(pieces)) if bit_counts[branch] > bit_id]
        lower_side = seq_index // 2**bit_id % 2 == 0
        kept_parts, sent_parts = ([], [])
        for branch in active_ids:
            half_size = pieces[branch].shape[0] // 2
            first_part = pieces[branch][:half_size]
            second_part = pieces[branch][half_size:]
            kept_parts.append(jnp.where(lower_side, first_part, second_part))
            sent_parts.append(jnp.where(lower_side, second_part, first_part))
        partner = from_partner(for_sending(jnp.concatenate(sent_parts, axis=0)), "seq", bit_id)
        offset_at = 0
        for branch, kept_part in zip(active_ids, kept_parts):
            part_size = kept_part.shape[0]
            pieces[branch] = kept_part + partner[offset_at : offset_at + part_size]
            offset_at = offset_at + part_size
    return pieces


def score_block(query_rows, key_rows, query_docs, key_docs):
    raw_scores = jnp.einsum(
        "sqhd,skhd->shqk", query_rows, key_rows, preferred_element_type=jnp.float32
    ) * HEAD_DIM ** (-0.5)
    same_slide = (
        jnp.transpose(query_docs, (0, 2, 1))[..., None]
        == jnp.transpose(key_docs, (0, 2, 1))[:, :, None, :]
    )
    return jnp.where(same_slide, raw_scores, masked_score)


def attend_forward(packed, lengths_row, seq_len, seq_index):
    tok_dev = packed.shape[0]
    triple = packed.reshape(tok_dev, 3, HEADS, HEAD_DIM)
    queries, key_all, value_all = (triple[:, 0], triple[:, 1], triple[:, 2])
    geoms = [branch_geom(branch, tok_dev, seq_len) for branch in range(BRANCHES)]
    local_pairs = [
        jnp.stack([pick_rows(key_all, geom[0]), pick_rows(value_all, geom[0])], axis=1).reshape(
            -1, 2 * D
        )
        for geom in geoms
    ]
    bit_counts = [geom[2].bit_length() - 1 for geom in geoms]
    joined = collect_pairs(local_pairs, bit_counts, seq_index)
    kept_state, outputs, totals_all = ([], [], [])
    for branch in range(BRANCHES):
        dilation, segment, group_size = geoms[branch]
        sections = max(1, tok_dev // segment)
        query_rows = pick_rows(queries, dilation).reshape(sections, -1, HEADS, HEAD_DIM)
        pair_rows = joined[branch].reshape(sections, -1, 2, HEADS, HEAD_DIM)
        key_rows = pair_rows[:, :, 0]
        value_rows = pair_rows[:, :, 1]
        query_docs = branch_docs(
            lengths_row, seq_index * tok_dev, tok_dev // dilation, dilation
        ).reshape(sections, -1, HEADS)
        group_first = seq_index // group_size * group_size * tok_dev
        key_docs = branch_docs(lengths_row, group_first, joined[branch].shape[0], dilation).reshape(
            sections, -1, HEADS
        )
        scores = score_block(query_rows, key_rows, query_docs, key_docs)
        totals = jax.nn.logsumexp(scores, axis=-1)
        softmax_rows = jnp.exp(scores - totals[..., None]).astype(jnp.bfloat16)
        output = jnp.einsum(
            "shqk,skhd->sqhd", softmax_rows, value_rows, preferred_element_type=jnp.float32
        ).reshape(-1, HEADS, HEAD_DIM)
        totals_rows = jnp.transpose(totals, (0, 2, 1)).reshape(-1, HEADS)
        kept_state.append(
            (query_rows, key_rows, value_rows, query_docs, key_docs, output, totals_rows)
        )
        outputs.append(spread_rows(output, dilation, 0.0))
        totals_all.append(spread_rows(totals_rows, dilation, masked_score))
    stacked = jnp.stack(totals_all)
    grand_total = jax.nn.logsumexp(stacked, axis=0)
    mixed_out = jnp.zeros_like(outputs[0])
    for branch in range(BRANCHES):
        mixed_out = mixed_out + jnp.exp(stacked[branch] - grand_total)[..., None] * outputs[branch]
    return (mixed_out, (mixed_out, grand_total, kept_state))


def attend_backward(grad_mixed, attention_state, seq_len, seq_index):
    mixed_out, grand_total, kept_state = attention_state
    tok_dev = grad_mixed.shape[0]
    score_scale = HEAD_DIM ** (-0.5)
    grad_query = jnp.zeros(grad_mixed.shape, jnp.float32)
    key_terms, bit_counts, dilations = ([], [], [])
    for branch in range(BRANCHES):
        dilation, segment, group_size = branch_geom(branch, tok_dev, seq_len)
        query_rows, key_rows, value_rows, query_docs, key_docs, output, totals_rows = kept_state[
            branch
        ]
        sections = query_rows.shape[0]
        weight = jnp.exp(totals_rows - pick_rows(grand_total, dilation))
        grad_picked = pick_rows(grad_mixed, dilation)
        grad_output = (
            (weight[..., None] * grad_picked)
            .astype(jnp.bfloat16)
            .reshape(sections, -1, HEADS, HEAD_DIM)
        )
        grad_totals = weight * jnp.sum(
            grad_picked * (output - pick_rows(mixed_out, dilation)), axis=-1
        )
        grad_totals = jnp.transpose(grad_totals.reshape(sections, -1, HEADS), (0, 2, 1))
        totals = jnp.transpose(totals_rows.reshape(sections, -1, HEADS), (0, 2, 1))
        softmax_rows = jnp.exp(
            score_block(query_rows, key_rows, query_docs, key_docs) - totals[..., None]
        )
        grad_value = jnp.einsum(
            "shqk,sqhd->skhd",
            softmax_rows.astype(jnp.bfloat16),
            grad_output,
            preferred_element_type=jnp.float32,
        )
        grad_probs = jnp.einsum(
            "sqhd,skhd->shqk", grad_output, value_rows, preferred_element_type=jnp.float32
        )
        inner_sum = jnp.sum(softmax_rows * grad_probs, axis=-1, keepdims=True)
        grad_scores = (softmax_rows * (grad_probs - inner_sum + grad_totals[..., None])).astype(
            jnp.bfloat16
        )
        grad_q = (
            jnp.einsum("shqk,skhd->sqhd", grad_scores, key_rows, preferred_element_type=jnp.float32)
            * score_scale
        )
        grad_k = (
            jnp.einsum(
                "shqk,sqhd->skhd", grad_scores, query_rows, preferred_element_type=jnp.float32
            )
            * score_scale
        )
        grad_query = grad_query + spread_rows(grad_q.reshape(-1, HEADS, HEAD_DIM), dilation, 0.0)
        key_terms.append(
            jnp.stack(
                [grad_k.reshape(-1, HEADS, HEAD_DIM), grad_value.reshape(-1, HEADS, HEAD_DIM)],
                axis=1,
            ).reshape(-1, 2 * D)
        )
        bit_counts.append(group_size.bit_length() - 1)
        dilations.append(dilation)
    own_terms = return_pairs(key_terms, bit_counts, seq_index)
    grad_key = jnp.zeros(grad_mixed.shape, jnp.float32)
    grad_val = jnp.zeros(grad_mixed.shape, jnp.float32)
    for branch in range(BRANCHES):
        pair_rows = own_terms[branch].reshape(-1, 2, HEADS, HEAD_DIM)
        grad_key = grad_key + spread_rows(pair_rows[:, 0], dilations[branch], 0.0)
        grad_val = grad_val + spread_rows(pair_rows[:, 1], dilations[branch], 0.0)
    return jnp.stack([grad_query, grad_key, grad_val], axis=1).reshape(tok_dev, 3 * D)


def layer_forward(hidden, upper_mat, lower_mat, row_set, lengths_row, seq_len, seq_index):
    normed = layer_norm(hidden, row_set[0], row_set[1]).astype(jnp.bfloat16)
    biases = jnp.concatenate([row_set[2], jnp.zeros_like(row_set[2]), row_set[3]])
    packed = (
        jnp.dot(normed, upper_mat[:, : 3 * D], preferred_element_type=jnp.float32) + biases[None, :]
    ).astype(jnp.bfloat16)
    mixed_out, attention_state = attend_forward(packed, lengths_row, seq_len, seq_index)
    mixed_low = mixed_out.reshape(-1, D).astype(jnp.bfloat16)
    middle = (
        hidden
        + jnp.dot(mixed_low, upper_mat[:, 3 * D : 4 * D], preferred_element_type=jnp.float32)
        + row_set[4][None, :]
    )
    second = layer_norm(middle, row_set[5], row_set[6]).astype(jnp.bfloat16)
    before = (
        jnp.dot(second, upper_mat[:, 4 * D :], preferred_element_type=jnp.float32)
        + row_set[8:].reshape(-1)[None, :]
    )
    active = jax.nn.gelu(before, approximate=True).astype(jnp.bfloat16)
    result = (
        middle
        + jnp.dot(active, lower_mat, preferred_element_type=jnp.float32)
        + row_set[7][None, :]
    )
    return (result, (hidden, normed, mixed_low, middle, second, before, active, attention_state))


def layer_backward(grad_result, upper_mat, lower_mat, row_set, layer_state, seq_len, seq_index):
    hidden, normed, mixed_low, middle, second, before, active, attention_state = layer_state
    grad_out = grad_result.astype(jnp.bfloat16)
    grad_lower = contract_rows(active, grad_out)
    grad_fc2_bias = jnp.sum(grad_out, axis=0, dtype=jnp.float32)
    grad_active = contract_cols(grad_out, lower_mat)
    gelu_value, gelu_back = jax.vjp(partial(jax.nn.gelu, approximate=True), before)
    grad_before = gelu_back(grad_active)[0].astype(jnp.bfloat16)
    grad_fc1 = contract_rows(second, grad_before)
    grad_fc1_bias = jnp.sum(grad_before, axis=0, dtype=jnp.float32)
    grad_second = contract_cols(grad_before, upper_mat[:, 4 * D :])
    norm_value, norm_back = jax.vjp(layer_norm, middle, row_set[5], row_set[6])
    grad_middle, grad_gain_two, grad_shift_two = norm_back(grad_second)
    grad_middle = grad_middle + grad_result
    grad_branch = grad_middle.astype(jnp.bfloat16)
    grad_proj = contract_rows(mixed_low, grad_branch)
    grad_proj_bias = jnp.sum(grad_branch, axis=0, dtype=jnp.float32)
    grad_mixed = contract_cols(grad_branch, upper_mat[:, 3 * D : 4 * D]).reshape(
        -1, HEADS, HEAD_DIM
    )
    grad_packed = attend_backward(grad_mixed, attention_state, seq_len, seq_index).astype(
        jnp.bfloat16
    )
    grad_qkv = contract_rows(normed, grad_packed)
    packed_sums = jnp.sum(grad_packed, axis=0, dtype=jnp.float32)
    grad_normed = contract_cols(grad_packed, upper_mat[:, : 3 * D])
    first_value, first_back = jax.vjp(layer_norm, hidden, row_set[0], row_set[1])
    grad_hidden, grad_gain_one, grad_shift_one = first_back(grad_normed)
    grad_hidden = grad_hidden + grad_middle
    grad_upper = jnp.concatenate([grad_qkv, grad_proj, grad_fc1], axis=1)
    small_rows = jnp.stack(
        [
            grad_gain_one,
            grad_shift_one,
            packed_sums[:D],
            packed_sums[2 * D :],
            grad_proj_bias,
            grad_gain_two,
            grad_shift_two,
            grad_fc2_bias,
        ]
    )
    grad_rows = jnp.concatenate([small_rows, grad_fc1_bias.reshape(-1, D)], axis=0)
    return (grad_hidden, (grad_upper, grad_lower, grad_rows))


def inverse_root(matrix):
    identity = jnp.eye(matrix.shape[-1], dtype=jnp.float32)
    regular = matrix + root_eps * identity
    frob_norm = jnp.sqrt(jnp.sum(regular * regular, axis=(1, 2), keepdims=True))
    scaled = 2.5 / frob_norm
    root_mat = identity * jnp.sqrt(jnp.sqrt(scaled))
    moving = regular * scaled
    for sweep_id in range(NEWTON):
        factor = (5.0 * identity - moving) * 0.25
        root_mat = jnp.einsum("kij,kjl->kil", root_mat, factor, precision=highest)
        square = jnp.einsum("kij,kjl->kil", factor, factor, precision=highest)
        fourth = jnp.einsum("kij,kjl->kil", square, square, precision=highest)
        moving = jnp.einsum("kij,kjl->kil", fourth, moving, precision=highest)
    return root_mat


def adam_update(weight, first_mom, second_mom, grad, rate, decay):
    first_new = beta_one * first_mom + (1.0 - beta_one) * grad
    second_new = beta_two * second_mom + (1.0 - beta_two) * grad * grad
    first_hat = first_new / (1.0 - beta_one**STEP)
    second_hat = second_new / (1.0 - beta_two**STEP)
    return (
        first_new,
        second_new,
        weight - rate * (first_hat / (jnp.sqrt(second_hat) + adam_eps) + decay * weight),
    )


def per_device(
    features,
    tile_mask,
    lengths,
    owners,
    layer_blocks,
    stat_left,
    stat_right,
    io_weights,
    io_first,
    io_second,
    vectors,
    vec_first,
    vec_second,
):
    tok_dev = features.shape[1]
    seq_size = lax.axis_size("seq")
    seq_len = tok_dev * seq_size
    seq_index = lax.axis_index("seq")
    core_index = lax.axis_index("opt")
    targets = features[0].astype(jnp.float32)
    chosen = tile_mask[0][:, None] > 0
    lengths_row = lax.dynamic_index_in_dim(lengths, core_index, 0, keepdims=False)
    places = seq_index * tok_dev + jnp.arange(tok_dev, dtype=jnp.int32)
    all_blocks, all_io = (
        lax.all_gather(layer_blocks.astype(jnp.bfloat16), ("seq", "opt"), axis=0, tiled=True),
        lax.all_gather(io_weights.astype(jnp.bfloat16), ("seq", "opt"), axis=0, tiled=True),
    )
    natural = jnp.zeros_like(all_blocks).at[owners].set(all_blocks)
    upper_mats, lower_mats = assemble(natural)
    tile_count = lax.psum(jnp.sum(tile_mask.astype(jnp.float32)), ("seq", "opt"))
    layer_rows, tail_rows = unpack(vectors)
    token_vec = tail_rows[3 + FEAT // D :].reshape(FEAT)
    head_bias = tail_rows[3 : 3 + FEAT // D].reshape(FEAT)
    inputs = jnp.where(chosen, token_vec[None, :], targets).astype(jnp.bfloat16)
    in_weight = all_io[:, 0]
    head_weight = all_io[:, 1]
    hidden = jnp.dot(inputs, in_weight, preferred_element_type=jnp.float32) + tail_rows[2][None, :]
    hidden = hidden + sine_places(slide_offsets(lengths_row, places))
    layer_id = 0
    hidden, layer_state = layer_forward(
        hidden,
        upper_mats[layer_id],
        lower_mats[layer_id],
        layer_rows[layer_id],
        lengths_row,
        seq_len,
        seq_index,
    )
    layer_states = [layer_state]
    final, final_back = jax.vjp(layer_norm, hidden, tail_rows[0], tail_rows[1])
    final_low = final.astype(jnp.bfloat16)
    predict = contract_cols(final_low, head_weight) + head_bias[None, :]
    difference = predict - targets
    error_local = jnp.sum(jnp.where(chosen, difference * difference, 0.0))
    grad_pred = jnp.where(chosen, 2.0 * difference / tile_count, 0.0).astype(jnp.bfloat16)
    grad_head = contract_rows(grad_pred, final_low)
    grad_head_bias = jnp.sum(grad_pred, axis=0, dtype=jnp.float32)
    grad_final = jnp.dot(grad_pred, head_weight, preferred_element_type=jnp.float32)
    grad_hidden, grad_gain_last, grad_shift_last = final_back(grad_final)
    layer_grads = [None] * LAYERS
    for layer_id in reversed(range(LAYERS)):
        grad_hidden, layer_grads[layer_id] = layer_backward(
            grad_hidden,
            upper_mats[layer_id],
            lower_mats[layer_id],
            layer_rows[layer_id],
            layer_states[layer_id],
            seq_len,
            seq_index,
        )
    grad_in_low = grad_hidden.astype(jnp.bfloat16)
    grad_in = contract_rows(inputs, grad_in_low)
    grad_in_bias = jnp.sum(grad_in_low, axis=0, dtype=jnp.float32)
    grad_inputs = contract_cols(grad_in_low, in_weight)
    grad_token = jnp.sum(jnp.where(chosen, grad_inputs, 0.0), axis=0)
    grad_upper = jnp.stack([item[0] for item in layer_grads])
    grad_lower = jnp.stack([item[1] for item in layer_grads])
    slot_grads = disassemble(grad_upper, grad_lower)[owners]
    io_grads = jnp.stack([grad_in, grad_head], axis=1)
    vec_grads = jnp.concatenate(
        [
            jnp.stack([item[2] for item in layer_grads]).reshape(-1, D),
            jnp.stack([grad_gain_last, grad_shift_last, grad_in_bias]),
            grad_head_bias.reshape(-1, D),
            grad_token.reshape(-1, D),
        ],
        axis=0,
    )
    slot_sum, io_sum = (
        lax.psum_scatter(slot_grads, ("seq", "opt"), scatter_dimension=0, tiled=True),
        lax.psum_scatter(io_grads, ("seq", "opt"), scatter_dimension=0, tiled=True),
    )
    vec_sum, error_sum = lax.psum((vec_grads, error_local), ("seq", "opt"))
    local_sq = jnp.sum(slot_sum * slot_sum) + jnp.sum(io_sum * io_sum)
    grad_norm = jnp.sqrt(lax.psum(local_sq, ("seq", "opt")) + jnp.sum(vec_sum * vec_sum))
    factor = jnp.minimum(1.0, clip_limit / grad_norm)
    block_grads = slot_sum * factor
    left_new = beta_stat * stat_left + (1.0 - beta_stat) * jnp.einsum(
        "kij,klj->kil", block_grads, block_grads, precision=highest
    )
    right_new = beta_stat * stat_right + (1.0 - beta_stat) * jnp.einsum(
        "kji,kjl->kil", block_grads, block_grads, precision=highest
    )
    direction = jnp.einsum("kij,kjl->kil", inverse_root(left_new), block_grads, precision=highest)
    direction = jnp.einsum("kij,kjl->kil", direction, inverse_root(right_new), precision=highest)
    blocks_new = layer_blocks - rate_shampoo * direction
    io_first_new, io_second_new, io_new = adam_update(
        io_weights, io_first, io_second, io_sum * factor, rate_adam, weight_decay
    )
    vec_first_new, vec_second_new, vec_new = adam_update(
        vectors, vec_first, vec_second, vec_sum * factor, rate_vector, 0.0
    )
    return (
        grad_norm,
        error_sum,
        tile_count,
        block_grads,
        left_new,
        right_new,
        blocks_new,
        io_first_new,
        io_second_new,
        io_new,
        vec_first_new,
        vec_second_new,
        vec_new,
    )


BF=jnp.bfloat16; LANE=128; IO=48
def swap(value, axis, mask):
    return lax.ppermute(value, axis, [(s, s ^ mask) for s in range(lax.axis_size(axis))])
def gate(*values):
    return lax.optimization_barrier(values)

GROUP_ROWS=3*BLOCK
IO_AT=2*GROUP_ROWS; COUNT_AT=IO_AT+6*IO; THIRD_AT=COUNT_AT+16
SHARD_HALF=THIRD_AT+GROUP_ROWS
PIECE=8*SHARD_HALF; THIRDS=8*THIRD_AT
def pack_kernel(blocks_ref, io_ref, mask_ref, first_ref, second_ref, both_ref):
    count=jnp.sum(mask_ref[...].astype(jnp.float32),keepdims=True)
    lane=lax.broadcasted_iota(jnp.int32,(BLOCK,LANE),1)
    pad=lambda x: jnp.concatenate([x,jnp.zeros((BLOCK,LANE-BLOCK),x.dtype)],axis=1)
    for h,out_ref in enumerate((first_ref,second_ref)):
        for g in range(3):
            b=[pad(blocks_ref[(h*3+g)*4+t]) for t in range(4)]
            for v in range(3):
                tile=jnp.where(lane<BLOCK,b[v],pltpu.roll(b[3],BLOCK-32*v,1))
                at=(g*GROUP_ROWS if g<2 else THIRD_AT)+v*BLOCK
                out_ref[at:at+BLOCK,:]=tile.astype(BF)
        for v in range(6):
            at=IO_AT+v*IO
            out_ref[at:at+IO,:]=io_ref[:,h,v*LANE:(v+1)*LANE].astype(BF)
        out_ref[COUNT_AT:THIRD_AT,:]=jnp.broadcast_to(count,(16,LANE)).astype(BF)
        both_ref[h*THIRD_AT:(h+1)*THIRD_AT,:]=out_ref[:THIRD_AT,:]
def vmem(): return pl.BlockSpec(memory_space=pltpu.VMEM)
def smem(): return pl.BlockSpec(memory_space=pltpu.SMEM)
def hbm(): return pl.BlockSpec(memory_space=pltpu.HBM)
def from_hbm(body, name, outs, ins, scratch, smem_args=(), late=(), vmem_mib=48, micros=10):
    n_s,n_i,n_o=len(smem_args),len(ins),len(outs)
    def kernel(*refs):
        scalars,args,results=refs[:n_s],refs[n_s:n_s+n_i],refs[n_s+n_i:n_s+n_i+n_o]
        rest=refs[n_s+n_i+n_o:]
        held,made,more=rest[:n_i],rest[n_i:n_i+n_o],rest[n_i+n_o:-2]
        in_sem,out_sem=rest[-2:]
        loads=[pltpu.make_async_copy(a,h,in_sem.at[i]) for i,(a,h) in enumerate(zip(args,held))]
        for c in loads: c.start()
        for i,c in enumerate(loads):
            if i not in late: c.wait()
        body(*([loads[i].wait for i in late]),*scalars,*held,*made,*more)
        stores=[pltpu.make_async_copy(m,r,out_sem.at[i]) for i,(m,r) in enumerate(zip(made,results))]
        for c in stores: c.start()
        for c in stores: c.wait()
    ins=[pltpu.with_memory_space_constraint(a,pltpu.HBM) for a in ins]
    return pl.pallas_call(kernel,out_shape=[pltpu.HBM(s,t) for s,t in outs],
        in_specs=[smem()]*n_s+[hbm()]*n_i,out_specs=[hbm()]*n_o,
        scratch_shapes=[pltpu.VMEM(a.shape,a.dtype) for a in ins]+[pltpu.VMEM(s,t) for s,t in outs]+list(scratch)
            +[pltpu.SemaphoreType.DMA((n_i,)),pltpu.SemaphoreType.DMA((n_o,))],
        compiler_params=pltpu.CompilerParams(vmem_limit_bytes=vmem_mib<<20),
        cost_estimate=pl.CostEstimate(flops=0,transcendentals=0,bytes_accessed=int(micros*3.3e6)),name=name)(*smem_args,*ins)
def pack_shard(blocks, io, mask):
    return pl.pallas_call(pack_kernel,out_shape=[jax.ShapeDtypeStruct((n,LANE),BF) for n in (SHARD_HALF,SHARD_HALF,2*THIRD_AT)],in_specs=[vmem()]*3,out_specs=[vmem()]*3,name="pack_shard")(blocks,io,mask)

HOPS=(("opt",1),("seq",1),("seq",2),("seq",4),("seq",8))
def hop(value, k):
    return value+swap(value,*HOPS[k])

def stack_rows(arrays, *plans):
    n=len(arrays); total=sum(len(p) for p in plans)
    shapes=[(sum(c for _,_,c in p),LANE) for p in plans]
    def kernel(*refs):
        ins,outs,held,(in_sem,out_sem)=refs[:n],refs[n:n+len(plans)],refs[n+len(plans):-2],refs[-2:]
        copies=[]; stores=[]
        for i,plan in enumerate(plans):
            at=0
            for k,first,count in plan:
                copies.append((i,pltpu.make_async_copy(ins[k].at[pl.ds(first,count)],held[i].at[pl.ds(at,count)],in_sem.at[len(copies)])))
                copies[-1][1].start()
                at+=count
        for i,out in enumerate(outs):
            for k,c in copies:
                if k==i: c.wait()
            stores.append(pltpu.make_async_copy(held[i],out,out_sem.at[i]))
            stores[-1].start()
        for c in stores: c.wait()
    return pl.pallas_call(kernel,out_shape=[jax.ShapeDtypeStruct(s,BF) for s in shapes],
        in_specs=[pl.BlockSpec(memory_space=pl.ANY)]*n,out_specs=[pl.BlockSpec(memory_space=pl.ANY)]*len(plans),
        scratch_shapes=[pltpu.VMEM(s,BF) for s in shapes]+[pltpu.SemaphoreType.DMA((total,)),pltpu.SemaphoreType.DMA((len(plans),))],
        compiler_params=pltpu.CompilerParams(vmem_limit_bytes=16<<20),name="stack_rows")(*arrays)

def gather_tree(first, second, both):
    near=[None]*4; cross=[None]*4; third=[None]*4
    def first_step(k,a,b):
        near[k]=(swap(a,"seq",1),swap(b,"seq",2))
    def second_step(k,a,b,rows):
        sent=stack_rows([a[0],near[k][0],b[0],near[k][1]],[(0,a[1],rows),(1,0,rows)],[(2,b[1],rows),(3,0,rows)])
        cross[k]=(swap(sent[0],"seq",2),swap(sent[1],"seq",1))
    def halves_of(far): return (far,0),(far,THIRD_AT)
    far1=swap(both,"seq",4)
    far2=swap(both,"seq",8)
    first_step(0,first,second)
    second_step(0,(first,0),(second,0),SHARD_HALF)
    arrays=[first,second,*near[0],*cross[0]]
    units=[(0,0),(1,0),(2,0),(3,0),(4,0),(4,SHARD_HALF),(5,0),(5,SHARD_HALF)]
    third[0]=stack_rows(arrays,[(k,at+THIRD_AT,GROUP_ROWS) for k,at in units])[0]
    third[2]=swap(third[0],"seq",8)
    third[1]=swap(third[0],"seq",4)
    first_step(1,far1[:THIRD_AT],far1[THIRD_AT:])
    first_step(2,far2[:THIRD_AT],far2[THIRD_AT:])
    far3=swap(far2,"seq",4)
    near[1],near[2],far3=gate(near[1],near[2],far3)
    second_step(1,*halves_of(far1),THIRD_AT)
    first_step(3,far3[:THIRD_AT],far3[THIRD_AT:])
    near[2],near[3]=gate(near[2],near[3])
    second_step(2,*halves_of(far2),THIRD_AT)
    near[3],third[2]=gate(near[3],third[2])
    second_step(3,*halves_of(far3),THIRD_AT)
    third[3]=swap(third[2],"seq",4)
    out=list(stack_rows(arrays+[third[0]],[(k,at,THIRD_AT) for k,at in units]+[(len(arrays),0,third[0].shape[0])]))
    for k,far in ((1,far1),(2,far2),(3,far3)):
        arrays=[far,*near[k],*cross[k],third[k]]
        out+=stack_rows(arrays,[(i,0,part.shape[0]) for i,part in enumerate(arrays)])
    return out+[swap(piece,"opt",1) for piece in out]

HELD=64*SHARD_HALF
N_BLOCK=768
def load_shards(bufs, held, sem, fourths):
    rows=bufs[0].shape[0]
    loads=[pltpu.make_async_copy(b,held.at[pl.ds(k*rows,rows)],sem.at[k]) for k,b in enumerate(bufs)]
    for c in loads: c.start()
    fourths()
    for k,c in enumerate(loads):
        c.wait()
        def unpack(u,carry,k=k):
            for g in range(3):
                at=k*PIECE+(u*THIRD_AT+g*GROUP_ROWS if g<2 else THIRDS+u*GROUP_ROWS)
                parts=[held[pl.ds(pl.multiple_of(at+v*BLOCK,16),BLOCK),BLOCK:] for v in range(3)]
                to=HELD+((k*8+u)*3+g)*BLOCK
                held[pl.ds(pl.multiple_of(to,16),BLOCK),:BLOCK]=jnp.concatenate(parts,axis=1)
            return carry
        lax.fori_loop(0,8,unpack,0,unroll=8)

def join_kernel(plan, io_out, owners_ref, row_ref, io_ref, *refs):
    bufs=refs[:8]; n_out=len(plan); outs=refs[8:8+n_out]; io_ref_out,count_ref=refs[8+n_out:8+n_out+2]
    held,stage,where,in_sem,out_sem,io_sem=refs[8+n_out+2:]
    def invert():
        def one(i,carry):
            for j in range(8):
                where[owners_ref[i*8+j]]=row_ref[i*8+j]
            return carry
        lax.fori_loop(0,N_BLOCK//8,one,0)
    load_shards(bufs,held,in_sem,invert)
    def io_copy(d,total):
        at=io_ref[io_out,d]
        for v in range(6):
            pltpu.make_async_copy(held.at[pl.ds(pl.multiple_of(at+v*IO,16),IO)],
                io_ref_out.at[pl.ds(pl.multiple_of(d*IO,IO),IO),pl.ds(v*LANE,LANE)],io_sem).start()
        return total+held[pl.ds(pl.multiple_of(at+6*IO,16),16),:].astype(jnp.float32)
    count_ref[...]=lax.fori_loop(0,io_ref.shape[1],io_copy,jnp.zeros((16,LANE),jnp.float32))
    def block(n):
        return held[pl.ds(pl.multiple_of(where[n],16),BLOCK),:BLOCK]
    pending=[]; index=0
    for (first,stride,rows,stripes),out in zip(plan,outs):
        per=8//stripes if stripes<8 else 1
        for i0 in range(0,rows,per):
            slot=index%2
            if index>=2:
                for c in pending[index-2]: c.wait()
            for b in range(per):
                def one(c,carry,b=b,i0=i0):
                    n=first+(i0+b)*stride+4*c
                    stage[slot,:,pl.ds(pl.multiple_of((b*stripes+c)*4*BLOCK,128),4*BLOCK)]=jnp.concatenate([block(n+t) for t in range(4)],axis=1)
                    return carry
                lax.fori_loop(0,stripes,one,0,unroll=stripes)
            w=stripes*4*BLOCK
            cs=[pltpu.make_async_copy(stage.at[slot,:,pl.ds(b*w,w)],out.at[pl.ds((i0+b)*BLOCK,BLOCK)],out_sem.at[slot,b]) for b in range(per)]
            for c in cs: c.start()
            pending.append(cs); index+=1
    for cs in pending[-2:]:
        for c in cs: c.wait()
    pltpu.make_async_copy(io_ref_out,io_ref_out,io_sem).wait()

COLS=(4*D+FF)//BLOCK
FIRST_PLAN=((0,COLS,8,6),(24,COLS,8,2))
SECOND_PLAN=((32,COLS,8,8),(8*COLS,8,32,2))
def join_weights(plan, io_out, bufs, owners, rows, io_rows):
    shapes=[(r*BLOCK,s*4*BLOCK) for _,_,r,s in plan]+[(FEAT,D)]
    return pl.pallas_call(partial(join_kernel,plan,io_out),
        out_shape=[pltpu.HBM(s,BF) for s in shapes]+[jax.ShapeDtypeStruct((16,LANE),jnp.float32)],
        in_specs=[smem()]*3+[hbm()]*8, out_specs=[hbm()]*len(shapes)+[vmem()],
        scratch_shapes=[pltpu.VMEM((HELD+N_BLOCK//4*BLOCK,LANE),BF),pltpu.VMEM((2,BLOCK,FF),BF),pltpu.SMEM((N_BLOCK,),jnp.int32),
            pltpu.SemaphoreType.DMA((8,)),pltpu.SemaphoreType.DMA((2,4)),pltpu.SemaphoreType.DMA],
        compiler_params=pltpu.CompilerParams(vmem_limit_bytes=40<<20), cost_estimate=pl.CostEstimate(flops=0,transcendentals=0,bytes_accessed=int((13 if io_out==0 else 17)*3.3e6)), name="join_weights")(owners,rows,io_rows,*[pltpu.with_memory_space_constraint(b,pltpu.HBM) for b in bufs])

def shard_rows(seq_index, core):
    def unit(dev,h):
        rel=(dev//2)^seq_index; xy=rel%4
        u=jnp.where(xy==0,h,jnp.where(h==0,jnp.where(xy==1,2,xy+2),jnp.where(xy==2,3,jnp.where(xy==1,6,7))))
        return (rel//4+4*((dev%2)^core))*8+u
    slot=jnp.arange(N_BLOCK,dtype=jnp.int32); s=slot%24
    u=unit(slot//24,s//12); g=s%12//4; t=s%4
    start=u//8*PIECE+jnp.where(g<2,u%8*THIRD_AT+g*GROUP_ROWS,THIRDS+u%8*GROUP_ROWS)
    rows=jnp.where(t<3,start+t*BLOCK,HELD+(u*3+g)*BLOCK)
    dev=jnp.arange(32,dtype=jnp.int32)
    io=jnp.stack([unit(dev,h)//8*PIECE+unit(dev,h)%8*THIRD_AT+IO_AT for h in (0,1)])
    return rows.astype(jnp.int32),io.astype(jnp.int32)
def gather_shards(layer_blocks, io_weights, mask):
    return gather_tree(*pack_shard(layer_blocks,io_weights,mask))

HD=48; HEADS=16; SLIDES=4; SEG=1024; N=2048; H=512; TQ=256; TQF=512; TK=256
C2=HD**-0.5*math.log2(math.e)
def place_facts(index, head, lengths_ref, core):
    parity=(head+(index>>(H.bit_length()-1)))&1
    pos=((index>>(SEG.bit_length()-1))<<(SEG.bit_length()-1))+((index&(H-1))<<1)+parity
    slide=jnp.zeros_like(index); end=jnp.int32(0)
    for i in range(SLIDES-1):
        end=end+lengths_ref[core,i]
        slide=slide+jnp.where(pos>=end,1,0)
    d=(pos-head)&15
    level=jnp.where((d&1)==0,jnp.where((d&3)==0,jnp.where((d&7)==0,jnp.where(d==0,4,3),2),1),0)
    return slide.astype(jnp.float32), level.astype(jnp.float32)

def arrange(src, dst, odd):
    for pair in range(8):
        first, second = src[2*pair], src[2*pair+1]
        turn=lambda t: jnp.concatenate([t[:,64:],t[:,:64]],axis=1)
        ft, st = turn(first), turn(second)
        low=lax.broadcasted_iota(jnp.int32,first.shape,1)<64
        evens=jnp.where(low,first,st); odds=jnp.where(low,ft,second)
        near=jnp.where(odd,odds,evens); far=jnp.where(odd,evens,odds)
        at=(pair//4)*SEG+(pair%4)*128
        dst[:,at:at+128]=near.astype(dst.dtype); dst[:,at+H:at+H+128]=far.astype(dst.dtype)

def restore(get, put, odd):
    for pair in range(8):
        at=(pair//4)*SEG+(pair%4)*128
        near, far = get(at), get(at+H)
        evens=jnp.where(odd,far,near); odds=jnp.where(odd,near,far)
        turn=lambda t: jnp.concatenate([t[:,64:],t[:,:64]],axis=1)
        low=lax.broadcasted_iota(jnp.int32,evens.shape,1)<64
        put(2*pair, jnp.where(low,evens,turn(odds)))
        put(2*pair+1, jnp.where(low,turn(evens),odds))

def setup(lengths_ref, ids_ref, slide_k, level_k, row_facts):
    head, core = ids_ref[0], ids_ref[1]
    def fill(i, c):
        idx=lax.broadcasted_iota(jnp.int32,(TK,128),0)+i*TK
        s,l=place_facts(idx,head,lengths_ref,core)
        slide_k[pl.ds(pl.multiple_of(i*TK,TK),TK),:]=s
        level_k[pl.ds(pl.multiple_of(i*TK,TK),TK),:]=l
        return c
    lax.fori_loop(0,N//TK,fill,0)
    idx=lax.broadcasted_iota(jnp.int32,(8,N),1)
    s,l=place_facts(idx,head,lengths_ref,core)
    row_facts[0:8,:]=s; row_facts[8:16,:]=l

def key_rows(seg, near):
    own=[(seg*SEG+i*TK,True) for i in range(SEG//TK)]
    other=[((1-seg)*SEG+i*TK,False) for i in range(H//TK)] if near else []
    return own+other

def wide(x, queries): return jnp.concatenate([x]*(queries//128),axis=1)

def forward_kernel(lengths_ref, ids_ref, qkv_ref, o_ref, out_ref, lse_ref, qkvT, krow, slide_k, level_k, row_facts, s_ref, p_ref):
    odd=lax.rem(ids_ref[0],2)==1
    arrange(qkv_ref, qkvT, odd)
    setup(lengths_ref, ids_ref, slide_k, level_k, row_facts)
    for i in range(N//128):
        krow[i*128:(i+1)*128,:]=qkvT[HD:2*HD,i*128:(i+1)*128].astype(jnp.float32).T.astype(jnp.bfloat16)
    for seg in range(2):
        for near in (True,False):
            tiles=key_rows(seg,near)
            def part(c, carry, seg=seg, near=near, tiles=tiles):
                at=pl.multiple_of(seg*SEG+(0 if near else H)+c*TQF,TQF)
                qT=qkvT[0:HD,pl.ds(at,TQF)]
                sq=row_facts[0:1,pl.ds(at,TQF)]; lq=row_facts[8:9,pl.ds(at,TQF)]
                top=jnp.full((8,TQF),-jnp.inf,jnp.float32)
                for t,(r,own) in enumerate(tiles):
                    s=jnp.dot(krow[r:r+TK,:],qT,preferred_element_type=jnp.float32)
                    s=jnp.where(wide(slide_k[r:r+TK,:],TQF)==sq,s,-1e30)
                    s_ref[t*TK:(t+1)*TK,:]=s
                    top=jnp.maximum(top,jnp.max(s.reshape(TK//8,8,TQF),axis=0))
                m=jnp.max(top,axis=0,keepdims=True)
                total=jnp.zeros((8,TQF),jnp.float32)
                for t,(r,own) in enumerate(tiles):
                    e=jnp.exp2((s_ref[t*TK:(t+1)*TK,:]-m)*C2)
                    if near:
                        lk=wide(level_k[r:r+TK,:],TQF)
                        e=e*(jnp.minimum(lk,lq)+1.0 if own else jnp.minimum(lk,lq))
                    total=total+jnp.sum(e.reshape(TK//8,8,TQF),axis=0)
                    p_ref[t*TK:(t+1)*TK,:]=e.astype(jnp.bfloat16)
                l=jnp.sum(total,axis=0,keepdims=True)
                acc=jnp.zeros((HD,TQF),jnp.float32)
                acc=jnp.dot(qkvT[2*HD:3*HD,seg*SEG:(seg+1)*SEG],p_ref[0:SEG,:],preferred_element_type=jnp.float32)
                if near:
                    acc=acc+jnp.dot(qkvT[2*HD:3*HD,(1-seg)*SEG:(1-seg)*SEG+H],p_ref[SEG:SEG+H,:],preferred_element_type=jnp.float32)
                o_ref[:,pl.ds(at,TQF)]=acc/l
                lse_ref[:,pl.ds(at,TQF)]=jnp.broadcast_to(m*C2+jnp.log2(l),(8,TQF))
                return carry
            lax.fori_loop(0,H//TQF,part,0)
    def put(c,v): out_ref[c]=v.astype(jnp.bfloat16)
    restore(lambda at: o_ref[:,at:at+128], put, odd)

def turned_product(a,b): return lax.dot_general(a,b,(((1,),(1,)),((),())),preferred_element_type=jnp.float32)
def backward_kernel(lengths_ref, ids_ref, qkv_ref, do_ref, o_ref, lse_ref, out_ref, qkvT, doT, rows, slide_k, level_k, row_facts, dqT, dkv, p_ref, ds_ref):
    odd=lax.rem(ids_ref[0],2)==1
    arrange(qkv_ref, qkvT, odd)
    arrange(do_ref, doT, odd)
    setup(lengths_ref, ids_ref, slide_k, level_k, row_facts)
    for i in range(N//128):
        l=slice(i*128,(i+1)*128)
        for j in range(2):
            rows[j,l,:]=qkvT[(j+1)*HD:(j+2)*HD,l].astype(jnp.float32).T.astype(jnp.bfloat16)
    dkv[...]=jnp.zeros_like(dkv)
    for seg in range(2):
        for near in (True,False):
            tiles=key_rows(seg,near)
            def part(c, carry, seg=seg, near=near, tiles=tiles):
                at=pl.multiple_of(seg*SEG+(0 if near else H)+c*TQ,TQ)
                qT=qkvT[0:HD,pl.ds(at,TQ)]; gT=doT[:,pl.ds(at,TQ)]
                sq=row_facts[0:1,pl.ds(at,TQ)]; lq=row_facts[8:9,pl.ds(at,TQ)]
                lse=lse_ref[0:1,pl.ds(at,TQ)]
                inner=jnp.sum(gT.astype(jnp.float32)*o_ref[:,pl.ds(at,TQ)],axis=0,keepdims=True)
                for t,(r,own) in enumerate(tiles):
                    s=jnp.dot(rows[0,r:r+TK,:],qT,preferred_element_type=jnp.float32)
                    dp=jnp.dot(rows[1,r:r+TK,:],gT,preferred_element_type=jnp.float32)
                    e=jnp.exp2(s*C2-lse)
                    if near:
                        lk=wide(level_k[r:r+TK,:],TQ)
                        e=e*(jnp.minimum(lk,lq)+1.0 if own else jnp.minimum(lk,lq))
                    e=jnp.where(wide(slide_k[r:r+TK,:],TQ)==sq,e,0.0)
                    p_ref[t*TK:(t+1)*TK,:]=e.astype(jnp.bfloat16)
                    ds_ref[t*TK:(t+1)*TK,:]=(e*(dp-inner)).astype(jnp.bfloat16)
                dq=jnp.dot(qkvT[HD:2*HD,seg*SEG:(seg+1)*SEG],ds_ref[0:SEG,:],preferred_element_type=jnp.float32)
                if near:
                    dq=dq+jnp.dot(qkvT[HD:2*HD,(1-seg)*SEG:(1-seg)*SEG+H],ds_ref[SEG:SEG+H,:],preferred_element_type=jnp.float32)
                dqT[:,pl.ds(at,TQ)]=dq*HD**-0.5
                own=slice(seg*SEG,(seg+1)*SEG)
                dkv[0,:,own]+=turned_product(qT,ds_ref[0:SEG,:])
                dkv[1,:,own]+=turned_product(gT,p_ref[0:SEG,:])
                if near:
                    oth=slice((1-seg)*SEG,(1-seg)*SEG+H)
                    dkv[0,:,oth]+=turned_product(qT,ds_ref[SEG:SEG+H,:])
                    dkv[1,:,oth]+=turned_product(gT,p_ref[SEG:SEG+H,:])
                return carry
            lax.fori_loop(0,H//TQ,part,0)
    def putter(j):
        def put(c,v): out_ref[c,j*HD:(j+1)*HD,:]=v.astype(jnp.bfloat16)
        return put
    restore(lambda at: dqT[:,at:at+128], putter(0), odd)
    restore(lambda at: dkv[0,:,at:at+128]*HD**-0.5, putter(1), odd)
    restore(lambda at: dkv[1,:,at:at+128], putter(2), odd)

def attend(lengths, ids, qkv):
    return from_hbm(forward_kernel,"attend_forward",[((HD,N),F32),((16,HD,128),BF),((8,N),F32)],[qkv],
        [pltpu.VMEM((3*HD,N),BF),pltpu.VMEM((N,HD),BF),pltpu.VMEM((N,128),F32),pltpu.VMEM((N,128),F32),pltpu.VMEM((16,N),F32),
            pltpu.VMEM((SEG+H,TQF),F32),pltpu.VMEM((SEG+H,TQF),BF)],(lengths,ids))
def attend_back(lengths, ids, qkv, do, o, lse):
    return from_hbm(backward_kernel,"attend_backward",[((16,3*HD,128),BF)],[qkv,do,o,lse],
        [pltpu.VMEM((3*HD,N),BF),pltpu.VMEM((HD,N),BF),pltpu.VMEM((2,N,HD),BF),pltpu.VMEM((N,128),F32),pltpu.VMEM((N,128),F32),pltpu.VMEM((16,N),F32),
            pltpu.VMEM((HD,N),F32),pltpu.VMEM((2,HD,N),F32),pltpu.VMEM((SEG+H,TQ),BF),pltpu.VMEM((SEG+H,TQ),BF)],(lengths,ids),micros=13)[0]

F32=jnp.float32
EPS=1e-05
def norm_parts(x):
    centred=x-jnp.mean(x,axis=-1,keepdims=True)
    spread=lax.rsqrt(jnp.mean(centred*centred,axis=-1,keepdims=True)+EPS)
    return centred*spread,spread
def norm_back(grad,unit,spread,gain):
    inner=grad*gain
    back=spread*(inner-jnp.mean(inner,axis=-1,keepdims=True)-unit*jnp.mean(inner*unit,axis=-1,keepdims=True))
    return back,jnp.sum(grad*unit,axis=0,keepdims=True),jnp.sum(grad,axis=0,keepdims=True)
def put_turned(ref,at,x):
    for c in range(x.shape[1]//LANE):
        ref[at+c*LANE:at+(c+1)*LANE,:]=x[:,c*LANE:(c+1)*LANE].astype(F32).T.astype(BF)
def turned(ref,rows):
    return jnp.concatenate([ref[c*LANE:(c+1)*LANE,:].astype(F32).T for c in range(rows//LANE)],axis=1)
def mm(a,b): return jnp.dot(a,b,preferred_element_type=F32)
def mm_t(a,b): return lax.dot_general(a,b,(((1,),(1,)),((),())),preferred_element_type=F32)
LATE_ROWS=4*D+2*FF+FEAT
GELU_A=math.sqrt(2.0/math.pi); GELU_B=0.044715
def mlp_kernel(up_here, down_here, head_here, count_ref, hidden_ref, mixed_ref, targets_ref, chosen_ref, vec_ref, wo_ref, up_ref, down_ref, head_ref,
               middle_grad_ref, mixed_grad_ref, late_ref, rows_ref, kept):
    row=lambda i: vec_ref[i:i+1,:]
    mixed=turned(mixed_ref,D).astype(BF)
    middle=hidden_ref[...]+mm(mixed,wo_ref[...])+row(4)
    unit2,spread2=norm_parts(middle)
    second=(unit2*row(5)+row(6)).astype(BF)
    put_turned(late_ref,0,second)
    result=middle+row(7)
    up_here(); down_here()
    for c in range(FF//D):
        s=slice(c*D,(c+1)*D)
        before=mm(second,up_ref[:,s])+row(8+c)
        kept[:,s]=before
        active=(before*(0.5*(1.0+jnp.tanh(GELU_A*(before+GELU_B*(before*before*before)))))).astype(BF)
        put_turned(late_ref,D+c*D,active)
        result=result+mm(active,down_ref[s,:])
    unit,spread=norm_parts(result)
    final=(unit*row(12)+row(13)).astype(BF)
    put_turned(late_ref,3*D+2*FF+FEAT,final)
    head_here()
    chosen=chosen_ref[...]>0.0
    error=jnp.zeros((1,1),F32); grad_final=jnp.zeros_like(middle)
    for c in range(FEAT//D):
        s=slice(c*D,(c+1)*D)
        difference=mm_t(final,head_ref[s,:])+row(15+c)-targets_ref[:,s].astype(F32)
        error=error+jnp.sum(jnp.where(chosen,difference*difference,0.0),keepdims=True)
        pred=jnp.where(chosen,2.0*difference/count_ref[0],0.0).astype(BF)
        put_turned(late_ref,3*D+2*FF+c*D,pred)
        rows_ref[10+c:11+c,:]=jnp.sum(pred.astype(F32),axis=0,keepdims=True)
        grad_final=grad_final+mm(pred,head_ref[s,:])
    rows_ref[12:13,:]=jnp.broadcast_to(error,(1,D))
    grad_result,rows_ref[8:9,:],rows_ref[9:10,:]=norm_back(grad_final,unit,spread,row(12))
    grad_out=grad_result.astype(BF)
    put_turned(late_ref,2*D+2*FF,grad_out)
    rows_ref[3:4,:]=jnp.sum(grad_out.astype(F32),axis=0,keepdims=True)
    grad_second=jnp.zeros_like(middle)
    for c in range(FF//D):
        s=slice(c*D,(c+1)*D)
        grad_active=mm_t(grad_out,down_ref[s,:])
        x=kept[:,s]
        t=jnp.tanh(GELU_A*(x+GELU_B*(x*x*x)))
        slope=0.5*(1.0+t)+x*(0.5*(1.0-t*t)*(GELU_A*(1.0+3.0*GELU_B*(x*x))))
        grad_before=(grad_active*slope).astype(BF)
        put_turned(late_ref,2*D+FF+c*D,grad_before)
        rows_ref[4+c:5+c,:]=jnp.sum(grad_before.astype(F32),axis=0,keepdims=True)
        grad_second=grad_second+mm_t(grad_before,up_ref[:,s])
    back,rows_ref[1:2,:],rows_ref[2:3,:]=norm_back(grad_second,unit2,spread2,row(5))
    grad_middle=back+grad_result
    middle_grad_ref[...]=grad_middle
    grad_branch=grad_middle.astype(BF)
    put_turned(late_ref,D+FF,grad_branch)
    rows_ref[0:1,:]=jnp.sum(grad_branch.astype(F32),axis=0,keepdims=True)
    mixed_grad_ref[...]=mm_t(wo_ref[...],grad_branch).astype(BF)
    rows_ref[13:16,:]=jnp.zeros((3,D),F32)
def mlp_step(count, hidden, mixed, targets, chosen, vectors, wo, up, down, head):
    t=hidden.shape[0]
    low=lambda rows: ((rows,t),BF)
    return from_hbm(mlp_kernel,"mlp_step",[((t,D),F32),low(D),low(LATE_ROWS),((16,D),F32)],
        [hidden,mixed,targets,chosen,vectors,wo,up,down,head],[pltpu.VMEM((t,FF),F32)],(count.reshape(1),),late=(6,7,8),micros=13)

def input_kernel(in_here, parts_ref, hidden_ref, middle_grad_ref, chosen_ref, vec_ref, rows_ref, qkv_ref, in_ref, last_ref, sums_ref):
    heads,wide,t=parts_ref.shape; hd=wide//3
    for j in range(3):
        for h in range(heads):
            last_ref[j*D+h*hd:j*D+(h+1)*hd,:]=parts_ref[h,j*hd:(j+1)*hd,:]
    packed=last_ref[:3*D,:]
    grad_t=mm(qkv_ref[...],packed)
    grad=jnp.concatenate([grad_t[c*LANE:(c+1)*LANE,:].T for c in range(D//LANE)],axis=1)
    unit,spread=norm_parts(hidden_ref[...])
    back,gain,shift=norm_back(grad,unit,spread,vec_ref[0:1,:])
    grad_hidden=back+middle_grad_ref[...]
    low=grad_hidden.astype(BF)
    put_turned(last_ref,3*D,low)
    sums_ref[0:1,:]=gain; sums_ref[1:2,:]=shift
    ones=jnp.ones((8,t),BF)
    sums_ref[2:3,:]=mm_t(ones,packed[:D])[0:1]
    sums_ref[3:4,:]=mm_t(ones,packed[2*D:])[0:1]
    sums_ref[4:14,:]=rows_ref[0:10,:]
    sums_ref[14:15,:]=jnp.sum(low.astype(F32),axis=0,keepdims=True)
    sums_ref[15:17,:]=rows_ref[10:12,:]
    in_here()
    masked=jnp.where(chosen_ref[...]>0.0,low.astype(F32),0.0).astype(BF)
    for c in range(FEAT//D):
        sums_ref[17+c:18+c,:]=jnp.sum(mm_t(masked,in_ref[c*D:(c+1)*D,:]),axis=0,keepdims=True)
    sums_ref[19:20,:]=rows_ref[12:13,:]
    sums_ref[20:24,:]=jnp.zeros((4,D),F32)
def input_step(parts, hidden, middle_grad, chosen, vectors, rows, qkv, w_in):
    t=hidden.shape[0]
    return from_hbm(input_kernel,"input_step",[((4*D,t),BF),((24,D),F32)],[parts,hidden,middle_grad,chosen,vectors,rows,qkv,w_in],[],late=(7,),micros=5)

def front_kernel(qkv_here, features_ref, chosen_ref, places_ref, vec_ref, in_ref, qkv_ref, hidden_ref, early_ref, heads_ref, turned_ref):
    row=lambda i: vec_ref[i:i+1,:]
    chosen=chosen_ref[...]>0.0
    hidden=places_ref[...]+row(14)
    for c in range(FEAT//D):
        s=slice(c*D,(c+1)*D)
        part=jnp.where(chosen,row(17+c),features_ref[:,s].astype(F32)).astype(BF)
        put_turned(early_ref,D+c*D,part)
        hidden=hidden+mm(part,in_ref[s,:])
    hidden_ref[...]=hidden
    unit,spread=norm_parts(hidden)
    normed=(unit*row(0)+row(1)).astype(BF)
    put_turned(early_ref,0,normed)
    qkv_here()
    heads,wide,t=heads_ref.shape; hd=wide//3
    for j in range(3):
        out=mm(normed,qkv_ref[:,j*D:(j+1)*D])
        if j!=1: out=out+row(2 if j==0 else 3)
        put_turned(turned_ref,j*D,out.astype(BF))
        for h in range(heads):
            heads_ref[h,j*hd:(j+1)*hd,:]=turned_ref[j*D+h*hd:j*D+(h+1)*hd,:]
def front_step(features, chosen, places, vectors, w_in, qkv, heads):
    t=features.shape[0]
    return from_hbm(front_kernel,"front_step",[((t,D),F32),((D+FEAT,t),BF),((heads,3*D//heads,t),BF)],[features,chosen,places,vectors,w_in,qkv],
        [pltpu.VMEM((3*D,t),BF)],late=(5,),micros=5)

I16=jnp.int16; F32=jnp.float32; BF=jnp.bfloat16
GROUP=48; LANE=128; IO=48
STEP_Q=32000.0
UNITS=24; CODE_ROWS=32; PART=UNITS*GROUP+CODE_ROWS
A_ROWS=3*D+FF; X_ROWS=3*D+D+FF+D
ROUND=12582912.0

def encode(x):
    top=jnp.max(jnp.abs(x),axis=0,keepdims=True)
    code=jnp.ceil(jnp.log2(jnp.maximum(top,1e-30))*256.0)
    v=x*(STEP_Q*jnp.exp2(code*(-1.0/256.0)))
    return ((v+ROUND)-ROUND).astype(jnp.int32).astype(I16), code
def scale_of(code16):
    return jnp.exp2(code16.astype(jnp.int32).astype(F32)*(1.0/256.0))*(1.0/STEP_Q)
def pack_codes(codes):
    codes=codes+[jnp.zeros((CODE_ROWS-len(codes),LANE),F32)]
    return jnp.concatenate(codes,axis=0).astype(jnp.int32).astype(I16)

EARLY,MIXED,LATE,LAST=range(4)
PARTS=(((EARLY,0,D),("a",0)),((MIXED,0,D),("a",D)),((LATE,0,D),("a",2*D)),((LATE,D,FF),("a",3*D)),
    ((LAST,0,3*D),("x",0)),((LATE,D+FF,D),("x",3*D)),((LATE,2*D+FF,FF),("x",4*D)),((LATE,2*D+2*FF,D),("x",4*D+FF)),
    ((EARLY,D,FEAT),("a_in",0)),((LAST,3*D,D),("x_in",0)),((LATE,3*D+2*FF,FEAT),("a_head",0)),((LATE,3*D+2*FF+FEAT,D),("x_head",0)))
def grads_kernel(zone, ids_ref, owners_ref, *refs):
    operands=refs[:8]; outs=refs[8:12]
    a_all,x_all,a_in,x_in,a_head,x_head,sem=refs[12:]
    buf_of=dict(a=a_all,x=x_all,a_in=a_in,x_in=x_in,a_head=a_head,x_head=x_head)
    seq,core=ids_ref[0],ids_ref[1]
    copies=[]
    for (source,first,count),(buf,at) in PARTS:
        for side in range(2):
            c=pltpu.make_async_copy(operands[2*source+side].at[pl.ds(first,count)],buf_of[buf].at[pl.ds(at,count),pl.ds(side*LANE,LANE)],sem.at[len(copies)])
            c.start(); copies.append(c)
    for c in copies: c.wait()
    lane=lax.broadcasted_iota(jnp.int32,(BLOCK,LANE),1)
    cols=(4*D+FF)//BLOCK; wide_count=D//BLOCK*cols
    def block(slot):
        n=owners_ref[slot]
        i=n//cols; j=n%cols
        m=n-wide_count
        group=jnp.where(j>=3*D//BLOCK,1,0)+jnp.where(j>=4*D//BLOCK,1,0)
        a_at=jnp.where(m<0,i*BLOCK+group*D,3*D+m//(D//BLOCK)*BLOCK)
        x_at=jnp.where(m<0,j*BLOCK,4*D+FF+m%(D//BLOCK)*BLOCK)
        a=a_all[pl.ds(pl.multiple_of(a_at,32),BLOCK),:]
        x=x_all[pl.ds(pl.multiple_of(x_at,32),BLOCK),:]
        w=lax.dot_general(a,x,(((1,),(1,)),((),())),preferred_element_type=F32)
        return jnp.concatenate([w,jnp.zeros((BLOCK,LANE-BLOCK),F32)],axis=1)
    for out,h,first,step in ((outs[0],0,2,1),(outs[2],1,1,2),(outs[1],0,0,1),(outs[3],1,0,2)):
        def one(j,carry,out=out,h=h,first=first,step=step):
            device=2*jnp.bitwise_xor(seq,zone*4+first+step*j)+core
            codes=[]
            for g in range(3):
                w=[block(device*24+(h*3+g)*4+t) for t in range(4)]
                for v in range(3):
                    tile=jnp.where(lane<BLOCK,w[v],pltpu.roll(w[3],BLOCK-32*v,1))
                    for half in range(2):
                        q,code=encode(tile[half*GROUP:(half+1)*GROUP])
                        at=((g*3+v)*2+half)*GROUP
                        out[j,at:at+GROUP,:]=q; codes.append(code)
            a_ref,x_ref=((a_in,x_in),(a_head,x_head))[h]
            w=lax.dot_general(a_ref[pl.ds(pl.multiple_of(device*IO,16),IO),:],x_ref[...],(((1,),(1,)),((),())),preferred_element_type=F32)
            for v in range(6):
                q,code=encode(w[:,v*LANE:(v+1)*LANE])
                at=(18+v)*GROUP
                out[j,at:at+GROUP,:]=q; codes.append(code)
            out[j,UNITS*GROUP:,:]=pack_codes(codes)
            return carry
        lax.fori_loop(0,2,one,0)

def weight_grads(zone, ids, owners, operands):
    n=len(operands)
    return pl.pallas_call(partial(grads_kernel,zone),
        out_shape=[jax.ShapeDtypeStruct((2,PART,LANE),I16)]*4,
        in_specs=[pl.BlockSpec(memory_space=pltpu.SMEM)]*2+[pl.BlockSpec(memory_space=pl.ANY)]*n,
        out_specs=[pl.BlockSpec(memory_space=pltpu.VMEM)]*4,
        scratch_shapes=[pltpu.VMEM((A_ROWS,2*LANE),BF),pltpu.VMEM((X_ROWS,2*LANE),BF),pltpu.VMEM((FEAT,2*LANE),BF),pltpu.VMEM((D,2*LANE),BF),
            pltpu.VMEM((FEAT,2*LANE),BF),pltpu.VMEM((D,2*LANE),BF),pltpu.SemaphoreType.DMA((2*len(PARTS),))],
        compiler_params=pltpu.CompilerParams(vmem_limit_bytes=40<<20), cost_estimate=takes(0.8), name="weight_grads")(ids,owners,*operands)

class At:
    def __init__(s,ref,*i): s.ref,s.i=ref,i
    def __getitem__(s,k): return s.ref[(*s.i,k,slice(None))]
    def __setitem__(s,k,v): s.ref[(*s.i,k,slice(None))]=v
def summed(views):
    scales=[scale_of(v[UNITS*GROUP:PART]) for v in views]
    for k in range(UNITS):
        total=None
        for v,s in zip(views,scales):
            x=v[k*GROUP:(k+1)*GROUP].astype(jnp.int32).astype(F32)*s[k:k+1,:]
            total=x if total is None else total+x
        yield k,total
def add_codes(views, out):
    codes=[]
    for k,total in summed(views):
        q,code=encode(total)
        out[k*GROUP:(k+1)*GROUP]=q
        codes.append(code)
    out[UNITS*GROUP:PART]=pack_codes(codes)
def takes(micros):
    return pl.CostEstimate(flops=0,transcendentals=0,bytes_accessed=int(micros*3.3e6))
def code_call(kernel, name, outs, *args):
    return pl.pallas_call(kernel, out_shape=[jax.ShapeDtypeStruct(s,t) for s,t in outs],
        in_specs=[pl.BlockSpec(memory_space=pltpu.VMEM)]*len(args), out_specs=[pl.BlockSpec(memory_space=pltpu.VMEM)]*len(outs),
        compiler_params=pltpu.CompilerParams(vmem_limit_bytes=32<<20), cost_estimate=takes(0.15), name=name)(*args)
def plane_kernel(*refs):
    n=len(refs)//2
    for i in range(0,n,2):
        (keep,got),(send,stay)=refs[i:i+2],refs[n+i:n+i+2]
        add_codes([At(keep,1),At(got,1)],At(send))
        add_codes([At(keep,0),At(got,0)],At(stay))
def line_kernel(*refs):
    stay_a,got_a,stay_b,got_b=refs[:4]; more=refs[4:-1]; out=refs[-1]
    for h,(stay,got) in enumerate(((stay_a,got_a),(stay_b,got_b))):
        add_codes([At(stay),At(got)]+[At(m,h) for m in more],At(out,h))
def final_kernel(*refs):
    stay_a,got_a,stay_b,got_b=refs[:4]; more=refs[4:-4]; vec,blocks,io,sums=refs[-4:]
    square=jnp.zeros((1,LANE),F32)
    for h,(stay,got) in enumerate(((stay_a,got_a),(stay_b,got_b))):
        for k,total in summed([At(stay),At(got)]+[At(m,h) for m in more]):
            square=square+jnp.sum(total*total,axis=0,keepdims=True)
            if k<18:
                g,v,half=k//6,k//2%3,k%2
                rows=slice(half*GROUP,(half+1)*GROUP)
                blocks[(h*3+g)*4+v,rows,:]=total[:,:BLOCK]
                blocks[(h*3+g)*4+3,rows,32*v:32*(v+1)]=total[:,BLOCK:]
            else:
                io[:,h,(k-18)*LANE:(k-17)*LANE]=total
    sums[0:23,:]=vec[0:23,:]
    sums[23:24,:]=jnp.broadcast_to(jnp.sum(square,keepdims=True),(1,D))
HALF=(PART,LANE)
def reduce_tree(ids, owners, operands, vec):
    send={}; keep={}; got={}; stay={}; far={}
    def make(k):
        send_a,keep_a,send_b,keep_b=weight_grads(k,ids,owners,operands)
        send[k]=(send_a,send_b); keep[k]=(keep_a,keep_b)
    def leave(k,*masks):
        got[k]=tuple(swap(part,"seq",mask) for part,mask in zip(send[k],masks))
    def plane(*pieces):
        outs=code_call(plane_kernel,"add_plane",[(HALF,I16)]*4*len(pieces),*[ref for k in pieces for ref in (keep[k][0],got[k][0],keep[k][1],got[k][1])])
        for i,k in enumerate(pieces):
            send_a,stay_a,send_b,stay_b=outs[4*i:4*i+4]
            stay[k]=(stay_a,stay_b); send[k]=(send_a,send_b)
            leave(k,1,2)
    def line(k,mask,*more):
        far[k]=swap(code_call(line_kernel,"add_line",[((2,)+HALF,I16)],stay[k][0],got[k][0],stay[k][1],got[k][1],*more)[0],"seq",mask)
    make(3); leave(3,2,1)
    make(2); leave(2,2,1)
    make(1)
    (got[3],got[2]),keep[1]=gate((got[3],got[2]),keep[1])
    plane(3,2)
    (send[1],ids),got[3],got[2]=gate((send[1],ids),got[3],got[2])
    line(3,4)
    leave(1,2,1)
    make(0)
    got[1],far[3],keep[0]=gate(got[1],far[3],keep[0])
    line(2,8,far[3])
    plane(1)
    line(1,4)
    send[0],got[1]=gate(send[0],got[1])
    leave(0,2,1)
    plane(0)
    return code_call(final_kernel,"add_final",[((24,BLOCK,BLOCK),F32),((IO,2,D),F32),((24,D),F32)],stay[0][0],got[0][0],stay[0][1],got[0][1],far[1],far[2],vec)

BLOCK=96; NEWTON=6; F32=jnp.float32; BF=jnp.bfloat16; LANE=128
def halves(x):
    hi=x.astype(BF); return hi,(x-hi.astype(F32)).astype(BF)
def left_of(parts):
    return jnp.concatenate(parts,axis=1)
def right_of(parts):
    hi,lo=parts
    rest=jnp.zeros((LANE-BLOCK,LANE),BF)
    top=jnp.concatenate([hi,lo],axis=1); low=jnp.concatenate([hi,jnp.zeros_like(lo)],axis=1)
    both=jnp.zeros((LANE-BLOCK,2*LANE),BF)
    return jnp.concatenate([top,both,low,both],axis=0)
def times(a,b):
    w=jnp.dot(left_of(a),right_of(b),preferred_element_type=F32)
    return w[:,:LANE]+w[:,LANE:]
def shampoo_kernel(sums_ref, grad_ref, left_ref, right_ref, block_ref, io_grad_ref, io_ref, io_first_ref, io_second_ref, vec_ref, vec_first_ref, vec_second_ref,
                   grad_out, left_out, right_out, block_out, io_first_out, io_second_out, io_out, vec_first_out, vec_second_out, vec_out, norm_out, *, beta, rate, eps, n_side):
    n_vec=vec_ref.shape[0]
    vec_grad=sums_ref[0:n_vec,:]
    norm=jnp.sqrt(sums_ref[23:24,0:1]+jnp.sum(vec_grad*vec_grad,keepdims=True))
    norm_out[...]=jnp.broadcast_to(norm,norm_out.shape)
    factor=jnp.minimum(1.0,clip_limit/norm)
    vec_first_out[...],vec_second_out[...],vec_out[...]=adam_update(vec_ref[...],vec_first_ref[...],vec_second_ref[...],vec_grad*factor,rate_vector,0.0)
    for m in range(2):
        parts=[ref[:,m,:] for ref in (io_ref,io_first_ref,io_second_ref,io_grad_ref)]
        io_first_out[:,m,:],io_second_out[:,m,:],io_out[:,m,:]=adam_update(*parts[:3],parts[3]*factor,rate_adam,weight_decay)
    row=lax.broadcasted_iota(jnp.int32,(BLOCK,LANE),0); col=lax.broadcasted_iota(jnp.int32,(BLOCK,LANE),1)
    eye=jnp.where(row==col,1.0,0.0)
    none=jnp.zeros((BLOCK,LANE-BLOCK),F32)
    def full(x): return jnp.concatenate([x,none],axis=1)
    def one(i,carry):
        stats=[]; grads=[]
        for j in range(n_side):
            s=i*n_side+j
            g=full(grad_ref[s]*factor)
            grad_out[s]=g[:,:BLOCK]
            g=halves(g); t=halves(full((grad_ref[s]*factor).T)); grads.append(g)
            l=beta*full(left_ref[s])+(1.0-beta)*times(g,t)
            r=beta*full(right_ref[s])+(1.0-beta)*times(t,g)
            left_out[s]=l[:,:BLOCK]; right_out[s]=r[:,:BLOCK]
            stats+=[l,r]
        regular=[m+eps*eye for m in stats]
        scaled=[2.5*lax.rsqrt(jnp.sum(m*m,keepdims=True)) for m in regular]
        moving=[m*s for m,s in zip(regular,scaled)]
        root=None
        for sweep in range(NEWTON):
            factors=[1.25*eye-0.25*m for m in moving]
            split=[halves(f) for f in factors]
            if sweep==0: root=[f*jnp.sqrt(jnp.sqrt(s)) for f,s in zip(factors,scaled)]
            else: root=[times(halves(x),f) for x,f in zip(root,split)]
            if sweep<NEWTON-1:
                square=[halves(times(f,f)) for f in split]
                fourth=[halves(times(q,q)) for q in square]
                moving=[times(q,halves(m)) for q,m in zip(fourth,moving)]
        for j in range(n_side):
            s=i*n_side+j
            d=times(halves(root[2*j]),grads[j])
            d=times(halves(d),halves(root[2*j+1]))
            block_out[s]=block_ref[s]-rate*d[:,:BLOCK]
        return carry
    lax.fori_loop(0,grad_ref.shape[0]//n_side,one,0)
def update_step(sums, grads, left, right, blocks, io_grad, io_set, vec_set, n_side=24):
    like=lambda *xs: [jax.ShapeDtypeStruct(x.shape,F32) for x in xs]
    args=(sums,grads,left,right,blocks,io_grad,*io_set,*vec_set)
    return pl.pallas_call(partial(shampoo_kernel,beta=beta_stat,rate=rate_shampoo,eps=root_eps,n_side=n_side),
        out_shape=like(grads,grads,grads,grads,*io_set,*vec_set)+[jax.ShapeDtypeStruct((8,LANE),F32)],
        in_specs=[vmem()]*len(args),out_specs=[vmem()]*11,
        compiler_params=pltpu.CompilerParams(vmem_limit_bytes=48<<20),name="update_step")(*args)


def fits(mesh):
    return mesh.shape["seq"] == 16 and mesh.shape["opt"] == 2


def sum_everywhere(value):
    value = value + swap(value, "opt", 1)
    for bit in range((lax.axis_size("seq") - 1).bit_length()):
        value = value + swap(value, "seq", 2**bit)
    return value


def to_heads(parts):
    return lax.all_to_all(parts, "seq", 0, 0, tiled=True)


def evens_first(rows):
    return rows.reshape((rows.shape[0] // 2, 2) + rows.shape[1:]).swapaxes(0, 1).reshape(rows.shape)


def fast_device(
    features,
    tile_mask,
    lengths,
    owners,
    layer_blocks,
    stat_left,
    stat_right,
    io_weights,
    io_first,
    io_second,
    vectors,
    vec_first,
    vec_second,
):
    tok_dev = features.shape[1]
    seq_index = lax.axis_index("seq")
    core_index = lax.axis_index("opt")
    ids = jnp.stack([seq_index, core_index]).astype(jnp.int32)
    low_targets = evens_first(features[0])
    chosen_rows = evens_first(tile_mask[0]).astype(jnp.float32)[:, None]
    lengths_row = lax.dynamic_index_in_dim(lengths, core_index, 0, keepdims=False)
    places = seq_index * tok_dev + evens_first(jnp.arange(tok_dev, dtype=jnp.int32))
    shards = gather_shards(layer_blocks, io_weights, tile_mask)
    block_rows, io_rows = shard_rows(seq_index, core_index)
    qkv_weight, out_weight, in_weight, tile_counts = join_weights(
        FIRST_PLAN, 0, shards, owners, block_rows, io_rows
    )
    tile_count = tile_counts[0, 0]
    hidden, early_low, by_head = front_step(
        low_targets,
        chosen_rows,
        sine_places(slide_offsets(lengths_row, places)),
        vectors,
        in_weight,
        qkv_weight,
        HEADS,
    )
    late_owners, by_head = gate(owners, by_head)
    up_weight, down_weight, head_weight, late_counts = join_weights(
        SECOND_PLAN, 1, shards, late_owners, block_rows, io_rows
    )
    own_head, head_weight = gate(to_heads(by_head), head_weight)
    head_out, mixed_parts, head_totals = attend(lengths, ids, own_head)
    mixed_low = to_heads(mixed_parts).reshape(D, tok_dev)
    grad_middle, grad_mixed, late_low, late_rows = mlp_step(
        tile_count,
        hidden,
        mixed_low,
        low_targets,
        chosen_rows,
        vectors,
        out_weight,
        up_weight,
        down_weight,
        head_weight,
    )
    grad_head_out = to_heads(grad_mixed.reshape(HEADS, HEAD_DIM, tok_dev))
    grad_parts = attend_back(lengths, ids, own_head, grad_head_out, head_out, head_totals)
    others = [swap(operand, "opt", 1) for operand in (early_low, mixed_low, late_low)]
    own_parts, others[0], others[1] = gate(to_heads(grad_parts), others[0], others[1])
    last_low, vec_grads = input_step(
        own_parts,
        hidden,
        grad_middle,
        chosen_rows,
        vectors,
        late_rows,
        qkv_weight,
        in_weight,
    )
    others.append(swap(last_low, "opt", 1))
    operands = []
    for pair in zip((early_low, mixed_low, late_low, last_low), others):
        operands += pair
    slot_sum, io_sum, own_sums = reduce_tree(ids, owners, operands, vec_grads)
    all_sums = sum_everywhere(own_sums)
    (
        block_grads,
        left_new,
        right_new,
        blocks_new,
        io_first_new,
        io_second_new,
        io_new,
        vec_first_new,
        vec_second_new,
        vec_new,
        norms,
    ) = update_step(
        all_sums,
        slot_sum,
        stat_left,
        stat_right,
        layer_blocks,
        io_sum,
        (io_weights, io_first, io_second),
        (vectors, vec_first, vec_second),
    )
    grad_norm = norms[0, 0]
    error_sum = all_sums[vectors.shape[0], 0]
    return (
        grad_norm,
        error_sum,
        tile_count,
        block_grads,
        left_new,
        right_new,
        blocks_new,
        io_first_new,
        io_second_new,
        io_new,
        vec_first_new,
        vec_second_new,
        vec_new,
    )


def solution(mesh):
    return jax.shard_map(
        fast_device if fits(mesh) else per_device,
        mesh=mesh,
        in_specs=(
            P("opt", "seq", None),
            P("opt", "seq"),
            P(),
            P(),
            P(("seq", "opt"), None, None),
            P(("seq", "opt"), None, None),
            P(("seq", "opt"), None, None),
            P(("seq", "opt"), None, None),
            P(("seq", "opt"), None, None),
            P(("seq", "opt"), None, None),
            P(),
            P(),
            P(),
        ),
        out_specs=(
            P(),
            P(),
            P(),
            P(("seq", "opt"), None, None),
            P(("seq", "opt"), None, None),
            P(("seq", "opt"), None, None),
            P(("seq", "opt"), None, None),
            P(("seq", "opt"), None, None),
            P(("seq", "opt"), None, None),
            P(("seq", "opt"), None, None),
            P(),
            P(),
            P(),
        ),
        check_vma=False,
    )
```
